32 devices in a mesh: dp: 4 (over y, x), fsdp: 8 (over z, core).
Axes of the slice: x: 2, y: 2, z: 4, core: 2. Of those that a mesh axis runs over, the one named last changes fastest.
Arguments:
- short_tokens: bfloat16 [32, 512, 768], P(('dp', 'fsdp')), may hold values from -6 to 6
- long_tokens: bfloat16 [32, 1024, 768], P(('dp', 'fsdp')), may hold values from -6 to 6
- short_split: int32 [32], P(('dp', 'fsdp')), may hold values from 128 to 384, as said below
- long_split: int32 [32], P(('dp', 'fsdp')), may hold values from 256 to 768, as said below
- ln1_gain: bfloat16 [768], P(('dp', 'fsdp')), may hold values from 0.25 to 1.75
- ln1_bias: bfloat16 [768], P(('dp', 'fsdp')), may hold values from -4 to 4
- qkv_weight: bfloat16 [768, 2304], P(('dp', 'fsdp')), may hold values from -0.3125 to 0.3125
- qv_bias: bfloat16 [1536], P(('dp', 'fsdp')), may hold values from -4 to 4
- proj_weight: bfloat16 [768, 768], P(('dp', 'fsdp')), may hold values from -4 to 4
- proj_bias: bfloat16 [768], P(('dp', 'fsdp')), may hold values from -6 to 6
- ln2_gain: bfloat16 [768], P(('dp', 'fsdp')), may hold values from 0.25 to 1.75
- ln2_bias: bfloat16 [768], P(('dp', 'fsdp')), may hold values from -4 to 4
- fc_weight: bfloat16 [768, 3072], P(('dp', 'fsdp')), may hold values from -0.21875 to 0.21875
- fc_bias: bfloat16 [3072], P(('dp', 'fsdp')), may hold values from -4 to 4
- out_weight: bfloat16 [3072, 768], P(('dp', 'fsdp')), may hold values from -0.75 to 0.75
- out_bias: bfloat16 [768], P(('dp', 'fsdp')), may hold values from -6 to 6
- short_cotangent: bfloat16 [32, 512, 768], P(('dp', 'fsdp')), may hold values from -24 to 24
- long_cotangent: bfloat16 [32, 1024, 768], P(('dp', 'fsdp')), may hold values from -24 to 24
Outputs:
- short_output: bfloat16 [32, 512, 768], P(('dp', 'fsdp'))
- long_output: bfloat16 [32, 1024, 768], P(('dp', 'fsdp'))
- short_input_grad: float32 [32, 512, 768], P(('dp', 'fsdp'))
- long_input_grad: float32 [32, 1024, 768], P(('dp', 'fsdp'))
- ln1_gain_grad: float32 [768], P(('dp', 'fsdp'))
- ln1_bias_grad: float32 [768], P(('dp', 'fsdp'))
- qkv_weight_grad: float32 [768, 2304], P(('dp', 'fsdp'))
- qv_bias_grad: float32 [1536], P(('dp', 'fsdp'))
- proj_weight_grad: float32 [768, 768], P(('dp', 'fsdp'))
- proj_bias_grad: float32 [768], P(('dp', 'fsdp'))
- ln2_gain_grad: float32 [768], P(('dp', 'fsdp'))
- ln2_bias_grad: float32 [768], P(('dp', 'fsdp'))
- fc_weight_grad: float32 [768, 3072], P(('dp', 'fsdp'))
- fc_bias_grad: float32 [3072], P(('dp', 'fsdp'))
- out_weight_grad: float32 [3072, 768], P(('dp', 'fsdp'))
- out_bias_grad: float32 [768], P(('dp', 'fsdp'))
The draws below stay inside these ranges and needn't reach their ends.
Inputs may be any that keep to these rules, and one draw needn't show every extreme that they name: `short_split`: each short sequence packs two documents, the first ending here; some sequence takes each end of the range. `long_split`: each long sequence packs two documents, the first ending here; some sequence takes each end of the range.
All inputs are finite; a program needn't handle non-finite values.
Results may differ from the reference program's by a relative error of at most 0.013.
The reference program's roundings to bfloat16 on the way count: a program that leaves them out, or rounds other values in their place, can miss the bound.
Values may be sent and summed in bfloat16 or wider, within the bound.
A program may use at most 320 MiB of HBM per device.

```python
from functools import partial
import jax
import jax.numpy as jnp
from jax import lax

D = 768
HEAD_DIM = 64
FF = 3072
SHORT_LEN = 512
LONG_LEN = 1024
NS_ALL = 32
NL_ALL = 32


def split_points(key, seq_count, length):
    lower_end = length // 4
    upper_end = 3 * length // 4
    points = jax.random.randint(key, (seq_count,), lower_end, upper_end + 1)
    top_slot = jax.random.randint(jax.random.fold_in(key, 7), (), 0, seq_count)
    offset = jax.random.randint(jax.random.fold_in(key, 8), (), 1, seq_count)
    bottom_slot = (top_slot + offset) % seq_count
    points = points.at[top_slot].set(upper_end).at[bottom_slot].set(lower_end)
    return points.astype(jnp.int32)


def draw_short_split(key, part):
    key = jax.random.fold_in(key, 11)
    return split_points(key, NS_ALL, SHORT_LEN)


def draw_long_split(key, part):
    key = jax.random.fold_in(key, 12)
    return split_points(key, NL_ALL, LONG_LEN)


def rising_scale(key, base):
    seq_count = base.shape[0]
    ramp = 1.0 + 2.0 * jnp.arange(seq_count, dtype=jnp.float32) / (seq_count - 1)
    jitter = jax.random.uniform(jax.random.fold_in(key, 2), (seq_count,), jnp.float32, 0.8, 1.25)
    return base * (ramp * jitter)[:, None, None]


def draw_short_cotangent(key, part):
    key = jax.random.fold_in(key, 21)
    noise_key = jax.random.fold_in(key, 1)
    base = jnp.clip(jax.random.normal(noise_key, (NS_ALL, SHORT_LEN, D), jnp.float32), -6.0, 6.0)
    return rising_scale(key, base).astype(jnp.bfloat16)


def draw_long_cotangent(key, part):
    key = jax.random.fold_in(key, 22)
    noise_key = jax.random.fold_in(key, 1)
    base = jnp.clip(jax.random.normal(noise_key, (NL_ALL, LONG_LEN, D), jnp.float32), -6.0, 6.0)
    return rising_scale(key, base).astype(jnp.bfloat16)


def block_scale(own_key, extent, split, smallest, largest):
    def one(dim, shards_of):
        draws = jax.random.uniform(jax.random.fold_in(jax.random.fold_in(own_key, 6), dim), (shards_of,), jnp.float32, smallest / len(split), largest / len(split))
        return jnp.repeat(jnp.exp(draws), extent[dim] // shards_of).reshape((-1,) + (1,) * (len(extent) - dim - 1))

    gain = one(*split[0])
    for cut in split[1:]:
        gain = gain * one(*cut)
    return gain


def scatter_about(key, extent, width, limit, pieces=(), kind=jnp.bfloat16):
    array = jax.random.normal(key, extent, jnp.float32) * width
    if len(pieces) > 0:
        array = block_scale(key, extent, pieces, -0.22, 0.18) * array
    return jnp.clip(array, min=-limit, max=limit).astype(kind)


def setup_inputs(seed: int = 0) -> dict:
    streams_of = jax.random.split(jax.random.key(seed), 19)
    return {
        "short_tokens": scatter_about(streams_of[0], (NS_ALL, SHORT_LEN, D), 1.0, 6.0, ((0, 32),)),
        "long_tokens": scatter_about(streams_of[1], (NL_ALL, LONG_LEN, D), 1.0, 6.0, ((0, 32),)),
        "short_split": draw_short_split(jax.random.fold_in(streams_of[18], 71), 0),
        "long_split": draw_long_split(jax.random.fold_in(streams_of[18], 71), 0),
        "ln1_gain": jnp.clip(1.0 + 0.15 * jax.random.normal(streams_of[4], (D,), jnp.float32), 0.25, 1.75).astype(jnp.bfloat16),
        "ln1_bias": scatter_about(streams_of[5], (D,), 0.3, 4.0, ((0, 32),)),
        "qkv_weight": scatter_about(streams_of[6], (D, 3 * D), (D // 2) ** -0.5, 0.3125, ((0, 32),)),
        "qv_bias": scatter_about(streams_of[7], (2 * D,), 0.3, 4.0, ((0, 32),)),
        "proj_weight": scatter_about(streams_of[8], (D, D), (max(1, D // 384)) ** -0.5, 4.0, ((0, 32),)),
        "proj_bias": scatter_about(streams_of[9], (D,), 1.0, 6.0, ((0, 32),)),
        "ln2_gain": jnp.clip(1.0 + 0.15 * jax.random.normal(streams_of[10], (D,), jnp.float32), 0.25, 1.75).astype(jnp.bfloat16),
        "ln2_bias": scatter_about(streams_of[11], (D,), 0.3, 4.0, ((0, 32),)),
        "fc_weight": scatter_about(streams_of[12], (D, FF), D ** -0.5, 0.21875, ((0, 32),)),
        "fc_bias": scatter_about(streams_of[13], (FF,), 0.3, 4.0, ((0, 32),)),
        "out_weight": scatter_about(streams_of[14], (FF, D), (FF // 48) ** -0.5, 0.75, ((0, 32),)),
        "out_bias": scatter_about(streams_of[15], (D,), 1.0, 6.0, ((0, 32),)),
        "short_cotangent": draw_short_cotangent(jax.random.fold_in(streams_of[18], 71), 0),
        "long_cotangent": draw_long_cotangent(jax.random.fold_in(streams_of[18], 71), 0),
    }


@jax.custom_vjp
def low(v):
    return lax.optimization_barrier(v.astype(jnp.bfloat16)).astype(jnp.float32)

@jax.custom_vjp
def low_back(v):
    return v

def low_keep(v):
    return (low(v), None)

def low_pass(kept, grad):
    return (grad,)

def back_keep(v):
    return (v, None)

def back_low(kept, grad):
    return (low(grad),)
low.defvjp(low_keep, low_pass)
low_back.defvjp(back_keep, back_low)
branch_scale = 0.14433756729740643
ln_epsilon = 1e-05
neg_large = -1e+30
highest = lax.Precision.HIGHEST

def layer_norm(values, norm_gain, norm_shift):
    center = values - lax.optimization_barrier(jnp.mean(values, axis=-1, keepdims=True))
    spread = lax.optimization_barrier(jnp.mean(center * center, axis=-1, keepdims=True))
    return center * lax.rsqrt(spread + ln_epsilon) * norm_gain + norm_shift

def group_forward(params, batch):
    tokens, splits = batch
    gain_one, shift_one, qkv_weights, qv_shift, proj_weights, proj_shift, gain_two, shift_two, fc_weights, fc_shift, out_weights, out_shift = params
    seq_count, length, model_width = tokens.shape
    inputs = tokens.reshape(seq_count * length, model_width)
    norm_one = low(layer_norm(inputs, gain_one, shift_one))
    shift_full = jnp.concatenate([qv_shift[:model_width], jnp.zeros((model_width,), jnp.float32), qv_shift[model_width:]])
    mixed = low(low_back(jnp.dot(norm_one, qkv_weights, precision=highest) + shift_full))
    split_qkv = mixed.reshape(seq_count, length, 3, model_width // HEAD_DIM, HEAD_DIM)
    queries = split_qkv[:, :, 0]
    keys_all = split_qkv[:, :, 1]
    values_all = split_qkv[:, :, 2]
    scores = jnp.einsum('gqhd,gkhd->ghqk', queries, keys_all, precision=highest) * HEAD_DIM ** (-0.5)
    scores = low_back(scores)
    positions = jnp.arange(length, dtype=jnp.int32)
    causal = positions[None, :] <= positions[:, None]
    key_side = positions[None, None, :] >= splits[:, None, None]
    query_side = positions[None, :, None] >= splits[:, None, None]
    allowed = causal[None] & (key_side == query_side)
    scores = jnp.where(allowed[:, None], scores, neg_large)
    row_peak = lax.optimization_barrier(jnp.max(scores, axis=-1, keepdims=True))
    exponent = jnp.exp(scores - row_peak)
    totals = lax.optimization_barrier(jnp.sum(exponent, axis=-1, keepdims=True))
    prob_low = low(exponent / totals)
    attended = jnp.einsum('ghqk,gkhd->gqhd', prob_low, values_all, precision=highest)
    attended = low(low_back(attended.reshape(seq_count * length, model_width)))
    attn_out = low_back(jnp.dot(attended, proj_weights, precision=highest) + proj_shift)
    middle = inputs + branch_scale * attn_out
    norm_two = low(layer_norm(middle, gain_two, shift_two))
    pre_act = low_back(jnp.dot(norm_two, fc_weights, precision=highest) + fc_shift)
    activated = low(jax.nn.gelu(pre_act, approximate=True))
    mlp_out = low_back(jnp.dot(activated, out_weights, precision=highest) + out_shift)
    return (middle + branch_scale * mlp_out).reshape(seq_count, length, model_width)

def run_group(params, tokens, splits):
    seq_count, length, model_width = tokens.shape
    together = min(seq_count, max(1, 2048 // length))
    stacked = tokens.reshape(seq_count // together, together, length, model_width)
    split_stack = splits.reshape(seq_count // together, together)
    outputs = lax.map(jax.checkpoint(partial(group_forward, params)), (stacked, split_stack))
    return outputs.reshape(seq_count, length, model_width)

def reference(short_tokens, long_tokens, short_split, long_split, ln1_gain, ln1_bias, qkv_weight, qv_bias, proj_weight, proj_bias, ln2_gain, ln2_bias, fc_weight, fc_bias, out_weight, out_bias, short_cotangent, long_cotangent):
    params = tuple((weight_arg.astype(jnp.float32) for weight_arg in (ln1_gain, ln1_bias, qkv_weight, qv_bias, proj_weight, proj_bias, ln2_gain, ln2_bias, fc_weight, fc_bias, out_weight, out_bias)))

    def whole_layer(layer_params, short_inputs, long_inputs):
        return (run_group(layer_params, short_inputs, short_split), run_group(layer_params, long_inputs, long_split))
    outputs, pull_back = jax.vjp(whole_layer, params, short_tokens.astype(jnp.float32), long_tokens.astype(jnp.float32))
    param_grads, short_grad, long_grad = pull_back((short_cotangent.astype(jnp.float32), long_cotangent.astype(jnp.float32)))
    return (outputs[0].astype(jnp.bfloat16), outputs[1].astype(jnp.bfloat16), short_grad, long_grad, param_grads[0], param_grads[1], param_grads[2], param_grads[3], param_grads[4], param_grads[5], param_grads[6], param_grads[7], param_grads[8], param_grads[9], param_grads[10], param_grads[11])
```

```python
import functools

import jax
import jax.numpy as jnp
from jax import lax
from jax.experimental import pallas as pl
from jax.experimental.pallas import tpu as pltpu
from jax.sharding import PartitionSpec as P

F32 = jnp.float32
BF16 = jnp.bfloat16
D = 768
FF = 3072
HEAD_DIM = 64
PAIRS = D // 128
TILE = 256
BRANCH = 0.14433756729740643
EPS = 1e-05
NEG = -1e30
VMEM_LIMIT = 60 * 2**20

LN1G, LN1B, QB, VB, PROJB, LN2G, LN2B, OUTB, FCB = 0, 1, 2, 3, 4, 5, 6, 7, 8


def dot(a, b):
    return jnp.dot(a, b, preferred_element_type=F32)


def dot_nt(a, b):
    return lax.dot_general(a, b, (((1,), (1,)), ((), ())), preferred_element_type=F32)


def dot_tn(a, b):
    return lax.dot_general(a, b, (((0,), (0,)), ((), ())), preferred_element_type=F32)


def normalize(x):
    center = x - jnp.mean(x, axis=-1, keepdims=True)
    rstd = lax.rsqrt(jnp.mean(center * center, axis=-1, keepdims=True) + EPS)
    return center * rstd, rstd


def norm_backward(g, n, rstd, gain):
    e = g * gain
    return rstd * (
        e
        - jnp.mean(e, axis=-1, keepdims=True)
        - n * jnp.mean(e * n, axis=-1, keepdims=True)
    )


def rows_of(base, tile):
    return pl.ds(pl.multiple_of(base + tile * TILE, TILE), TILE)


def lanes_of(start):
    return pl.ds(pl.multiple_of(start, 128), 128)


def group_refs(short, long):
    return ((short, 0), (long, short.shape[0]))


def qkv_tile(x_ref, table_ref, w_ref, a1_ref, qkv_ref, base, t):
    n, _ = normalize(x_ref[rows_of(0, t), :].astype(F32))
    a1 = (n * table_ref[LN1G : LN1G + 1, :] + table_ref[LN1B : LN1B + 1, :]).astype(BF16)
    rows = rows_of(base, t)
    a1_ref[rows, :] = a1
    for part, bias in ((0, QB), (1, None), (2, VB)):
        cols = slice(part * D, (part + 1) * D)
        out = dot(a1, w_ref[:, cols])
        if bias is not None:
            out = out + table_ref[bias : bias + 1, :]
        qkv_ref[rows, cols] = out.astype(BF16)


def attend_pair(split, qkv_ref, att_ref, lse_ref, base, length, pair):
    first = lax.broadcasted_iota(jnp.int32, (TILE, 128), 1) < HEAD_DIM
    head_lane = lax.broadcasted_iota(jnp.int32, (TILE, 128), 1)
    for qb in range(length // TILE):
        qrows = slice(base + qb * TILE, base + (qb + 1) * TILE)
        keys = (qb + 1) * TILE
        krows = slice(base, base + keys)
        q_pair = qkv_ref[qrows, lanes_of(pair * 128)] * BF16(HEAD_DIM**-0.5)
        k_pair = qkv_ref[krows, lanes_of(D + pair * 128)]
        v_pair = qkv_ref[krows, lanes_of(2 * D + pair * 128)]
        q_pos = qb * TILE + lax.broadcasted_iota(jnp.int32, (TILE, 1), 0)
        low = jnp.where(q_pos >= split, split, 0)
        k_pos = lax.broadcasted_iota(jnp.int32, (TILE, keys), 1)
        visible = (k_pos >= low) & (k_pos <= q_pos)
        outs = []
        lse_new = lse_ref[qrows, :]
        for half in (0, 1):
            mine = first if half == 0 else ~first
            s = dot_nt(jnp.where(mine, q_pair, BF16(0)), k_pair)
            s = jnp.where(visible, s, NEG)
            peak = jnp.max(s, axis=-1, keepdims=True)
            e = jnp.exp(s - peak)
            total = jnp.sum(e, axis=-1, keepdims=True)
            p = (e * (1.0 / total)).astype(BF16)
            outs.append(dot(p, v_pair))
            lse_new = jnp.where(head_lane == 2 * pair + half, peak + jnp.log(total), lse_new)
        lse_ref[qrows, :] = lse_new
        att_ref[qrows, lanes_of(pair * 128)] = jnp.where(first, outs[0], outs[1]).astype(BF16)


def mid_tile(x_ref, table_ref, w_ref, att_ref, mid_ref, base, t):
    rows = rows_of(base, t)
    out = dot(att_ref[rows, :], w_ref[:, 3 * D : 4 * D]) + table_ref[PROJB : PROJB + 1, :]
    mid_ref[rows, :] = x_ref[rows_of(0, t), :].astype(F32) + BRANCH * out


def forward_kernel(
    ssplit, lsplit, xs, xl, table_ref, w_ref, a1_ref, qkv_ref, att_ref, lse_t_ref, mid_ref, lse_ref
):
    for x_ref, base in group_refs(xs, xl):
        lax.fori_loop(
            0,
            x_ref.shape[0] // TILE,
            lambda t, c: (qkv_tile(x_ref, table_ref, w_ref, a1_ref, qkv_ref, base, t), c)[1],
            0,
        )
    lse_ref[...] = jnp.zeros_like(lse_ref)

    def pair_step(pair, c):
        attend_pair(ssplit[0], qkv_ref, att_ref, lse_ref, 0, xs.shape[0], pair)
        attend_pair(lsplit[0], qkv_ref, att_ref, lse_ref, xs.shape[0], xl.shape[0], pair)
        return c

    lax.fori_loop(0, PAIRS, pair_step, 0)
    lse_t_ref[...] = jnp.transpose(lse_ref[...])[:16, :]
    for x_ref, base in group_refs(xs, xl):
        lax.fori_loop(
            0,
            x_ref.shape[0] // TILE,
            lambda t, c: (mid_tile(x_ref, table_ref, w_ref, att_ref, mid_ref, base, t), c)[1],
            0,
        )


VM = pl.BlockSpec(memory_space=pltpu.VMEM)
SM = pl.BlockSpec(memory_space=pltpu.SMEM)


def forward_local(ssplit, lsplit, xs, xl, table, w_attn):
    rows = xs.shape[0] + xl.shape[0]
    return pl.pallas_call(
        forward_kernel,
        out_shape=(
            jax.ShapeDtypeStruct((rows, D), BF16),
            jax.ShapeDtypeStruct((rows, 3 * D), BF16),
            jax.ShapeDtypeStruct((rows, D), BF16),
            jax.ShapeDtypeStruct((16, rows), F32),
            jax.ShapeDtypeStruct((rows, D), F32),
        ),
        in_specs=[SM, SM, VM, VM, VM, VM],
        out_specs=[VM] * 5,
        scratch_shapes=[pltpu.VMEM((rows, 128), F32)],
        compiler_params=pltpu.CompilerParams(vmem_limit_bytes=VMEM_LIMIT),
        name="attention_forward",
    )(ssplit, lsplit, xs, xl, table, w_attn)


GELU_A = 0.7978845608028654
GELU_B = 0.044715


def mlp_tile(mid, g_out, table_ref, wf_ref, wo_ref):
    n2, rstd = normalize(mid)
    gain = table_ref[LN2G : LN2G + 1, :]
    a2 = (n2 * gain + table_ref[LN2B : LN2B + 1, :]).astype(BF16)
    g_mlp = (BRANCH * g_out).astype(BF16)
    out = None
    g_a2 = None
    acts, g_pres = [], []
    for j in range(FF // D):
        cols = slice(j * D, (j + 1) * D)
        pre = dot(a2, wf_ref[:, cols]) + table_ref[FCB + j : FCB + j + 1, :]
        g_act = dot_nt(g_mlp, wo_ref[cols, :])
        square = pre * pre
        t = jnp.tanh(pre * (GELU_A + (GELU_A * GELU_B) * square))
        half = 0.5 + 0.5 * t
        act = (pre * half).astype(BF16)
        slope = half + pre * (0.5 - 0.5 * t * t) * (GELU_A + (3 * GELU_A * GELU_B) * square)
        g_pre = (g_act * slope).astype(BF16)
        acts.append(act)
        g_pres.append(g_pre)
        part = dot(act, wo_ref[cols, :])
        out = part if out is None else out + part
        part = dot_nt(g_pre, wf_ref[:, cols])
        g_a2 = part if g_a2 is None else g_a2 + part
    out = mid + BRANCH * (out + table_ref[OUTB : OUTB + 1, :])
    g_mid = g_out + norm_backward(g_a2, n2, rstd, gain)
    return out, g_mid, a2, g_mlp, acts, g_pres, g_a2, n2


def colsum(x):
    return jnp.sum(x, axis=0, keepdims=True)


def mlp_kernel(
    n_tiles,
    slabs,
    mid_ref,
    cs_ref,
    cl_ref,
    table_ref,
    wf_ref,
    wo_ref,
    os_ref,
    ol_ref,
    g_mid_ref,
    sums_ref,
    dwf_ref,
    dwo_ref,
    a2_ref,
    g_mlp_ref,
    act_ref,
    g_pre_ref,
):
    step = pl.program_id(0)
    short_tiles = n_tiles[0]
    tiles = n_tiles[0] + n_tiles[1]

    @pl.when(step == 0)
    def _():
        sums_ref[...] = jnp.zeros_like(sums_ref)

    @pl.when(step < tiles)
    def _():
        cot = jnp.where(step < short_tiles, cs_ref[...], cl_ref[...]).astype(F32)
        out, g_mid, a2, g_mlp, acts, g_pres, g_a2, n2 = mlp_tile(
            mid_ref[...], cot, table_ref, wf_ref, wo_ref
        )
        out = out.astype(BF16)

        @pl.when(step < short_tiles)
        def _():
            os_ref[...] = out

        @pl.when(step >= short_tiles)
        def _():
            ol_ref[...] = out

        g_mid_ref[...] = g_mid
        rows = rows_of(0, step)
        a2_ref[rows, :] = a2
        g_mlp_ref[rows, :] = g_mlp
        sums_ref[0:1, :] += colsum(g_a2 * n2)
        sums_ref[1:2, :] += colsum(g_a2)
        sums_ref[2:3, :] += colsum(g_mlp.astype(F32))
        for j in range(FF // D):
            act_ref[rows, j * D : (j + 1) * D] = acts[j]
            g_pre_ref[rows, j * D : (j + 1) * D] = g_pres[j]
            sums_ref[3 + j : 4 + j, :] += colsum(g_pres[j].astype(F32))

    for j in range(4):

        @pl.when(step == tiles + j)
        def _(j=j):
            res = dot_tn(act_ref[:, j * D : (j + 1) * D], g_mlp_ref[...])
            if slabs:
                dwo_ref[...] = res.astype(BF16).reshape(dwo_ref.shape)
            else:
                dwo_ref[...] = res

    for j in range(2 if slabs else 4):

        @pl.when(step == tiles + 4 + j)
        def _(j=j):
            if slabs:
                dev = D // 24
                left = dot_tn(a2_ref[...], g_pre_ref[:, 2 * j * D : (2 * j + 1) * D])
                right = dot_tn(a2_ref[...], g_pre_ref[:, (2 * j + 1) * D : (2 * j + 2) * D])
                both = jnp.concatenate(
                    [left.reshape(dev, 24, D), right.reshape(dev, 24, D)], axis=1
                )
                dwf_ref[...] = both.astype(BF16)
            else:
                dwf_ref[...] = dot_tn(a2_ref[...], g_pre_ref[:, j * D : (j + 1) * D])


def mlp_local(mid, cs, cl, table, w_fc, w_out, slabs):
    rows = mid.shape[0]
    ns, nl = cs.shape[0] // TILE, cl.shape[0] // TILE
    tiles = ns + nl
    steps = tiles + (6 if slabs else 8)
    whole = lambda shape: pl.BlockSpec(shape, lambda i: (0, 0), pipeline_mode=pl.Buffered(1))
    tile = lambda f: pl.BlockSpec((TILE, D), f)
    short_at = lambda i: (jnp.minimum(i, ns - 1), 0)
    long_at = lambda i: (jnp.clip(i - ns, 0, nl - 1), 0)
    all_at = lambda i: (jnp.minimum(i, tiles - 1), 0)
    if slabs:
        dev = D // 24
        dwo_shape = jax.ShapeDtypeStruct((dev, 96, D), BF16)
        dwo_spec = pl.BlockSpec((dev // 4, 96, D), lambda i: (jnp.clip(i - tiles, 0, 3), 0, 0))
        dwf_shape = jax.ShapeDtypeStruct((dev, 96, D), BF16)
        dwf_spec = pl.BlockSpec((dev, 48, D), lambda i: (0, jnp.clip(i - tiles - 4, 0, 1), 0))
    else:
        dwo_shape = jax.ShapeDtypeStruct((FF, D), F32)
        dwo_spec = pl.BlockSpec((D, D), lambda i: (jnp.clip(i - tiles, 0, 3), 0))
        dwf_shape = jax.ShapeDtypeStruct((D, FF), F32)
        dwf_spec = pl.BlockSpec((D, D), lambda i: (0, jnp.clip(i - tiles - 4, 0, 3)))
    return pl.pallas_call(
        functools.partial(mlp_kernel, (ns, nl), slabs),
        grid=(steps,),
        out_shape=(
            jax.ShapeDtypeStruct(cs.shape, BF16),
            jax.ShapeDtypeStruct(cl.shape, BF16),
            jax.ShapeDtypeStruct((rows, D), F32),
            jax.ShapeDtypeStruct((8, D), F32),
            dwf_shape,
            dwo_shape,
        ),
        in_specs=[
            tile(all_at),
            tile(short_at),
            tile(long_at),
            whole(table.shape),
            whole(w_fc.shape),
            whole(w_out.shape),
        ],
        out_specs=[
            tile(short_at),
            tile(long_at),
            tile(all_at),
            pl.BlockSpec((8, D), lambda i: (0, 0)),
            dwf_spec,
            dwo_spec,
        ],
        scratch_shapes=[
            pltpu.VMEM((rows, D), BF16),
            pltpu.VMEM((rows, D), BF16),
            pltpu.VMEM((rows, FF), BF16),
            pltpu.VMEM((rows, FF), BF16),
        ],
        compiler_params=pltpu.CompilerParams(vmem_limit_bytes=VMEM_LIMIT),
        name="mlp",
    )(mid, cs, cl, table, w_fc, w_out)


def proj_back_tile(g_mid_ref, w_ref, g_attn_ref, g_att_ref, sums_ref, t):
    rows = rows_of(0, t)
    g_attn = (BRANCH * g_mid_ref[rows, :]).astype(BF16)
    g_attn_ref[rows, :] = g_attn
    g_att_ref[rows, :] = dot_nt(g_attn, w_ref[:, 3 * D : 4 * D]).astype(BF16)
    sums_ref[PROJB : PROJB + 1, :] += colsum(g_attn.astype(F32))


def attend_back_pair(split, qkv_ref, g_att_ref, lse_t_ref, g_qkv_ref, dk_ref, dv_ref, base, length, pair):
    first = lax.broadcasted_iota(jnp.int32, (TILE, 128), 1) < HEAD_DIM
    dk_ref[0:length, :] = jnp.zeros((length, 128), F32)
    dv_ref[0:length, :] = jnp.zeros((length, 128), F32)
    for qb in range(length // TILE):
        qrows = slice(base + qb * TILE, base + (qb + 1) * TILE)
        keys = (qb + 1) * TILE
        krows = slice(base, base + keys)
        q_pair = qkv_ref[qrows, lanes_of(pair * 128)] * BF16(HEAD_DIM**-0.5)
        g_pair = g_att_ref[qrows, lanes_of(pair * 128)]
        k_pair = qkv_ref[krows, lanes_of(D + pair * 128)]
        v_pair = qkv_ref[krows, lanes_of(2 * D + pair * 128)]
        q_pos = qb * TILE + lax.broadcasted_iota(jnp.int32, (1, TILE), 1)
        low = jnp.where(q_pos >= split, split, 0)
        k_pos = lax.broadcasted_iota(jnp.int32, (keys, TILE), 0)
        visible = (k_pos >= low) & (k_pos <= q_pos)
        dqs = []
        dk = dk_ref[0:keys, :]
        dv = dv_ref[0:keys, :]
        for half in (0, 1):
            mine = first if half == 0 else ~first
            q_half = jnp.where(mine, q_pair, BF16(0))
            g_half = jnp.where(mine, g_pair, BF16(0))
            lse = lse_t_ref[pl.ds(2 * pair + half, 1), qrows]
            s = jnp.where(visible, dot_nt(k_pair, q_half), NEG)
            p = jnp.exp(s - lse)
            dp = dot_nt(v_pair, g_half)
            inner = jnp.sum(p * dp, axis=0, keepdims=True)
            ds = (p * (dp - inner)).astype(BF16)
            dv = dv + dot(p.astype(BF16), g_half)
            dk = dk + dot(ds, q_half)
            dqs.append(dot_tn(ds, k_pair))
        dk_ref[0:keys, :] = dk
        dv_ref[0:keys, :] = dv
        dq = jnp.where(first, dqs[0], dqs[1]) * (HEAD_DIM**-0.5)
        g_qkv_ref[qrows, lanes_of(pair * 128)] = dq.astype(BF16)
    all_rows = slice(base, base + length)
    g_qkv_ref[all_rows, lanes_of(D + pair * 128)] = dk_ref[0:length, :].astype(BF16)
    g_qkv_ref[all_rows, lanes_of(2 * D + pair * 128)] = dv_ref[0:length, :].astype(BF16)


def ln1_back_tile(x_ref, g_mid_ref, table_ref, w_ref, g_qkv_ref, gx_ref, sums_ref, base, t):
    rows = rows_of(base, t)
    g_qkv = g_qkv_ref[rows, :]
    g_a1 = dot_nt(g_qkv, w_ref[:, 0 : 3 * D])
    own = rows_of(0, t)
    n, rstd = normalize(x_ref[own, :].astype(F32))
    gx_ref[own, :] = g_mid_ref[rows, :] + norm_backward(
        g_a1, n, rstd, table_ref[LN1G : LN1G + 1, :]
    )
    sums_ref[LN1G : LN1G + 1, :] += colsum(g_a1 * n)
    sums_ref[LN1B : LN1B + 1, :] += colsum(g_a1)
    sums_ref[QB : QB + 1, :] += colsum(g_qkv[:, 0:D].astype(F32))
    sums_ref[VB : VB + 1, :] += colsum(g_qkv[:, 2 * D : 3 * D].astype(F32))


def backward_kernel(
    ssplit,
    lsplit,
    xs,
    xl,
    table_ref,
    w_ref,
    a1_ref,
    qkv_ref,
    att_ref,
    lse_t_ref,
    g_mid_ref,
    gxs_ref,
    gxl_ref,
    dwp_ref,
    dwq_ref,
    sums_ref,
    g_attn_ref,
    g_att_ref,
    g_qkv_ref,
    dk_ref,
    dv_ref,
):
    sums_ref[...] = jnp.zeros_like(sums_ref)
    rows = xs.shape[0] + xl.shape[0]
    lax.fori_loop(
        0,
        rows // TILE,
        lambda t, c: (
            proj_back_tile(g_mid_ref, w_ref, g_attn_ref, g_att_ref, sums_ref, t),
            c,
        )[1],
        0,
    )
    dwp_ref[...] = dot_tn(att_ref[...], g_attn_ref[...])

    def pair_step(pair, c):
        for split, x_ref, base in ((ssplit[0], xs, 0), (lsplit[0], xl, xs.shape[0])):
            attend_back_pair(
                split, qkv_ref, g_att_ref, lse_t_ref, g_qkv_ref, dk_ref, dv_ref, base, x_ref.shape[0], pair
            )
        return c

    lax.fori_loop(0, PAIRS, pair_step, 0)
    for j in range(3):
        dwq_ref[:, j * D : (j + 1) * D] = dot_tn(a1_ref[...], g_qkv_ref[:, j * D : (j + 1) * D])
    for x_ref, gx_ref, base in ((xs, gxs_ref, 0), (xl, gxl_ref, xs.shape[0])):
        lax.fori_loop(
            0,
            x_ref.shape[0] // TILE,
            lambda t, c: (
                ln1_back_tile(
                    x_ref, g_mid_ref, table_ref, w_ref, g_qkv_ref, gx_ref, sums_ref, base, t
                ),
                c,
            )[1],
            0,
        )


def backward_local(ssplit, lsplit, xs, xl, table, w_attn, a1, qkv, att, lse_t, g_mid):
    rows = xs.shape[0] + xl.shape[0]
    return pl.pallas_call(
        backward_kernel,
        out_shape=(
            jax.ShapeDtypeStruct(xs.shape, F32),
            jax.ShapeDtypeStruct(xl.shape, F32),
            jax.ShapeDtypeStruct((D, D), F32),
            jax.ShapeDtypeStruct((D, 3 * D), F32),
            jax.ShapeDtypeStruct((8, D), F32),
        ),
        in_specs=[SM, SM] + [VM] * 9,
        out_specs=[VM] * 5,
        scratch_shapes=[
            pltpu.VMEM((rows, D), BF16),
            pltpu.VMEM((rows, D), BF16),
            pltpu.VMEM((rows, 3 * D), BF16),
            pltpu.VMEM((xl.shape[0], 128), F32),
            pltpu.VMEM((xl.shape[0], 128), F32),
        ],
        compiler_params=pltpu.CompilerParams(vmem_limit_bytes=VMEM_LIMIT),
        name="attention_backward",
    )(ssplit, lsplit, xs, xl, table, w_attn, a1, qkv, att, lse_t, g_mid)


AXES = ("dp", "fsdp")


def gather(x, axis=0):
    return lax.all_gather(x, AXES, axis=axis, tiled=True)


def scatter(x):
    return lax.psum_scatter(x, AXES, scatter_dimension=0, tiled=True)


def general(args, devices):
    (st, lt, ss, ls, ln1g, ln1b, wqkv, qvb, wproj, projb, ln2g, ln2b, wfc, fcb, wout, outb, sc, lc) = args
    xs, xl = st.reshape(-1, D), lt.reshape(-1, D)
    cs, cl = sc.reshape(-1, D), lc.reshape(-1, D)
    vectors = (ln1g, ln1b, qvb, projb, ln2g, ln2b, outb, fcb)
    sizes = [v.shape[0] for v in vectors]
    every = lax.all_gather(jnp.concatenate(vectors), AXES, axis=0)
    starts = [sum(sizes[:i]) for i in range(len(sizes))]
    full = [every[:, s : s + n].reshape(-1, D) for s, n in zip(starts, sizes)]
    table = jnp.concatenate(full + [jnp.zeros((4, D), BF16)]).astype(F32)
    w_attn = gather(jnp.concatenate([wqkv, wproj], axis=1))
    w_fc, w_out = gather(wfc), gather(wout)
    a1, qkv, att, lse_t, mid = forward_local(ss, ls, xs, xl, table, w_attn)
    out_s, out_l, g_mid, sums2, dwf, dwo = mlp_local(mid, cs, cl, table, w_fc, w_out, False)
    gxs, gxl, dwp, dwq, sums1 = backward_local(
        ss, ls, xs, xl, table, w_attn, a1, qkv, att, lse_t, g_mid
    )
    rs = lambda x: x.reshape(devices, -1)
    small = jnp.concatenate(
        [
            rs(sums1[0]),
            rs(sums1[1]),
            rs(sums1[2:4]),
            rs(sums1[4]),
            rs(sums2[0]),
            rs(sums2[1]),
            rs(sums2[2]),
            rs(sums2[3:7]),
        ],
        axis=1,
    )
    small = scatter(small)[0]
    parts = [small[s : s + n] for s, n in zip(starts, sizes)]
    d_ln1g, d_ln1b, d_qvb, d_projb, d_ln2g, d_ln2b, d_outb, d_fcb = parts
    return (
        out_s.reshape(st.shape),
        out_l.reshape(lt.shape),
        gxs.reshape(st.shape),
        gxl.reshape(lt.shape),
        d_ln1g,
        d_ln1b,
        scatter(dwq),
        d_qvb,
        scatter(dwp),
        d_projb,
        d_ln2g,
        d_ln2b,
        scatter(dwf),
        d_fcb,
        scatter(dwo),
        d_outb,
    )


def per_device(devices, *args):
    return general(args, devices)


def solution(mesh):
    vec, mat, seq = P(AXES), P(AXES, None), P(AXES, None, None)
    in_specs = (seq, seq, vec, vec) + (vec, vec, mat, vec, mat, vec) * 1 + (vec, vec, mat, vec, mat, vec) + (seq, seq)
    out_specs = (seq,) * 4 + (vec, vec, mat, vec, mat, vec) * 2
    return jax.shard_map(
        functools.partial(per_device, mesh.size),
        mesh=mesh,
        in_specs=in_specs,
        out_specs=out_specs,
        check_vma=False,
    )
```

```python
import functools

import jax
import jax.numpy as jnp
from jax import lax
from jax.experimental import pallas as pl
from jax.experimental.pallas import tpu as pltpu
from jax.sharding import PartitionSpec as P

F32 = jnp.float32
BF16 = jnp.bfloat16
D = 768
FF = 3072
HEAD_DIM = 64
PAIRS = D // 128
TILE = 256
BRANCH = 0.14433756729740643
EPS = 1e-05
NEG = -1e30
VMEM_LIMIT = 60 * 2**20

LN1G, LN1B, QB, VB, PROJB, LN2G, LN2B, OUTB, FCB = 0, 1, 2, 3, 4, 5, 6, 7, 8


def dot(a, b):
    return jnp.dot(a, b, preferred_element_type=F32)


def dot_nt(a, b):
    return lax.dot_general(a, b, (((1,), (1,)), ((), ())), preferred_element_type=F32)


def dot_tn(a, b):
    return lax.dot_general(a, b, (((0,), (0,)), ((), ())), preferred_element_type=F32)


def normalize(x):
    center = x - jnp.mean(x, axis=-1, keepdims=True)
    rstd = lax.rsqrt(jnp.mean(center * center, axis=-1, keepdims=True) + EPS)
    return center * rstd, rstd


def norm_backward(g, n, rstd, gain):
    e = g * gain
    return rstd * (
        e
        - jnp.mean(e, axis=-1, keepdims=True)
        - n * jnp.mean(e * n, axis=-1, keepdims=True)
    )


def rows_of(base, tile):
    return pl.ds(pl.multiple_of(base + tile * TILE, TILE), TILE)


def lanes_of(start):
    return pl.ds(pl.multiple_of(start, 128), 128)


def loop(count, body):
    lax.fori_loop(0, count, lambda i, c: (body(i), c)[1], 0)


def group_refs(short, long):
    return ((short, 0), (long, short.shape[0]))


def norm_tile(x_ref, table_ref, a1_ref, base, t):
    n, _ = normalize(x_ref[rows_of(0, t), :].astype(F32))
    a1 = n * table_ref[LN1G : LN1G + 1, :] + table_ref[LN1B : LN1B + 1, :]
    a1_ref[rows_of(base, t), :] = a1.astype(BF16)


def qkv_tile(table_ref, w_ref, a1_ref, qkv_ref, t):
    rows = rows_of(0, t)
    a1 = a1_ref[rows, :]
    for part, bias in ((0, QB), (1, None), (2, VB)):
        cols = slice(part * D, (part + 1) * D)
        out = dot(a1, w_ref[:, cols])
        if bias is not None:
            out = out + table_ref[bias : bias + 1, :]
        qkv_ref[rows, cols] = out.astype(BF16)


def attend_pair(split, qkv_ref, att_ref, lse_ref, base, length, pair):
    first = lax.broadcasted_iota(jnp.int32, (TILE, 128), 1) < HEAD_DIM
    head_lane = lax.broadcasted_iota(jnp.int32, (TILE, 128), 1)
    for qb in range(length // TILE):
        qrows = slice(base + qb * TILE, base + (qb + 1) * TILE)
        keys = (qb + 1) * TILE
        krows = slice(base, base + keys)
        q_pair = qkv_ref[qrows, lanes_of(pair * 128)] * BF16(HEAD_DIM**-0.5)
        k_pair = qkv_ref[krows, lanes_of(D + pair * 128)]
        v_pair = qkv_ref[krows, lanes_of(2 * D + pair * 128)]
        q_pos = qb * TILE + lax.broadcasted_iota(jnp.int32, (TILE, 1), 0)
        low = jnp.where(q_pos >= split, split, 0)
        k_pos = lax.broadcasted_iota(jnp.int32, (TILE, keys), 1)
        visible = (k_pos >= low) & (k_pos <= q_pos)
        outs = []
        lse_new = lse_ref[qrows, :]
        for half in (0, 1):
            mine = first if half == 0 else ~first
            s = dot_nt(jnp.where(mine, q_pair, BF16(0)), k_pair)
            s = jnp.where(visible, s, NEG)
            peak = jnp.max(s, axis=-1, keepdims=True)
            e = jnp.exp(s - peak)
            total = jnp.sum(e, axis=-1, keepdims=True)
            p = (e * (1.0 / total)).astype(BF16)
            outs.append(dot(p, v_pair))
            lse_new = jnp.where(head_lane == 2 * pair + half, peak + jnp.log(total), lse_new)
        lse_ref[qrows, :] = lse_new
        att_ref[qrows, lanes_of(pair * 128)] = jnp.where(first, outs[0], outs[1]).astype(BF16)


def mid_tile(x_ref, table_ref, w_ref, att_ref, mid_ref, base, t):
    rows = rows_of(base, t)
    out = dot(att_ref[rows, :], w_ref[:, 3 * D : 4 * D]) + table_ref[PROJB : PROJB + 1, :]
    mid_ref[rows, :] = x_ref[rows_of(0, t), :].astype(F32) + BRANCH * out


def forward_kernel(
    ssplit, lsplit, xs, xl, table_ref, w_ref, a1_ref, qkv_ref, att_ref, lse_t_ref, mid_ref, lse_ref
):
    for x_ref, base in group_refs(xs, xl):
        loop(x_ref.shape[0] // TILE, lambda t: norm_tile(x_ref, table_ref, a1_ref, base, t))
    loop(a1_ref.shape[0] // TILE, lambda t: qkv_tile(table_ref, w_ref, a1_ref, qkv_ref, t))
    lse_ref[...] = jnp.zeros_like(lse_ref)

    def pair_step(pair, c):
        attend_pair(ssplit[0], qkv_ref, att_ref, lse_ref, 0, xs.shape[0], pair)
        attend_pair(lsplit[0], qkv_ref, att_ref, lse_ref, xs.shape[0], xl.shape[0], pair)
        return c

    lax.fori_loop(0, PAIRS, pair_step, 0)
    lse_t_ref[...] = jnp.transpose(lse_ref[...])[:16, :]
    for x_ref, base in group_refs(xs, xl):
        lax.fori_loop(
            0,
            x_ref.shape[0] // TILE,
            lambda t, c: (mid_tile(x_ref, table_ref, w_ref, att_ref, mid_ref, base, t), c)[1],
            0,
        )


VM = pl.BlockSpec(memory_space=pltpu.VMEM)
SM = pl.BlockSpec(memory_space=pltpu.SMEM)


def forward_local(ssplit, lsplit, xs, xl, table, w_attn):
    rows = xs.shape[0] + xl.shape[0]
    return pl.pallas_call(
        forward_kernel,
        out_shape=(
            jax.ShapeDtypeStruct((rows, D), BF16),
            jax.ShapeDtypeStruct((rows, 3 * D), BF16),
            jax.ShapeDtypeStruct((rows, D), BF16),
            jax.ShapeDtypeStruct((16, rows), F32),
            jax.ShapeDtypeStruct((rows, D), F32),
        ),
        in_specs=[SM, SM, VM, VM, VM, VM],
        out_specs=[VM] * 5,
        scratch_shapes=[pltpu.VMEM((rows, 128), F32)],
        compiler_params=pltpu.CompilerParams(vmem_limit_bytes=VMEM_LIMIT),
        name="attention_forward",
    )(ssplit, lsplit, xs, xl, table, w_attn)


GELU_A = 0.7978845608028654
GELU_B = 0.044715


def mlp_tile(mid, g_out, table_ref, wf_ref, wo_ref):
    n2, rstd = normalize(mid)
    gain = table_ref[LN2G : LN2G + 1, :]
    a2 = (n2 * gain + table_ref[LN2B : LN2B + 1, :]).astype(BF16)
    g_mlp = (BRANCH * g_out).astype(BF16)
    out = None
    g_a2 = None
    acts, g_pres = [], []
    for j in range(FF // D):
        cols = slice(j * D, (j + 1) * D)
        pre = dot(a2, wf_ref[:, cols]) + table_ref[FCB + j : FCB + j + 1, :]
        g_act = dot_nt(g_mlp, wo_ref[cols, :])
        square = pre * pre
        t = jnp.tanh(pre * (GELU_A + (GELU_A * GELU_B) * square))
        half = 0.5 + 0.5 * t
        act = (pre * half).astype(BF16)
        slope = half + pre * (0.5 - 0.5 * t * t) * (GELU_A + (3 * GELU_A * GELU_B) * square)
        g_pre = (g_act * slope).astype(BF16)
        acts.append(act)
        g_pres.append(g_pre)
        part = dot(act, wo_ref[cols, :])
        out = part if out is None else out + part
        part = dot_nt(g_pre, wf_ref[:, cols])
        g_a2 = part if g_a2 is None else g_a2 + part
    out = mid + BRANCH * (out + table_ref[OUTB : OUTB + 1, :])
    g_mid = g_out + norm_backward(g_a2, n2, rstd, gain)
    return out, g_mid, a2, g_mlp, acts, g_pres, g_a2, n2


def colsum(x):
    return jnp.sum(x, axis=0, keepdims=True)


def mlp_kernel(
    n_tiles,
    slabs,
    mid_ref,
    cs_ref,
    cl_ref,
    table_ref,
    wf_ref,
    wo_ref,
    os_ref,
    ol_ref,
    g_mid_ref,
    sums_ref,
    dwf_ref,
    dwo_ref,
    a2_ref,
    g_mlp_ref,
    act_ref,
    g_pre_ref,
):
    step = pl.program_id(0)
    short_tiles = n_tiles[0]
    tiles = n_tiles[0] + n_tiles[1]

    @pl.when(step == 0)
    def _():
        sums_ref[...] = jnp.zeros_like(sums_ref)

    @pl.when(step < tiles)
    def _():
        cot = jnp.where(step < short_tiles, cs_ref[...], cl_ref[...]).astype(F32)
        out, g_mid, a2, g_mlp, acts, g_pres, g_a2, n2 = mlp_tile(
            mid_ref[...], cot, table_ref, wf_ref, wo_ref
        )
        out = out.astype(BF16)

        @pl.when(step < short_tiles)
        def _():
            os_ref[...] = out

        @pl.when(step >= short_tiles)
        def _():
            ol_ref[...] = out

        g_mid_ref[...] = g_mid
        rows = rows_of(0, step)
        a2_ref[rows, :] = a2
        g_mlp_ref[rows, :] = g_mlp
        sums_ref[0:1, :] += colsum(g_a2 * n2)
        sums_ref[1:2, :] += colsum(g_a2)
        sums_ref[2:3, :] += colsum(g_mlp.astype(F32))
        for j in range(FF // D):
            act_ref[rows, j * D : (j + 1) * D] = acts[j]
            g_pre_ref[rows, j * D : (j + 1) * D] = g_pres[j]
            sums_ref[3 + j : 4 + j, :] += colsum(g_pres[j].astype(F32))

    for j in range(4):

        @pl.when(step == tiles + j)
        def _(j=j):
            res = dot_tn(act_ref[:, j * D : (j + 1) * D], g_mlp_ref[...])
            if slabs:
                dwo_ref[...] = res.astype(BF16).reshape(dwo_ref.shape)
            else:
                dwo_ref[...] = res

    for j in range(2 if slabs else 4):

        @pl.when(step == tiles + 4 + j)
        def _(j=j):
            if slabs:
                dev = D // 24
                left = dot_tn(a2_ref[...], g_pre_ref[:, 2 * j * D : (2 * j + 1) * D])
                right = dot_tn(a2_ref[...], g_pre_ref[:, (2 * j + 1) * D : (2 * j + 2) * D])
                both = jnp.concatenate(
                    [left.reshape(dev, 24, D), right.reshape(dev, 24, D)], axis=1
                )
                dwf_ref[...] = both.astype(BF16)
            else:
                dwf_ref[...] = dot_tn(a2_ref[...], g_pre_ref[:, j * D : (j + 1) * D])


def mlp_local(mid, cs, cl, table, w_fc, w_out, slabs):
    rows = mid.shape[0]
    ns, nl = cs.shape[0] // TILE, cl.shape[0] // TILE
    tiles = ns + nl
    steps = tiles + (6 if slabs else 8)
    whole = lambda shape: pl.BlockSpec(shape, lambda i: (0, 0), pipeline_mode=pl.Buffered(1))
    tile = lambda f: pl.BlockSpec((TILE, D), f)
    short_at = lambda i: (jnp.minimum(i, ns - 1), 0)
    long_at = lambda i: (jnp.clip(i - ns, 0, nl - 1), 0)
    all_at = lambda i: (jnp.minimum(i, tiles - 1), 0)
    if slabs:
        dev = D // 24
        dwo_shape = jax.ShapeDtypeStruct((dev, 96, D), BF16)
        dwo_spec = pl.BlockSpec((dev // 4, 96, D), lambda i: (jnp.clip(i - tiles, 0, 3), 0, 0))
        dwf_shape = jax.ShapeDtypeStruct((dev, 96, D), BF16)
        dwf_spec = pl.BlockSpec((dev, 48, D), lambda i: (0, jnp.clip(i - tiles - 4, 0, 1), 0))
    else:
        dwo_shape = jax.ShapeDtypeStruct((FF, D), F32)
        dwo_spec = pl.BlockSpec((D, D), lambda i: (jnp.clip(i - tiles, 0, 3), 0))
        dwf_shape = jax.ShapeDtypeStruct((D, FF), F32)
        dwf_spec = pl.BlockSpec((D, D), lambda i: (0, jnp.clip(i - tiles - 4, 0, 3)))
    return pl.pallas_call(
        functools.partial(mlp_kernel, (ns, nl), slabs),
        grid=(steps,),
        out_shape=(
            jax.ShapeDtypeStruct(cs.shape, BF16),
            jax.ShapeDtypeStruct(cl.shape, BF16),
            jax.ShapeDtypeStruct((rows, D), F32),
            jax.ShapeDtypeStruct((8, D), F32),
            dwf_shape,
            dwo_shape,
        ),
        in_specs=[
            tile(all_at),
            tile(short_at),
            tile(long_at),
            whole(table.shape),
            whole(w_fc.shape),
            whole(w_out.shape),
        ],
        out_specs=[
            tile(short_at),
            tile(long_at),
            tile(all_at),
            pl.BlockSpec((8, D), lambda i: (0, 0)),
            dwf_spec,
            dwo_spec,
        ],
        scratch_shapes=[
            pltpu.VMEM((rows, D), BF16),
            pltpu.VMEM((rows, D), BF16),
            pltpu.VMEM((rows, FF), BF16),
            pltpu.VMEM((rows, FF), BF16),
        ],
        compiler_params=pltpu.CompilerParams(vmem_limit_bytes=VMEM_LIMIT),
        name="mlp",
    )(mid, cs, cl, table, w_fc, w_out)


def proj_back_tile(g_mid_ref, w_ref, g_attn_ref, g_att_ref, sums_ref, t):
    rows = rows_of(0, t)
    g_attn = (BRANCH * g_mid_ref[rows, :]).astype(BF16)
    g_attn_ref[rows, :] = g_attn
    g_att_ref[rows, :] = dot_nt(g_attn, w_ref[:, 3 * D : 4 * D]).astype(BF16)
    sums_ref[PROJB : PROJB + 1, :] += colsum(g_attn.astype(F32))


def attend_back_pair(split, qkv_ref, g_att_ref, lse_t_ref, g_qkv_ref, dk_ref, dv_ref, base, length, pair):
    first = lax.broadcasted_iota(jnp.int32, (TILE, 128), 1) < HEAD_DIM
    dk_ref[0:length, :] = jnp.zeros((length, 128), F32)
    dv_ref[0:length, :] = jnp.zeros((length, 128), F32)
    for qb in range(length // TILE):
        qrows = slice(base + qb * TILE, base + (qb + 1) * TILE)
        keys = (qb + 1) * TILE
        krows = slice(base, base + keys)
        q_pair = qkv_ref[qrows, lanes_of(pair * 128)] * BF16(HEAD_DIM**-0.5)
        g_pair = g_att_ref[qrows, lanes_of(pair * 128)]
        k_pair = qkv_ref[krows, lanes_of(D + pair * 128)]
        v_pair = qkv_ref[krows, lanes_of(2 * D + pair * 128)]
        q_pos = qb * TILE + lax.broadcasted_iota(jnp.int32, (1, TILE), 1)
        low = jnp.where(q_pos >= split, split, 0)
        k_pos = lax.broadcasted_iota(jnp.int32, (keys, TILE), 0)
        visible = (k_pos >= low) & (k_pos <= q_pos)
        dqs = []
        dk = dk_ref[0:keys, :]
        dv = dv_ref[0:keys, :]
        for half in (0, 1):
            mine = first if half == 0 else ~first
            q_half = jnp.where(mine, q_pair, BF16(0))
            g_half = jnp.where(mine, g_pair, BF16(0))
            lse = lse_t_ref[pl.ds(2 * pair + half, 1), qrows]
            s = jnp.where(visible, dot_nt(k_pair, q_half), NEG)
            p = jnp.exp(s - lse)
            dp = dot_nt(v_pair, g_half)
            inner = jnp.sum(p * dp, axis=0, keepdims=True)
            ds = (p * (dp - inner)).astype(BF16)
            dv = dv + dot(p.astype(BF16), g_half)
            dk = dk + dot(ds, q_half)
            dqs.append(dot_tn(ds, k_pair))
        dk_ref[0:keys, :] = dk
        dv_ref[0:keys, :] = dv
        dq = jnp.where(first, dqs[0], dqs[1]) * (HEAD_DIM**-0.5)
        g_qkv_ref[qrows, lanes_of(pair * 128)] = dq.astype(BF16)
    all_rows = slice(base, base + length)
    g_qkv_ref[all_rows, lanes_of(D + pair * 128)] = dk_ref[0:length, :].astype(BF16)
    g_qkv_ref[all_rows, lanes_of(2 * D + pair * 128)] = dv_ref[0:length, :].astype(BF16)


def ln1_back_tile(x_ref, g_mid_ref, table_ref, w_ref, g_qkv_ref, gx_ref, sums_ref, base, t):
    rows = rows_of(base, t)
    g_qkv = g_qkv_ref[rows, :]
    g_a1 = dot_nt(g_qkv, w_ref[:, 0 : 3 * D])
    own = rows_of(0, t)
    n, rstd = normalize(x_ref[own, :].astype(F32))
    gx_ref[own, :] = g_mid_ref[rows, :] + norm_backward(
        g_a1, n, rstd, table_ref[LN1G : LN1G + 1, :]
    )
    sums_ref[LN1G : LN1G + 1, :] += colsum(g_a1 * n)
    sums_ref[LN1B : LN1B + 1, :] += colsum(g_a1)
    sums_ref[QB : QB + 1, :] += colsum(g_qkv[:, 0:D].astype(F32))
    sums_ref[VB : VB + 1, :] += colsum(g_qkv[:, 2 * D : 3 * D].astype(F32))


def backward_kernel(
    ssplit,
    lsplit,
    xs,
    xl,
    table_ref,
    w_ref,
    a1_ref,
    qkv_ref,
    att_ref,
    lse_t_ref,
    g_mid_ref,
    gxs_ref,
    gxl_ref,
    dwp_ref,
    dwq_ref,
    sums_ref,
    g_attn_ref,
    g_att_ref,
    g_qkv_ref,
    dk_ref,
    dv_ref,
):
    sums_ref[...] = jnp.zeros_like(sums_ref)
    rows = xs.shape[0] + xl.shape[0]
    lax.fori_loop(
        0,
        rows // TILE,
        lambda t, c: (
            proj_back_tile(g_mid_ref, w_ref, g_attn_ref, g_att_ref, sums_ref, t),
            c,
        )[1],
        0,
    )
    dwp_ref[...] = dot_tn(att_ref[...], g_attn_ref[...])

    def pair_step(pair, c):
        for split, x_ref, base in ((ssplit[0], xs, 0), (lsplit[0], xl, xs.shape[0])):
            attend_back_pair(
                split, qkv_ref, g_att_ref, lse_t_ref, g_qkv_ref, dk_ref, dv_ref, base, x_ref.shape[0], pair
            )
        return c

    lax.fori_loop(0, PAIRS, pair_step, 0)
    for j in range(3):
        dwq_ref[:, j * D : (j + 1) * D] = dot_tn(a1_ref[...], g_qkv_ref[:, j * D : (j + 1) * D])
    for x_ref, gx_ref, base in ((xs, gxs_ref, 0), (xl, gxl_ref, xs.shape[0])):
        lax.fori_loop(
            0,
            x_ref.shape[0] // TILE,
            lambda t, c: (
                ln1_back_tile(
                    x_ref, g_mid_ref, table_ref, w_ref, g_qkv_ref, gx_ref, sums_ref, base, t
                ),
                c,
            )[1],
            0,
        )


def backward_local(ssplit, lsplit, xs, xl, table, w_attn, a1, qkv, att, lse_t, g_mid):
    rows = xs.shape[0] + xl.shape[0]
    return pl.pallas_call(
        backward_kernel,
        out_shape=(
            jax.ShapeDtypeStruct(xs.shape, F32),
            jax.ShapeDtypeStruct(xl.shape, F32),
            jax.ShapeDtypeStruct((D, D), F32),
            jax.ShapeDtypeStruct((D, 3 * D), F32),
            jax.ShapeDtypeStruct((8, D), F32),
        ),
        in_specs=[SM, SM] + [VM] * 9,
        out_specs=[VM] * 5,
        scratch_shapes=[
            pltpu.VMEM((rows, D), BF16),
            pltpu.VMEM((rows, D), BF16),
            pltpu.VMEM((rows, 3 * D), BF16),
            pltpu.VMEM((xl.shape[0], 128), F32),
            pltpu.VMEM((xl.shape[0], 128), F32),
        ],
        compiler_params=pltpu.CompilerParams(vmem_limit_bytes=VMEM_LIMIT),
        name="attention_backward",
    )(ssplit, lsplit, xs, xl, table, w_attn, a1, qkv, att, lse_t, g_mid)


MESH = pl.DeviceIdType.MESH
COLS, DEPTH = 4, 4


class Place:
    def __init__(self):
        q, f = lax.axis_index("dp"), lax.axis_index("fsdp")
        z = lax.div(f, 2)
        self.core = lax.rem(f, 2)
        self.col = [q, q + 1 - 2 * lax.rem(q, 2), lax.rem(q + 2, 4), 3 - q]
        self.depth = [lax.rem(z + k, DEPTH) for k in range(DEPTH)]
        self.index = q * 2 * DEPTH + f
        self.partner = (q, 2 * z + 1 - self.core)
        self.x = (self.col[1], f)
        self.y = (self.col[2], f)
        self.along = [(q, 2 * d + self.core) for d in self.depth]

    def greet(self):
        barrier = pltpu.get_barrier_semaphore()
        others = [self.partner, self.x, self.y] + self.along[1:]
        for device in others:
            pl.semaphore_signal(barrier, inc=1, device_id=device, device_id_type=MESH)
        pl.semaphore_wait(barrier, len(others))


def remote(src, dst, send, recv, device):
    return pltpu.make_async_remote_copy(
        src_ref=src, dst_ref=dst, send_sem=send, recv_sem=recv, device_id=device, device_id_type=MESH
    )


def at(start, size, step):
    return pl.ds(pl.multiple_of(start, step), size)


Z, X, Y, ACROSS, PAIR = 0, 3, 7, 11, 15
N_GATHER = 31
Y_PATH = (0, 3)


class Gather:
    def __init__(self, place, full, own, wide, send, recv):
        self.place, self.full, self.own, self.wide = place, full, own, wide
        self.send, self.recv = send, recv
        self.spots = {}
        for core in (0, 1):
            c = place.core if core == 0 else 1 - place.core
            for r in range(COLS):
                for k in range(DEPTH):
                    chip = place.col[r] * DEPTH + place.depth[k]
                    if wide:
                        half = full.shape[1] // 2
                        spot = full.at[at(chip * 48, 48, 16), at(c * half, half, 128)]
                    else:
                        spot = full.at[at((chip * 2 + c) * 96, 96, 16), :]
                    self.spots[core, r, k] = spot

    def copy(self, kind, r, k, arriving=False):
        place = self.place
        here = self.spots[0, r, k]
        src = self.own if (r, k) == (0, 0) and not arriving else here
        if kind == Z:
            n, device = (DEPTH - k if not arriving else k) - 1, place.along[k]
            src, here = (self.own, self.spots[0, 0, 0]) if not arriving else (here, here)
        elif kind == X:
            n, device = X + k, place.x
        elif kind == Y:
            n, device = Y + k, place.y
        elif kind == ACROSS:
            n, device = ACROSS + k, (place.y if k in Y_PATH else place.x)
        else:
            n, device = PAIR + 4 * r + k, place.partner
            if arriving:
                src = here = self.spots[1, r, k]
        sent = n if kind != Z else k - 1
        return remote(src, here, self.send.at[sent], self.recv.at[n], device)

    def begin(self):
        for k in range(1, DEPTH):
            self.copy(Z, 0, k).start()
        self.spread(0)

    def spread(self, k):
        self.copy(X, 0, k).start()
        self.copy(Y, 0, k).start()
        self.copy(PAIR, 0, k).start()

    def along(self, k):
        self.copy(Z, 0, k, True).wait_recv()
        self.spread(k)

    def across(self, k):
        self.copy(X, 1, k, True).wait_recv()
        if k in Y_PATH:
            self.copy(ACROSS, 1, k).start()
        self.copy(PAIR, 1, k).start()
        self.copy(Y, 2, k, True).wait_recv()
        if k not in Y_PATH:
            self.copy(ACROSS, 2, k).start()
        self.copy(PAIR, 2, k).start()

    def last(self, k):
        self.copy(ACROSS, 3, k, True).wait_recv()
        self.copy(PAIR, 3, k).start()

    def arrive(self):
        for r in range(COLS):
            for k in range(DEPTH):
                self.copy(PAIR, r, k, True).wait_recv()

    def end(self):
        for k in range(1, DEPTH):
            self.copy(Z, 0, k).wait_send()
        for k in range(DEPTH):
            self.copy(X, 0, k).wait_send()
            self.copy(Y, 0, k).wait_send()
            self.copy(ACROSS, 1 if k in Y_PATH else 2, k).wait_send()
            for r in range(COLS):
                self.copy(PAIR, r, k).wait_send()


def place_vectors(place, vectors, out):
    out[...] = jnp.zeros_like(out)
    for ref, row in zip(vectors, (LN1G, LN1B, QB, PROJB, LN2G, LN2B, OUTB, FCB)):
        size = ref.shape[1]
        start = place.index * size
        at_row, at_lane = lax.div(start, D), lax.rem(start, D)
        lane = lax.broadcasted_iota(jnp.int32, (size, D), 1)
        pick = lax.broadcasted_iota(jnp.int32, (size, D), 0) + at_lane == lane
        values = dot(ref[...], jnp.where(pick, 1.0, 0.0).astype(BF16))
        rows = (size * 32) // D
        mine = lax.broadcasted_iota(jnp.int32, (rows, D), 0) == at_row
        out[row : row + rows, :] = jnp.where(mine, values, 0.0)


SUM_STEPS = 6


class TableSum:
    def __init__(self, place, total, got, send, recv):
        self.place, self.total, self.got, self.send, self.recv = place, total, got, send, recv

    def copy(self, step, arriving=False):
        place = self.place
        if step == 0:
            device, n = place.partner, 0
        elif step <= 3:
            device, n = place.along[step], (step if arriving else 4 - step)
        else:
            device, n = (place.x, place.y)[step - 4], step
        stage = 0 if step == 0 else (1 if step <= 3 else step - 2)
        return remote(self.total.at[stage], self.got.at[n], self.send.at[step], self.recv.at[n], device)

    def begin(self, steps):
        for step in steps:
            self.copy(step).start()

    def add(self, stage, steps):
        for step in steps:
            self.copy(step, True).wait_recv()
        total = self.total[stage]
        for step in steps:
            total = total + self.got[step]
        self.total[stage + 1] = total

    def end(self):
        for step in range(SUM_STEPS):
            self.copy(step).wait_send()


def forward_gather_kernel(
    ssplit,
    lsplit,
    xs_hbm,
    xl_hbm,
    wqkv,
    wproj,
    wfc,
    wout,
    v0,
    v1,
    v2,
    v3,
    v4,
    v5,
    v6,
    v7,
    table_ref,
    wa_hbm,
    wf_hbm,
    wo_hbm,
    a1_hbm,
    qkv_hbm,
    att_hbm,
    lse_t_ref,
    mid_hbm,
    xs,
    xl,
    wa,
    a1_ref,
    qkv_ref,
    att_ref,
    mid_ref,
    lse_ref,
    slab_f,
    swap_out,
    swap_in,
    total,
    got,
    io_sem,
    swap_send,
    swap_recv,
    sum_send,
    sum_recv,
    g_send,
    g_recv,
):
    place = Place()
    loads = [pltpu.make_async_copy(xs_hbm, xs, io_sem.at[0]), pltpu.make_async_copy(xl_hbm, xl, io_sem.at[1])]
    for copy in loads:
        copy.start()
    place_vectors(place, (v0, v1, v2, v3, v4, v5, v6, v7), total.at[0])
    half = wa.shape[1] // 2
    mine, theirs = place.core * half, (1 - place.core) * half
    n_qkv = wqkv.shape[1]
    a_share = jnp.concatenate([wqkv[...], wproj[...]], axis=1).astype(F32)
    f_share = wfc[...].astype(F32)
    first = place.core == 0
    keep = []
    for n, share in enumerate((a_share, f_share)):
        left, right = share[:, 0:half], share[:, half : 2 * half]
        swap_out[n] = jnp.where(first, right, left)
        keep.append(jnp.where(first, left, right))
    place.greet()
    swaps = [
        remote(swap_out.at[n], swap_in.at[n], swap_send.at[n], swap_recv.at[n], place.partner)
        for n in range(2)
    ]
    sums = TableSum(place, total, got, sum_send, sum_recv)
    swaps[0].start()
    sums.begin((0,))
    swaps[1].start()

    def joined(n):
        swaps[n].wait_recv()
        other = swap_in[n]
        top, bottom = jnp.where(first, keep[n], other), jnp.where(first, other, keep[n])
        return jnp.concatenate([top, bottom], axis=0).astype(BF16)

    chip = place.col[0] * DEPTH + place.depth[0]
    spot = (at(chip * 48, 48, 16), at(mine, half, 128))
    wa[spot] = joined(0)
    ga = Gather(place, wa, wa.at[spot], True, g_send.at[0], g_recv.at[0])
    ga.begin()
    sums.add(0, (0,))
    sums.begin((1, 2, 3))
    slab_f[...] = joined(1)
    gf = Gather(place, wf_hbm, slab_f, True, g_send.at[1], g_recv.at[1])
    go = Gather(place, wo_hbm, wout, False, g_send.at[2], g_recv.at[2])
    own_f = pltpu.make_async_copy(slab_f, gf.spots[0, 0, 0], io_sem.at[2])
    own_o = pltpu.make_async_copy(wout, go.spots[0, 0, 0], io_sem.at[3])
    own_f.start()
    own_o.start()
    sums.add(1, (1, 2, 3))
    sums.begin((4,))
    ga.along(1)
    sums.add(2, (4,))
    sums.begin((5,))
    ga.along(3)
    sums.add(3, (5,))
    table_ref[...] = total[4]
    ga.along(2)
    for copy in loads:
        copy.wait()
    groups = group_refs(xs, xl)
    loop(groups[0][0].shape[0] // TILE, lambda t: norm_tile(xs, table_ref, a1_ref, 0, t))
    ga.across(0)
    gf.begin()
    loop(2, lambda t: norm_tile(xl, table_ref, a1_ref, groups[1][1], t))
    ga.across(1)
    ga.across(3)
    loop(xl.shape[0] // TILE - 2, lambda t: norm_tile(xl, table_ref, a1_ref, groups[1][1], t + 2))
    ga.across(2)
    go.begin()
    for k in range(DEPTH):
        ga.last(k)
    ga.arrive()
    stores = [
        pltpu.make_async_copy(src, dst, io_sem.at[4 + n])
        for n, (src, dst) in enumerate(
            (
                (wa, wa_hbm),
                (a1_ref, a1_hbm),
                (qkv_ref, qkv_hbm),
                (att_ref, att_hbm),
                (mid_ref, mid_hbm),
            )
        )
    ]
    stores[0].start()
    stores[1].start()

    def hooks(table):
        def run(i):
            for n, actions in table.items():

                @pl.when(i == n)
                def _():
                    for action, k in actions:
                        action(k)

        return run

    after = hooks(
        {
            0: ((gf.along, 1),),
            1: ((gf.along, 3),),
            2: ((gf.along, 2),),
            3: ((go.along, 1),),
            4: ((go.along, 3),),
            5: ((go.along, 2), (gf.across, 0)),
        }
    )

    def qkv_step(t):
        qkv_tile(table_ref, wa, a1_ref, qkv_ref, t)
        after(t)

    loop(a1_ref.shape[0] // TILE, qkv_step)
    stores[2].start()
    lse_ref[...] = jnp.zeros_like(lse_ref)
    after_short = hooks(
        {
            0: ((gf.across, 1),),
            1: ((gf.across, 2),),
            2: ((go.across, 1), (gf.last, 0)),
            3: ((go.across, 2), (gf.last, 3)),
            4: ((go.last, 0),),
            5: ((go.last, 1),),
        }
    )
    after_long = hooks(
        {
            0: ((gf.across, 3),),
            1: ((go.across, 0), (gf.last, 1)),
            2: ((go.across, 3), (gf.last, 2)),
            4: ((go.last, 3),),
            5: ((go.last, 2),),
        }
    )

    def pair_step(pair):
        attend_pair(ssplit[0], qkv_ref, att_ref, lse_ref, 0, xs.shape[0], pair)
        after_short(pair)
        attend_pair(lsplit[0], qkv_ref, att_ref, lse_ref, xs.shape[0], xl.shape[0], pair)
        after_long(pair)

    loop(PAIRS, pair_step)
    stores[3].start()
    lse_t_ref[...] = jnp.transpose(lse_ref[...])[:16, :]
    for x_ref, base in groups:
        loop(
            x_ref.shape[0] // TILE,
            lambda t: mid_tile(x_ref, table_ref, wa, att_ref, mid_ref, base, t),
        )
    stores[4].start()
    gf.arrive()
    go.arrive()
    own_f.wait()
    own_o.wait()
    for swap in swaps:
        swap.wait_send()
    sums.end()
    for g in (ga, gf, go):
        g.end()
    for copy in stores:
        copy.wait()


ANY = pl.BlockSpec(memory_space=pl.ANY)


def forward_gather(ssplit, lsplit, xs, xl, wqkv, wproj, wfc, wout, vectors):
    rows = xs.shape[0] + xl.shape[0]
    devices = 2 * COLS * DEPTH
    wide = wqkv.shape[1] + wproj.shape[1]
    full_out = jax.ShapeDtypeStruct((wout.shape[0] * devices, wout.shape[1]), BF16)
    sem = pltpu.SemaphoreType.DMA
    return pl.pallas_call(
        forward_gather_kernel,
        out_shape=(
            jax.ShapeDtypeStruct((16, D), F32),
            jax.ShapeDtypeStruct((D, wide), BF16),
            jax.ShapeDtypeStruct((D, wfc.shape[1]), BF16),
            full_out,
            jax.ShapeDtypeStruct((rows, D), BF16),
            jax.ShapeDtypeStruct((rows, 3 * D), BF16),
            jax.ShapeDtypeStruct((rows, D), BF16),
            jax.ShapeDtypeStruct((16, rows), F32),
            jax.ShapeDtypeStruct((rows, D), F32),
        ),
        in_specs=[SM, SM, ANY, ANY] + [VM] * 12,
        out_specs=[VM, ANY, ANY, ANY, ANY, ANY, ANY, VM, ANY],
        scratch_shapes=[
            pltpu.VMEM(xs.shape, BF16),
            pltpu.VMEM(xl.shape, BF16),
            pltpu.VMEM((D, wide), BF16),
            pltpu.VMEM((rows, D), BF16),
            pltpu.VMEM((rows, 3 * D), BF16),
            pltpu.VMEM((rows, D), BF16),
            pltpu.VMEM((rows, D), F32),
            pltpu.VMEM((rows, 128), F32),
            pltpu.VMEM((48, wfc.shape[1] // 2), BF16),
            pltpu.VMEM((2, 24, wide // 2), F32),
            pltpu.VMEM((2, 24, wide // 2), F32),
            pltpu.VMEM((5, 16, D), F32),
            pltpu.VMEM((SUM_STEPS, 16, D), F32),
            sem((9,)),
            sem((2,)),
            sem((2,)),
            sem((SUM_STEPS,)),
            sem((SUM_STEPS,)),
            sem((3, N_GATHER)),
            sem((3, N_GATHER)),
        ],
        compiler_params=pltpu.CompilerParams(
            vmem_limit_bytes=VMEM_LIMIT, collective_id=0, has_side_effects=True
        ),
        name="attention_forward_gather",
    )(ssplit, lsplit, xs, xl, wqkv, wproj, wfc, wout, *[v.reshape(1, -1) for v in vectors])


AXES = ("dp", "fsdp")


def gather(x, axis=0):
    return lax.all_gather(x, AXES, axis=axis, tiled=True)


def scatter(x):
    return lax.psum_scatter(x, AXES, scatter_dimension=0, tiled=True)


def general(args, devices):
    (st, lt, ss, ls, ln1g, ln1b, wqkv, qvb, wproj, projb, ln2g, ln2b, wfc, fcb, wout, outb, sc, lc) = args
    xs, xl = st.reshape(-1, D), lt.reshape(-1, D)
    cs, cl = sc.reshape(-1, D), lc.reshape(-1, D)
    vectors = (ln1g, ln1b, qvb, projb, ln2g, ln2b, outb, fcb)
    sizes = [v.shape[0] for v in vectors]
    every = lax.all_gather(jnp.concatenate(vectors), AXES, axis=0)
    starts = [sum(sizes[:i]) for i in range(len(sizes))]
    full = [every[:, s : s + n].reshape(-1, D) for s, n in zip(starts, sizes)]
    table = jnp.concatenate(full + [jnp.zeros((4, D), BF16)]).astype(F32)
    w_attn = gather(jnp.concatenate([wqkv, wproj], axis=1))
    w_fc, w_out = gather(wfc), gather(wout)
    a1, qkv, att, lse_t, mid = forward_local(ss, ls, xs, xl, table, w_attn)
    out_s, out_l, g_mid, sums2, dwf, dwo = mlp_local(mid, cs, cl, table, w_fc, w_out, False)
    gxs, gxl, dwp, dwq, sums1 = backward_local(
        ss, ls, xs, xl, table, w_attn, a1, qkv, att, lse_t, g_mid
    )
    return finish(args, devices, starts, sizes, out_s, out_l, gxs, gxl, sums1, sums2, dwq, dwp, dwf, dwo)


def finish(args, devices, starts, sizes, out_s, out_l, gxs, gxl, sums1, sums2, dwq, dwp, dwf, dwo):
    st, lt = args[0], args[1]
    rs = lambda x: x.reshape(devices, -1)
    small = jnp.concatenate(
        [
            rs(sums1[0]),
            rs(sums1[1]),
            rs(sums1[2:4]),
            rs(sums1[4]),
            rs(sums2[0]),
            rs(sums2[1]),
            rs(sums2[2]),
            rs(sums2[3:7]),
        ],
        axis=1,
    )
    small = scatter(small)[0]
    parts = [small[s : s + n] for s, n in zip(starts, sizes)]
    d_ln1g, d_ln1b, d_qvb, d_projb, d_ln2g, d_ln2b, d_outb, d_fcb = parts
    return (
        out_s.reshape(st.shape),
        out_l.reshape(lt.shape),
        gxs.reshape(st.shape),
        gxl.reshape(lt.shape),
        d_ln1g,
        d_ln1b,
        scatter(dwq),
        d_qvb,
        scatter(dwp),
        d_projb,
        d_ln2g,
        d_ln2b,
        scatter(dwf),
        d_fcb,
        scatter(dwo),
        d_outb,
    )


def on_torus(args, devices):
    (st, lt, ss, ls, ln1g, ln1b, wqkv, qvb, wproj, projb, ln2g, ln2b, wfc, fcb, wout, outb, sc, lc) = args
    xs, xl = st.reshape(-1, D), lt.reshape(-1, D)
    cs, cl = sc.reshape(-1, D), lc.reshape(-1, D)
    vectors = (ln1g, ln1b, qvb, projb, ln2g, ln2b, outb, fcb)
    sizes = [v.shape[0] for v in vectors]
    starts = [sum(sizes[:i]) for i in range(len(sizes))]
    table, w_attn, w_fc, w_out, a1, qkv, att, lse_t, mid = forward_gather(
        ss, ls, xs, xl, wqkv, wproj, wfc, wout, vectors
    )
    out_s, out_l, g_mid, sums2, dwf, dwo = mlp_local(mid, cs, cl, table, w_fc, w_out, False)
    gxs, gxl, dwp, dwq, sums1 = backward_local(
        ss, ls, xs, xl, table, w_attn, a1, qkv, att, lse_t, g_mid
    )
    return finish(args, devices, starts, sizes, out_s, out_l, gxs, gxl, sums1, sums2, dwq, dwp, dwf, dwo)


def per_device(shape, *args):
    devices = shape["dp"] * shape["fsdp"]
    if shape == {"dp": COLS, "fsdp": 2 * DEPTH}:
        return on_torus(args, devices)
    return general(args, devices)


def solution(mesh):
    vec, mat, seq = P(AXES), P(AXES, None), P(AXES, None, None)
    in_specs = (seq, seq, vec, vec) + (vec, vec, mat, vec, mat, vec) * 1 + (vec, vec, mat, vec, mat, vec) + (seq, seq)
    out_specs = (seq,) * 4 + (vec, vec, mat, vec, mat, vec) * 2
    return jax.shard_map(
        functools.partial(per_device, dict(mesh.shape)),
        mesh=mesh,
        in_specs=in_specs,
        out_specs=out_specs,
        check_vma=False,
    )
```

```python
import functools

import jax
import jax.numpy as jnp
from jax import lax
from jax.experimental import pallas as pl
from jax.experimental.pallas import tpu as pltpu
from jax.sharding import PartitionSpec as P

F32 = jnp.float32
BF16 = jnp.bfloat16
D = 768
FF = 3072
HEAD_DIM = 64
PAIRS = D // 128
TILE = 256
BRANCH = 0.14433756729740643
EPS = 1e-05
NEG = -1e30
VMEM_LIMIT = 60 * 2**20

LN1G, LN1B, QB, VB, PROJB, LN2G, LN2B, OUTB, FCB = 0, 1, 2, 3, 4, 5, 6, 7, 8


def dot(a, b):
    return jnp.dot(a, b, preferred_element_type=F32)


def dot_nt(a, b):
    return lax.dot_general(a, b, (((1,), (1,)), ((), ())), preferred_element_type=F32)


def dot_tn(a, b):
    return lax.dot_general(a, b, (((0,), (0,)), ((), ())), preferred_element_type=F32)


def normalize(x):
    center = x - jnp.mean(x, axis=-1, keepdims=True)
    rstd = lax.rsqrt(jnp.mean(center * center, axis=-1, keepdims=True) + EPS)
    return center * rstd, rstd


def norm_backward(g, n, rstd, gain):
    e = g * gain
    return rstd * (
        e
        - jnp.mean(e, axis=-1, keepdims=True)
        - n * jnp.mean(e * n, axis=-1, keepdims=True)
    )


def rows_of(base, tile):
    return pl.ds(pl.multiple_of(base + tile * TILE, TILE), TILE)


def lanes_of(start):
    return pl.ds(pl.multiple_of(start, 128), 128)


def loop(count, body):
    lax.fori_loop(0, count, lambda i, c: (body(i), c)[1], 0)


def group_refs(short, long):
    return ((short, 0), (long, short.shape[0]))


def norm_tile(x_ref, table_ref, a1_ref, base, t):
    n, _ = normalize(x_ref[rows_of(0, t), :].astype(F32))
    a1 = n * table_ref[LN1G : LN1G + 1, :] + table_ref[LN1B : LN1B + 1, :]
    a1_ref[rows_of(base, t), :] = a1.astype(BF16)


def qkv_tile(table_ref, w_ref, a1_ref, qkv_ref, t):
    rows = rows_of(0, t)
    a1 = a1_ref[rows, :]
    for part, bias in ((0, QB), (1, None), (2, VB)):
        cols = slice(part * D, (part + 1) * D)
        out = dot(a1, w_ref[:, cols])
        if bias is not None:
            out = out + table_ref[bias : bias + 1, :]
        qkv_ref[rows, cols] = out.astype(BF16)


def attend_pair(split, qkv_ref, att_ref, lse_ref, base, length, pair):
    first = lax.broadcasted_iota(jnp.int32, (TILE, 128), 1) < HEAD_DIM
    head_lane = lax.broadcasted_iota(jnp.int32, (TILE, 128), 1)
    for qb in range(length // TILE):
        qrows = slice(base + qb * TILE, base + (qb + 1) * TILE)
        keys = (qb + 1) * TILE
        krows = slice(base, base + keys)
        q_pair = qkv_ref[qrows, lanes_of(pair * 128)] * BF16(HEAD_DIM**-0.5)
        k_pair = qkv_ref[krows, lanes_of(D + pair * 128)]
        v_pair = qkv_ref[krows, lanes_of(2 * D + pair * 128)]
        q_pos = qb * TILE + lax.broadcasted_iota(jnp.int32, (TILE, 1), 0)
        low = jnp.where(q_pos >= split, split, 0)
        k_pos = lax.broadcasted_iota(jnp.int32, (TILE, keys), 1)
        visible = (k_pos >= low) & (k_pos <= q_pos)
        outs = []
        lse_new = lse_ref[qrows, :]
        for half in (0, 1):
            mine = first if half == 0 else ~first
            s = dot_nt(jnp.where(mine, q_pair, BF16(0)), k_pair)
            s = jnp.where(visible, s, NEG)
            peak = jnp.max(s, axis=-1, keepdims=True)
            e = jnp.exp(s - peak)
            total = jnp.sum(e, axis=-1, keepdims=True)
            p = (e * (1.0 / total)).astype(BF16)
            outs.append(dot(p, v_pair))
            lse_new = jnp.where(head_lane == 2 * pair + half, peak + jnp.log(total), lse_new)
        lse_ref[qrows, :] = lse_new
        att_ref[qrows, lanes_of(pair * 128)] = jnp.where(first, outs[0], outs[1]).astype(BF16)


def mid_tile(x_ref, table_ref, w_ref, att_ref, mid_ref, base, t):
    rows = rows_of(base, t)
    out = dot(att_ref[rows, :], w_ref[:, 3 * D : 4 * D]) + table_ref[PROJB : PROJB + 1, :]
    mid_ref[rows, :] = x_ref[rows_of(0, t), :].astype(F32) + BRANCH * out


def forward_kernel(
    ssplit, lsplit, xs, xl, table_ref, w_ref, a1_ref, qkv_ref, att_ref, lse_t_ref, mid_ref, lse_ref
):
    for x_ref, base in group_refs(xs, xl):
        loop(x_ref.shape[0] // TILE, lambda t: norm_tile(x_ref, table_ref, a1_ref, base, t))
    loop(a1_ref.shape[0] // TILE, lambda t: qkv_tile(table_ref, w_ref, a1_ref, qkv_ref, t))
    lse_ref[...] = jnp.zeros_like(lse_ref)

    def pair_step(pair, c):
        attend_pair(ssplit[0], qkv_ref, att_ref, lse_ref, 0, xs.shape[0], pair)
        attend_pair(lsplit[0], qkv_ref, att_ref, lse_ref, xs.shape[0], xl.shape[0], pair)
        return c

    lax.fori_loop(0, PAIRS, pair_step, 0)
    lse_t_ref[...] = jnp.transpose(lse_ref[...])[:16, :]
    for x_ref, base in group_refs(xs, xl):
        lax.fori_loop(
            0,
            x_ref.shape[0] // TILE,
            lambda t, c: (mid_tile(x_ref, table_ref, w_ref, att_ref, mid_ref, base, t), c)[1],
            0,
        )


VM = pl.BlockSpec(memory_space=pltpu.VMEM)
SM = pl.BlockSpec(memory_space=pltpu.SMEM)


def forward_local(ssplit, lsplit, xs, xl, table, w_attn):
    rows = xs.shape[0] + xl.shape[0]
    return pl.pallas_call(
        forward_kernel,
        out_shape=(
            jax.ShapeDtypeStruct((rows, D), BF16),
            jax.ShapeDtypeStruct((rows, 3 * D), BF16),
            jax.ShapeDtypeStruct((rows, D), BF16),
            jax.ShapeDtypeStruct((16, rows), F32),
            jax.ShapeDtypeStruct((rows, D), F32),
        ),
        in_specs=[SM, SM, VM, VM, VM, VM],
        out_specs=[VM] * 5,
        scratch_shapes=[pltpu.VMEM((rows, 128), F32)],
        compiler_params=pltpu.CompilerParams(vmem_limit_bytes=VMEM_LIMIT),
        name="attention_forward",
    )(ssplit, lsplit, xs, xl, table, w_attn)


GELU_A = 0.7978845608028654
GELU_B = 0.044715


def mlp_tile(mid, g_out, table_ref, wf_ref, wo_ref):
    n2, rstd = normalize(mid)
    gain = table_ref[LN2G : LN2G + 1, :]
    a2 = (n2 * gain + table_ref[LN2B : LN2B + 1, :]).astype(BF16)
    g_mlp = (BRANCH * g_out).astype(BF16)
    out = None
    g_a2 = None
    acts, g_pres = [], []
    for j in range(FF // D):
        cols = slice(j * D, (j + 1) * D)
        pre = dot(a2, wf_ref[:, cols]) + table_ref[FCB + j : FCB + j + 1, :]
        g_act = dot_nt(g_mlp, wo_ref[cols, :])
        square = pre * pre
        t = jnp.tanh(pre * (GELU_A + (GELU_A * GELU_B) * square))
        half = 0.5 + 0.5 * t
        act = (pre * half).astype(BF16)
        slope = half + pre * (0.5 - 0.5 * t * t) * (GELU_A + (3 * GELU_A * GELU_B) * square)
        g_pre = (g_act * slope).astype(BF16)
        acts.append(act)
        g_pres.append(g_pre)
        part = dot(act, wo_ref[cols, :])
        out = part if out is None else out + part
        part = dot_nt(g_pre, wf_ref[:, cols])
        g_a2 = part if g_a2 is None else g_a2 + part
    out = mid + BRANCH * (out + table_ref[OUTB : OUTB + 1, :])
    g_mid = g_out + norm_backward(g_a2, n2, rstd, gain)
    return out, g_mid, a2, g_mlp, acts, g_pres, g_a2, n2


def colsum(x):
    return jnp.sum(x, axis=0, keepdims=True)


def mlp_kernel(
    n_tiles,
    slabs,
    mid_ref,
    cs_ref,
    cl_ref,
    table_ref,
    wf_ref,
    wo_ref,
    os_ref,
    ol_ref,
    g_mid_ref,
    sums_ref,
    dwf_ref,
    dwo_ref,
    a2_ref,
    g_mlp_ref,
    act_ref,
    g_pre_ref,
):
    step = pl.program_id(0)
    short_tiles = n_tiles[0]
    tiles = n_tiles[0] + n_tiles[1]

    @pl.when(step == 0)
    def _():
        sums_ref[...] = jnp.zeros_like(sums_ref)

    @pl.when(step < tiles)
    def _():
        cot = jnp.where(step < short_tiles, cs_ref[...], cl_ref[...]).astype(F32)
        out, g_mid, a2, g_mlp, acts, g_pres, g_a2, n2 = mlp_tile(
            mid_ref[...], cot, table_ref, wf_ref, wo_ref
        )
        out = out.astype(BF16)

        @pl.when(step < short_tiles)
        def _():
            os_ref[...] = out

        @pl.when(step >= short_tiles)
        def _():
            ol_ref[...] = out

        g_mid_ref[...] = g_mid
        rows = rows_of(0, step)
        a2_ref[rows, :] = a2
        g_mlp_ref[rows, :] = g_mlp
        sums_ref[0:1, :] += colsum(g_a2 * n2)
        sums_ref[1:2, :] += colsum(g_a2)
        sums_ref[2:3, :] += colsum(g_mlp.astype(F32))
        for j in range(FF // D):
            act_ref[rows, j * D : (j + 1) * D] = acts[j]
            g_pre_ref[rows, j * D : (j + 1) * D] = g_pres[j]
            sums_ref[3 + j : 4 + j, :] += colsum(g_pres[j].astype(F32))

    for j in range(4):

        @pl.when(step == tiles + j)
        def _(j=j):
            res = dot_tn(act_ref[:, j * D : (j + 1) * D], g_mlp_ref[...])
            if slabs:
                dwo_ref[...] = res.astype(BF16).reshape(dwo_ref.shape)
            else:
                dwo_ref[...] = res

    for j in range(2 if slabs else 4):

        @pl.when(step == tiles + 4 + j)
        def _(j=j):
            if slabs:
                dev = D // 24
                left = dot_tn(a2_ref[...], g_pre_ref[:, 2 * j * D : (2 * j + 1) * D])
                right = dot_tn(a2_ref[...], g_pre_ref[:, (2 * j + 1) * D : (2 * j + 2) * D])
                both = jnp.concatenate(
                    [left.reshape(dev, 24, D), right.reshape(dev, 24, D)], axis=1
                )
                dwf_ref[...] = both.astype(BF16)
            else:
                dwf_ref[...] = dot_tn(a2_ref[...], g_pre_ref[:, j * D : (j + 1) * D])


def mlp_local(mid, cs, cl, table, w_fc, w_out, slabs):
    rows = mid.shape[0]
    ns, nl = cs.shape[0] // TILE, cl.shape[0] // TILE
    tiles = ns + nl
    steps = tiles + (6 if slabs else 8)
    whole = lambda shape: pl.BlockSpec(shape, lambda i: (0, 0), pipeline_mode=pl.Buffered(1))
    tile = lambda f: pl.BlockSpec((TILE, D), f)
    short_at = lambda i: (jnp.minimum(i, ns - 1), 0)
    long_at = lambda i: (jnp.clip(i - ns, 0, nl - 1), 0)
    all_at = lambda i: (jnp.minimum(i, tiles - 1), 0)
    if slabs:
        dev = D // 24
        dwo_shape = jax.ShapeDtypeStruct((dev, 96, D), BF16)
        dwo_spec = pl.BlockSpec((dev // 4, 96, D), lambda i: (jnp.clip(i - tiles, 0, 3), 0, 0))
        dwf_shape = jax.ShapeDtypeStruct((dev, 96, D), BF16)
        dwf_spec = pl.BlockSpec((dev, 48, D), lambda i: (0, jnp.clip(i - tiles - 4, 0, 1), 0))
    else:
        dwo_shape = jax.ShapeDtypeStruct((FF, D), F32)
        dwo_spec = pl.BlockSpec((D, D), lambda i: (jnp.clip(i - tiles, 0, 3), 0))
        dwf_shape = jax.ShapeDtypeStruct((D, FF), F32)
        dwf_spec = pl.BlockSpec((D, D), lambda i: (0, jnp.clip(i - tiles - 4, 0, 3)))
    return pl.pallas_call(
        functools.partial(mlp_kernel, (ns, nl), slabs),
        grid=(steps,),
        out_shape=(
            jax.ShapeDtypeStruct(cs.shape, BF16),
            jax.ShapeDtypeStruct(cl.shape, BF16),
            jax.ShapeDtypeStruct((rows, D), F32),
            jax.ShapeDtypeStruct((8, D), F32),
            dwf_shape,
            dwo_shape,
        ),
        in_specs=[
            tile(all_at),
            tile(short_at),
            tile(long_at),
            whole(table.shape),
            whole(w_fc.shape),
            whole(w_out.shape),
        ],
        out_specs=[
            tile(short_at),
            tile(long_at),
            tile(all_at),
            pl.BlockSpec((8, D), lambda i: (0, 0)),
            dwf_spec,
            dwo_spec,
        ],
        scratch_shapes=[
            pltpu.VMEM((rows, D), BF16),
            pltpu.VMEM((rows, D), BF16),
            pltpu.VMEM((rows, FF), BF16),
            pltpu.VMEM((rows, FF), BF16),
        ],
        compiler_params=pltpu.CompilerParams(vmem_limit_bytes=VMEM_LIMIT),
        name="mlp",
    )(mid, cs, cl, table, w_fc, w_out)


def proj_back_tile(g_mid_ref, w_ref, g_attn_ref, g_att_ref, sums_ref, t):
    rows = rows_of(0, t)
    g_attn = (BRANCH * g_mid_ref[rows, :]).astype(BF16)
    g_attn_ref[rows, :] = g_attn
    g_att_ref[rows, :] = dot_nt(g_attn, w_ref[:, 3 * D : 4 * D]).astype(BF16)
    sums_ref[PROJB : PROJB + 1, :] += colsum(g_attn.astype(F32))


def attend_back_pair(split, qkv_ref, g_att_ref, lse_t_ref, g_qkv_ref, dk_ref, dv_ref, base, length, pair):
    first = lax.broadcasted_iota(jnp.int32, (TILE, 128), 1) < HEAD_DIM
    dk_ref[0:length, :] = jnp.zeros((length, 128), F32)
    dv_ref[0:length, :] = jnp.zeros((length, 128), F32)
    for qb in range(length // TILE):
        qrows = slice(base + qb * TILE, base + (qb + 1) * TILE)
        keys = (qb + 1) * TILE
        krows = slice(base, base + keys)
        q_pair = qkv_ref[qrows, lanes_of(pair * 128)] * BF16(HEAD_DIM**-0.5)
        g_pair = g_att_ref[qrows, lanes_of(pair * 128)]
        k_pair = qkv_ref[krows, lanes_of(D + pair * 128)]
        v_pair = qkv_ref[krows, lanes_of(2 * D + pair * 128)]
        q_pos = qb * TILE + lax.broadcasted_iota(jnp.int32, (1, TILE), 1)
        low = jnp.where(q_pos >= split, split, 0)
        k_pos = lax.broadcasted_iota(jnp.int32, (keys, TILE), 0)
        visible = (k_pos >= low) & (k_pos <= q_pos)
        dqs = []
        dk = dk_ref[0:keys, :]
        dv = dv_ref[0:keys, :]
        for half in (0, 1):
            mine = first if half == 0 else ~first
            q_half = jnp.where(mine, q_pair, BF16(0))
            g_half = jnp.where(mine, g_pair, BF16(0))
            lse = lse_t_ref[pl.ds(2 * pair + half, 1), qrows]
            s = jnp.where(visible, dot_nt(k_pair, q_half), NEG)
            p = jnp.exp(s - lse)
            dp = dot_nt(v_pair, g_half)
            inner = jnp.sum(p * dp, axis=0, keepdims=True)
            ds = (p * (dp - inner)).astype(BF16)
            dv = dv + dot(p.astype(BF16), g_half)
            dk = dk + dot(ds, q_half)
            dqs.append(dot_tn(ds, k_pair))
        dk_ref[0:keys, :] = dk
        dv_ref[0:keys, :] = dv
        dq = jnp.where(first, dqs[0], dqs[1]) * (HEAD_DIM**-0.5)
        g_qkv_ref[qrows, lanes_of(pair * 128)] = dq.astype(BF16)
    all_rows = slice(base, base + length)
    g_qkv_ref[all_rows, lanes_of(D + pair * 128)] = dk_ref[0:length, :].astype(BF16)
    g_qkv_ref[all_rows, lanes_of(2 * D + pair * 128)] = dv_ref[0:length, :].astype(BF16)


def ln1_back_tile(x_ref, g_mid_ref, table_ref, w_ref, g_qkv_ref, gx_ref, sums_ref, base, t):
    rows = rows_of(base, t)
    g_qkv = g_qkv_ref[rows, :]
    g_a1 = dot_nt(g_qkv, w_ref[:, 0 : 3 * D])
    own = rows_of(0, t)
    n, rstd = normalize(x_ref[own, :].astype(F32))
    gx_ref[own, :] = g_mid_ref[rows, :] + norm_backward(
        g_a1, n, rstd, table_ref[LN1G : LN1G + 1, :]
    )
    sums_ref[LN1G : LN1G + 1, :] += colsum(g_a1 * n)
    sums_ref[LN1B : LN1B + 1, :] += colsum(g_a1)
    sums_ref[QB : QB + 1, :] += colsum(g_qkv[:, 0:D].astype(F32))
    sums_ref[VB : VB + 1, :] += colsum(g_qkv[:, 2 * D : 3 * D].astype(F32))


def backward_kernel(
    ssplit,
    lsplit,
    xs,
    xl,
    table_ref,
    w_ref,
    a1_ref,
    qkv_ref,
    att_ref,
    lse_t_ref,
    g_mid_ref,
    gxs_ref,
    gxl_ref,
    dwp_ref,
    dwq_ref,
    sums_ref,
    g_attn_ref,
    g_att_ref,
    g_qkv_ref,
    dk_ref,
    dv_ref,
):
    sums_ref[...] = jnp.zeros_like(sums_ref)
    rows = xs.shape[0] + xl.shape[0]
    lax.fori_loop(
        0,
        rows // TILE,
        lambda t, c: (
            proj_back_tile(g_mid_ref, w_ref, g_attn_ref, g_att_ref, sums_ref, t),
            c,
        )[1],
        0,
    )
    dwp_ref[...] = dot_tn(att_ref[...], g_attn_ref[...])

    def pair_step(pair, c):
        for split, x_ref, base in ((ssplit[0], xs, 0), (lsplit[0], xl, xs.shape[0])):
            attend_back_pair(
                split, qkv_ref, g_att_ref, lse_t_ref, g_qkv_ref, dk_ref, dv_ref, base, x_ref.shape[0], pair
            )
        return c

    lax.fori_loop(0, PAIRS, pair_step, 0)
    for j in range(3):
        dwq_ref[:, j * D : (j + 1) * D] = dot_tn(a1_ref[...], g_qkv_ref[:, j * D : (j + 1) * D])
    for x_ref, gx_ref, base in ((xs, gxs_ref, 0), (xl, gxl_ref, xs.shape[0])):
        lax.fori_loop(
            0,
            x_ref.shape[0] // TILE,
            lambda t, c: (
                ln1_back_tile(
                    x_ref, g_mid_ref, table_ref, w_ref, g_qkv_ref, gx_ref, sums_ref, base, t
                ),
                c,
            )[1],
            0,
        )


def backward_local(ssplit, lsplit, xs, xl, table, w_attn, a1, qkv, att, lse_t, g_mid):
    rows = xs.shape[0] + xl.shape[0]
    return pl.pallas_call(
        backward_kernel,
        out_shape=(
            jax.ShapeDtypeStruct(xs.shape, F32),
            jax.ShapeDtypeStruct(xl.shape, F32),
            jax.ShapeDtypeStruct((D, D), F32),
            jax.ShapeDtypeStruct((D, 3 * D), F32),
            jax.ShapeDtypeStruct((8, D), F32),
        ),
        in_specs=[SM, SM] + [VM] * 9,
        out_specs=[VM] * 5,
        scratch_shapes=[
            pltpu.VMEM((rows, D), BF16),
            pltpu.VMEM((rows, D), BF16),
            pltpu.VMEM((rows, 3 * D), BF16),
            pltpu.VMEM((xl.shape[0], 128), F32),
            pltpu.VMEM((xl.shape[0], 128), F32),
        ],
        compiler_params=pltpu.CompilerParams(vmem_limit_bytes=VMEM_LIMIT),
        name="attention_backward",
    )(ssplit, lsplit, xs, xl, table, w_attn, a1, qkv, att, lse_t, g_mid)


MESH = pl.DeviceIdType.MESH
COLS, DEPTH = 4, 4


class Place:
    def __init__(self):
        q, f = lax.axis_index("dp"), lax.axis_index("fsdp")
        z = lax.div(f, 2)
        self.core = lax.rem(f, 2)
        self.col = [q, q + 1 - 2 * lax.rem(q, 2), lax.rem(q + 2, 4), 3 - q]
        self.depth = [lax.rem(z + k, DEPTH) for k in range(DEPTH)]
        self.index = q * 2 * DEPTH + f
        self.partner = (q, 2 * z + 1 - self.core)
        self.x = (self.col[1], f)
        self.y = (self.col[2], f)
        self.along = [(q, 2 * d + self.core) for d in self.depth]

    def greet(self):
        barrier = pltpu.get_barrier_semaphore()
        others = [self.partner, self.x, self.y] + self.along[1:]
        for device in others:
            pl.semaphore_signal(barrier, inc=1, device_id=device, device_id_type=MESH)
        pl.semaphore_wait(barrier, len(others))


def remote(src, dst, send, recv, device):
    return pltpu.make_async_remote_copy(
        src_ref=src, dst_ref=dst, send_sem=send, recv_sem=recv, device_id=device, device_id_type=MESH
    )


def at(start, size, step):
    return pl.ds(pl.multiple_of(start, step), size)


Z, X, Y, ACROSS, PAIR = 0, 3, 7, 11, 15
N_GATHER = 31
Y_PATH = (0, 3)


class Gather:
    def __init__(self, place, full, own, wide, send, recv):
        self.place, self.full, self.own, self.wide = place, full, own, wide
        self.send, self.recv = send, recv
        self.spots = {}
        for core in (0, 1):
            c = place.core if core == 0 else 1 - place.core
            for r in range(COLS):
                for k in range(DEPTH):
                    chip = place.col[r] * DEPTH + place.depth[k]
                    if wide:
                        half = full.shape[1] // 2
                        spot = full.at[at(chip * 48, 48, 16), at(c * half, half, 128)]
                    else:
                        spot = full.at[at((chip * 2 + c) * 96, 96, 16), :]
                    self.spots[core, r, k] = spot

    def copy(self, kind, r, k, arriving=False):
        place = self.place
        here = self.spots[0, r, k]
        src = self.own if (r, k) == (0, 0) and not arriving else here
        if kind == Z:
            n, device = (DEPTH - k if not arriving else k) - 1, place.along[k]
            src, here = (self.own, self.spots[0, 0, 0]) if not arriving else (here, here)
        elif kind == X:
            n, device = X + k, place.x
        elif kind == Y:
            n, device = Y + k, place.y
        elif kind == ACROSS:
            n, device = ACROSS + k, (place.y if k in Y_PATH else place.x)
        else:
            n, device = PAIR + 4 * r + k, place.partner
            if arriving:
                src = here = self.spots[1, r, k]
        sent = n if kind != Z else k - 1
        return remote(src, here, self.send.at[sent], self.recv.at[n], device)

    def begin(self):
        for k in range(1, DEPTH):
            self.copy(Z, 0, k).start()
        self.spread(0)

    def spread(self, k):
        self.copy(X, 0, k).start()
        self.copy(Y, 0, k).start()
        self.copy(PAIR, 0, k).start()

    def along(self, k):
        self.copy(Z, 0, k, True).wait_recv()
        self.spread(k)

    def across(self, k):
        self.copy(X, 1, k, True).wait_recv()
        if k in Y_PATH:
            self.copy(ACROSS, 1, k).start()
        self.copy(PAIR, 1, k).start()
        self.copy(Y, 2, k, True).wait_recv()
        if k not in Y_PATH:
            self.copy(ACROSS, 2, k).start()
        self.copy(PAIR, 2, k).start()

    def last(self, k):
        self.copy(ACROSS, 3, k, True).wait_recv()
        self.copy(PAIR, 3, k).start()

    def arrive(self):
        for r in range(COLS):
            for k in range(DEPTH):
                self.copy(PAIR, r, k, True).wait_recv()

    def end(self):
        for k in range(1, DEPTH):
            self.copy(Z, 0, k).wait_send()
        for k in range(DEPTH):
            self.copy(X, 0, k).wait_send()
            self.copy(Y, 0, k).wait_send()
            self.copy(ACROSS, 1 if k in Y_PATH else 2, k).wait_send()
            for r in range(COLS):
                self.copy(PAIR, r, k).wait_send()


def place_vectors(place, vectors, out):
    out[...] = jnp.zeros_like(out)
    for ref, row in zip(vectors, (LN1G, LN1B, QB, PROJB, LN2G, LN2B, OUTB, FCB)):
        size = ref.shape[1]
        start = place.index * size
        at_row, at_lane = lax.div(start, D), lax.rem(start, D)
        lane = lax.broadcasted_iota(jnp.int32, (size, D), 1)
        pick = lax.broadcasted_iota(jnp.int32, (size, D), 0) + at_lane == lane
        values = dot(ref[...], jnp.where(pick, 1.0, 0.0).astype(BF16))
        rows = (size * 32) // D
        mine = lax.broadcasted_iota(jnp.int32, (rows, D), 0) == at_row
        out[row : row + rows, :] = jnp.where(mine, values, 0.0)


SUM_STEPS = 6


class TableSum:
    def __init__(self, place, total, got, send, recv):
        self.place, self.total, self.got, self.send, self.recv = place, total, got, send, recv

    def copy(self, step, arriving=False):
        place = self.place
        if step == 0:
            device, n = place.partner, 0
        elif step <= 3:
            device, n = place.along[step], (step if arriving else 4 - step)
        else:
            device, n = (place.x, place.y)[step - 4], step
        stage = 0 if step == 0 else (1 if step <= 3 else step - 2)
        return remote(self.total.at[stage], self.got.at[n], self.send.at[step], self.recv.at[n], device)

    def begin(self, steps):
        for step in steps:
            self.copy(step).start()

    def add(self, stage, steps):
        for step in steps:
            self.copy(step, True).wait_recv()
        total = self.total[stage]
        for step in steps:
            total = total + self.got[step]
        self.total[stage + 1] = total

    def end(self):
        for step in range(SUM_STEPS):
            self.copy(step).wait_send()


def forward_gather_kernel(
    ssplit,
    lsplit,
    xs_hbm,
    xl_hbm,
    wqkv,
    wproj,
    wfc,
    wout,
    v0,
    v1,
    v2,
    v3,
    v4,
    v5,
    v6,
    v7,
    table_ref,
    wa_hbm,
    wf_hbm,
    wo_hbm,
    a1_hbm,
    qkv_hbm,
    att_hbm,
    lse_t_ref,
    mid_hbm,
    xs,
    xl,
    wa,
    a1_ref,
    qkv_ref,
    att_ref,
    mid_ref,
    lse_ref,
    slab_f,
    swap_out,
    swap_in,
    total,
    got,
    io_sem,
    swap_send,
    swap_recv,
    sum_send,
    sum_recv,
    g_send,
    g_recv,
):
    place = Place()
    loads = [pltpu.make_async_copy(xs_hbm, xs, io_sem.at[0]), pltpu.make_async_copy(xl_hbm, xl, io_sem.at[1])]
    for copy in loads:
        copy.start()
    place_vectors(place, (v0, v1, v2, v3, v4, v5, v6, v7), total.at[0])
    half = wa.shape[1] // 2
    mine, theirs = place.core * half, (1 - place.core) * half
    n_qkv = wqkv.shape[1]
    a_share = jnp.concatenate([wqkv[...], wproj[...]], axis=1).astype(F32)
    f_share = wfc[...].astype(F32)
    first = place.core == 0
    keep = []
    for n, share in enumerate((a_share, f_share)):
        left, right = share[:, 0:half], share[:, half : 2 * half]
        swap_out[n] = jnp.where(first, right, left)
        keep.append(jnp.where(first, left, right))
    place.greet()
    swaps = [
        remote(swap_out.at[n], swap_in.at[n], swap_send.at[n], swap_recv.at[n], place.partner)
        for n in range(2)
    ]
    sums = TableSum(place, total, got, sum_send, sum_recv)
    swaps[0].start()
    sums.begin((0,))
    swaps[1].start()

    def joined(n):
        swaps[n].wait_recv()
        other = swap_in[n]
        top, bottom = jnp.where(first, keep[n], other), jnp.where(first, other, keep[n])
        return jnp.concatenate([top, bottom], axis=0).astype(BF16)

    chip = place.col[0] * DEPTH + place.depth[0]
    spot = (at(chip * 48, 48, 16), at(mine, half, 128))
    wa[spot] = joined(0)
    ga = Gather(place, wa, wa.at[spot], True, g_send.at[0], g_recv.at[0])
    ga.begin()
    sums.add(0, (0,))
    sums.begin((1, 2, 3))
    slab_f[...] = joined(1)
    gf = Gather(place, wf_hbm, slab_f, True, g_send.at[1], g_recv.at[1])
    go = Gather(place, wo_hbm, wout, False, g_send.at[2], g_recv.at[2])
    own_f = pltpu.make_async_copy(slab_f, gf.spots[0, 0, 0], io_sem.at[2])
    own_o = pltpu.make_async_copy(wout, go.spots[0, 0, 0], io_sem.at[3])
    own_f.start()
    own_o.start()
    sums.add(1, (1, 2, 3))
    sums.begin((4,))
    ga.along(1)
    sums.add(2, (4,))
    sums.begin((5,))
    ga.along(3)
    sums.add(3, (5,))
    table_ref[...] = total[4]
    ga.along(2)
    for copy in loads:
        copy.wait()
    groups = group_refs(xs, xl)
    loop(groups[0][0].shape[0] // TILE, lambda t: norm_tile(xs, table_ref, a1_ref, 0, t))
    ga.across(0)
    gf.begin()
    loop(2, lambda t: norm_tile(xl, table_ref, a1_ref, groups[1][1], t))
    ga.across(1)
    ga.across(3)
    loop(xl.shape[0] // TILE - 2, lambda t: norm_tile(xl, table_ref, a1_ref, groups[1][1], t + 2))
    ga.across(2)
    go.begin()
    for k in range(DEPTH):
        ga.last(k)
    ga.arrive()
    stores = [
        pltpu.make_async_copy(src, dst, io_sem.at[4 + n])
        for n, (src, dst) in enumerate(
            (
                (wa, wa_hbm),
                (a1_ref, a1_hbm),
                (qkv_ref, qkv_hbm),
                (att_ref, att_hbm),
                (mid_ref, mid_hbm),
            )
        )
    ]
    stores[0].start()
    stores[1].start()

    def hooks(table):
        def run(i):
            for n, actions in table.items():

                @pl.when(i == n)
                def _():
                    for action, k in actions:
                        action(k)

        return run

    after = hooks(
        {
            0: ((gf.along, 1),),
            1: ((gf.along, 3),),
            2: ((gf.along, 2),),
            3: ((go.along, 1),),
            4: ((go.along, 3),),
            5: ((go.along, 2), (gf.across, 0)),
        }
    )

    def qkv_step(t):
        qkv_tile(table_ref, wa, a1_ref, qkv_ref, t)
        after(t)

    loop(a1_ref.shape[0] // TILE, qkv_step)
    stores[2].start()
    lse_ref[...] = jnp.zeros_like(lse_ref)
    after_short = hooks(
        {
            0: ((gf.across, 1),),
            1: ((gf.across, 2),),
            2: ((go.across, 1), (gf.last, 0)),
            3: ((go.across, 2), (gf.last, 3)),
            4: ((go.last, 0),),
            5: ((go.last, 1),),
        }
    )
    after_long = hooks(
        {
            0: ((gf.across, 3),),
            1: ((go.across, 0), (gf.last, 1)),
            2: ((go.across, 3), (gf.last, 2)),
            4: ((go.last, 3),),
            5: ((go.last, 2),),
        }
    )

    def pair_step(pair):
        attend_pair(ssplit[0], qkv_ref, att_ref, lse_ref, 0, xs.shape[0], pair)
        after_short(pair)
        attend_pair(lsplit[0], qkv_ref, att_ref, lse_ref, xs.shape[0], xl.shape[0], pair)
        after_long(pair)

    loop(PAIRS, pair_step)
    stores[3].start()
    lse_t_ref[...] = jnp.transpose(lse_ref[...])[:16, :]
    for x_ref, base in groups:
        loop(
            x_ref.shape[0] // TILE,
            lambda t: mid_tile(x_ref, table_ref, wa, att_ref, mid_ref, base, t),
        )
    stores[4].start()
    gf.arrive()
    go.arrive()
    own_f.wait()
    own_o.wait()
    for swap in swaps:
        swap.wait_send()
    sums.end()
    for g in (ga, gf, go):
        g.end()
    for copy in stores:
        copy.wait()


ANY = pl.BlockSpec(memory_space=pl.ANY)


def forward_gather(ssplit, lsplit, xs, xl, wqkv, wproj, wfc, wout, vectors):
    rows = xs.shape[0] + xl.shape[0]
    devices = 2 * COLS * DEPTH
    wide = wqkv.shape[1] + wproj.shape[1]
    full_out = jax.ShapeDtypeStruct((wout.shape[0] * devices, wout.shape[1]), BF16)
    sem = pltpu.SemaphoreType.DMA
    return pl.pallas_call(
        forward_gather_kernel,
        out_shape=(
            jax.ShapeDtypeStruct((16, D), F32),
            jax.ShapeDtypeStruct((D, wide), BF16),
            jax.ShapeDtypeStruct((D, wfc.shape[1]), BF16),
            full_out,
            jax.ShapeDtypeStruct((rows, D), BF16),
            jax.ShapeDtypeStruct((rows, 3 * D), BF16),
            jax.ShapeDtypeStruct((rows, D), BF16),
            jax.ShapeDtypeStruct((16, rows), F32),
            jax.ShapeDtypeStruct((rows, D), F32),
        ),
        in_specs=[SM, SM, ANY, ANY] + [VM] * 12,
        out_specs=[VM, ANY, ANY, ANY, ANY, ANY, ANY, VM, ANY],
        scratch_shapes=[
            pltpu.VMEM(xs.shape, BF16),
            pltpu.VMEM(xl.shape, BF16),
            pltpu.VMEM((D, wide), BF16),
            pltpu.VMEM((rows, D), BF16),
            pltpu.VMEM((rows, 3 * D), BF16),
            pltpu.VMEM((rows, D), BF16),
            pltpu.VMEM((rows, D), F32),
            pltpu.VMEM((rows, 128), F32),
            pltpu.VMEM((48, wfc.shape[1] // 2), BF16),
            pltpu.VMEM((2, 24, wide // 2), F32),
            pltpu.VMEM((2, 24, wide // 2), F32),
            pltpu.VMEM((5, 16, D), F32),
            pltpu.VMEM((SUM_STEPS, 16, D), F32),
            sem((9,)),
            sem((2,)),
            sem((2,)),
            sem((SUM_STEPS,)),
            sem((SUM_STEPS,)),
            sem((3, N_GATHER)),
            sem((3, N_GATHER)),
        ],
        compiler_params=pltpu.CompilerParams(
            vmem_limit_bytes=VMEM_LIMIT, collective_id=0, has_side_effects=True
        ),
        name="attention_forward_gather",
    )(ssplit, lsplit, xs, xl, wqkv, wproj, wfc, wout, *[v.reshape(1, -1) for v in vectors])


R_PAIR, R_X, R_Y, R_XB, R_YB, R_Z = 0, 4, 6, 8, 9, 10
N_REDUCE = 13
ORDER = (3, 1, 2, 0)


class Reduce:
    def __init__(self, place, src, own, total, xa, ya, xb, yb, zr, send, recv, own_sem):
        self.place, self.src, self.own, self.total = place, src, own, total
        self.xa, self.ya, self.xb, self.yb, self.zr = xa, ya, xb, yb, zr
        self.send, self.recv, self.own_sem = send, recv, own_sem

    def slabs(self, r, core):
        return self.src.at[pl.ds(self.place.col[r] * DEPTH, DEPTH), core]

    def pair(self, r):
        place = self.place
        n = R_PAIR + r
        return remote(
            self.slabs(r, 1 - place.core), self.total.at[r], self.send.at[n], self.recv.at[n], place.partner
        )

    def load(self, r):
        slot = ORDER.index(r) % 2
        return pltpu.make_async_copy(self.slabs(r, self.place.core), self.own.at[slot], self.own_sem.at[r])

    def to_x(self, n):
        src = self.total.at[(1, 3)[n], pl.ds(0, 2)]
        return remote(src, self.xa.at[n], self.send.at[R_X + n], self.recv.at[R_X + n], self.place.x)

    def to_y(self, n):
        src = self.total.at[(2, 3)[n], pl.ds(2, 2)]
        return remote(src, self.ya.at[n], self.send.at[R_Y + n], self.recv.at[R_Y + n], self.place.y)

    def to_xb(self):
        src = self.total.at[1, pl.ds(2, 2)]
        return remote(src, self.xb, self.send.at[R_XB], self.recv.at[R_XB], self.place.x)

    def to_yb(self):
        src = self.total.at[2, pl.ds(0, 2)]
        return remote(src, self.yb, self.send.at[R_YB], self.recv.at[R_YB], self.place.y)

    def to_z(self, k, arriving=False):
        n = (k if arriving else DEPTH - k) - 1
        src = self.total.at[0, self.place.depth[k]]
        return remote(
            src, self.zr.at[n], self.send.at[R_Z + k - 1], self.recv.at[R_Z + n], self.place.along[k]
        )

    def begin(self, loads=True):
        for r in ORDER:
            self.pair(r).start()
        if loads:
            self.begin_loads()

    def begin_loads(self):
        if self.own is not None:
            for r in ORDER[:2]:
                self.load(r).start()

    def chip(self, r):
        if self.own is not None:
            self.load(r).wait()
            mine = self.own[ORDER.index(r) % 2]
        else:
            mine = self.src[pl.ds(self.place.col[r] * DEPTH, DEPTH), self.place.core]
        self.pair(r).wait_recv()
        self.total[r] = self.total[r] + mine
        if self.own is not None and ORDER.index(r) < 2:
            self.load(ORDER[ORDER.index(r) + 2]).start()
        if r == 1:
            self.to_x(1).start()
            self.to_x(0).start()
        if r == 2:
            self.to_y(1).start()
            self.to_y(0).start()

    def chip_all(self):
        for r in ORDER:
            self.chip(r)

    def cross(self):
        self.to_x(1).wait_recv()
        self.total[2, 0:2] = self.total[2, 0:2] + self.xa[1]
        self.to_yb().start()
        self.to_y(1).wait_recv()
        self.total[1, 2:4] = self.total[1, 2:4] + self.ya[1]
        self.to_xb().start()

    def column(self):
        self.to_x(0).wait_recv()
        self.to_yb().wait_recv()
        add = lambda a, b, c: (a.astype(F32) + b.astype(F32) + c.astype(F32)).astype(BF16)
        self.total[0, 0:2] = add(self.total[0, 0:2], self.xa[0], self.yb[...])
        self.to_y(0).wait_recv()
        self.to_xb().wait_recv()
        self.total[0, 2:4] = add(self.total[0, 2:4], self.ya[0], self.xb[...])
        for k in (2, 1, 3):
            self.to_z(k).start()

    def result(self):
        out = self.total[0, self.place.depth[0]].astype(F32)
        for k in range(1, DEPTH):
            self.to_z(k, True).wait_recv()
            out = out + self.zr[k - 1].astype(F32)
        return out

    def end(self):
        for r in range(COLS):
            self.pair(r).wait_send()
        for n in range(2):
            self.to_x(n).wait_send()
            self.to_y(n).wait_send()
        self.to_xb().wait_send()
        self.to_yb().wait_send()
        for k in range(1, DEPTH):
            self.to_z(k).wait_send()


def take_vectors(place, table, outs):
    for ref, row in zip(outs, (LN1G, LN1B, QB, PROJB, LN2G, LN2B, OUTB, FCB)):
        size = ref.shape[1]
        rows = (size * 32) // D
        start = place.index * size
        at_row, at_lane = lax.div(start, D), lax.rem(start, D)
        mine = lax.broadcasted_iota(jnp.int32, (rows, D), 0) == at_row
        line = jnp.sum(jnp.where(mine, table[row : row + rows, :], 0.0), axis=0, keepdims=True)
        lane = lax.broadcasted_iota(jnp.int32, (size, D), 1)
        pick = lax.broadcasted_iota(jnp.int32, (size, D), 0) + at_lane == lane
        ref[...] = lax.dot_general(
            line,
            jnp.where(pick, 1.0, 0.0),
            (((1,), (1,)), ((), ())),
            preferred_element_type=F32,
            precision=lax.Precision.HIGHEST,
        )


def small_slabs(blocks):
    whole = jnp.concatenate(blocks, axis=1) if len(blocks) > 1 else blocks[0]
    devices, half = 2 * COLS * DEPTH, D // 2
    left = whole[:, 0:half].reshape(devices, 24, half)
    right = whole[:, half:D].reshape(devices, 24, half)
    both = jnp.concatenate([left, right], axis=1).astype(BF16)
    return both.reshape(COLS * DEPTH, 2, 48, half)


def backward_reduce_kernel(
    ssplit,
    lsplit,
    xs_hbm,
    xl_hbm,
    table_ref,
    wa_hbm,
    a1_hbm,
    qkv_hbm,
    att_hbm,
    lse_t_ref,
    g_mid_hbm,
    sums2_ref,
    go_hbm,
    gf_hbm,
    gxs_hbm,
    gxl_hbm,
    d0,
    d1,
    d2,
    d3,
    d4,
    d5,
    d6,
    d7,
    d_qkv,
    d_proj,
    d_fc,
    d_out,
    wa,
    a1_ref,
    qkv_ref,
    att_ref,
    g_mid_ref,
    g_att_ref,
    g_qkv_ref,
    dk_ref,
    dv_ref,
    big_own,
    big_total,
    big_xa,
    big_ya,
    big_xb,
    big_yb,
    big_zr,
    small_src,
    small_total,
    small_xa,
    small_ya,
    small_xb,
    small_yb,
    small_zr,
    total,
    got,
    io_sem,
    own_sem,
    r_send,
    r_recv,
    sum_send,
    sum_recv,
):
    place = Place()
    g_attn_ref = g_qkv_ref.at[:, pl.ds(0, D)]
    short, long = gxs_hbm.shape[0], gxl_hbm.shape[0]
    rows = short + long
    proj_cols = pl.ds(3 * D, D)
    qkv_cols = pl.ds(0, 3 * D)
    loads = [
        pltpu.make_async_copy(src, dst, io_sem.at[n])
        for n, (src, dst) in enumerate(
            (
                (wa_hbm.at[:, proj_cols], wa.at[:, proj_cols]),
                (g_mid_hbm, g_mid_ref),
                (att_hbm, att_ref),
                (qkv_hbm, qkv_ref),
                (a1_hbm, a1_ref),
                (wa_hbm.at[:, qkv_cols], wa.at[:, qkv_cols]),
            )
        )
    ]
    for copy in loads:
        copy.start()
    sums = TableSum(place, total, got, sum_send, sum_recv)
    sums_ref = total.at[0]
    sums_ref[...] = jnp.zeros_like(sums_ref)
    sums_ref[LN2G : LN2G + 7, :] = sums2_ref[0:7, :]
    big = [
        Reduce(
            place, src, big_own, big_total.at[n], big_xa.at[n], big_ya.at[n], big_xb.at[n],
            big_yb.at[n], big_zr.at[n], r_send.at[n], r_recv.at[n], own_sem.at[n],
        )
        for n, src in enumerate((go_hbm, gf_hbm))
    ]
    small = [
        Reduce(
            place, small_src.at[n], None, small_total.at[n], small_xa.at[n], small_ya.at[n], small_xb.at[n],
            small_yb.at[n], small_zr.at[n], r_send.at[2 + n], r_recv.at[2 + n], None,
        )
        for n in range(4)
    ]
    ro, rf = big
    rp, rh = small[3], small[0:3]
    place.greet()
    ro.begin()
    rf.begin(False)
    loads[0].wait()
    loads[1].wait()

    def hooks(table):
        def run(i):
            for n, actions in table.items():

                @pl.when(i == n)
                def _():
                    for action, *args in actions:
                        action(*args)

        return run

    after = hooks(
        {
            0: ((ro.chip, 3),),
            1: ((ro.chip, 1),),
            2: ((ro.chip, 2),),
            3: ((ro.chip, 0), (rf.begin_loads,)),
            4: ((rf.chip, 3),),
            5: ((rf.chip, 1),),
        }
    )

    def proj_step(t):
        proj_back_tile(g_mid_ref, wa, g_attn_ref, g_att_ref, sums_ref, t)
        after(t)

    loop(rows // TILE, proj_step)
    loads[2].wait()
    small_src[3] = small_slabs([dot_tn(att_ref[...], g_attn_ref[...])])
    rp.begin()
    rf.chip(2)
    rf.chip(0)
    x_loads = [
        pltpu.make_async_copy(xs_hbm, att_ref.at[pl.ds(0, short)], io_sem.at[6]),
        pltpu.make_async_copy(xl_hbm, att_ref.at[pl.ds(short, long)], io_sem.at[7]),
    ]
    for copy in x_loads:
        copy.start()
    for copy in loads[3:]:
        copy.wait()

    def give_out():
        d_out[...] = ro.result()

    def give_fc():
        res = rf.result()
        for j in range(4):
            d_fc[:, j * D : (j + 1) * D] = res[24 * j : 24 * j + 24, :]

    def give_proj():
        res = rp.result()
        d_proj[:, 0 : D // 2] = res[0:24]
        d_proj[:, D // 2 : D] = res[24:48]

    def give_qkv(g):
        res = rh[g].result()
        line = jnp.concatenate([res[0:24], res[24:48]], axis=1)
        for j in range(3):
            d_qkv[:, j * D + g * 256 : j * D + g * 256 + 256] = line[:, j * 256 : j * 256 + 256]

    def heads_begin(g):
        rh[g].begin()

    after_short = hooks(
        {
            0: ((rp.chip_all,),),
            2: ((rh[0].chip_all,),),
            3: ((ro.column,),),
            4: ((rh[1].chip_all,),),
            5: ((rh[0].column,), (rh[1].cross,)),
        }
    )
    after_long = hooks(
        {
            0: ((ro.cross,),),
            1: ((heads_begin, 0),),
            2: ((rf.cross,), (rp.cross,)),
            3: ((heads_begin, 1), (rf.column,), (rp.column,), (rh[0].cross,)),
            4: ((give_out,), (give_proj,)),
            5: ((heads_begin, 2), (give_fc,), (give_qkv, 0), (rh[1].column,)),
        }
    )

    def pair_step(pair):
        attend_back_pair(
            ssplit[0], qkv_ref, g_att_ref, lse_t_ref, g_qkv_ref, dk_ref, dv_ref, 0, short, pair
        )
        after_short(pair)
        attend_back_pair(
            lsplit[0], qkv_ref, g_att_ref, lse_t_ref, g_qkv_ref, dk_ref, dv_ref, short, long, pair
        )

        @pl.when(lax.rem(pair, 2) == 1)
        def _():
            g = lax.div(pair, 2)
            blocks = [
                dot_tn(a1_ref[...], g_qkv_ref[:, pl.ds(pl.multiple_of(j * D + g * 256, 128), 256)])
                for j in range(3)
            ]
            small_src[g] = small_slabs(blocks)

        after_long(pair)

    loop(PAIRS, pair_step)
    for copy in x_loads:
        copy.wait()
    after_norm = hooks(
        {
            0: ((rh[2].chip_all,),),
            2: ((rh[2].cross,),),
            3: ((give_qkv, 1),),
            4: ((rh[2].column,),),
        }
    )

    def norm_step(t):
        ln1_back_tile(att_ref, g_mid_ref, table_ref, wa, g_qkv_ref, g_mid_ref, sums_ref, 0, t)
        after_norm(t)

    loop(rows // TILE, norm_step)
    stores = [
        pltpu.make_async_copy(g_mid_ref.at[pl.ds(0, short)], gxs_hbm, io_sem.at[8]),
        pltpu.make_async_copy(g_mid_ref.at[pl.ds(short, long)], gxl_hbm, io_sem.at[9]),
    ]
    for copy in stores:
        copy.start()
    sums.begin((0,))
    sums.add(0, (0,))
    sums.begin((1, 2, 3))
    give_qkv(2)
    sums.add(1, (1, 2, 3))
    sums.begin((4,))
    sums.add(2, (4,))
    sums.begin((5,))
    sums.add(3, (5,))
    take_vectors(place, total.at[4], (d0, d1, d2, d3, d4, d5, d6, d7))
    sums.end()
    for reduce in big + small:
        reduce.end()
    for copy in stores:
        copy.wait()


def backward_reduce(ssplit, lsplit, xs, xl, table, w_attn, a1, qkv, att, lse_t, g_mid, sums2, dwo, dwf, sizes):
    short, long = xs.shape[0], xl.shape[0]
    rows = short + long
    chips = COLS * DEPTH
    devices = 2 * chips
    big, little = (96, D), (48, D // 2)
    slabs = lambda g: g.reshape(chips, 2, *big)
    sem = pltpu.SemaphoreType.DMA
    buffers = lambda n, shape: [
        pltpu.VMEM((n, COLS, DEPTH) + shape, BF16),
        pltpu.VMEM((n, 2, 2) + shape, BF16),
        pltpu.VMEM((n, 2, 2) + shape, BF16),
        pltpu.VMEM((n, 2) + shape, BF16),
        pltpu.VMEM((n, 2) + shape, BF16),
        pltpu.VMEM((n, DEPTH - 1) + shape, BF16),
    ]
    return pl.pallas_call(
        backward_reduce_kernel,
        out_shape=(
            jax.ShapeDtypeStruct(xs.shape, F32),
            jax.ShapeDtypeStruct(xl.shape, F32),
            *[jax.ShapeDtypeStruct((1, n), F32) for n in sizes],
            jax.ShapeDtypeStruct((D // devices, 3 * D), F32),
            jax.ShapeDtypeStruct((D // devices, D), F32),
            jax.ShapeDtypeStruct((D // devices, FF), F32),
            jax.ShapeDtypeStruct((FF // devices, D), F32),
        ),
        in_specs=[SM, SM, ANY, ANY, VM, ANY, ANY, ANY, ANY, VM, ANY, VM, ANY, ANY],
        out_specs=[ANY, ANY] + [VM] * 12,
        scratch_shapes=[
            pltpu.VMEM((D, 4 * D), BF16),
            pltpu.VMEM((rows, D), BF16),
            pltpu.VMEM((rows, 3 * D), BF16),
            pltpu.VMEM((rows, D), BF16),
            pltpu.VMEM((rows, D), F32),
            pltpu.VMEM((rows, D), BF16),
            pltpu.VMEM((rows, 3 * D), BF16),
            pltpu.VMEM((long, 128), F32),
            pltpu.VMEM((long, 128), F32),
            pltpu.VMEM((2, DEPTH) + big, BF16),
            *buffers(2, big),
            pltpu.VMEM((4, chips, 2) + little, BF16),
            *buffers(4, little),
            pltpu.VMEM((5, 16, D), F32),
            pltpu.VMEM((SUM_STEPS, 16, D), F32),
            sem((10,)),
            sem((2, COLS)),
            sem((6, N_REDUCE)),
            sem((6, N_REDUCE)),
            sem((SUM_STEPS,)),
            sem((SUM_STEPS,)),
        ],
        compiler_params=pltpu.CompilerParams(
            vmem_limit_bytes=BACK_VMEM, collective_id=1, has_side_effects=True
        ),
        name="attention_backward_reduce",
    )(ssplit, lsplit, xs, xl, table, w_attn, a1, qkv, att, lse_t, g_mid, sums2, slabs(dwo), slabs(dwf))


BACK_VMEM = 60 * 2**20


AXES = ("dp", "fsdp")


def gather(x, axis=0):
    return lax.all_gather(x, AXES, axis=axis, tiled=True)


def scatter(x):
    return lax.psum_scatter(x, AXES, scatter_dimension=0, tiled=True)


def general(args, devices):
    (st, lt, ss, ls, ln1g, ln1b, wqkv, qvb, wproj, projb, ln2g, ln2b, wfc, fcb, wout, outb, sc, lc) = args
    xs, xl = st.reshape(-1, D), lt.reshape(-1, D)
    cs, cl = sc.reshape(-1, D), lc.reshape(-1, D)
    vectors = (ln1g, ln1b, qvb, projb, ln2g, ln2b, outb, fcb)
    sizes = [v.shape[0] for v in vectors]
    every = lax.all_gather(jnp.concatenate(vectors), AXES, axis=0)
    starts = [sum(sizes[:i]) for i in range(len(sizes))]
    full = [every[:, s : s + n].reshape(-1, D) for s, n in zip(starts, sizes)]
    table = jnp.concatenate(full + [jnp.zeros((4, D), BF16)]).astype(F32)
    w_attn = gather(jnp.concatenate([wqkv, wproj], axis=1))
    w_fc, w_out = gather(wfc), gather(wout)
    a1, qkv, att, lse_t, mid = forward_local(ss, ls, xs, xl, table, w_attn)
    out_s, out_l, g_mid, sums2, dwf, dwo = mlp_local(mid, cs, cl, table, w_fc, w_out, False)
    gxs, gxl, dwp, dwq, sums1 = backward_local(
        ss, ls, xs, xl, table, w_attn, a1, qkv, att, lse_t, g_mid
    )
    return finish(args, devices, starts, sizes, out_s, out_l, gxs, gxl, sums1, sums2, dwq, dwp, dwf, dwo)


def finish(args, devices, starts, sizes, out_s, out_l, gxs, gxl, sums1, sums2, dwq, dwp, dwf, dwo):
    st, lt = args[0], args[1]
    rs = lambda x: x.reshape(devices, -1)
    small = jnp.concatenate(
        [
            rs(sums1[0]),
            rs(sums1[1]),
            rs(sums1[2:4]),
            rs(sums1[4]),
            rs(sums2[0]),
            rs(sums2[1]),
            rs(sums2[2]),
            rs(sums2[3:7]),
        ],
        axis=1,
    )
    small = scatter(small)[0]
    parts = [small[s : s + n] for s, n in zip(starts, sizes)]
    d_ln1g, d_ln1b, d_qvb, d_projb, d_ln2g, d_ln2b, d_outb, d_fcb = parts
    return (
        out_s.reshape(st.shape),
        out_l.reshape(lt.shape),
        gxs.reshape(st.shape),
        gxl.reshape(lt.shape),
        d_ln1g,
        d_ln1b,
        scatter(dwq),
        d_qvb,
        scatter(dwp),
        d_projb,
        d_ln2g,
        d_ln2b,
        scatter(dwf),
        d_fcb,
        scatter(dwo),
        d_outb,
    )


def on_torus(args):
    (st, lt, ss, ls, ln1g, ln1b, wqkv, qvb, wproj, projb, ln2g, ln2b, wfc, fcb, wout, outb, sc, lc) = args
    xs, xl = st.reshape(-1, D), lt.reshape(-1, D)
    cs, cl = sc.reshape(-1, D), lc.reshape(-1, D)
    vectors = (ln1g, ln1b, qvb, projb, ln2g, ln2b, outb, fcb)
    table, w_attn, w_fc, w_out, a1, qkv, att, lse_t, mid = forward_gather(
        ss, ls, xs, xl, wqkv, wproj, wfc, wout, vectors
    )
    out_s, out_l, g_mid, sums2, dwf, dwo = mlp_local(mid, cs, cl, table, w_fc, w_out, True)
    gxs, gxl, *rest = backward_reduce(
        ss, ls, xs, xl, table, w_attn, a1, qkv, att, lse_t, g_mid, sums2, dwo, dwf, [v.shape[0] for v in vectors]
    )
    d_ln1g, d_ln1b, d_qvb, d_projb, d_ln2g, d_ln2b, d_outb, d_fcb = [v.reshape(-1) for v in rest[:8]]
    d_qkv, d_proj, d_fc, d_out = rest[8:]
    return (
        out_s.reshape(st.shape),
        out_l.reshape(lt.shape),
        gxs.reshape(st.shape),
        gxl.reshape(lt.shape),
        d_ln1g,
        d_ln1b,
        d_qkv,
        d_qvb,
        d_proj,
        d_projb,
        d_ln2g,
        d_ln2b,
        d_fc,
        d_fcb,
        d_out,
        d_outb,
    )


def per_device(shape, *args):
    devices = shape["dp"] * shape["fsdp"]
    sizes = (args[0].shape[1], args[1].shape[1], args[6].shape, args[14].shape)
    if shape == {"dp": COLS, "fsdp": 2 * DEPTH} and sizes == (512, 1024, (24, 3 * D), (96, D)):
        return on_torus(args)
    return general(args, devices)


def solution(mesh):
    vec, mat, seq = P(AXES), P(AXES, None), P(AXES, None, None)
    in_specs = (seq, seq, vec, vec) + (vec, vec, mat, vec, mat, vec) * 1 + (vec, vec, mat, vec, mat, vec) + (seq, seq)
    out_specs = (seq,) * 4 + (vec, vec, mat, vec, mat, vec) * 2
    return jax.shard_map(
        functools.partial(per_device, dict(mesh.shape)),
        mesh=mesh,
        in_specs=in_specs,
        out_specs=out_specs,
        check_vma=False,
    )
```

```python
import functools

import jax
import jax.numpy as jnp
from jax import lax
from jax.experimental import pallas as pl
from jax.experimental.pallas import tpu as pltpu
from jax.sharding import PartitionSpec as P

F32 = jnp.float32
BF16 = jnp.bfloat16
D = 768
FF = 3072
HEAD_DIM = 64
PAIRS = D // 128
GROUP = 256
GROUPS = D // GROUP
TILE = 256
BRANCH = 0.14433756729740643
EPS = 1e-05
NEG = -1e30
VMEM_LIMIT = 60 * 2**20

LN1G, LN1B, QB, VB, PROJB, LN2G, LN2B, OUTB, FCB = 0, 1, 2, 3, 4, 5, 6, 7, 8


def dot(a, b):
    return jnp.dot(a, b, preferred_element_type=F32)


def dot_nt(a, b):
    return lax.dot_general(a, b, (((1,), (1,)), ((), ())), preferred_element_type=F32)


def dot_tn(a, b):
    return lax.dot_general(a, b, (((0,), (0,)), ((), ())), preferred_element_type=F32)


def normalize(x):
    center = x - jnp.mean(x, axis=-1, keepdims=True)
    rstd = lax.rsqrt(jnp.mean(center * center, axis=-1, keepdims=True) + EPS)
    return center * rstd, rstd


def norm_backward(g, n, rstd, gain):
    e = g * gain
    return rstd * (
        e
        - jnp.mean(e, axis=-1, keepdims=True)
        - n * jnp.mean(e * n, axis=-1, keepdims=True)
    )


def rows_of(base, tile):
    return pl.ds(pl.multiple_of(base + tile * TILE, TILE), TILE)


def lanes_of(start):
    return pl.ds(pl.multiple_of(start, 128), 128)


def loop(count, body):
    lax.fori_loop(0, count, lambda i, c: (body(i), c)[1], 0)


def group_refs(short, long):
    return ((short, 0), (long, short.shape[0]))


def norm_tile(x_ref, table_ref, a1_ref, base, t):
    n, _ = normalize(x_ref[rows_of(0, t), :].astype(F32))
    a1 = n * table_ref[LN1G : LN1G + 1, :] + table_ref[LN1B : LN1B + 1, :]
    a1_ref[rows_of(base, t), :] = a1.astype(BF16)


def group_cols(g, part):
    start = g * D + part * GROUP
    return pl.ds(start if isinstance(start, int) else pl.multiple_of(start, 128), GROUP)


def pair_cols(pair, part):
    return lanes_of(lax.div(pair, 2) * D + part * GROUP + lax.rem(pair, 2) * 128)


def vector_cols(g):
    return pl.ds(g * GROUP if isinstance(g, int) else pl.multiple_of(g * GROUP, 128), GROUP)


def qkv_tile(table_ref, w_ref, a1_ref, qkv_ref, g, t):
    rows = rows_of(0, t)
    a1 = a1_ref[rows, :]
    for part, bias in ((0, QB), (1, None), (2, VB)):
        out = dot(a1, w_ref[:, group_cols(g, part)])
        if bias is not None:
            out = out + table_ref[bias : bias + 1, vector_cols(g)]
        qkv_ref[rows, group_cols(g, part)] = out.astype(BF16)


def attend_pair(split, qkv_ref, att_ref, lse_ref, base, length, pair):
    first = lax.broadcasted_iota(jnp.int32, (TILE, 128), 1) < HEAD_DIM
    head_lane = lax.broadcasted_iota(jnp.int32, (TILE, 128), 1)
    for qb in range(length // TILE):
        qrows = slice(base + qb * TILE, base + (qb + 1) * TILE)
        keys = (qb + 1) * TILE
        krows = slice(base, base + keys)
        q_pair = qkv_ref[qrows, pair_cols(pair, 0)] * BF16(HEAD_DIM**-0.5)
        k_pair = qkv_ref[krows, pair_cols(pair, 1)]
        v_pair = qkv_ref[krows, pair_cols(pair, 2)]
        q_pos = qb * TILE + lax.broadcasted_iota(jnp.int32, (TILE, 1), 0)
        low = jnp.where(q_pos >= split, split, 0)
        k_pos = lax.broadcasted_iota(jnp.int32, (TILE, keys), 1)
        visible = (k_pos >= low) & (k_pos <= q_pos)
        outs = []
        lse_new = lse_ref[qrows, :]
        for half in (0, 1):
            mine = first if half == 0 else ~first
            s = dot_nt(jnp.where(mine, q_pair, BF16(0)), k_pair)
            s = jnp.where(visible, s, NEG)
            peak = jnp.max(s, axis=-1, keepdims=True)
            e = jnp.exp(s - peak)
            total = jnp.sum(e, axis=-1, keepdims=True)
            p = (e * (1.0 / total)).astype(BF16)
            outs.append(dot(p, v_pair))
            lse_new = jnp.where(head_lane == 2 * pair + half, peak + jnp.log(total), lse_new)
        lse_ref[qrows, :] = lse_new
        att_ref[qrows, lanes_of(pair * 128)] = jnp.where(first, outs[0], outs[1]).astype(BF16)


def mid_tile(x_ref, table_ref, w_ref, att_ref, mid_ref, base, t):
    rows = rows_of(base, t)
    out = dot(att_ref[rows, :], w_ref[:, 3 * D : 4 * D]) + table_ref[PROJB : PROJB + 1, :]
    mid_ref[rows, :] = x_ref[rows_of(0, t), :].astype(F32) + BRANCH * out


def forward_kernel(
    ssplit, lsplit, xs, xl, table_ref, w_ref, a1_ref, qkv_ref, att_ref, lse_t_ref, mid_ref, lse_ref
):
    for x_ref, base in group_refs(xs, xl):
        loop(x_ref.shape[0] // TILE, lambda t: norm_tile(x_ref, table_ref, a1_ref, base, t))
    for g in range(GROUPS):
        loop(a1_ref.shape[0] // TILE, lambda t: qkv_tile(table_ref, w_ref, a1_ref, qkv_ref, g, t))
    lse_ref[...] = jnp.zeros_like(lse_ref)

    def pair_step(pair, c):
        attend_pair(ssplit[0], qkv_ref, att_ref, lse_ref, 0, xs.shape[0], pair)
        attend_pair(lsplit[0], qkv_ref, att_ref, lse_ref, xs.shape[0], xl.shape[0], pair)
        return c

    lax.fori_loop(0, PAIRS, pair_step, 0)
    lse_t_ref[...] = jnp.transpose(lse_ref[...])[:16, :]
    for x_ref, base in group_refs(xs, xl):
        lax.fori_loop(
            0,
            x_ref.shape[0] // TILE,
            lambda t, c: (mid_tile(x_ref, table_ref, w_ref, att_ref, mid_ref, base, t), c)[1],
            0,
        )


VM = pl.BlockSpec(memory_space=pltpu.VMEM)
SM = pl.BlockSpec(memory_space=pltpu.SMEM)


def forward_local(ssplit, lsplit, xs, xl, table, w_attn):
    rows = xs.shape[0] + xl.shape[0]
    return pl.pallas_call(
        forward_kernel,
        out_shape=(
            jax.ShapeDtypeStruct((rows, D), BF16),
            jax.ShapeDtypeStruct((rows, 3 * D), BF16),
            jax.ShapeDtypeStruct((rows, D), BF16),
            jax.ShapeDtypeStruct((16, rows), F32),
            jax.ShapeDtypeStruct((rows, D), F32),
        ),
        in_specs=[SM, SM, VM, VM, VM, VM],
        out_specs=[VM] * 5,
        scratch_shapes=[pltpu.VMEM((rows, 128), F32)],
        compiler_params=pltpu.CompilerParams(vmem_limit_bytes=VMEM_LIMIT),
        name="attention_forward",
    )(ssplit, lsplit, xs, xl, table, w_attn)


GELU_A = 0.7978845608028654
GELU_B = 0.044715


def mlp_tile(mid, g_out, table_ref, wf_ref, wo_ref):
    n2, rstd = normalize(mid)
    gain = table_ref[LN2G : LN2G + 1, :]
    a2 = (n2 * gain + table_ref[LN2B : LN2B + 1, :]).astype(BF16)
    g_mlp = (BRANCH * g_out).astype(BF16)
    out = None
    g_a2 = None
    acts, g_pres = [], []
    for j in range(FF // D):
        cols = slice(j * D, (j + 1) * D)
        pre = dot(a2, wf_ref[:, cols]) + table_ref[FCB + j : FCB + j + 1, :]
        g_act = dot_nt(g_mlp, wo_ref[cols, :])
        square = pre * pre
        t = jnp.tanh(pre * (GELU_A + (GELU_A * GELU_B) * square))
        half = 0.5 + 0.5 * t
        act = (pre * half).astype(BF16)
        slope = half + pre * (0.5 - 0.5 * t * t) * (GELU_A + (3 * GELU_A * GELU_B) * square)
        g_pre = (g_act * slope).astype(BF16)
        acts.append(act)
        g_pres.append(g_pre)
        part = dot(act, wo_ref[cols, :])
        out = part if out is None else out + part
        part = dot_nt(g_pre, wf_ref[:, cols])
        g_a2 = part if g_a2 is None else g_a2 + part
    out = mid + BRANCH * (out + table_ref[OUTB : OUTB + 1, :])
    g_mid = g_out + norm_backward(g_a2, n2, rstd, gain)
    return out, g_mid, a2, g_mlp, acts, g_pres, g_a2, n2


def colsum(x):
    return jnp.sum(x, axis=0, keepdims=True)


def mlp_kernel(
    n_tiles,
    slabs,
    mid_ref,
    cs_ref,
    cl_ref,
    table_ref,
    wf_ref,
    wo_ref,
    os_ref,
    ol_ref,
    g_mid_ref,
    sums_ref,
    dwf_ref,
    dwo_ref,
    a2_ref,
    g_mlp_ref,
    act_ref,
    g_pre_ref,
):
    step = pl.program_id(0)
    short_tiles = n_tiles[0]
    tiles = n_tiles[0] + n_tiles[1]

    @pl.when(step == 0)
    def _():
        sums_ref[...] = jnp.zeros_like(sums_ref)

    @pl.when(step < tiles)
    def _():
        cot = jnp.where(step < short_tiles, cs_ref[...], cl_ref[...]).astype(F32)
        out, g_mid, a2, g_mlp, acts, g_pres, g_a2, n2 = mlp_tile(
            mid_ref[...], cot, table_ref, wf_ref, wo_ref
        )
        out = out.astype(BF16)

        @pl.when(step < short_tiles)
        def _():
            os_ref[...] = out

        @pl.when(step >= short_tiles)
        def _():
            ol_ref[...] = out

        g_mid_ref[...] = g_mid
        rows = rows_of(0, step)
        a2_ref[rows, :] = a2
        g_mlp_ref[rows, :] = g_mlp
        sums_ref[0:1, :] += colsum(g_a2 * n2)
        sums_ref[1:2, :] += colsum(g_a2)
        sums_ref[2:3, :] += colsum(g_mlp.astype(F32))
        for j in range(FF // D):
            act_ref[rows, j * D : (j + 1) * D] = acts[j]
            g_pre_ref[rows, j * D : (j + 1) * D] = g_pres[j]
            sums_ref[3 + j : 4 + j, :] += colsum(g_pres[j].astype(F32))

    for j in range(4):

        @pl.when(step == tiles + j)
        def _(j=j):
            res = dot_tn(act_ref[:, j * D : (j + 1) * D], g_mlp_ref[...])
            if slabs:
                dwo_ref[...] = res.astype(BF16).reshape(dwo_ref.shape)
            else:
                dwo_ref[...] = res

    for j in range(2 if slabs else 4):

        @pl.when(step == tiles + 4 + j)
        def _(j=j):
            if slabs:
                dev = D // 24
                left = dot_tn(a2_ref[...], g_pre_ref[:, 2 * j * D : (2 * j + 1) * D])
                right = dot_tn(a2_ref[...], g_pre_ref[:, (2 * j + 1) * D : (2 * j + 2) * D])
                both = jnp.concatenate(
                    [left.reshape(dev, 24, D), right.reshape(dev, 24, D)], axis=1
                )
                dwf_ref[...] = both.astype(BF16)
            else:
                dwf_ref[...] = dot_tn(a2_ref[...], g_pre_ref[:, j * D : (j + 1) * D])


def mlp_local(mid, cs, cl, table, w_fc, w_out, slabs):
    rows = mid.shape[0]
    ns, nl = cs.shape[0] // TILE, cl.shape[0] // TILE
    tiles = ns + nl
    steps = tiles + (6 if slabs else 8)
    whole = lambda shape: pl.BlockSpec(shape, lambda i: (0, 0), pipeline_mode=pl.Buffered(1))
    tile = lambda f: pl.BlockSpec((TILE, D), f)
    short_at = lambda i: (jnp.minimum(i, ns - 1), 0)
    long_at = lambda i: (jnp.clip(i - ns, 0, nl - 1), 0)
    all_at = lambda i: (jnp.minimum(i, tiles - 1), 0)
    if slabs:
        dev = D // 24
        dwo_shape = jax.ShapeDtypeStruct((dev, 96, D), BF16)
        dwo_spec = pl.BlockSpec((dev // 4, 96, D), lambda i: (jnp.clip(i - tiles, 0, 3), 0, 0))
        dwf_shape = jax.ShapeDtypeStruct((dev, 96, D), BF16)
        dwf_spec = pl.BlockSpec((dev, 48, D), lambda i: (0, jnp.clip(i - tiles - 4, 0, 1), 0))
    else:
        dwo_shape = jax.ShapeDtypeStruct((FF, D), F32)
        dwo_spec = pl.BlockSpec((D, D), lambda i: (jnp.clip(i - tiles, 0, 3), 0))
        dwf_shape = jax.ShapeDtypeStruct((D, FF), F32)
        dwf_spec = pl.BlockSpec((D, D), lambda i: (0, jnp.clip(i - tiles - 4, 0, 3)))
    return pl.pallas_call(
        functools.partial(mlp_kernel, (ns, nl), slabs),
        grid=(steps,),
        out_shape=(
            jax.ShapeDtypeStruct(cs.shape, BF16),
            jax.ShapeDtypeStruct(cl.shape, BF16),
            jax.ShapeDtypeStruct((rows, D), F32),
            jax.ShapeDtypeStruct((8, D), F32),
            dwf_shape,
            dwo_shape,
        ),
        in_specs=[
            tile(all_at),
            tile(short_at),
            tile(long_at),
            whole(table.shape),
            whole(w_fc.shape),
            whole(w_out.shape),
        ],
        out_specs=[
            tile(short_at),
            tile(long_at),
            tile(all_at),
            pl.BlockSpec((8, D), lambda i: (0, 0)),
            dwf_spec,
            dwo_spec,
        ],
        scratch_shapes=[
            pltpu.VMEM((rows, D), BF16),
            pltpu.VMEM((rows, D), BF16),
            pltpu.VMEM((rows, FF), BF16),
            pltpu.VMEM((rows, FF), BF16),
        ],
        compiler_params=pltpu.CompilerParams(vmem_limit_bytes=VMEM_LIMIT),
        name="mlp",
    )(mid, cs, cl, table, w_fc, w_out)


def proj_back_tile(g_mid_ref, w_ref, g_attn_ref, g_att_ref, sums_ref, t):
    rows = rows_of(0, t)
    g_attn = (BRANCH * g_mid_ref[rows, :]).astype(BF16)
    g_attn_ref[rows, :] = g_attn
    g_att_ref[rows, :] = dot_nt(g_attn, w_ref[:, 3 * D : 4 * D]).astype(BF16)
    sums_ref[PROJB : PROJB + 1, :] += colsum(g_attn.astype(F32))


def attend_back_pair(split, qkv_ref, g_att_ref, lse_t_ref, g_qkv_ref, dk_ref, dv_ref, base, length, pair):
    first = lax.broadcasted_iota(jnp.int32, (TILE, 128), 1) < HEAD_DIM
    dk_ref[0:length, :] = jnp.zeros((length, 128), F32)
    dv_ref[0:length, :] = jnp.zeros((length, 128), F32)
    for qb in range(length // TILE):
        qrows = slice(base + qb * TILE, base + (qb + 1) * TILE)
        keys = (qb + 1) * TILE
        krows = slice(base, base + keys)
        q_pair = qkv_ref[qrows, pair_cols(pair, 0)] * BF16(HEAD_DIM**-0.5)
        g_pair = g_att_ref[qrows, lanes_of(pair * 128)]
        k_pair = qkv_ref[krows, pair_cols(pair, 1)]
        v_pair = qkv_ref[krows, pair_cols(pair, 2)]
        q_pos = qb * TILE + lax.broadcasted_iota(jnp.int32, (1, TILE), 1)
        low = jnp.where(q_pos >= split, split, 0)
        k_pos = lax.broadcasted_iota(jnp.int32, (keys, TILE), 0)
        visible = (k_pos >= low) & (k_pos <= q_pos)
        dqs = []
        dk = dk_ref[0:keys, :]
        dv = dv_ref[0:keys, :]
        for half in (0, 1):
            mine = first if half == 0 else ~first
            q_half = jnp.where(mine, q_pair, BF16(0))
            g_half = jnp.where(mine, g_pair, BF16(0))
            lse = lse_t_ref[pl.ds(2 * pair + half, 1), qrows]
            s = jnp.where(visible, dot_nt(k_pair, q_half), NEG)
            p = jnp.exp(s - lse)
            dp = dot_nt(v_pair, g_half)
            inner = jnp.sum(p * dp, axis=0, keepdims=True)
            ds = (p * (dp - inner)).astype(BF16)
            dv = dv + dot(p.astype(BF16), g_half)
            dk = dk + dot(ds, q_half)
            dqs.append(dot_tn(ds, k_pair))
        dk_ref[0:keys, :] = dk
        dv_ref[0:keys, :] = dv
        dq = jnp.where(first, dqs[0], dqs[1]) * (HEAD_DIM**-0.5)
        g_qkv_ref[qrows, pair_cols(pair, 0)] = dq.astype(BF16)
    all_rows = slice(base, base + length)
    g_qkv_ref[all_rows, pair_cols(pair, 1)] = dk_ref[0:length, :].astype(BF16)
    g_qkv_ref[all_rows, pair_cols(pair, 2)] = dv_ref[0:length, :].astype(BF16)


def ln1_back_tile(x_ref, g_mid_ref, table_ref, w_ref, g_qkv_ref, gx_ref, ln_sums_ref, base, t):
    rows = rows_of(base, t)
    g_qkv = g_qkv_ref[rows, :]
    g_a1 = dot_nt(g_qkv, w_ref[:, 0 : 3 * D])
    own = rows_of(0, t)
    n, rstd = normalize(x_ref[own, :].astype(F32))
    gx_ref[own, :] = g_mid_ref[rows, :] + norm_backward(
        g_a1, n, rstd, table_ref[LN1G : LN1G + 1, :]
    )
    ln_sums_ref[0:1, :] += colsum(g_a1 * n)
    ln_sums_ref[1:2, :] += colsum(g_a1)


def qv_sums(g_qkv_ref, sums_ref, g):
    for row, part in ((QB, 0), (VB, 2)):
        sums_ref[row : row + 1, vector_cols(g)] = colsum(g_qkv_ref[:, group_cols(g, part)].astype(F32))


def backward_kernel(
    ssplit,
    lsplit,
    xs,
    xl,
    table_ref,
    w_ref,
    a1_ref,
    qkv_ref,
    att_ref,
    lse_t_ref,
    g_mid_ref,
    gxs_ref,
    gxl_ref,
    dwp_ref,
    dwq_ref,
    sums_ref,
    g_attn_ref,
    g_att_ref,
    g_qkv_ref,
    dk_ref,
    dv_ref,
):
    sums_ref[...] = jnp.zeros_like(sums_ref)
    rows = xs.shape[0] + xl.shape[0]
    lax.fori_loop(
        0,
        rows // TILE,
        lambda t, c: (
            proj_back_tile(g_mid_ref, w_ref, g_attn_ref, g_att_ref, sums_ref, t),
            c,
        )[1],
        0,
    )
    dwp_ref[...] = dot_tn(att_ref[...], g_attn_ref[...])

    def pair_step(pair, c):
        for split, x_ref, base in ((ssplit[0], xs, 0), (lsplit[0], xl, xs.shape[0])):
            attend_back_pair(
                split, qkv_ref, g_att_ref, lse_t_ref, g_qkv_ref, dk_ref, dv_ref, base, x_ref.shape[0], pair
            )
        return c

    lax.fori_loop(0, PAIRS, pair_step, 0)
    for g in range(GROUPS):
        qv_sums(g_qkv_ref, sums_ref, g)
    for j in range(3):
        dwq_ref[:, j * D : (j + 1) * D] = dot_tn(a1_ref[...], g_qkv_ref[:, j * D : (j + 1) * D])
    for x_ref, gx_ref, base in ((xs, gxs_ref, 0), (xl, gxl_ref, xs.shape[0])):
        lax.fori_loop(
            0,
            x_ref.shape[0] // TILE,
            lambda t, c: (
                ln1_back_tile(
                    x_ref, g_mid_ref, table_ref, w_ref, g_qkv_ref, gx_ref, sums_ref.at[LN1G : LN1B + 1], base, t
                ),
                c,
            )[1],
            0,
        )


def backward_local(ssplit, lsplit, xs, xl, table, w_attn, a1, qkv, att, lse_t, g_mid):
    rows = xs.shape[0] + xl.shape[0]
    return pl.pallas_call(
        backward_kernel,
        out_shape=(
            jax.ShapeDtypeStruct(xs.shape, F32),
            jax.ShapeDtypeStruct(xl.shape, F32),
            jax.ShapeDtypeStruct((D, D), F32),
            jax.ShapeDtypeStruct((D, 3 * D), F32),
            jax.ShapeDtypeStruct((8, D), F32),
        ),
        in_specs=[SM, SM] + [VM] * 9,
        out_specs=[VM] * 5,
        scratch_shapes=[
            pltpu.VMEM((rows, D), BF16),
            pltpu.VMEM((rows, D), BF16),
            pltpu.VMEM((rows, 3 * D), BF16),
            pltpu.VMEM((xl.shape[0], 128), F32),
            pltpu.VMEM((xl.shape[0], 128), F32),
        ],
        compiler_params=pltpu.CompilerParams(vmem_limit_bytes=VMEM_LIMIT),
        name="attention_backward",
    )(ssplit, lsplit, xs, xl, table, w_attn, a1, qkv, att, lse_t, g_mid)


MESH = pl.DeviceIdType.MESH
COLS, DEPTH = 4, 4


class Place:
    def __init__(self):
        q, f = lax.axis_index("dp"), lax.axis_index("fsdp")
        z = lax.div(f, 2)
        self.core = lax.rem(f, 2)
        self.col = [q, q + 1 - 2 * lax.rem(q, 2), lax.rem(q + 2, 4), 3 - q]
        self.depth = [lax.rem(z + k, DEPTH) for k in range(DEPTH)]
        self.index = q * 2 * DEPTH + f
        self.partner = (q, 2 * z + 1 - self.core)
        self.x = (self.col[1], f)
        self.y = (self.col[2], f)
        self.across = (self.col[3], f)
        self.over = [(q, 2 * d + 1 - self.core) for d in self.depth]
        self.along = [(q, 2 * d + self.core) for d in self.depth]

    def greet(self):
        barrier = pltpu.get_barrier_semaphore()
        others = [self.partner, self.x, self.y, self.across] + self.along[1:] + self.over[1:]
        for device in others:
            pl.semaphore_signal(barrier, inc=1, device_id=device, device_id_type=MESH)
        return lambda: pl.semaphore_wait(barrier, len(others))


def hooks(table):
    def run(i):
        for n, actions in table.items():

            @pl.when(i == n)
            def _():
                for action, *args in actions:
                    action(*args)

    return run


def remote(src, dst, send, recv, device):
    return pltpu.make_async_remote_copy(
        src_ref=src, dst_ref=dst, send_sem=send, recv_sem=recv, device_id=device, device_id_type=MESH
    )


def at(start, size, step):
    return pl.ds(pl.multiple_of(start, step), size)


Z, X, Y, VIA_X, VIA_Y, PAIR = 0, 3, 4, 5, 6, 7
N_GATHER = 11


class Gather:
    def __init__(self, place, spot, own, send, recv):
        self.place, self.own, self.send, self.recv = place, own, send, recv
        self.spot = spot

    def share(self, k):
        return self.spot(self.place.col[0], self.place.depth[k], 1, self.place.core)

    def column(self, r, z=0, n=DEPTH):
        return self.spot(self.place.col[r], z, n, self.place.core)

    def along(self, k, arriving=False):
        n = (k if arriving else DEPTH - k) - 1
        src, dst = (self.share(k),) * 2 if arriving else (self.own, self.share(0))
        return remote(src, dst, self.send.at[Z + k - 1], self.recv.at[Z + n], self.place.along[k])

    def near(self, kind, r):
        device = self.place.x if kind == X else self.place.y
        ref = self.column(r)
        return remote(ref, ref, self.send.at[kind], self.recv.at[kind], device)

    def across(self, kind, r):
        device, z = (self.place.x, DEPTH // 2) if kind == VIA_X else (self.place.y, 0)
        ref = self.column(r, z, DEPTH // 2)
        return remote(ref, ref, self.send.at[kind], self.recv.at[kind], device)

    def pair(self, r, arriving=False):
        core = 1 - self.place.core if arriving else self.place.core
        ref = self.spot(self.place.col[r], 0, DEPTH, core)
        return remote(ref, ref, self.send.at[PAIR + r], self.recv.at[PAIR + r], self.place.partner)

    def a(self):
        for k in (1, 3, 2):
            self.along(k).start()

    def b(self):
        for k in (1, 3, 2):
            self.along(k, True).wait_recv()
        self.near(X, 0).start()
        self.near(Y, 0).start()
        self.pair(0).start()

    def c(self):
        self.near(X, 1).wait_recv()
        self.across(VIA_Y, 1).start()
        self.pair(1).start()
        self.near(Y, 2).wait_recv()
        self.across(VIA_X, 2).start()
        self.pair(2).start()

    def d(self):
        self.across(VIA_Y, 3).wait_recv()
        self.across(VIA_X, 3).wait_recv()
        self.pair(3).start()

    def e(self):
        for r in range(COLS):
            self.pair(r, True).wait_recv()

    def end(self):
        for k in range(1, DEPTH):
            self.along(k).wait_send()
        self.near(X, 0).wait_send()
        self.near(Y, 0).wait_send()
        self.across(VIA_Y, 1).wait_send()
        self.across(VIA_X, 2).wait_send()
        for r in range(COLS):
            self.pair(r).wait_send()


def wide_spot(full, start, half):
    def spot(col, z, n, core):
        rows = at(col * (48 * DEPTH) + z * 48, 48 * n, 16)
        return full.at[rows, at(start + core * half, half, 128)]

    return spot


def tall_spot(full, start, size):
    def spot(col, z, n, core):
        return full.at[col, pl.ds(z, n), core, pl.ds(start, size)]

    return spot


def place_vectors(place, vectors, out):
    lines = []
    for ref, row in zip(vectors, (LN1G, LN1B, QB, PROJB, LN2G, LN2B, OUTB, FCB)):
        size = ref.shape[1]
        start = place.index * size
        at_row, at_lane = lax.div(start, D), lax.rem(start, D)
        lane = lax.broadcasted_iota(jnp.int32, (size, D), 1)
        pick = lax.broadcasted_iota(jnp.int32, (size, D), 0) + at_lane == lane
        values = dot(ref[...], jnp.where(pick, 1.0, 0.0).astype(BF16))
        rows = (size * 32) // D
        mine = lax.broadcasted_iota(jnp.int32, (rows, D), 0) == at_row
        lines.append(jnp.where(mine, values, 0.0))
    lines.append(jnp.zeros((4, D), F32))
    out[...] = jnp.concatenate(lines, axis=0).astype(out.dtype)


SUM_STEPS = 7
SUM_STAGES = ((0,), (1, 2, 3), (4, 5, 6))


class TableSum:
    def __init__(self, place, total, got, send, recv):
        self.place, self.total, self.got, self.send, self.recv = place, total, got, send, recv

    def copy(self, step, arriving=False):
        place = self.place
        if step == 0:
            device, n, stage = place.partner, 0, 0
        elif step <= 3:
            device, n, stage = place.along[step], (step if arriving else 4 - step), 1
        else:
            device, n, stage = (place.x, place.y, place.across)[step - 4], step, 2
        return remote(self.total.at[stage], self.got.at[n], self.send.at[step], self.recv.at[n], device)

    def begin(self, stage):
        for step in SUM_STAGES[stage]:
            self.copy(step).start()

    def add(self, stage):
        for step in SUM_STAGES[stage]:
            self.copy(step, True).wait_recv()
        total = self.total[stage]
        for step in SUM_STAGES[stage]:
            total = total + self.got[step]
        self.total[stage + 1] = total

    def next(self, stage):
        self.add(stage)
        self.begin(stage + 1)

    def end(self):
        for step in range(SUM_STEPS):
            self.copy(step).wait_send()


def forward_gather_kernel(
    ssplit,
    lsplit,
    xs_hbm,
    xl_hbm,
    wqkv,
    wproj,
    wfc,
    wout,
    v0,
    v1,
    v2,
    v3,
    v4,
    v5,
    v6,
    v7,
    table_ref,
    wa_hbm,
    wf_hbm,
    wo_hbm,
    a1_hbm,
    qkv_hbm,
    att_hbm,
    lse_t_ref,
    mid_hbm,
    xs,
    xl,
    wa,
    a1_ref,
    qkv_ref,
    att_ref,
    mid_ref,
    lse_ref,
    slab_f,
    swap_out,
    swap_in,
    total,
    got,
    io_sem,
    swap_send,
    swap_recv,
    sum_send,
    sum_recv,
    g_send,
    g_recv,
):
    place = Place()
    welcome = place.greet()
    loads = [pltpu.make_async_copy(xs_hbm, xs, io_sem.at[0]), pltpu.make_async_copy(xl_hbm, xl, io_sem.at[1])]
    for copy in loads:
        copy.start()
    part = D // 2
    first = place.core == 0
    swaps = [
        remote(swap_out.at[n], swap_in.at[n], swap_send.at[n], swap_recv.at[n], place.partner)
        for n in range(2)
    ]
    sums = TableSum(place, total, got, sum_send, sum_recv)

    def halves(share, step):
        starts = range(0, share.shape[1], 2 * step)
        lefts = jnp.concatenate([share[:, i : i + step] for i in starts], axis=1)
        rights = jnp.concatenate([share[:, i + step : i + 2 * step] for i in starts], axis=1)
        return jnp.where(first, lefts, rights), jnp.where(first, rights, lefts)

    cols = [wqkv[:, j * D + g * GROUP : j * D + (g + 1) * GROUP] for g in range(GROUPS) for j in range(3)]
    keep_a, swap_out[0] = halves(jnp.concatenate(cols + [wproj[...]], axis=1).astype(F32), part)
    welcome()
    swaps[0].start()
    place_vectors(place, (v0, v1, v2, v3, v4, v5, v6, v7), total.at[0])
    sums.begin(0)
    keep_f, swap_out[1] = halves(wfc[...].astype(F32), D)
    swaps[1].start()
    sums.next(0)

    def joined(n, mine):
        swaps[n].wait_recv()
        other = swap_in[n]
        top, bottom = jnp.where(first, mine, other), jnp.where(first, other, mine)
        return jnp.concatenate([top, bottom], axis=0).astype(BF16)

    chip = place.col[0] * DEPTH + place.depth[0]
    rows = at(chip * 48, 48, 16)
    share = joined(0, keep_a)
    ps = []
    for n in range(4):
        cols = at(n * D + place.core * part, part, 128)
        wa[rows, cols] = share[:, n * part : (n + 1) * part]
        ps.append(Gather(place, wide_spot(wa, n * D, part), wa.at[rows, cols], g_send.at[n], g_recv.at[n]))
    for n in range(2):
        spot = wide_spot(wf_hbm, n * 2 * D, D)
        ps.append(Gather(place, spot, slab_f.at[n], g_send.at[4 + n], g_recv.at[4 + n]))
    for n in range(2):
        spot, own = tall_spot(wo_hbm, n * 48, 48), wout.at[:, pl.ds(n * 48, 48)]
        ps.append(Gather(place, spot, own, g_send.at[6 + n], g_recv.at[6 + n]))
    h0, h1, h2, pp, f0, f1, o0, o1 = ps
    for piece in ps[:4]:
        piece.a()
    share = joined(1, keep_f)
    for n in range(2):
        slab_f[n] = share[:, n * D : (n + 1) * D]
    for piece in ps[4:]:
        piece.a()
    own_copies = []
    for n, piece in enumerate((f0, f1, o0, o1)):
        copy = pltpu.make_async_copy(piece.own, piece.share(0), io_sem.at[2 + n])
        copy.start()
        own_copies.append(copy)
    sums.next(1)
    h0.b()
    sums.add(2)
    table_ref[...] = total[3].astype(F32)
    h1.b()
    for copy in loads + own_copies:
        copy.wait()
    groups = group_refs(xs, xl)
    short_tiles, long_tiles = xs.shape[0] // TILE, xl.shape[0] // TILE
    loop(short_tiles, lambda t: norm_tile(xs, table_ref, a1_ref, 0, t))
    h0.c()
    h2.b()
    loop(2, lambda t: norm_tile(xl, table_ref, a1_ref, groups[1][1], t))
    h1.c()
    pp.b()
    h0.d()
    loop(long_tiles - 2, lambda t: norm_tile(xl, table_ref, a1_ref, groups[1][1], t + 2))
    h2.c()
    h1.d()
    h0.e()
    stores = [
        pltpu.make_async_copy(src, dst, io_sem.at[6 + n])
        for n, (src, dst) in enumerate(
            (
                (a1_ref, a1_hbm),
                (wa, wa_hbm),
                (qkv_ref, qkv_hbm),
                (att_ref, att_hbm),
                (mid_ref, mid_hbm),
            )
        )
    ]
    stores[0].start()
    lse_ref[...] = jnp.zeros_like(lse_ref)
    before_group = hooks({1: ((h1.e,),), 2: ((h2.e,),)})
    after_qkv = hooks({1: ((o0.b,),)})
    after_short = hooks({0: ((f0.b,),), 1: ((f1.b,),), 3: ((f0.d,),), 4: ((f1.d,),)})
    after_long = hooks(
        {
            0: ((pp.c,), (h2.d,)),
            1: ((f0.c,), (pp.d,)),
            2: ((f1.c,), (o1.b,)),
            3: ((o0.c,),),
            4: ((o1.c,),),
            5: ((o0.d,),),
        }
    )

    def group_step(g):
        before_group(g)
        loop(a1_ref.shape[0] // TILE, lambda t: qkv_tile(table_ref, wa, a1_ref, qkv_ref, g, t))
        after_qkv(g)

        def pair_step(j):
            pair = 2 * g + j
            attend_pair(ssplit[0], qkv_ref, att_ref, lse_ref, 0, xs.shape[0], pair)
            after_short(pair)
            attend_pair(lsplit[0], qkv_ref, att_ref, lse_ref, xs.shape[0], xl.shape[0], pair)
            after_long(pair)

        loop(2, pair_step)

    loop(GROUPS, group_step)
    pp.e()
    for copy in stores[1:4]:
        copy.start()
    lse_t_ref[...] = jnp.transpose(lse_ref[...])[:16, :]
    for x_ref, base in groups:
        loop(
            x_ref.shape[0] // TILE,
            lambda t: mid_tile(x_ref, table_ref, wa, att_ref, mid_ref, base, t),
        )
    stores[4].start()
    o1.d()
    for piece in (f0, f1, o0, o1):
        piece.e()
    for swap in swaps:
        swap.wait_send()
    sums.end()
    for piece in ps:
        piece.end()
    for copy in stores:
        copy.wait()


ANY = pl.BlockSpec(memory_space=pl.ANY)


def forward_gather(ssplit, lsplit, xs, xl, wqkv, wproj, wfc, wout, vectors):
    rows = xs.shape[0] + xl.shape[0]
    wide = wqkv.shape[1] + wproj.shape[1]
    full_out = jax.ShapeDtypeStruct((COLS, DEPTH, 2) + wout.shape, BF16)
    sem = pltpu.SemaphoreType.DMA
    return pl.pallas_call(
        forward_gather_kernel,
        out_shape=(
            jax.ShapeDtypeStruct((16, D), F32),
            jax.ShapeDtypeStruct((D, wide), BF16),
            jax.ShapeDtypeStruct((D, wfc.shape[1]), BF16),
            full_out,
            jax.ShapeDtypeStruct((rows, D), BF16),
            jax.ShapeDtypeStruct((rows, 3 * D), BF16),
            jax.ShapeDtypeStruct((rows, D), BF16),
            jax.ShapeDtypeStruct((16, rows), F32),
            jax.ShapeDtypeStruct((rows, D), F32),
        ),
        in_specs=[SM, SM, ANY, ANY] + [VM] * 12,
        out_specs=[VM, ANY, ANY, ANY, ANY, ANY, ANY, VM, ANY],
        scratch_shapes=[
            pltpu.VMEM(xs.shape, BF16),
            pltpu.VMEM(xl.shape, BF16),
            pltpu.VMEM((D, wide), BF16),
            pltpu.VMEM((rows, D), BF16),
            pltpu.VMEM((rows, 3 * D), BF16),
            pltpu.VMEM((rows, D), BF16),
            pltpu.VMEM((rows, D), F32),
            pltpu.VMEM((rows, 128), F32),
            pltpu.VMEM((2, 48, D), BF16),
            pltpu.VMEM((2, 24, wide // 2), F32),
            pltpu.VMEM((2, 24, wide // 2), F32),
            pltpu.VMEM((4, 16, D), BF16),
            pltpu.VMEM((SUM_STEPS, 16, D), BF16),
            sem((11,)),
            sem((2,)),
            sem((2,)),
            sem((SUM_STEPS,)),
            sem((SUM_STEPS,)),
            sem((8, N_GATHER)),
            sem((8, N_GATHER)),
        ],
        compiler_params=pltpu.CompilerParams(
            vmem_limit_bytes=VMEM_LIMIT, collective_id=0, has_side_effects=True
        ),
        name="attention_forward_gather",
    )(ssplit, lsplit, xs, xl, wqkv, wproj, wfc, wout[None], *[v.reshape(1, -1) for v in vectors])


R_PAIR, R_X, R_Y, R_XB, R_YB, R_Z = 0, 4, 6, 8, 9, 10
N_REDUCE = 13
ORDER = (3, 1, 2, 0)


class Reduce:
    def __init__(self, place, src, own, total, xa, ya, xb, yb, zr, send, recv, own_sem):
        self.place, self.src, self.own, self.total = place, src, own, total
        self.xa, self.ya, self.xb, self.yb, self.zr = xa, ya, xb, yb, zr
        self.send, self.recv, self.own_sem = send, recv, own_sem

    def slabs(self, r, core):
        return self.src.at[pl.ds(self.place.col[r] * DEPTH, DEPTH), core]

    def pair(self, r):
        place = self.place
        n = R_PAIR + r
        return remote(
            self.slabs(r, 1 - place.core), self.total.at[r], self.send.at[n], self.recv.at[n], place.partner
        )

    def load(self, r):
        slot = ORDER.index(r) % 2
        return pltpu.make_async_copy(self.slabs(r, self.place.core), self.own.at[slot], self.own_sem.at[r])

    def to_x(self, n):
        src = self.total.at[(1, 3)[n], pl.ds(0, 2)]
        return remote(src, self.xa.at[n], self.send.at[R_X + n], self.recv.at[R_X + n], self.place.x)

    def to_y(self, n):
        src = self.total.at[(2, 3)[n], pl.ds(2, 2)]
        return remote(src, self.ya.at[n], self.send.at[R_Y + n], self.recv.at[R_Y + n], self.place.y)

    def to_xb(self):
        src = self.total.at[1, pl.ds(2, 2)]
        return remote(src, self.xb, self.send.at[R_XB], self.recv.at[R_XB], self.place.x)

    def to_yb(self):
        src = self.total.at[2, pl.ds(0, 2)]
        return remote(src, self.yb, self.send.at[R_YB], self.recv.at[R_YB], self.place.y)

    def to_z(self, k, arriving=False):
        n = (k if arriving else DEPTH - k) - 1
        src = self.total.at[0, self.place.depth[k]]
        return remote(
            src, self.zr.at[n], self.send.at[R_Z + k - 1], self.recv.at[R_Z + n], self.place.along[k]
        )

    def begin(self, loads=True):
        for r in ORDER:
            self.pair(r).start()
        if loads:
            self.begin_loads()

    def begin_loads(self):
        if self.own is not None:
            for r in ORDER[:2]:
                self.load(r).start()

    def chip(self, r):
        if self.own is not None:
            self.load(r).wait()
            mine = self.own[ORDER.index(r) % 2]
        else:
            mine = self.src[pl.ds(self.place.col[r] * DEPTH, DEPTH), self.place.core]
        self.pair(r).wait_recv()
        self.total[r] = self.total[r] + mine
        if self.own is not None and ORDER.index(r) < 2:
            self.load(ORDER[ORDER.index(r) + 2]).start()
        if r == 1:
            self.to_x(1).start()
            self.to_x(0).start()
        if r == 2:
            self.to_y(1).start()
            self.to_y(0).start()

    def chip_all(self):
        for r in ORDER:
            self.chip(r)

    def cross(self):
        self.to_x(1).wait_recv()
        self.total[2, 0:2] = self.total[2, 0:2] + self.xa[1]
        self.to_yb().start()
        self.to_y(1).wait_recv()
        self.total[1, 2:4] = self.total[1, 2:4] + self.ya[1]
        self.to_xb().start()

    def column(self):
        self.to_x(0).wait_recv()
        self.to_yb().wait_recv()
        add = lambda a, b, c: (a.astype(F32) + b.astype(F32) + c.astype(F32)).astype(BF16)
        self.total[0, 0:2] = add(self.total[0, 0:2], self.xa[0], self.yb[...])
        self.to_y(0).wait_recv()
        self.to_xb().wait_recv()
        self.total[0, 2:4] = add(self.total[0, 2:4], self.ya[0], self.xb[...])
        for k in (2, 1, 3):
            self.to_z(k).start()

    def result(self):
        out = self.total[0, self.place.depth[0]].astype(F32)
        for k in range(1, DEPTH):
            self.to_z(k, True).wait_recv()
            out = out + self.zr[k - 1].astype(F32)
        return out

    def end(self):
        for r in range(COLS):
            self.pair(r).wait_send()
        for n in range(2):
            self.to_x(n).wait_send()
            self.to_y(n).wait_send()
        self.to_xb().wait_send()
        self.to_yb().wait_send()
        for k in range(1, DEPTH):
            self.to_z(k).wait_send()


class LastSum:
    def __init__(self, place, total, got, send, recv):
        self.place, self.total, self.got, self.send, self.recv = place, total, got, send, recv

    def copy(self, n, arriving=False):
        place = self.place
        if n < 3:
            device, m = place.along[n + 1], (n if arriving else 2 - n)
        elif n < 6:
            device, m = place.over[n - 2], (n if arriving else 8 - n)
        else:
            device, m = (place.partner, place.x, place.y, place.across)[n - 6], n
        stage = 0 if n < 7 else 1
        return remote(self.total.at[stage], self.got.at[m], self.send.at[n], self.recv.at[m], device)

    def run(self):
        for stage, steps in enumerate((range(7), range(7, 10))):
            for n in steps:
                self.copy(n).start()
            total = self.total[stage]
            for n in steps:
                self.copy(n, True).wait_recv()
                total = total + self.got[n]
            self.total[stage + 1] = total
        for n in range(10):
            self.copy(n).wait_send()


def take_vectors(place, table, outs):
    for ref, row in zip(outs, (LN1G, LN1B, QB, PROJB, LN2G, LN2B, OUTB, FCB)):
        size = ref.shape[1]
        rows = (size * 32) // D
        start = place.index * size
        at_row, at_lane = lax.div(start, D), lax.rem(start, D)
        mine = lax.broadcasted_iota(jnp.int32, (rows, D), 0) == at_row
        line = jnp.sum(jnp.where(mine, table[row : row + rows, :], 0.0), axis=0, keepdims=True)
        lane = lax.broadcasted_iota(jnp.int32, (size, D), 1)
        pick = lax.broadcasted_iota(jnp.int32, (size, D), 0) + at_lane == lane
        ref[...] = lax.dot_general(
            line,
            jnp.where(pick, 1.0, 0.0),
            (((1,), (1,)), ((), ())),
            preferred_element_type=F32,
            precision=lax.Precision.HIGHEST,
        )


def small_slabs(whole):
    devices, half = 2 * COLS * DEPTH, D // 2
    left = whole[:, 0:half].reshape(devices, 24, half)
    right = whole[:, half:D].reshape(devices, 24, half)
    both = jnp.concatenate([left, right], axis=1).astype(BF16)
    return both.reshape(COLS * DEPTH, 2, 48, half)


def backward_reduce_kernel(
    ssplit,
    lsplit,
    xs_hbm,
    xl_hbm,
    table_ref,
    wa_hbm,
    a1_hbm,
    qkv_hbm,
    att_hbm,
    lse_t_ref,
    g_mid_hbm,
    sums2_ref,
    go_hbm,
    gf_hbm,
    gxs_hbm,
    gxl_hbm,
    d0,
    d1,
    d2,
    d3,
    d4,
    d5,
    d6,
    d7,
    d_qkv,
    d_proj,
    d_fc,
    d_out,
    wa,
    a1_ref,
    qkv_ref,
    att_ref,
    g_mid_ref,
    g_att_ref,
    g_qkv_ref,
    dk_ref,
    dv_ref,
    big_own,
    big_total,
    big_xa,
    big_ya,
    big_xb,
    big_yb,
    big_zr,
    small_src,
    small_total,
    small_xa,
    small_ya,
    small_xb,
    small_yb,
    small_zr,
    total,
    got,
    io_sem,
    own_sem,
    r_send,
    r_recv,
    sum_send,
    sum_recv,
    ln_sums_ref,
    last_total,
    last_got,
    last_send,
    last_recv,
):
    place = Place()
    g_attn_ref = g_qkv_ref.at[:, pl.ds(0, D)]
    short, long = gxs_hbm.shape[0], gxl_hbm.shape[0]
    rows = short + long
    proj_cols = pl.ds(3 * D, D)
    qkv_cols = pl.ds(0, 3 * D)
    loads = [
        pltpu.make_async_copy(src, dst, io_sem.at[n])
        for n, (src, dst) in enumerate(
            (
                (wa_hbm.at[:, proj_cols], wa.at[:, proj_cols]),
                (g_mid_hbm, g_mid_ref),
                (att_hbm, att_ref),
                (qkv_hbm, qkv_ref),
                (a1_hbm, a1_ref),
                (wa_hbm.at[:, qkv_cols], wa.at[:, qkv_cols]),
            )
        )
    ]
    for copy in loads:
        copy.start()
    sums = TableSum(place, total, got, sum_send, sum_recv)
    sums_ref = total.at[0]
    sums_ref[...] = jnp.zeros_like(sums_ref)
    sums_ref[LN2G : LN2G + 7, :] = sums2_ref[0:7, :]
    big = [
        Reduce(
            place, src, big_own, big_total.at[n], big_xa.at[n], big_ya.at[n], big_xb.at[n],
            big_yb.at[n], big_zr.at[n], r_send.at[n], r_recv.at[n], own_sem.at[n],
        )
        for n, src in enumerate((go_hbm, gf_hbm))
    ]
    small = [
        Reduce(
            place, small_src.at[n], None, small_total.at[n], small_xa.at[n], small_ya.at[n], small_xb.at[n],
            small_yb.at[n], small_zr.at[n], r_send.at[2 + n], r_recv.at[2 + n], None,
        )
        for n in range(4)
    ]
    ro, rf = big
    rp, rh = small[3], small[0:3]
    place.greet()()
    ro.begin()
    rf.begin(False)
    last_total[...] = jnp.zeros_like(last_total)
    loads[0].wait()
    loads[1].wait()

    after = hooks(
        {
            0: ((ro.chip, 3),),
            1: ((ro.chip, 1),),
            2: ((ro.chip, 2),),
            3: ((ro.chip, 0), (rf.begin_loads,)),
            5: ((rf.chip, 3),),
        }
    )

    def proj_step(t):
        proj_back_tile(g_mid_ref, wa, g_attn_ref, g_att_ref, sums_ref, t)
        after(t)

    loop(rows // TILE, proj_step)
    loads[2].wait()
    small_src[3] = small_slabs(dot_tn(att_ref[...], g_attn_ref[...]))
    rp.begin()
    x_loads = [
        pltpu.make_async_copy(xs_hbm, att_ref.at[pl.ds(0, short)], io_sem.at[6]),
        pltpu.make_async_copy(xl_hbm, att_ref.at[pl.ds(short, long)], io_sem.at[7]),
    ]
    for copy in x_loads:
        copy.start()
    for copy in loads[3:]:
        copy.wait()

    def give_out():
        d_out[...] = ro.result()

    def give_fc():
        res = rf.result()
        for j in range(4):
            d_fc[:, j * D : (j + 1) * D] = res[24 * j : 24 * j + 24, :]

    def give_proj():
        res = rp.result()
        d_proj[:, 0 : D // 2] = res[0:24]
        d_proj[:, D // 2 : D] = res[24:48]

    def give_qkv(g):
        res = rh[g].result()
        line = jnp.concatenate([res[0:24], res[24:48]], axis=1)
        for j in range(3):
            d_qkv[:, j * D + g * 256 : j * D + g * 256 + 256] = line[:, j * 256 : j * 256 + 256]

    def heads_begin(g):
        rh[g].begin()

    after_short = hooks(
        {
            0: ((ro.cross,), (rf.chip, 1), (rf.chip, 2), (rf.chip, 0)),
            3: ((rh[0].chip_all,),),
            4: ((rf.column,),),
        }
    )
    after_long = hooks(
        {
            1: ((heads_begin, 0), (ro.column,)),
            2: ((rf.cross,), (rp.chip_all,)),
            3: ((heads_begin, 1),),
            4: ((rp.cross,), (rh[0].cross,), (rh[1].chip_all,), (give_out,)),
            5: ((heads_begin, 2), (sums.begin, 0), (rp.column,), (rh[0].column,), (rh[1].cross,)),
        }
    )

    def pair_step(pair):
        attend_back_pair(
            ssplit[0], qkv_ref, g_att_ref, lse_t_ref, g_qkv_ref, dk_ref, dv_ref, 0, short, pair
        )
        after_short(pair)
        attend_back_pair(
            lsplit[0], qkv_ref, g_att_ref, lse_t_ref, g_qkv_ref, dk_ref, dv_ref, short, long, pair
        )

        @pl.when(lax.rem(pair, 2) == 1)
        def _():
            g = lax.div(pair, 2)
            cols = pl.ds(pl.multiple_of(g * D, 128), D)
            small_src[g] = small_slabs(dot_tn(a1_ref[...], g_qkv_ref[:, cols]))
            qv_sums(g_qkv_ref, sums_ref, g)

        after_long(pair)

    loop(PAIRS, pair_step)
    for copy in x_loads:
        copy.wait()
    after_norm = hooks(
        {
            0: ((rh[2].chip_all,), (sums.next, 0)),
            1: ((rh[1].column,),),
            2: ((rh[2].cross,), (sums.next, 1)),
            3: ((give_proj,),),
            4: ((rh[2].column,), (give_fc,)),
            5: ((give_qkv, 0), (sums.add, 2)),
        }
    )

    def norm_step(t):
        ln1_back_tile(att_ref, g_mid_ref, table_ref, wa, g_qkv_ref, g_mid_ref, ln_sums_ref, 0, t)
        after_norm(t)

    ln_sums_ref[...] = jnp.zeros_like(ln_sums_ref)
    loop(short // TILE, norm_step)
    stores = [
        pltpu.make_async_copy(g_mid_ref.at[pl.ds(0, short)], gxs_hbm, io_sem.at[8]),
        pltpu.make_async_copy(g_mid_ref.at[pl.ds(short, long)], gxl_hbm, io_sem.at[9]),
    ]
    stores[0].start()
    loop(long // TILE, lambda t: norm_step(t + short // TILE))
    stores[1].start()
    lanes = D // 128
    lines = [ln_sums_ref[r : r + 1, 128 * j : 128 * j + 128] for r in range(2) for j in range(lanes)]
    last_total[0, 0 : 2 * lanes] = jnp.concatenate(lines, axis=0)
    last = LastSum(place, last_total, last_got, last_send, last_recv)
    last.run()
    give_qkv(1)
    give_qkv(2)
    final = total.at[3]
    for r in range(2):
        final[r : r + 1, :] = jnp.concatenate(
            [last_total[2, r * lanes + j : r * lanes + j + 1, :] for j in range(lanes)], axis=1
        )
    take_vectors(place, final, (d0, d1, d2, d3, d4, d5, d6, d7))
    sums.end()
    for reduce in big + small:
        reduce.end()
    for copy in stores:
        copy.wait()


def backward_reduce(ssplit, lsplit, xs, xl, table, w_attn, a1, qkv, att, lse_t, g_mid, sums2, dwo, dwf, sizes):
    short, long = xs.shape[0], xl.shape[0]
    rows = short + long
    chips = COLS * DEPTH
    devices = 2 * chips
    big, little = (96, D), (48, D // 2)
    slabs = lambda g: g.reshape(chips, 2, *big)
    sem = pltpu.SemaphoreType.DMA
    buffers = lambda n, shape: [
        pltpu.VMEM((n, COLS, DEPTH) + shape, BF16),
        pltpu.VMEM((n, 2, 2) + shape, BF16),
        pltpu.VMEM((n, 2, 2) + shape, BF16),
        pltpu.VMEM((n, 2) + shape, BF16),
        pltpu.VMEM((n, 2) + shape, BF16),
        pltpu.VMEM((n, DEPTH - 1) + shape, BF16),
    ]
    return pl.pallas_call(
        backward_reduce_kernel,
        out_shape=(
            jax.ShapeDtypeStruct(xs.shape, F32),
            jax.ShapeDtypeStruct(xl.shape, F32),
            *[jax.ShapeDtypeStruct((1, n), F32) for n in sizes],
            jax.ShapeDtypeStruct((D // devices, 3 * D), F32),
            jax.ShapeDtypeStruct((D // devices, D), F32),
            jax.ShapeDtypeStruct((D // devices, FF), F32),
            jax.ShapeDtypeStruct((FF // devices, D), F32),
        ),
        in_specs=[SM, SM, ANY, ANY, VM, ANY, ANY, ANY, ANY, VM, ANY, VM, ANY, ANY],
        out_specs=[ANY, ANY] + [VM] * 12,
        scratch_shapes=[
            pltpu.VMEM((D, 4 * D), BF16),
            pltpu.VMEM((rows, D), BF16),
            pltpu.VMEM((rows, 3 * D), BF16),
            pltpu.VMEM((rows, D), BF16),
            pltpu.VMEM((rows, D), F32),
            pltpu.VMEM((rows, D), BF16),
            pltpu.VMEM((rows, 3 * D), BF16),
            pltpu.VMEM((long, 128), F32),
            pltpu.VMEM((long, 128), F32),
            pltpu.VMEM((2, DEPTH) + big, BF16),
            *buffers(2, big),
            pltpu.VMEM((4, chips, 2) + little, BF16),
            *buffers(4, little),
            pltpu.VMEM((4, 16, D), F32),
            pltpu.VMEM((SUM_STEPS, 16, D), F32),
            sem((10,)),
            sem((2, COLS)),
            sem((6, N_REDUCE)),
            sem((6, N_REDUCE)),
            sem((SUM_STEPS,)),
            sem((SUM_STEPS,)),
            pltpu.VMEM((8, D), F32),
            pltpu.VMEM((3, 16, 128), F32),
            pltpu.VMEM((10, 16, 128), F32),
            sem((10,)),
            sem((10,)),
        ],
        compiler_params=pltpu.CompilerParams(
            vmem_limit_bytes=BACK_VMEM, collective_id=1, has_side_effects=True
        ),
        name="attention_backward_reduce",
    )(ssplit, lsplit, xs, xl, table, w_attn, a1, qkv, att, lse_t, g_mid, sums2, slabs(dwo), slabs(dwf))


BACK_VMEM = 60 * 2**20


def hand_over_kernel(count, *refs):
    sems = refs[-1]
    copies = [pltpu.make_async_copy(refs[n], refs[count + n], sems.at[n]) for n in range(count)]
    for copy in copies:
        copy.start()
    for copy in copies:
        copy.wait()


def hand_over(*arrays):
    count = len(arrays)
    return pl.pallas_call(
        functools.partial(hand_over_kernel, count),
        out_shape=tuple(jax.ShapeDtypeStruct(a.shape, a.dtype) for a in arrays),
        in_specs=[ANY] * count,
        out_specs=[ANY] * count,
        scratch_shapes=[pltpu.SemaphoreType.DMA((count,))],
        name="hand_over",
    )(*arrays)


AXES = ("dp", "fsdp")


def gather(x, axis=0):
    return lax.all_gather(x, AXES, axis=axis, tiled=True)


def scatter(x):
    return lax.psum_scatter(x, AXES, scatter_dimension=0, tiled=True)


def general(args, devices):
    (st, lt, ss, ls, ln1g, ln1b, wqkv, qvb, wproj, projb, ln2g, ln2b, wfc, fcb, wout, outb, sc, lc) = args
    xs, xl = st.reshape(-1, D), lt.reshape(-1, D)
    cs, cl = sc.reshape(-1, D), lc.reshape(-1, D)
    vectors = (ln1g, ln1b, qvb, projb, ln2g, ln2b, outb, fcb)
    sizes = [v.shape[0] for v in vectors]
    every = lax.all_gather(jnp.concatenate(vectors), AXES, axis=0)
    starts = [sum(sizes[:i]) for i in range(len(sizes))]
    full = [every[:, s : s + n].reshape(-1, D) for s, n in zip(starts, sizes)]
    table = jnp.concatenate(full + [jnp.zeros((4, D), BF16)]).astype(F32)
    by_group = lambda w: w.reshape(-1, 3, GROUPS, GROUP).swapaxes(1, 2).reshape(-1, 3 * D)
    w_attn = gather(jnp.concatenate([by_group(wqkv), wproj], axis=1))
    w_fc, w_out = gather(wfc), gather(wout)
    a1, qkv, att, lse_t, mid = forward_local(ss, ls, xs, xl, table, w_attn)
    out_s, out_l, g_mid, sums2, dwf, dwo = mlp_local(mid, cs, cl, table, w_fc, w_out, False)
    gxs, gxl, dwp, dwq, sums1 = backward_local(
        ss, ls, xs, xl, table, w_attn, a1, qkv, att, lse_t, g_mid
    )
    dwq = dwq.reshape(-1, GROUPS, 3, GROUP).swapaxes(1, 2).reshape(-1, 3 * D)
    return finish(args, devices, starts, sizes, out_s, out_l, gxs, gxl, sums1, sums2, dwq, dwp, dwf, dwo)


def finish(args, devices, starts, sizes, out_s, out_l, gxs, gxl, sums1, sums2, dwq, dwp, dwf, dwo):
    st, lt = args[0], args[1]
    rs = lambda x: x.reshape(devices, -1)
    small = jnp.concatenate(
        [
            rs(sums1[0]),
            rs(sums1[1]),
            rs(sums1[2:4]),
            rs(sums1[4]),
            rs(sums2[0]),
            rs(sums2[1]),
            rs(sums2[2]),
            rs(sums2[3:7]),
        ],
        axis=1,
    )
    small = scatter(small)[0]
    parts = [small[s : s + n] for s, n in zip(starts, sizes)]
    d_ln1g, d_ln1b, d_qvb, d_projb, d_ln2g, d_ln2b, d_outb, d_fcb = parts
    return (
        out_s.reshape(st.shape),
        out_l.reshape(lt.shape),
        gxs.reshape(st.shape),
        gxl.reshape(lt.shape),
        d_ln1g,
        d_ln1b,
        scatter(dwq),
        d_qvb,
        scatter(dwp),
        d_projb,
        d_ln2g,
        d_ln2b,
        scatter(dwf),
        d_fcb,
        scatter(dwo),
        d_outb,
    )


def on_torus(args):
    (st, lt, ss, ls, ln1g, ln1b, wqkv, qvb, wproj, projb, ln2g, ln2b, wfc, fcb, wout, outb, sc, lc) = args
    xs, xl = st.reshape(-1, D), lt.reshape(-1, D)
    cs, cl = sc.reshape(-1, D), lc.reshape(-1, D)
    vectors = (ln1g, ln1b, qvb, projb, ln2g, ln2b, outb, fcb)
    table, w_attn, w_fc, w_out, a1, qkv, att, lse_t, mid = forward_gather(
        ss, ls, xs, xl, wqkv, wproj, wfc, wout, vectors
    )
    out_s, out_l, g_mid, sums2, dwf, dwo = mlp_local(mid, cs, cl, table, w_fc, w_out.reshape(FF, D), True)
    gxs, gxl, *rest = hand_over(*backward_reduce(
        ss, ls, xs, xl, table, w_attn, a1, qkv, att, lse_t, g_mid, sums2, dwo, dwf, [v.shape[0] for v in vectors]
    ))
    d_ln1g, d_ln1b, d_qvb, d_projb, d_ln2g, d_ln2b, d_outb, d_fcb = [v.reshape(-1) for v in rest[:8]]
    d_qkv, d_proj, d_fc, d_out = rest[8:]
    return (
        out_s.reshape(st.shape),
        out_l.reshape(lt.shape),
        gxs.reshape(st.shape),
        gxl.reshape(lt.shape),
        d_ln1g,
        d_ln1b,
        d_qkv,
        d_qvb,
        d_proj,
        d_projb,
        d_ln2g,
        d_ln2b,
        d_fc,
        d_fcb,
        d_out,
        d_outb,
    )


def per_device(shape, *args):
    devices = shape["dp"] * shape["fsdp"]
    sizes = (args[0].shape[1], args[1].shape[1], args[6].shape, args[14].shape)
    if shape == {"dp": COLS, "fsdp": 2 * DEPTH} and sizes == (512, 1024, (24, 3 * D), (96, D)):
        return on_torus(args)
    return general(args, devices)


def solution(mesh):
    vec, mat, seq = P(AXES), P(AXES, None), P(AXES, None, None)
    in_specs = (seq, seq, vec, vec) + (vec, vec, mat, vec, mat, vec) * 1 + (vec, vec, mat, vec, mat, vec) + (seq, seq)
    out_specs = (seq,) * 4 + (vec, vec, mat, vec, mat, vec) * 2
    return jax.shard_map(
        functools.partial(per_device, dict(mesh.shape)),
        mesh=mesh,
        in_specs=in_specs,
        out_specs=out_specs,
        check_vma=False,
    )
```

```python
import functools

import jax
import jax.numpy as jnp
from jax import lax
from jax.experimental import pallas as pl
from jax.experimental.pallas import tpu as pltpu
from jax.sharding import PartitionSpec as P

F32 = jnp.float32
BF16 = jnp.bfloat16
D = 768
FF = 3072
HEAD_DIM = 64
PAIRS = D // 128
GROUP = 256
GROUPS = D // GROUP
TILE = 256
BRANCH = 0.14433756729740643
EPS = 1e-05
NEG = -1e30
VMEM_LIMIT = 60 * 2**20

LN1G, LN1B, QB, VB, PROJB, LN2G, LN2B, OUTB, FCB = 0, 1, 2, 3, 4, 5, 6, 7, 8


def dot(a, b):
    return jnp.dot(a, b, preferred_element_type=F32)


def dot_nt(a, b):
    return lax.dot_general(a, b, (((1,), (1,)), ((), ())), preferred_element_type=F32)


def dot_tn(a, b):
    return lax.dot_general(a, b, (((0,), (0,)), ((), ())), preferred_element_type=F32)


def normalize(x):
    center = x - jnp.mean(x, axis=-1, keepdims=True)
    rstd = lax.rsqrt(jnp.mean(center * center, axis=-1, keepdims=True) + EPS)
    return center * rstd, rstd


def norm_backward(g, n, rstd, gain):
    e = g * gain
    return rstd * (
        e
        - jnp.mean(e, axis=-1, keepdims=True)
        - n * jnp.mean(e * n, axis=-1, keepdims=True)
    )


def rows_of(base, tile):
    return pl.ds(pl.multiple_of(base + tile * TILE, TILE), TILE)


def lanes_of(start):
    return pl.ds(pl.multiple_of(start, 128), 128)


def loop(count, body):
    lax.fori_loop(0, count, lambda i, c: (body(i), c)[1], 0)


def group_refs(short, long):
    return ((short, 0), (long, short.shape[0]))


def norm_tile(x_ref, table_ref, a1_ref, base, t):
    n, _ = normalize(x_ref[rows_of(0, t), :].astype(F32))
    a1 = n * table_ref[LN1G : LN1G + 1, :] + table_ref[LN1B : LN1B + 1, :]
    a1_ref[rows_of(base, t), :] = a1.astype(BF16)


def group_cols(g, part):
    start = g * D + part * GROUP
    return pl.ds(start if isinstance(start, int) else pl.multiple_of(start, 128), GROUP)


def pair_cols(pair, part):
    return lanes_of(lax.div(pair, 2) * D + part * GROUP + lax.rem(pair, 2) * 128)


def vector_cols(g):
    return pl.ds(g * GROUP if isinstance(g, int) else pl.multiple_of(g * GROUP, 128), GROUP)


def qkv_tile(table_ref, w_ref, a1_ref, qkv_ref, g, t):
    rows = rows_of(0, t)
    a1 = a1_ref[rows, :]
    for part, bias in ((0, QB), (1, None), (2, VB)):
        out = dot(a1, w_ref[:, group_cols(g, part)])
        if bias is not None:
            out = out + table_ref[bias : bias + 1, vector_cols(g)]
        qkv_ref[rows, group_cols(g, part)] = out.astype(BF16)


def attend_pair(split, qkv_ref, att_ref, lse_ref, base, length, pair):
    first = lax.broadcasted_iota(jnp.int32, (TILE, 128), 1) < HEAD_DIM
    head_lane = lax.broadcasted_iota(jnp.int32, (TILE, 128), 1)
    for qb in range(length // TILE):
        qrows = slice(base + qb * TILE, base + (qb + 1) * TILE)
        keys = (qb + 1) * TILE
        krows = slice(base, base + keys)
        q_pair = qkv_ref[qrows, pair_cols(pair, 0)] * BF16(HEAD_DIM**-0.5)
        k_pair = qkv_ref[krows, pair_cols(pair, 1)]
        v_pair = qkv_ref[krows, pair_cols(pair, 2)]
        q_pos = qb * TILE + lax.broadcasted_iota(jnp.int32, (TILE, 1), 0)
        low = jnp.where(q_pos >= split, split, 0)
        k_pos = lax.broadcasted_iota(jnp.int32, (TILE, keys), 1)
        visible = (k_pos >= low) & (k_pos <= q_pos)
        outs = []
        lse_new = lse_ref[qrows, :]
        for half in (0, 1):
            mine = first if half == 0 else ~first
            s = dot_nt(jnp.where(mine, q_pair, BF16(0)), k_pair)
            s = jnp.where(visible, s, NEG)
            peak = jnp.max(s, axis=-1, keepdims=True)
            e = jnp.exp(s - peak)
            total = jnp.sum(e, axis=-1, keepdims=True)
            p = (e * (1.0 / total)).astype(BF16)
            outs.append(dot(p, v_pair))
            lse_new = jnp.where(head_lane == 2 * pair + half, peak + jnp.log(total), lse_new)
        lse_ref[qrows, :] = lse_new
        att_ref[qrows, lanes_of(pair * 128)] = jnp.where(first, outs[0], outs[1]).astype(BF16)


def mid_tile(x_ref, table_ref, w_ref, att_ref, mid_ref, base, t):
    rows = rows_of(base, t)
    out = dot(att_ref[rows, :], w_ref[:, 3 * D : 4 * D]) + table_ref[PROJB : PROJB + 1, :]
    mid_ref[rows, :] = x_ref[rows_of(0, t), :].astype(F32) + BRANCH * out


def forward_kernel(
    ssplit, lsplit, xs, xl, table_ref, w_ref, a1_ref, qkv_ref, att_ref, lse_t_ref, mid_ref, lse_ref
):
    for x_ref, base in group_refs(xs, xl):
        loop(x_ref.shape[0] // TILE, lambda t: norm_tile(x_ref, table_ref, a1_ref, base, t))
    for g in range(GROUPS):
        loop(a1_ref.shape[0] // TILE, lambda t: qkv_tile(table_ref, w_ref, a1_ref, qkv_ref, g, t))
    lse_ref[...] = jnp.zeros_like(lse_ref)

    def pair_step(pair, c):
        attend_pair(ssplit[0], qkv_ref, att_ref, lse_ref, 0, xs.shape[0], pair)
        attend_pair(lsplit[0], qkv_ref, att_ref, lse_ref, xs.shape[0], xl.shape[0], pair)
        return c

    lax.fori_loop(0, PAIRS, pair_step, 0)
    lse_t_ref[...] = jnp.transpose(lse_ref[...])[:16, :]
    for x_ref, base in group_refs(xs, xl):
        lax.fori_loop(
            0,
            x_ref.shape[0] // TILE,
            lambda t, c: (mid_tile(x_ref, table_ref, w_ref, att_ref, mid_ref, base, t), c)[1],
            0,
        )


VM = pl.BlockSpec(memory_space=pltpu.VMEM)
SM = pl.BlockSpec(memory_space=pltpu.SMEM)


def forward_local(ssplit, lsplit, xs, xl, table, w_attn):
    rows = xs.shape[0] + xl.shape[0]
    return pl.pallas_call(
        forward_kernel,
        out_shape=(
            jax.ShapeDtypeStruct((rows, D), BF16),
            jax.ShapeDtypeStruct((rows, 3 * D), BF16),
            jax.ShapeDtypeStruct((rows, D), BF16),
            jax.ShapeDtypeStruct((16, rows), F32),
            jax.ShapeDtypeStruct((rows, D), F32),
        ),
        in_specs=[SM, SM, VM, VM, VM, VM],
        out_specs=[VM] * 5,
        scratch_shapes=[pltpu.VMEM((rows, 128), F32)],
        compiler_params=pltpu.CompilerParams(vmem_limit_bytes=VMEM_LIMIT),
        name="attention_forward",
    )(ssplit, lsplit, xs, xl, table, w_attn)


GELU_A = 0.7978845608028654
GELU_B = 0.044715


def mlp_tile(mid, g_out, table_ref, wf_ref, wo_ref):
    n2, rstd = normalize(mid)
    gain = table_ref[LN2G : LN2G + 1, :]
    a2 = (n2 * gain + table_ref[LN2B : LN2B + 1, :]).astype(BF16)
    g_mlp = (BRANCH * g_out).astype(BF16)
    out = None
    g_a2 = None
    acts, g_pres = [], []
    for j in range(FF // D):
        cols = slice(j * D, (j + 1) * D)
        pre = dot(a2, wf_ref[:, cols]) + table_ref[FCB + j : FCB + j + 1, :]
        g_act = dot_nt(g_mlp, wo_ref[cols, :])
        square = pre * pre
        t = jnp.tanh(pre * (GELU_A + (GELU_A * GELU_B) * square))
        half = 0.5 + 0.5 * t
        act = (pre * half).astype(BF16)
        slope = half + pre * (0.5 - 0.5 * t * t) * (GELU_A + (3 * GELU_A * GELU_B) * square)
        g_pre = (g_act * slope).astype(BF16)
        acts.append(act)
        g_pres.append(g_pre)
        part = dot(act, wo_ref[cols, :])
        out = part if out is None else out + part
        part = dot_nt(g_pre, wf_ref[:, cols])
        g_a2 = part if g_a2 is None else g_a2 + part
    out = mid + BRANCH * (out + table_ref[OUTB : OUTB + 1, :])
    g_mid = g_out + norm_backward(g_a2, n2, rstd, gain)
    return out, g_mid, a2, g_mlp, acts, g_pres, g_a2, n2


def colsum(x):
    return jnp.sum(x, axis=0, keepdims=True)


def mlp_kernel(
    n_tiles,
    slabs,
    mid_ref,
    cs_ref,
    cl_ref,
    table_ref,
    wf_ref,
    wo_ref,
    os_ref,
    ol_ref,
    g_mid_ref,
    sums_ref,
    dwf_ref,
    dwo_ref,
    a2_ref,
    g_mlp_ref,
    act_ref,
    g_pre_ref,
):
    step = pl.program_id(0)
    short_tiles = n_tiles[0]
    tiles = n_tiles[0] + n_tiles[1]

    @pl.when(step == 0)
    def _():
        sums_ref[...] = jnp.zeros_like(sums_ref)

    @pl.when(step < tiles)
    def _():
        cot = jnp.where(step < short_tiles, cs_ref[...], cl_ref[...]).astype(F32)
        out, g_mid, a2, g_mlp, acts, g_pres, g_a2, n2 = mlp_tile(
            mid_ref[...], cot, table_ref, wf_ref, wo_ref
        )
        out = out.astype(BF16)

        @pl.when(step < short_tiles)
        def _():
            os_ref[...] = out

        @pl.when(step >= short_tiles)
        def _():
            ol_ref[...] = out

        g_mid_ref[...] = g_mid
        rows = rows_of(0, step)
        a2_ref[rows, :] = a2
        g_mlp_ref[rows, :] = g_mlp
        sums_ref[0:1, :] += colsum(g_a2 * n2)
        sums_ref[1:2, :] += colsum(g_a2)
        sums_ref[2:3, :] += colsum(g_mlp.astype(F32))
        for j in range(FF // D):
            act_ref[rows, j * D : (j + 1) * D] = acts[j]
            g_pre_ref[rows, j * D : (j + 1) * D] = g_pres[j]
            sums_ref[3 + j : 4 + j, :] += colsum(g_pres[j].astype(F32))

    for j in range(4):

        @pl.when(step == tiles + j)
        def _(j=j):
            res = dot_tn(act_ref[:, j * D : (j + 1) * D], g_mlp_ref[...])
            if slabs:
                dwo_ref[...] = res.astype(BF16).reshape(dwo_ref.shape)
            else:
                dwo_ref[...] = res

    for j in range(2 if slabs else 4):

        @pl.when(step == tiles + 4 + j)
        def _(j=j):
            if slabs:
                dev = D // 24
                left = dot_tn(a2_ref[...], g_pre_ref[:, 2 * j * D : (2 * j + 1) * D])
                right = dot_tn(a2_ref[...], g_pre_ref[:, (2 * j + 1) * D : (2 * j + 2) * D])
                both = jnp.concatenate(
                    [left.reshape(dev, 24, D), right.reshape(dev, 24, D)], axis=1
                )
                dwf_ref[...] = both.astype(BF16)
            else:
                dwf_ref[...] = dot_tn(a2_ref[...], g_pre_ref[:, j * D : (j + 1) * D])


def mlp_local(mid, cs, cl, table, w_fc, w_out, slabs):
    rows = mid.shape[0]
    ns, nl = cs.shape[0] // TILE, cl.shape[0] // TILE
    tiles = ns + nl
    steps = tiles + (6 if slabs else 8)
    whole = lambda shape: pl.BlockSpec(shape, lambda i: (0, 0), pipeline_mode=pl.Buffered(1))
    tile = lambda f: pl.BlockSpec((TILE, D), f)
    short_at = lambda i: (jnp.minimum(i, ns - 1), 0)
    long_at = lambda i: (jnp.clip(i - ns, 0, nl - 1), 0)
    all_at = lambda i: (jnp.minimum(i, tiles - 1), 0)
    if slabs:
        dev = D // 24
        dwo_shape = jax.ShapeDtypeStruct((dev, 96, D), BF16)
        dwo_spec = pl.BlockSpec((dev // 4, 96, D), lambda i: (jnp.clip(i - tiles, 0, 3), 0, 0))
        dwf_shape = jax.ShapeDtypeStruct((dev, 96, D), BF16)
        dwf_spec = pl.BlockSpec((dev, 48, D), lambda i: (0, jnp.clip(i - tiles - 4, 0, 1), 0))
    else:
        dwo_shape = jax.ShapeDtypeStruct((FF, D), F32)
        dwo_spec = pl.BlockSpec((D, D), lambda i: (jnp.clip(i - tiles, 0, 3), 0))
        dwf_shape = jax.ShapeDtypeStruct((D, FF), F32)
        dwf_spec = pl.BlockSpec((D, D), lambda i: (0, jnp.clip(i - tiles - 4, 0, 3)))
    return pl.pallas_call(
        functools.partial(mlp_kernel, (ns, nl), slabs),
        grid=(steps,),
        out_shape=(
            jax.ShapeDtypeStruct(cs.shape, BF16),
            jax.ShapeDtypeStruct(cl.shape, BF16),
            jax.ShapeDtypeStruct((rows, D), F32),
            jax.ShapeDtypeStruct((8, D), F32),
            dwf_shape,
            dwo_shape,
        ),
        in_specs=[
            tile(all_at),
            tile(short_at),
            tile(long_at),
            whole(table.shape),
            whole(w_fc.shape),
            whole(w_out.shape),
        ],
        out_specs=[
            tile(short_at),
            tile(long_at),
            tile(all_at),
            pl.BlockSpec((8, D), lambda i: (0, 0)),
            dwf_spec,
            dwo_spec,
        ],
        scratch_shapes=[
            pltpu.VMEM((rows, D), BF16),
            pltpu.VMEM((rows, D), BF16),
            pltpu.VMEM((rows, FF), BF16),
            pltpu.VMEM((rows, FF), BF16),
        ],
        compiler_params=pltpu.CompilerParams(vmem_limit_bytes=VMEM_LIMIT),
        name="mlp",
    )(mid, cs, cl, table, w_fc, w_out)


def proj_back_tile(g_mid_ref, w_ref, g_attn_ref, g_att_ref, sums_ref, t):
    rows = rows_of(0, t)
    g_attn = (BRANCH * g_mid_ref[rows, :]).astype(BF16)
    g_attn_ref[rows, :] = g_attn
    g_att_ref[rows, :] = dot_nt(g_attn, w_ref[:, 3 * D : 4 * D]).astype(BF16)
    sums_ref[PROJB : PROJB + 1, :] += colsum(g_attn.astype(F32))


def attend_back_pair(split, qkv_ref, g_att_ref, lse_t_ref, g_qkv_ref, dk_ref, dv_ref, base, length, pair):
    first = lax.broadcasted_iota(jnp.int32, (TILE, 128), 1) < HEAD_DIM
    dk_ref[0:length, :] = jnp.zeros((length, 128), F32)
    dv_ref[0:length, :] = jnp.zeros((length, 128), F32)
    for qb in range(length // TILE):
        qrows = slice(base + qb * TILE, base + (qb + 1) * TILE)
        keys = (qb + 1) * TILE
        krows = slice(base, base + keys)
        q_pair = qkv_ref[qrows, pair_cols(pair, 0)] * BF16(HEAD_DIM**-0.5)
        g_pair = g_att_ref[qrows, lanes_of(pair * 128)]
        k_pair = qkv_ref[krows, pair_cols(pair, 1)]
        v_pair = qkv_ref[krows, pair_cols(pair, 2)]
        q_pos = qb * TILE + lax.broadcasted_iota(jnp.int32, (1, TILE), 1)
        low = jnp.where(q_pos >= split, split, 0)
        k_pos = lax.broadcasted_iota(jnp.int32, (keys, TILE), 0)
        visible = (k_pos >= low) & (k_pos <= q_pos)
        dqs = []
        dk = dk_ref[0:keys, :]
        dv = dv_ref[0:keys, :]
        for half in (0, 1):
            mine = first if half == 0 else ~first
            q_half = jnp.where(mine, q_pair, BF16(0))
            g_half = jnp.where(mine, g_pair, BF16(0))
            lse = lse_t_ref[pl.ds(2 * pair + half, 1), qrows]
            s = jnp.where(visible, dot_nt(k_pair, q_half), NEG)
            p = jnp.exp(s - lse)
            dp = dot_nt(v_pair, g_half)
            inner = jnp.sum(p * dp, axis=0, keepdims=True)
            ds = (p * (dp - inner)).astype(BF16)
            dv = dv + dot(p.astype(BF16), g_half)
            dk = dk + dot(ds, q_half)
            dqs.append(dot_tn(ds, k_pair))
        dk_ref[0:keys, :] = dk
        dv_ref[0:keys, :] = dv
        dq = jnp.where(first, dqs[0], dqs[1]) * (HEAD_DIM**-0.5)
        g_qkv_ref[qrows, pair_cols(pair, 0)] = dq.astype(BF16)
    all_rows = slice(base, base + length)
    g_qkv_ref[all_rows, pair_cols(pair, 1)] = dk_ref[0:length, :].astype(BF16)
    g_qkv_ref[all_rows, pair_cols(pair, 2)] = dv_ref[0:length, :].astype(BF16)


def ln1_back_tile(x_ref, g_mid_ref, table_ref, w_ref, g_qkv_ref, gx_ref, ln_sums_ref, base, t):
    rows = rows_of(base, t)
    g_qkv = g_qkv_ref[rows, :]
    g_a1 = dot_nt(g_qkv, w_ref[:, 0 : 3 * D])
    own = rows_of(0, t)
    n, rstd = normalize(x_ref[own, :].astype(F32))
    gx_ref[own, :] = g_mid_ref[rows, :] + norm_backward(
        g_a1, n, rstd, table_ref[LN1G : LN1G + 1, :]
    )
    ln_sums_ref[0:1, :] += colsum(g_a1 * n)
    ln_sums_ref[1:2, :] += colsum(g_a1)


def qv_sums(g_qkv_ref, sums_ref, g):
    for row, part in ((QB, 0), (VB, 2)):
        sums_ref[row : row + 1, vector_cols(g)] = colsum(g_qkv_ref[:, group_cols(g, part)].astype(F32))


def backward_kernel(
    ssplit,
    lsplit,
    xs,
    xl,
    table_ref,
    w_ref,
    a1_ref,
    qkv_ref,
    att_ref,
    lse_t_ref,
    g_mid_ref,
    gxs_ref,
    gxl_ref,
    dwp_ref,
    dwq_ref,
    sums_ref,
    g_attn_ref,
    g_att_ref,
    g_qkv_ref,
    dk_ref,
    dv_ref,
):
    sums_ref[...] = jnp.zeros_like(sums_ref)
    rows = xs.shape[0] + xl.shape[0]
    lax.fori_loop(
        0,
        rows // TILE,
        lambda t, c: (
            proj_back_tile(g_mid_ref, w_ref, g_attn_ref, g_att_ref, sums_ref, t),
            c,
        )[1],
        0,
    )
    dwp_ref[...] = dot_tn(att_ref[...], g_attn_ref[...])

    def pair_step(pair, c):
        for split, x_ref, base in ((ssplit[0], xs, 0), (lsplit[0], xl, xs.shape[0])):
            attend_back_pair(
                split, qkv_ref, g_att_ref, lse_t_ref, g_qkv_ref, dk_ref, dv_ref, base, x_ref.shape[0], pair
            )
        return c

    lax.fori_loop(0, PAIRS, pair_step, 0)
    for g in range(GROUPS):
        qv_sums(g_qkv_ref, sums_ref, g)
    for j in range(3):
        dwq_ref[:, j * D : (j + 1) * D] = dot_tn(a1_ref[...], g_qkv_ref[:, j * D : (j + 1) * D])
    for x_ref, gx_ref, base in ((xs, gxs_ref, 0), (xl, gxl_ref, xs.shape[0])):
        lax.fori_loop(
            0,
            x_ref.shape[0] // TILE,
            lambda t, c: (
                ln1_back_tile(
                    x_ref, g_mid_ref, table_ref, w_ref, g_qkv_ref, gx_ref, sums_ref.at[LN1G : LN1B + 1], base, t
                ),
                c,
            )[1],
            0,
        )


def backward_local(ssplit, lsplit, xs, xl, table, w_attn, a1, qkv, att, lse_t, g_mid):
    rows = xs.shape[0] + xl.shape[0]
    return pl.pallas_call(
        backward_kernel,
        out_shape=(
            jax.ShapeDtypeStruct(xs.shape, F32),
            jax.ShapeDtypeStruct(xl.shape, F32),
            jax.ShapeDtypeStruct((D, D), F32),
            jax.ShapeDtypeStruct((D, 3 * D), F32),
            jax.ShapeDtypeStruct((8, D), F32),
        ),
        in_specs=[SM, SM] + [VM] * 9,
        out_specs=[VM] * 5,
        scratch_shapes=[
            pltpu.VMEM((rows, D), BF16),
            pltpu.VMEM((rows, D), BF16),
            pltpu.VMEM((rows, 3 * D), BF16),
            pltpu.VMEM((xl.shape[0], 128), F32),
            pltpu.VMEM((xl.shape[0], 128), F32),
        ],
        compiler_params=pltpu.CompilerParams(vmem_limit_bytes=VMEM_LIMIT),
        name="attention_backward",
    )(ssplit, lsplit, xs, xl, table, w_attn, a1, qkv, att, lse_t, g_mid)


MESH = pl.DeviceIdType.MESH
COLS, DEPTH = 4, 4


class Place:
    def __init__(self):
        q, f = lax.axis_index("dp"), lax.axis_index("fsdp")
        z = lax.div(f, 2)
        self.core = lax.rem(f, 2)
        self.col = [q, q + 1 - 2 * lax.rem(q, 2), lax.rem(q + 2, 4), 3 - q]
        self.depth = [lax.rem(z + k, DEPTH) for k in range(DEPTH)]
        self.index = q * 2 * DEPTH + f
        self.partner = (q, 2 * z + 1 - self.core)
        self.x = (self.col[1], f)
        self.y = (self.col[2], f)
        self.across = (self.col[3], f)
        self.over = [(q, 2 * d + 1 - self.core) for d in self.depth]
        self.along = [(q, 2 * d + self.core) for d in self.depth]

    def greet(self):
        barrier = pltpu.get_barrier_semaphore()
        others = [self.partner, self.x, self.y, self.across] + self.along[1:] + self.over[1:]
        for device in others:
            pl.semaphore_signal(barrier, inc=1, device_id=device, device_id_type=MESH)
        return lambda: pl.semaphore_wait(barrier, len(others))


def hooks(table):
    def run(i):
        for n, actions in table.items():

            @pl.when(i == n)
            def _():
                for action, *args in actions:
                    action(*args)

    return run


def remote(src, dst, send, recv, device):
    return pltpu.make_async_remote_copy(
        src_ref=src, dst_ref=dst, send_sem=send, recv_sem=recv, device_id=device, device_id_type=MESH
    )


def at(start, size, step):
    return pl.ds(pl.multiple_of(start, step), size)


Z, X, Y, VIA_X, VIA_Y, PAIR = 0, 3, 4, 5, 6, 7
N_GATHER = 11


class Gather:
    def __init__(self, place, spot, own, send, recv):
        self.place, self.own, self.send, self.recv = place, own, send, recv
        self.spot = spot

    def share(self, k):
        return self.spot(self.place.col[0], self.place.depth[k], 1, self.place.core)

    def column(self, r, z=0, n=DEPTH):
        return self.spot(self.place.col[r], z, n, self.place.core)

    def along(self, k, arriving=False):
        n = (k if arriving else DEPTH - k) - 1
        src, dst = (self.share(k),) * 2 if arriving else (self.own, self.share(0))
        return remote(src, dst, self.send.at[Z + k - 1], self.recv.at[Z + n], self.place.along[k])

    def near(self, kind, r):
        device = self.place.x if kind == X else self.place.y
        ref = self.column(r)
        return remote(ref, ref, self.send.at[kind], self.recv.at[kind], device)

    def across(self, kind, r):
        device, z = (self.place.x, DEPTH // 2) if kind == VIA_X else (self.place.y, 0)
        ref = self.column(r, z, DEPTH // 2)
        return remote(ref, ref, self.send.at[kind], self.recv.at[kind], device)

    def pair(self, r, arriving=False):
        core = 1 - self.place.core if arriving else self.place.core
        ref = self.spot(self.place.col[r], 0, DEPTH, core)
        return remote(ref, ref, self.send.at[PAIR + r], self.recv.at[PAIR + r], self.place.partner)

    def a(self):
        for k in (1, 3, 2):
            self.along(k).start()

    def b(self):
        for k in (1, 3, 2):
            self.along(k, True).wait_recv()
        self.near(X, 0).start()
        self.near(Y, 0).start()
        self.pair(0).start()

    def c(self):
        self.near(X, 1).wait_recv()
        self.across(VIA_Y, 1).start()
        self.pair(1).start()
        self.near(Y, 2).wait_recv()
        self.across(VIA_X, 2).start()
        self.pair(2).start()

    def d(self):
        self.across(VIA_Y, 3).wait_recv()
        self.across(VIA_X, 3).wait_recv()
        self.pair(3).start()

    def e(self):
        for r in range(COLS):
            self.pair(r, True).wait_recv()

    def end(self):
        for k in range(1, DEPTH):
            self.along(k).wait_send()
        self.near(X, 0).wait_send()
        self.near(Y, 0).wait_send()
        self.across(VIA_Y, 1).wait_send()
        self.across(VIA_X, 2).wait_send()
        for r in range(COLS):
            self.pair(r).wait_send()


def wide_spot(full, start, half):
    def spot(col, z, n, core):
        rows = at(col * (48 * DEPTH) + z * 48, 48 * n, 16)
        return full.at[rows, at(start + core * half, half, 128)]

    return spot


def tall_spot(full, start, size):
    def spot(col, z, n, core):
        return full.at[col, pl.ds(z, n), core, pl.ds(start, size)]

    return spot


def vector_parts(refs):
    parts = []
    for ref, row in zip(refs, (LN1G, LN1B, QB, PROJB, LN2G, LN2B, OUTB, FCB)):
        count = 2 if row == FCB else 1
        size = ref.shape[1] // count
        for n in range(count):
            parts.append((ref, n * size, size, row + n * (size * 32) // D))
    return parts


def place_vectors(place, vectors, out):
    lines = []
    for ref, lo, size, row in vector_parts(vectors):
        start = place.index * size
        at_row, at_lane = lax.div(start, D), lax.rem(start, D)
        lane = lax.broadcasted_iota(jnp.int32, (size, D), 1)
        pick = lax.broadcasted_iota(jnp.int32, (size, D), 0) + at_lane == lane
        values = dot(ref[:, lo : lo + size], jnp.where(pick, 1.0, 0.0).astype(BF16))
        rows = (size * 32) // D
        mine = lax.broadcasted_iota(jnp.int32, (rows, D), 0) == at_row
        lines.append(jnp.where(mine, values, 0.0))
    lines.append(jnp.zeros((4, D), F32))
    out[...] = jnp.concatenate(lines, axis=0).astype(out.dtype)


SUM_STEPS = 7
SUM_STAGES = ((0,), (1, 2, 3), (4, 5, 6))


class TableSum:
    def __init__(self, place, total, got, send, recv):
        self.place, self.total, self.got, self.send, self.recv = place, total, got, send, recv

    def copy(self, step, arriving=False):
        place = self.place
        if step == 0:
            device, n, stage = place.partner, 0, 0
        elif step <= 3:
            device, n, stage = place.along[step], (step if arriving else 4 - step), 1
        else:
            device, n, stage = (place.x, place.y, place.across)[step - 4], step, 2
        return remote(self.total.at[stage], self.got.at[n], self.send.at[step], self.recv.at[n], device)

    def begin(self, stage):
        for step in SUM_STAGES[stage]:
            self.copy(step).start()

    def add(self, stage):
        for step in SUM_STAGES[stage]:
            self.copy(step, True).wait_recv()
        total = self.total[stage]
        for step in SUM_STAGES[stage]:
            total = total + self.got[step]
        self.total[stage + 1] = total

    def next(self, stage):
        self.add(stage)
        self.begin(stage + 1)

    def end(self):
        for step in range(SUM_STEPS):
            self.copy(step).wait_send()


def forward_gather_kernel(
    ssplit,
    lsplit,
    xs_hbm,
    xl_hbm,
    wqkv,
    wproj,
    wfc,
    wout,
    v0,
    v1,
    v2,
    v3,
    v4,
    v5,
    v6,
    v7,
    table_ref,
    wa_hbm,
    wf_hbm,
    wo_hbm,
    slab_f1,
    a1_hbm,
    qkv_hbm,
    att_hbm,
    lse_t_ref,
    mid_hbm,
    xs,
    xl,
    wa,
    a1_ref,
    qkv_ref,
    att_ref,
    mid_ref,
    lse_ref,
    slab_f,
    swap_out,
    swap_in,
    total,
    got,
    io_sem,
    swap_send,
    swap_recv,
    sum_send,
    sum_recv,
    g_send,
    g_recv,
):
    place = Place()
    welcome = place.greet()
    loads = [pltpu.make_async_copy(xs_hbm, xs, io_sem.at[0]), pltpu.make_async_copy(xl_hbm, xl, io_sem.at[1])]
    for copy in loads:
        copy.start()
    part = D // 2
    first = place.core == 0
    swaps = [
        remote(swap_out.at[n], swap_in.at[n], swap_send.at[n], swap_recv.at[n], place.partner)
        for n in range(2)
    ]
    sums = TableSum(place, total, got, sum_send, sum_recv)

    def halves(share, step):
        starts = range(0, share.shape[1], 2 * step)
        lefts = jnp.concatenate([share[:, i : i + step] for i in starts], axis=1)
        rights = jnp.concatenate([share[:, i + step : i + 2 * step] for i in starts], axis=1)
        return jnp.where(first, lefts, rights), jnp.where(first, rights, lefts)

    cols = [wqkv[:, j * D + g * GROUP : j * D + (g + 1) * GROUP] for g in range(GROUPS) for j in range(3)]
    keep_a, swap_out[0] = halves(jnp.concatenate(cols + [wproj[...]], axis=1).astype(F32), part)
    welcome()
    swaps[0].start()
    place_vectors(place, (v0, v1, v2, v3, v4, v5, v6, v7), total.at[0])
    sums.begin(0)
    keep_f, swap_out[1] = halves(by_pieces(wfc[...].astype(F32)), D)
    swaps[1].start()
    sums.next(0)

    def joined(n, mine):
        swaps[n].wait_recv()
        other = swap_in[n]
        top, bottom = jnp.where(first, mine, other), jnp.where(first, other, mine)
        return jnp.concatenate([top, bottom], axis=0).astype(BF16)

    chip = place.col[0] * DEPTH + place.depth[0]
    rows = at(chip * 48, 48, 16)
    share = joined(0, keep_a)
    ps = []
    for n in range(4):
        cols = at(n * D + place.core * part, part, 128)
        wa[rows, cols] = share[:, n * part : (n + 1) * part]
        ps.append(Gather(place, wide_spot(wa, n * D, part), wa.at[rows, cols], g_send.at[n], g_recv.at[n]))
    ps.append(Gather(place, wide_spot(wf_hbm, 0, D), slab_f, g_send.at[4], g_recv.at[4]))
    ps.append(Gather(place, tall_spot(wo_hbm, 0, 48), wout.at[:, pl.ds(0, 48)], g_send.at[5], g_recv.at[5]))
    h0, h1, h2, pp, f0, o0 = ps
    for piece in ps[:4]:
        piece.a()
    share = joined(1, keep_f)
    slab_f[...] = share[:, 0:D]
    slab_f1[...] = share[:, D : 2 * D]
    for piece in ps[4:]:
        piece.a()
    own_copies = []
    for n, piece in enumerate((f0, o0)):
        copy = pltpu.make_async_copy(piece.own, piece.share(0), io_sem.at[2 + n])
        copy.start()
        own_copies.append(copy)
    sums.next(1)
    h0.b()
    sums.add(2)
    table_ref[...] = total[3].astype(F32)
    h1.b()
    for copy in loads + own_copies:
        copy.wait()
    groups = group_refs(xs, xl)
    short_tiles, long_tiles = xs.shape[0] // TILE, xl.shape[0] // TILE
    loop(short_tiles, lambda t: norm_tile(xs, table_ref, a1_ref, 0, t))
    h0.c()
    h2.b()
    loop(2, lambda t: norm_tile(xl, table_ref, a1_ref, groups[1][1], t))
    h1.c()
    pp.b()
    h0.d()
    loop(long_tiles - 2, lambda t: norm_tile(xl, table_ref, a1_ref, groups[1][1], t + 2))
    h2.c()
    h1.d()
    h0.e()
    stores = [
        pltpu.make_async_copy(src, dst, io_sem.at[6 + n])
        for n, (src, dst) in enumerate(
            (
                (a1_ref, a1_hbm),
                (wa, wa_hbm),
                (qkv_ref, qkv_hbm),
                (att_ref, att_hbm),
                (mid_ref, mid_hbm),
            )
        )
    ]
    stores[0].start()
    lse_ref[...] = jnp.zeros_like(lse_ref)
    before_group = hooks({1: ((h1.e,),), 2: ((h2.e,),)})
    after_qkv = hooks({1: ((f0.c,),)})
    after_short = hooks({0: ((f0.b,),), 3: ((o0.c,),)})
    after_long = hooks(
        {
            0: ((pp.c,), (h2.d,)),
            1: ((o0.b,), (pp.d,)),
            2: ((f0.d,),),
            4: ((o0.d,),),
        }
    )

    def group_step(g):
        before_group(g)
        loop(a1_ref.shape[0] // TILE, lambda t: qkv_tile(table_ref, wa, a1_ref, qkv_ref, g, t))
        after_qkv(g)

        def pair_step(j):
            pair = 2 * g + j
            attend_pair(ssplit[0], qkv_ref, att_ref, lse_ref, 0, xs.shape[0], pair)
            after_short(pair)
            attend_pair(lsplit[0], qkv_ref, att_ref, lse_ref, xs.shape[0], xl.shape[0], pair)
            after_long(pair)

        loop(2, pair_step)

    loop(GROUPS, group_step)
    pp.e()
    for copy in stores[1:4]:
        copy.start()
    lse_t_ref[...] = jnp.transpose(lse_ref[...])[:16, :]
    for x_ref, base in groups:
        loop(
            x_ref.shape[0] // TILE,
            lambda t: mid_tile(x_ref, table_ref, wa, att_ref, mid_ref, base, t),
        )
    stores[4].start()
    f0.e()
    o0.e()
    for swap in swaps:
        swap.wait_send()
    sums.end()
    for piece in ps:
        piece.end()
    for copy in stores:
        copy.wait()


ANY = pl.BlockSpec(memory_space=pl.ANY)


def forward_gather(ssplit, lsplit, xs, xl, wqkv, wproj, wfc, wout, vectors):
    rows = xs.shape[0] + xl.shape[0]
    wide = wqkv.shape[1] + wproj.shape[1]
    half_out = jax.ShapeDtypeStruct((COLS, DEPTH, 2) + SLAB, BF16)
    sem = pltpu.SemaphoreType.DMA
    return pl.pallas_call(
        forward_gather_kernel,
        out_shape=(
            jax.ShapeDtypeStruct((16, D), F32),
            jax.ShapeDtypeStruct((D, wide), BF16),
            jax.ShapeDtypeStruct((D, HALF), BF16),
            half_out,
            jax.ShapeDtypeStruct(SLAB, BF16),
            jax.ShapeDtypeStruct((rows, D), BF16),
            jax.ShapeDtypeStruct((rows, 3 * D), BF16),
            jax.ShapeDtypeStruct((rows, D), BF16),
            jax.ShapeDtypeStruct((16, rows), F32),
            jax.ShapeDtypeStruct((rows, D), F32),
        ),
        in_specs=[SM, SM, ANY, ANY] + [VM] * 12,
        out_specs=[VM, ANY, ANY, ANY, VM, ANY, ANY, ANY, VM, ANY],
        scratch_shapes=[
            pltpu.VMEM(xs.shape, BF16),
            pltpu.VMEM(xl.shape, BF16),
            pltpu.VMEM((D, wide), BF16),
            pltpu.VMEM((rows, D), BF16),
            pltpu.VMEM((rows, 3 * D), BF16),
            pltpu.VMEM((rows, D), BF16),
            pltpu.VMEM((rows, D), F32),
            pltpu.VMEM((rows, 128), F32),
            pltpu.VMEM(SLAB, BF16),
            pltpu.VMEM((2, 24, wide // 2), F32),
            pltpu.VMEM((2, 24, wide // 2), F32),
            pltpu.VMEM((4, 16, D), BF16),
            pltpu.VMEM((SUM_STEPS, 16, D), BF16),
            sem((11,)),
            sem((2,)),
            sem((2,)),
            sem((SUM_STEPS,)),
            sem((SUM_STEPS,)),
            sem((6, N_GATHER)),
            sem((6, N_GATHER)),
        ],
        compiler_params=pltpu.CompilerParams(
            vmem_limit_bytes=VMEM_LIMIT, collective_id=0, has_side_effects=True
        ),
        name="attention_forward_gather",
    )(ssplit, lsplit, xs, xl, wqkv, wproj, wfc, wout[None], *[v.reshape(1, -1) for v in vectors])


R_PAIR, R_X, R_Y, R_XB, R_YB, R_Z = 0, 4, 6, 8, 9, 10
N_REDUCE = 13
ORDER = (3, 1, 2, 0)


class Reduce:
    def __init__(self, place, src, own, total, xa, ya, xb, yb, zr, send, recv, own_sem):
        self.place, self.src, self.own, self.total = place, src, own, total
        self.xa, self.ya, self.xb, self.yb, self.zr = xa, ya, xb, yb, zr
        self.send, self.recv, self.own_sem = send, recv, own_sem

    def slabs(self, r, core):
        return self.src.at[pl.ds(self.place.col[r] * DEPTH, DEPTH), core]

    def pair(self, r):
        place = self.place
        n = R_PAIR + r
        return remote(
            self.slabs(r, 1 - place.core), self.total.at[r], self.send.at[n], self.recv.at[n], place.partner
        )

    def load(self, r):
        slot = ORDER.index(r) % 2
        return pltpu.make_async_copy(self.slabs(r, self.place.core), self.own.at[slot], self.own_sem.at[r])

    def to_x(self, n):
        src = self.total.at[(1, 3)[n], pl.ds(0, 2)]
        return remote(src, self.xa.at[n], self.send.at[R_X + n], self.recv.at[R_X + n], self.place.x)

    def to_y(self, n):
        src = self.total.at[(2, 3)[n], pl.ds(2, 2)]
        return remote(src, self.ya.at[n], self.send.at[R_Y + n], self.recv.at[R_Y + n], self.place.y)

    def to_xb(self):
        src = self.total.at[1, pl.ds(2, 2)]
        return remote(src, self.xb, self.send.at[R_XB], self.recv.at[R_XB], self.place.x)

    def to_yb(self):
        src = self.total.at[2, pl.ds(0, 2)]
        return remote(src, self.yb, self.send.at[R_YB], self.recv.at[R_YB], self.place.y)

    def to_z(self, k, arriving=False):
        n = (k if arriving else DEPTH - k) - 1
        src = self.total.at[0, self.place.depth[k]]
        return remote(
            src, self.zr.at[n], self.send.at[R_Z + k - 1], self.recv.at[R_Z + n], self.place.along[k]
        )

    def begin(self, loads=True):
        for r in ORDER:
            self.pair(r).start()
        if loads:
            self.begin_loads()

    def begin_loads(self):
        if self.own is not None:
            for r in ORDER[:2]:
                self.load(r).start()

    def chip(self, r):
        if self.own is not None:
            self.load(r).wait()
            mine = self.own[ORDER.index(r) % 2]
        else:
            mine = self.src[pl.ds(self.place.col[r] * DEPTH, DEPTH), self.place.core]
        self.pair(r).wait_recv()
        self.total[r] = self.total[r] + mine
        if self.own is not None and ORDER.index(r) < 2:
            self.load(ORDER[ORDER.index(r) + 2]).start()
        if r == 1:
            self.to_x(1).start()
            self.to_x(0).start()
        if r == 2:
            self.to_y(1).start()
            self.to_y(0).start()

    def chip_all(self):
        for r in ORDER:
            self.chip(r)

    def cross(self):
        self.to_x(1).wait_recv()
        self.total[2, 0:2] = self.total[2, 0:2] + self.xa[1]
        self.to_yb().start()
        self.to_y(1).wait_recv()
        self.total[1, 2:4] = self.total[1, 2:4] + self.ya[1]
        self.to_xb().start()

    def column(self):
        self.to_x(0).wait_recv()
        self.to_yb().wait_recv()
        add = lambda a, b, c: (a.astype(F32) + b.astype(F32) + c.astype(F32)).astype(BF16)
        self.total[0, 0:2] = add(self.total[0, 0:2], self.xa[0], self.yb[...])
        self.to_y(0).wait_recv()
        self.to_xb().wait_recv()
        self.total[0, 2:4] = add(self.total[0, 2:4], self.ya[0], self.xb[...])
        for k in (2, 1, 3):
            self.to_z(k).start()

    def result(self):
        out = self.total[0, self.place.depth[0]].astype(F32)
        for k in range(1, DEPTH):
            self.to_z(k, True).wait_recv()
            out = out + self.zr[k - 1].astype(F32)
        return out

    def end(self):
        self.end_pairs()
        self.end_rest()

    def end_pairs(self):
        for r in range(COLS):
            self.pair(r).wait_send()

    def end_rest(self):
        for n in range(2):
            self.to_x(n).wait_send()
            self.to_y(n).wait_send()
        self.to_xb().wait_send()
        self.to_yb().wait_send()
        for k in range(1, DEPTH):
            self.to_z(k).wait_send()


class LastSum:
    def __init__(self, place, total, got, send, recv):
        self.place, self.total, self.got, self.send, self.recv = place, total, got, send, recv

    def copy(self, n, arriving=False):
        place = self.place
        if n < 3:
            device, m = place.along[n + 1], (n if arriving else 2 - n)
        elif n < 6:
            device, m = place.over[n - 2], (n if arriving else 8 - n)
        else:
            device, m = (place.partner, place.x, place.y, place.across)[n - 6], n
        stage = 0 if n < 7 else 1
        return remote(self.total.at[stage], self.got.at[m], self.send.at[n], self.recv.at[m], device)

    def run(self):
        for stage, steps in enumerate((range(7), range(7, 10))):
            for n in steps:
                self.copy(n).start()
            total = self.total[stage]
            for n in steps:
                self.copy(n, True).wait_recv()
                total = total + self.got[n]
            self.total[stage + 1] = total
        for n in range(10):
            self.copy(n).wait_send()


def take_vectors(place, table, outs):
    for ref, lo, size, row in vector_parts(outs):
        rows = (size * 32) // D
        start = place.index * size
        at_row, at_lane = lax.div(start, D), lax.rem(start, D)
        mine = lax.broadcasted_iota(jnp.int32, (rows, D), 0) == at_row
        line = jnp.sum(jnp.where(mine, table[row : row + rows, :], 0.0), axis=0, keepdims=True)
        lane = lax.broadcasted_iota(jnp.int32, (size, D), 1)
        pick = lax.broadcasted_iota(jnp.int32, (size, D), 0) + at_lane == lane
        ref[:, lo : lo + size] = lax.dot_general(
            line,
            jnp.where(pick, 1.0, 0.0),
            (((1,), (1,)), ((), ())),
            preferred_element_type=F32,
            precision=lax.Precision.HIGHEST,
        )


def small_slabs(whole):
    devices, half = 2 * COLS * DEPTH, D // 2
    left = whole[:, 0:half].reshape(devices, 24, half)
    right = whole[:, half:D].reshape(devices, 24, half)
    both = jnp.concatenate([left, right], axis=1).astype(BF16)
    return both.reshape(COLS * DEPTH, 2, 48, half)


HALF = FF // 2
SLAB = (48, D)


def by_pieces(w):
    size = w.shape[1] // 64
    cuts = [w[:, (2 * i + n) * size : (2 * i + n + 1) * size] for n in range(2) for i in range(32)]
    return jnp.concatenate(cuts, axis=1)


def from_pieces(first, second):
    size = first.shape[1] // 32
    cuts = [w[:, i * size : (i + 1) * size] for i in range(32) for w in (first, second)]
    return jnp.concatenate(cuts, axis=1)


def mlp_half_tile(n, t, refs):
    mid_ref, cot_ref, a2_ref, g_mlp_ref, act_ref, g_pre_ref, acc_ref, acc_g_ref, wf, wo, table_ref, sums_ref = refs
    rows = rows_of(0, t)
    gain = table_ref[LN2G : LN2G + 1, :]
    if n == 0:
        n2, _ = normalize(mid_ref[rows, :])
        a2 = (n2 * gain + table_ref[LN2B : LN2B + 1, :]).astype(BF16)
        g_mlp = (BRANCH * cot_ref[rows, :].astype(F32)).astype(BF16)
        a2_ref[rows, :] = a2
        g_mlp_ref[rows, :] = g_mlp
        sums_ref[2:3, :] += colsum(g_mlp.astype(F32))
    else:
        a2 = a2_ref[rows, :]
        g_mlp = g_mlp_ref[rows, :]
    out = None
    g_a2 = None
    for j in range(HALF // D):
        cols = slice(j * D, (j + 1) * D)
        row = 2 * n + j
        wf_j = wf[n, :, cols]
        wo_j = wo[n, 2 * j : 2 * j + 2].reshape(D, D)
        pre = dot(a2, wf_j) + table_ref[FCB + row : FCB + row + 1, :]
        g_act = dot_nt(g_mlp, wo_j)
        square = pre * pre
        th = jnp.tanh(pre * (GELU_A + (GELU_A * GELU_B) * square))
        half = 0.5 + 0.5 * th
        act = (pre * half).astype(BF16)
        slope = half + pre * (0.5 - 0.5 * th * th) * (GELU_A + (3 * GELU_A * GELU_B) * square)
        g_pre = (g_act * slope).astype(BF16)
        act_ref[rows, cols] = act
        g_pre_ref[rows, cols] = g_pre
        sums_ref[3 + row : 4 + row, :] += colsum(g_pre.astype(F32))
        part, part_g = dot(act, wo_j), dot_nt(g_pre, wf_j)
        out = part if out is None else out + part
        g_a2 = part_g if g_a2 is None else g_a2 + part_g
    if n == 0:
        acc_ref[rows, :] = out
        acc_g_ref[rows, :] = g_a2
        return
    out = acc_ref[rows, :] + out
    g_a2 = acc_g_ref[rows, :] + g_a2
    mid = mid_ref[rows, :]
    n2, rstd = normalize(mid)
    g_out = cot_ref[rows, :].astype(F32)
    cot_ref[rows, :] = (mid + BRANCH * (out + table_ref[OUTB : OUTB + 1, :])).astype(BF16)
    mid_ref[rows, :] = g_out + norm_backward(g_a2, n2, rstd, gain)
    sums_ref[0:1, :] += colsum(g_a2 * n2)
    sums_ref[1:2, :] += colsum(g_a2)


def out_slabs(act_ref, g_mlp_ref, dw_o):
    for j in range(HALF // D):
        res = dot_tn(act_ref[:, j * D : (j + 1) * D], g_mlp_ref[...])
        dw_o[8 * j : 8 * j + 8] = res.astype(BF16).reshape(8, 2, *SLAB)


def fc_slabs(a2_ref, g_pre_ref, dw_f):
    left = dot_tn(a2_ref[...], g_pre_ref[:, 0:D]).reshape(32, 24, D)
    right = dot_tn(a2_ref[...], g_pre_ref[:, D : 2 * D]).reshape(32, 24, D)
    dw_f[...] = jnp.concatenate([left, right], axis=1).astype(BF16).reshape(dw_f.shape)


def mlp_exchange_kernel(
    mid_hbm,
    cs_hbm,
    cl_hbm,
    table_ref,
    wf0_hbm,
    wo0_hbm,
    slab_f,
    wout,
    os_hbm,
    ol_hbm,
    g_mid_hbm,
    sums_ref,
    d_out0,
    d_fc0,
    so_hbm,
    sf_hbm,
    mid_ref,
    cot_ref,
    a2_ref,
    g_mlp_ref,
    act_ref,
    g_pre_ref,
    acc_ref,
    acc_g_ref,
    wf,
    wo,
    dw_o,
    dw_f,
    r_total,
    r_xa,
    r_ya,
    r_xb,
    r_yb,
    r_zr,
    io_sem,
    g_send,
    g_recv,
    r_send,
    r_recv,
):
    place = Place()
    welcome = place.greet()
    short, long = cs_hbm.shape[0], cl_hbm.shape[0]
    tiles = (short + long) // TILE
    parts = (pl.ds(0, short), pl.ds(short, long))
    pairs = (
        (mid_hbm, mid_ref),
        (cs_hbm, cot_ref.at[parts[0]]),
        (cl_hbm, cot_ref.at[parts[1]]),
        (wf0_hbm, wf.at[0]),
        (wo0_hbm, wo.at[0]),
    )
    loads = [pltpu.make_async_copy(src, dst, io_sem.at[n]) for n, (src, dst) in enumerate(pairs)]
    for copy in loads:
        copy.start()
    q, z, c = place.col[0], place.depth[0], place.core
    wf[1, at((q * DEPTH + z) * 48, 48, 16), at(c * D, D, 128)] = slab_f[...]
    wo[1, q, z, c] = wout[0, 48:96]
    f1 = Gather(place, wide_spot(wf.at[1], 0, D), slab_f, g_send.at[0], g_recv.at[0])
    o1 = Gather(place, tall_spot(wo.at[1], 0, 48), wout.at[:, pl.ds(48, 48)], g_send.at[1], g_recv.at[1])
    ro, rf = [
        Reduce(
            place, src, None, r_total.at[n], r_xa.at[n], r_ya.at[n], r_xb.at[n], r_yb.at[n],
            r_zr.at[n], r_send.at[n], r_recv.at[n], None,
        )
        for n, src in enumerate((dw_o, dw_f))
    ]
    sums_ref[...] = jnp.zeros_like(sums_ref)
    welcome()
    f1.a()
    o1.a()
    for copy in loads:
        copy.wait()
    refs = (
        mid_ref, cot_ref, a2_ref, g_mlp_ref, act_ref, g_pre_ref, acc_ref, acc_g_ref, wf, wo, table_ref, sums_ref,
    )
    after = hooks({2: ((f1.b,),), 3: ((o1.b,),), 4: ((f1.c,),)})

    def first_step(t):
        mlp_half_tile(0, t, refs)
        after(t)

    loop(tiles, first_step)
    out_slabs(act_ref, g_mlp_ref, dw_o)
    ro.begin()
    o1.c()
    fc_slabs(a2_ref, g_pre_ref, dw_f)
    rf.begin()
    ro.chip_all()
    f1.d()
    o1.d()
    f1.e()
    o1.e()

    def give_out():
        d_out0[...] = ro.result()

    after_second = hooks(
        {
            0: ((ro.cross,), (rf.chip_all,)),
            2: ((ro.column,),),
            3: ((rf.cross,),),
            5: ((rf.column,), (give_out,)),
        }
    )

    def second_step(t):
        mlp_half_tile(1, t, refs)
        after_second(t)

    loop(tiles, second_step)
    stores = [
        pltpu.make_async_copy(src, dst, io_sem.at[5 + n])
        for n, (src, dst) in enumerate(
            (
                (cot_ref.at[parts[0]], os_hbm),
                (cot_ref.at[parts[1]], ol_hbm),
                (mid_ref, g_mid_hbm),
                (dw_o, so_hbm),
                (dw_f, sf_hbm),
            )
        )
    ]
    for copy in stores[0:3]:
        copy.start()
    ro.end_pairs()
    out_slabs(act_ref, g_mlp_ref, dw_o)
    stores[3].start()
    rf.end_pairs()
    fc_slabs(a2_ref, g_pre_ref, dw_f)
    stores[4].start()
    res = rf.result()
    d_fc0[...] = jnp.concatenate([res[0:24], res[24:48]], axis=1)
    ro.end_rest()
    rf.end_rest()
    f1.end()
    o1.end()
    for copy in stores:
        copy.wait()


def reduce_buffers(n, shape):
    return [
        pltpu.VMEM((n, COLS, DEPTH) + shape, BF16),
        pltpu.VMEM((n, 2, 2) + shape, BF16),
        pltpu.VMEM((n, 2, 2) + shape, BF16),
        pltpu.VMEM((n, 2) + shape, BF16),
        pltpu.VMEM((n, 2) + shape, BF16),
        pltpu.VMEM((n, DEPTH - 1) + shape, BF16),
    ]


def mlp_exchange(mid, cs, cl, table, wf0, wo0, slab_f, wout):
    rows = mid.shape[0]
    chips = COLS * DEPTH
    sem = pltpu.SemaphoreType.DMA
    slabs = (chips, 2) + SLAB
    return pl.pallas_call(
        mlp_exchange_kernel,
        out_shape=(
            jax.ShapeDtypeStruct(cs.shape, BF16),
            jax.ShapeDtypeStruct(cl.shape, BF16),
            jax.ShapeDtypeStruct(mid.shape, F32),
            jax.ShapeDtypeStruct((8, D), F32),
            jax.ShapeDtypeStruct(SLAB, F32),
            jax.ShapeDtypeStruct((24, HALF), F32),
            jax.ShapeDtypeStruct(slabs, BF16),
            jax.ShapeDtypeStruct(slabs, BF16),
        ),
        in_specs=[ANY, ANY, ANY, VM, ANY, ANY, VM, VM],
        out_specs=[ANY, ANY, ANY, VM, VM, VM, ANY, ANY],
        scratch_shapes=[
            pltpu.VMEM((rows, D), F32),
            pltpu.VMEM((rows, D), BF16),
            pltpu.VMEM((rows, D), BF16),
            pltpu.VMEM((rows, D), BF16),
            pltpu.VMEM((rows, HALF), BF16),
            pltpu.VMEM((rows, HALF), BF16),
            pltpu.VMEM((rows, D), F32),
            pltpu.VMEM((rows, D), F32),
            pltpu.VMEM((2, D, HALF), BF16),
            pltpu.VMEM((2, COLS, DEPTH, 2) + SLAB, BF16),
            pltpu.VMEM(slabs, BF16),
            pltpu.VMEM(slabs, BF16),
            *reduce_buffers(2, SLAB),
            sem((10,)),
            sem((2, N_GATHER)),
            sem((2, N_GATHER)),
            sem((2, N_REDUCE)),
            sem((2, N_REDUCE)),
        ],
        compiler_params=pltpu.CompilerParams(
            vmem_limit_bytes=VMEM_LIMIT, collective_id=2, has_side_effects=True
        ),
        name="mlp_exchange",
    )(mid, cs, cl, table, wf0, wo0, slab_f, wout)


def backward_reduce_kernel(
    ssplit,
    lsplit,
    xs_hbm,
    xl_hbm,
    table_ref,
    wa_hbm,
    a1_hbm,
    qkv_hbm,
    att_hbm,
    lse_t_ref,
    g_mid_hbm,
    sums2_ref,
    go_hbm,
    gf_hbm,
    gxs_hbm,
    gxl_hbm,
    d0,
    d1,
    d2,
    d3,
    d4,
    d5,
    d6,
    d7,
    d_qkv,
    d_proj,
    d_fc1,
    d_out1,
    wa,
    a1_ref,
    qkv_ref,
    att_ref,
    g_mid_ref,
    g_att_ref,
    g_qkv_ref,
    dk_ref,
    dv_ref,
    big_own,
    big_total,
    big_xa,
    big_ya,
    big_xb,
    big_yb,
    big_zr,
    small_src,
    small_total,
    small_xa,
    small_ya,
    small_xb,
    small_yb,
    small_zr,
    total,
    got,
    io_sem,
    own_sem,
    r_send,
    r_recv,
    sum_send,
    sum_recv,
    ln_sums_ref,
    last_total,
    last_got,
    last_send,
    last_recv,
):
    place = Place()
    g_attn_ref = g_qkv_ref.at[:, pl.ds(0, D)]
    short, long = gxs_hbm.shape[0], gxl_hbm.shape[0]
    rows = short + long
    proj_cols = pl.ds(3 * D, D)
    qkv_cols = pl.ds(0, 3 * D)
    loads = [
        pltpu.make_async_copy(src, dst, io_sem.at[n])
        for n, (src, dst) in enumerate(
            (
                (wa_hbm.at[:, proj_cols], wa.at[:, proj_cols]),
                (g_mid_hbm, g_mid_ref),
                (att_hbm, att_ref),
                (qkv_hbm, qkv_ref),
                (a1_hbm, a1_ref),
                (wa_hbm.at[:, qkv_cols], wa.at[:, qkv_cols]),
            )
        )
    ]
    for copy in loads:
        copy.start()
    sums = TableSum(place, total, got, sum_send, sum_recv)
    sums_ref = total.at[0]
    sums_ref[...] = jnp.zeros_like(sums_ref)
    sums_ref[LN2G : LN2G + 7, :] = sums2_ref[0:7, :]
    big = [
        Reduce(
            place, src, big_own, big_total.at[n], big_xa.at[n], big_ya.at[n], big_xb.at[n],
            big_yb.at[n], big_zr.at[n], r_send.at[n], r_recv.at[n], own_sem.at[n],
        )
        for n, src in enumerate((go_hbm, gf_hbm))
    ]
    small = [
        Reduce(
            place, small_src.at[n], None, small_total.at[n], small_xa.at[n], small_ya.at[n], small_xb.at[n],
            small_yb.at[n], small_zr.at[n], r_send.at[2 + n], r_recv.at[2 + n], None,
        )
        for n in range(4)
    ]
    ro, rf = big
    rp, rh = small[3], small[0:3]
    place.greet()()
    ro.begin()
    rf.begin(False)
    last_total[...] = jnp.zeros_like(last_total)
    loads[0].wait()
    loads[1].wait()

    after = hooks(
        {
            0: ((ro.chip, 3),),
            1: ((ro.chip, 1),),
            2: ((ro.chip, 2),),
            3: ((ro.chip, 0), (rf.begin_loads,)),
            4: ((rf.chip, 3),),
            5: ((rf.chip, 1), (rf.chip, 2), (rf.chip, 0)),
        }
    )

    def proj_step(t):
        proj_back_tile(g_mid_ref, wa, g_attn_ref, g_att_ref, sums_ref, t)
        after(t)

    loop(rows // TILE, proj_step)
    loads[2].wait()
    small_src[3] = small_slabs(dot_tn(att_ref[...], g_attn_ref[...]))
    rp.begin()
    x_loads = [
        pltpu.make_async_copy(xs_hbm, att_ref.at[pl.ds(0, short)], io_sem.at[6]),
        pltpu.make_async_copy(xl_hbm, att_ref.at[pl.ds(short, long)], io_sem.at[7]),
    ]
    for copy in x_loads:
        copy.start()
    for copy in loads[3:]:
        copy.wait()

    def give_out():
        d_out1[...] = ro.result()

    def give_fc():
        res = rf.result()
        d_fc1[...] = jnp.concatenate([res[0:24], res[24:48]], axis=1)

    def give_proj():
        res = rp.result()
        d_proj[:, 0 : D // 2] = res[0:24]
        d_proj[:, D // 2 : D] = res[24:48]

    def give_qkv(g):
        res = rh[g].result()
        line = jnp.concatenate([res[0:24], res[24:48]], axis=1)
        for j in range(3):
            d_qkv[:, j * D + g * 256 : j * D + g * 256 + 256] = line[:, j * 256 : j * 256 + 256]

    def heads_begin(g):
        rh[g].begin()

    after_short = hooks(
        {
            0: ((ro.cross,),),
            2: ((rh[0].chip_all,), (rf.column,), (rp.cross,)),
            3: ((rp.column,), (give_out,)),
            4: ((rh[1].chip_all,),),
            5: ((give_qkv, 0),),
        }
    )
    after_long = hooks(
        {
            0: ((rf.cross,), (rp.chip_all,)),
            1: ((heads_begin, 0), (ro.column,)),
            2: ((rh[0].cross,),),
            3: ((heads_begin, 1), (rh[0].column,), (give_fc,)),
            4: ((rh[1].cross,), (give_proj,)),
            5: ((heads_begin, 2), (sums.begin, 0), (rh[1].column,)),
        }
    )

    def pair_step(pair):
        attend_back_pair(
            ssplit[0], qkv_ref, g_att_ref, lse_t_ref, g_qkv_ref, dk_ref, dv_ref, 0, short, pair
        )
        after_short(pair)
        attend_back_pair(
            lsplit[0], qkv_ref, g_att_ref, lse_t_ref, g_qkv_ref, dk_ref, dv_ref, short, long, pair
        )

        @pl.when(lax.rem(pair, 2) == 1)
        def _():
            g = lax.div(pair, 2)
            cols = pl.ds(pl.multiple_of(g * D, 128), D)
            small_src[g] = small_slabs(dot_tn(a1_ref[...], g_qkv_ref[:, cols]))
            qv_sums(g_qkv_ref, sums_ref, g)

        after_long(pair)

    loop(PAIRS, pair_step)
    for copy in x_loads:
        copy.wait()
    after_norm = hooks(
        {
            0: ((rh[2].chip_all,), (sums.next, 0)),
            2: ((rh[2].cross,), (sums.next, 1)),
            3: ((give_qkv, 1),),
            4: ((rh[2].column,), (sums.add, 2)),
        }
    )

    def norm_step(t):
        ln1_back_tile(att_ref, g_mid_ref, table_ref, wa, g_qkv_ref, g_mid_ref, ln_sums_ref, 0, t)
        after_norm(t)

    ln_sums_ref[...] = jnp.zeros_like(ln_sums_ref)
    loop(short // TILE, norm_step)
    stores = [
        pltpu.make_async_copy(g_mid_ref.at[pl.ds(0, short)], gxs_hbm, io_sem.at[8]),
        pltpu.make_async_copy(g_mid_ref.at[pl.ds(short, long)], gxl_hbm, io_sem.at[9]),
    ]
    stores[0].start()
    loop(long // TILE, lambda t: norm_step(t + short // TILE))
    stores[1].start()
    lanes = D // 128
    lines = [ln_sums_ref[r : r + 1, 128 * j : 128 * j + 128] for r in range(2) for j in range(lanes)]
    last_total[0, 0 : 2 * lanes] = jnp.concatenate(lines, axis=0)
    last = LastSum(place, last_total, last_got, last_send, last_recv)
    last.run()
    give_qkv(2)
    final = total.at[3]
    for r in range(2):
        final[r : r + 1, :] = jnp.concatenate(
            [last_total[2, r * lanes + j : r * lanes + j + 1, :] for j in range(lanes)], axis=1
        )
    take_vectors(place, final, (d0, d1, d2, d3, d4, d5, d6, d7))
    sums.end()
    for reduce in big + small:
        reduce.end()
    for copy in stores:
        copy.wait()


def backward_reduce(ssplit, lsplit, xs, xl, table, w_attn, a1, qkv, att, lse_t, g_mid, sums2, dwo, dwf, sizes):
    short, long = xs.shape[0], xl.shape[0]
    rows = short + long
    chips = COLS * DEPTH
    devices = 2 * chips
    big, little = SLAB, (48, D // 2)
    sem = pltpu.SemaphoreType.DMA
    return pl.pallas_call(
        backward_reduce_kernel,
        out_shape=(
            jax.ShapeDtypeStruct(xs.shape, F32),
            jax.ShapeDtypeStruct(xl.shape, F32),
            *[jax.ShapeDtypeStruct((1, n), F32) for n in sizes],
            jax.ShapeDtypeStruct((D // devices, 3 * D), F32),
            jax.ShapeDtypeStruct((D // devices, D), F32),
            jax.ShapeDtypeStruct((D // devices, HALF), F32),
            jax.ShapeDtypeStruct(SLAB, F32),
        ),
        in_specs=[SM, SM, ANY, ANY, VM, ANY, ANY, ANY, ANY, VM, ANY, VM, ANY, ANY],
        out_specs=[ANY, ANY] + [VM] * 12,
        scratch_shapes=[
            pltpu.VMEM((D, 4 * D), BF16),
            pltpu.VMEM((rows, D), BF16),
            pltpu.VMEM((rows, 3 * D), BF16),
            pltpu.VMEM((rows, D), BF16),
            pltpu.VMEM((rows, D), F32),
            pltpu.VMEM((rows, D), BF16),
            pltpu.VMEM((rows, 3 * D), BF16),
            pltpu.VMEM((long, 128), F32),
            pltpu.VMEM((long, 128), F32),
            pltpu.VMEM((2, DEPTH) + big, BF16),
            *reduce_buffers(2, big),
            pltpu.VMEM((4, chips, 2) + little, BF16),
            *reduce_buffers(4, little),
            pltpu.VMEM((4, 16, D), F32),
            pltpu.VMEM((SUM_STEPS, 16, D), F32),
            sem((10,)),
            sem((2, COLS)),
            sem((6, N_REDUCE)),
            sem((6, N_REDUCE)),
            sem((SUM_STEPS,)),
            sem((SUM_STEPS,)),
            pltpu.VMEM((8, D), F32),
            pltpu.VMEM((3, 16, 128), F32),
            pltpu.VMEM((10, 16, 128), F32),
            sem((10,)),
            sem((10,)),
        ],
        compiler_params=pltpu.CompilerParams(
            vmem_limit_bytes=BACK_VMEM, collective_id=1, has_side_effects=True
        ),
        name="attention_backward_reduce",
    )(ssplit, lsplit, xs, xl, table, w_attn, a1, qkv, att, lse_t, g_mid, sums2, dwo, dwf)


BACK_VMEM = 60 * 2**20


PARTS = 4


def hand_over_kernel(os_hbm, ol_hbm, gs_hbm, gl_hbm, *refs):
    small_in, outs = refs[:14], refs[14:30]
    buffers, load_sem, store_sem = refs[30:34], refs[34], refs[35]
    loads, stores = [], []
    for n, (src, dst, mid) in enumerate(zip((os_hbm, ol_hbm, gs_hbm, gl_hbm), outs[:4], buffers)):
        size = src.shape[0] // PARTS
        for p in range(PARTS):
            rows = pl.ds(p * size, size)
            loads.append(pltpu.make_async_copy(src.at[rows], mid.at[rows], load_sem.at[n, p]))
            stores.append(pltpu.make_async_copy(mid.at[rows], dst.at[rows], store_sem.at[n, p]))
    for copy in loads:
        copy.start()
    for n in range(10):
        outs[4 + n][...] = small_in[n][...]
    fc0, fc1, out0, out1 = small_in[10:]
    outs[14][...] = from_pieces(fc0[...], fc1[...])
    outs[15][0:48, :] = out0[...]
    outs[15][48:96, :] = out1[...]
    for load, store in zip(loads, stores):
        load.wait()
        store.start()
    for copy in stores:
        copy.wait()


def hand_over(big, small):
    shape = lambda a: jax.ShapeDtypeStruct(a.shape, a.dtype)
    sem = pltpu.SemaphoreType.DMA
    return pl.pallas_call(
        hand_over_kernel,
        out_shape=(
            *map(shape, big),
            *map(shape, small[:10]),
            jax.ShapeDtypeStruct((24, FF), F32),
            jax.ShapeDtypeStruct((96, D), F32),
        ),
        in_specs=[ANY] * 4 + [VM] * 14,
        out_specs=[ANY] * 4 + [VM] * 12,
        scratch_shapes=[pltpu.VMEM(a.shape, a.dtype) for a in big] + [sem((4, PARTS))] * 2,
        compiler_params=pltpu.CompilerParams(vmem_limit_bytes=VMEM_LIMIT),
        name="hand_over",
    )(*big, *small)


AXES = ("dp", "fsdp")


def gather(x, axis=0):
    return lax.all_gather(x, AXES, axis=axis, tiled=True)


def scatter(x):
    return lax.psum_scatter(x, AXES, scatter_dimension=0, tiled=True)


def general(args, devices):
    (st, lt, ss, ls, ln1g, ln1b, wqkv, qvb, wproj, projb, ln2g, ln2b, wfc, fcb, wout, outb, sc, lc) = args
    xs, xl = st.reshape(-1, D), lt.reshape(-1, D)
    cs, cl = sc.reshape(-1, D), lc.reshape(-1, D)
    vectors = (ln1g, ln1b, qvb, projb, ln2g, ln2b, outb, fcb)
    sizes = [v.shape[0] for v in vectors]
    every = lax.all_gather(jnp.concatenate(vectors), AXES, axis=0)
    starts = [sum(sizes[:i]) for i in range(len(sizes))]
    full = [every[:, s : s + n].reshape(-1, D) for s, n in zip(starts, sizes)]
    table = jnp.concatenate(full + [jnp.zeros((4, D), BF16)]).astype(F32)
    by_group = lambda w: w.reshape(-1, 3, GROUPS, GROUP).swapaxes(1, 2).reshape(-1, 3 * D)
    w_attn = gather(jnp.concatenate([by_group(wqkv), wproj], axis=1))
    w_fc, w_out = gather(wfc), gather(wout)
    a1, qkv, att, lse_t, mid = forward_local(ss, ls, xs, xl, table, w_attn)
    out_s, out_l, g_mid, sums2, dwf, dwo = mlp_local(mid, cs, cl, table, w_fc, w_out, False)
    gxs, gxl, dwp, dwq, sums1 = backward_local(
        ss, ls, xs, xl, table, w_attn, a1, qkv, att, lse_t, g_mid
    )
    dwq = dwq.reshape(-1, GROUPS, 3, GROUP).swapaxes(1, 2).reshape(-1, 3 * D)
    return finish(args, devices, starts, sizes, out_s, out_l, gxs, gxl, sums1, sums2, dwq, dwp, dwf, dwo)


def finish(args, devices, starts, sizes, out_s, out_l, gxs, gxl, sums1, sums2, dwq, dwp, dwf, dwo):
    st, lt = args[0], args[1]
    rs = lambda x: x.reshape(devices, -1)
    small = jnp.concatenate(
        [
            rs(sums1[0]),
            rs(sums1[1]),
            rs(sums1[2:4]),
            rs(sums1[4]),
            rs(sums2[0]),
            rs(sums2[1]),
            rs(sums2[2]),
            rs(sums2[3:7]),
        ],
        axis=1,
    )
    small = scatter(small)[0]
    parts = [small[s : s + n] for s, n in zip(starts, sizes)]
    d_ln1g, d_ln1b, d_qvb, d_projb, d_ln2g, d_ln2b, d_outb, d_fcb = parts
    return (
        out_s.reshape(st.shape),
        out_l.reshape(lt.shape),
        gxs.reshape(st.shape),
        gxl.reshape(lt.shape),
        d_ln1g,
        d_ln1b,
        scatter(dwq),
        d_qvb,
        scatter(dwp),
        d_projb,
        d_ln2g,
        d_ln2b,
        scatter(dwf),
        d_fcb,
        scatter(dwo),
        d_outb,
    )


def on_torus(args):
    (st, lt, ss, ls, ln1g, ln1b, wqkv, qvb, wproj, projb, ln2g, ln2b, wfc, fcb, wout, outb, sc, lc) = args
    xs, xl = st.reshape(-1, D), lt.reshape(-1, D)
    cs, cl = sc.reshape(-1, D), lc.reshape(-1, D)
    vectors = (ln1g, ln1b, qvb, projb, ln2g, ln2b, outb, fcb)
    table, w_attn, wf0, wo0, slab_f1, a1, qkv, att, lse_t, mid = forward_gather(
        ss, ls, xs, xl, wqkv, wproj, wfc, wout, vectors
    )
    out_s, out_l, g_mid, sums2, d_out0, d_fc0, dwo, dwf = mlp_exchange(
        mid, cs, cl, table, wf0, wo0, slab_f1, wout[None]
    )
    gxs, gxl, *rest = backward_reduce(
        ss, ls, xs, xl, table, w_attn, a1, qkv, att, lse_t, g_mid, sums2, dwo, dwf, [v.shape[0] for v in vectors]
    )
    d_fc1, d_out1 = rest[10:]
    out_s, out_l, gxs, gxl, *rest = hand_over(
        (out_s, out_l, gxs, gxl), (*rest[:10], d_fc0, d_fc1, d_out0, d_out1)
    )
    d_ln1g, d_ln1b, d_qvb, d_projb, d_ln2g, d_ln2b, d_outb, d_fcb = [v.reshape(-1) for v in rest[:8]]
    d_qkv, d_proj, d_fc, d_out = rest[8:]
    return (
        out_s.reshape(st.shape),
        out_l.reshape(lt.shape),
        gxs.reshape(st.shape),
        gxl.reshape(lt.shape),
        d_ln1g,
        d_ln1b,
        d_qkv,
        d_qvb,
        d_proj,
        d_projb,
        d_ln2g,
        d_ln2b,
        d_fc,
        d_fcb,
        d_out,
        d_outb,
    )


def per_device(shape, *args):
    devices = shape["dp"] * shape["fsdp"]
    sizes = (args[0].shape[1], args[1].shape[1], args[6].shape, args[14].shape)
    if shape == {"dp": COLS, "fsdp": 2 * DEPTH} and sizes == (512, 1024, (24, 3 * D), (96, D)):
        return on_torus(args)
    return general(args, devices)


def solution(mesh):
    vec, mat, seq = P(AXES), P(AXES, None), P(AXES, None, None)
    in_specs = (seq, seq, vec, vec) + (vec, vec, mat, vec, mat, vec) * 1 + (vec, vec, mat, vec, mat, vec) + (seq, seq)
    out_specs = (seq,) * 4 + (vec, vec, mat, vec, mat, vec) * 2
    return jax.shard_map(
        functools.partial(per_device, dict(mesh.shape)),
        mesh=mesh,
        in_specs=in_specs,
        out_specs=out_specs,
        check_vma=False,
    )
```

```python
import functools

import jax
import jax.numpy as jnp
from jax import lax
from jax.experimental import pallas as pl
from jax.experimental.pallas import tpu as pltpu
from jax.sharding import PartitionSpec as P

F32 = jnp.float32
BF16 = jnp.bfloat16
D = 768
FF = 3072
HEAD_DIM = 64
PAIRS = D // 128
GROUP = 256
GROUPS = D // GROUP
TILE = 256
BRANCH = 0.14433756729740643
EPS = 1e-05
NEG = -1e30
VMEM_LIMIT = 60 * 2**20

LN1G, LN1B, QB, VB, PROJB, LN2G, LN2B, OUTB, FCB = 0, 1, 2, 3, 4, 5, 6, 7, 8


def dot(a, b):
    return jnp.dot(a, b, preferred_element_type=F32)


def dot_nt(a, b):
    return lax.dot_general(a, b, (((1,), (1,)), ((), ())), preferred_element_type=F32)


def dot_tn(a, b):
    return lax.dot_general(a, b, (((0,), (0,)), ((), ())), preferred_element_type=F32)


def normalize(x):
    center = x - jnp.mean(x, axis=-1, keepdims=True)
    rstd = lax.rsqrt(jnp.mean(center * center, axis=-1, keepdims=True) + EPS)
    return center * rstd, rstd


def norm_backward(g, n, rstd, gain):
    e = g * gain
    return rstd * (
        e
        - jnp.mean(e, axis=-1, keepdims=True)
        - n * jnp.mean(e * n, axis=-1, keepdims=True)
    )


def rows_of(base, tile):
    return pl.ds(pl.multiple_of(base + tile * TILE, TILE), TILE)


def lanes_of(start):
    return pl.ds(pl.multiple_of(start, 128), 128)


def loop(count, body):
    lax.fori_loop(0, count, lambda i, c: (body(i), c)[1], 0)


def group_refs(short, long):
    return ((short, 0), (long, short.shape[0]))


def norm_tile(x_ref, table_ref, a1_ref, base, t):
    n, _ = normalize(x_ref[rows_of(0, t), :].astype(F32))
    a1 = n * table_ref[LN1G : LN1G + 1, :] + table_ref[LN1B : LN1B + 1, :]
    a1_ref[rows_of(base, t), :] = a1.astype(BF16)


def group_cols(g, part):
    start = g * D + part * GROUP
    return pl.ds(start if isinstance(start, int) else pl.multiple_of(start, 128), GROUP)


def pair_cols(pair, part):
    return lanes_of(lax.div(pair, 2) * D + part * GROUP + lax.rem(pair, 2) * 128)


def vector_cols(g):
    return pl.ds(g * GROUP if isinstance(g, int) else pl.multiple_of(g * GROUP, 128), GROUP)


def qkv_tile(table_ref, w_ref, a1_ref, qkv_ref, g, t):
    rows = rows_of(0, t)
    a1 = a1_ref[rows, :]
    for part, bias in ((0, QB), (1, None), (2, VB)):
        out = dot(a1, w_ref[:, group_cols(g, part)])
        if bias is not None:
            out = out + table_ref[bias : bias + 1, vector_cols(g)]
        qkv_ref[rows, group_cols(g, part)] = out.astype(BF16)


def attend_pair(split, qkv_ref, att_ref, lse_t_ref, base, length, pair):
    first = lax.broadcasted_iota(jnp.int32, (TILE, 128), 1) < HEAD_DIM
    v_t = jnp.transpose(qkv_ref[base : base + length, pair_cols(pair, 2)])
    for qb in range(length // TILE):
        start = qb * TILE
        qrows = slice(base + start, base + start + TILE)
        q_pair = qkv_ref[qrows, pair_cols(pair, 0)] * BF16(HEAD_DIM**-0.5)
        q_pos = start + lax.broadcasted_iota(jnp.int32, (1, TILE), 1)
        low = jnp.where(q_pos >= split, split, 0)
        spans = []
        for lo, hi in ((0, start), (start, start + TILE)):
            if lo == hi:
                continue
            k_pos = lo + lax.broadcasted_iota(jnp.int32, (hi - lo, TILE), 0)
            visible = k_pos >= low
            if hi > start:
                visible = visible & (k_pos <= q_pos)
            spans.append((lo, hi, visible))
        outs = []
        for half in (0, 1):
            q_half = jnp.where(first if half == 0 else ~first, q_pair, BF16(0))
            scores = [
                jnp.where(visible, dot_nt(qkv_ref[base + lo : base + hi, pair_cols(pair, 1)], q_half), NEG)
                for lo, hi, visible in spans
            ]
            peak = functools.reduce(jnp.maximum, [jnp.max(s, axis=0, keepdims=True) for s in scores])
            out = total = None
            for s, (lo, hi, _) in zip(scores, spans):
                e = jnp.exp(s - peak)
                part = jnp.sum(e, axis=0, keepdims=True)
                total = part if total is None else total + part
                part = dot(v_t[half * HEAD_DIM : (half + 1) * HEAD_DIM, lo:hi], e.astype(BF16))
                out = part if out is None else out + part
            outs.append(out * (1.0 / total))
            lse_t_ref[pl.ds(2 * pair + half, 1), qrows] = peak + jnp.log(total)
        out = jnp.transpose(jnp.concatenate(outs, axis=0).astype(BF16))
        att_ref[qrows, lanes_of(pair * 128)] = out


def mid_tile(x_ref, table_ref, w_ref, att_ref, mid_ref, base, t):
    rows = rows_of(base, t)
    out = dot(att_ref[rows, :], w_ref[:, 3 * D : 4 * D]) + table_ref[PROJB : PROJB + 1, :]
    mid_ref[rows, :] = x_ref[rows_of(0, t), :].astype(F32) + BRANCH * out


def forward_kernel(
    ssplit, lsplit, xs, xl, table_ref, w_ref, a1_ref, qkv_ref, att_ref, lse_t_ref, mid_ref
):
    for x_ref, base in group_refs(xs, xl):
        loop(x_ref.shape[0] // TILE, lambda t: norm_tile(x_ref, table_ref, a1_ref, base, t))
    for g in range(GROUPS):
        loop(a1_ref.shape[0] // TILE, lambda t: qkv_tile(table_ref, w_ref, a1_ref, qkv_ref, g, t))
    lse_t_ref[...] = jnp.zeros_like(lse_t_ref)

    def pair_step(pair, c):
        attend_pair(ssplit[0], qkv_ref, att_ref, lse_t_ref, 0, xs.shape[0], pair)
        attend_pair(lsplit[0], qkv_ref, att_ref, lse_t_ref, xs.shape[0], xl.shape[0], pair)
        return c

    lax.fori_loop(0, PAIRS, pair_step, 0)
    for x_ref, base in group_refs(xs, xl):
        lax.fori_loop(
            0,
            x_ref.shape[0] // TILE,
            lambda t, c: (mid_tile(x_ref, table_ref, w_ref, att_ref, mid_ref, base, t), c)[1],
            0,
        )


VM = pl.BlockSpec(memory_space=pltpu.VMEM)
SM = pl.BlockSpec(memory_space=pltpu.SMEM)


def forward_local(ssplit, lsplit, xs, xl, table, w_attn):
    rows = xs.shape[0] + xl.shape[0]
    return pl.pallas_call(
        forward_kernel,
        out_shape=(
            jax.ShapeDtypeStruct((rows, D), BF16),
            jax.ShapeDtypeStruct((rows, 3 * D), BF16),
            jax.ShapeDtypeStruct((rows, D), BF16),
            jax.ShapeDtypeStruct((16, rows), F32),
            jax.ShapeDtypeStruct((rows, D), F32),
        ),
        in_specs=[SM, SM, VM, VM, VM, VM],
        out_specs=[VM] * 5,
        compiler_params=pltpu.CompilerParams(vmem_limit_bytes=VMEM_LIMIT),
        name="attention_forward",
    )(ssplit, lsplit, xs, xl, table, w_attn)


GELU_A = 0.7978845608028654
GELU_B = 0.044715


def mlp_tile(mid, g_out, table_ref, wf_ref, wo_ref):
    n2, rstd = normalize(mid)
    gain = table_ref[LN2G : LN2G + 1, :]
    a2 = (n2 * gain + table_ref[LN2B : LN2B + 1, :]).astype(BF16)
    g_mlp = (BRANCH * g_out).astype(BF16)
    out = None
    g_a2 = None
    acts, g_pres = [], []
    for j in range(FF // D):
        cols = slice(j * D, (j + 1) * D)
        pre = dot(a2, wf_ref[:, cols]) + table_ref[FCB + j : FCB + j + 1, :]
        g_act = dot_nt(g_mlp, wo_ref[cols, :])
        square = pre * pre
        t = jnp.tanh(pre * (GELU_A + (GELU_A * GELU_B) * square))
        half = 0.5 + 0.5 * t
        act = (pre * half).astype(BF16)
        slope = half + pre * (0.5 - 0.5 * t * t) * (GELU_A + (3 * GELU_A * GELU_B) * square)
        g_pre = (g_act * slope).astype(BF16)
        acts.append(act)
        g_pres.append(g_pre)
        part = dot(act, wo_ref[cols, :])
        out = part if out is None else out + part
        part = dot_nt(g_pre, wf_ref[:, cols])
        g_a2 = part if g_a2 is None else g_a2 + part
    out = mid + BRANCH * (out + table_ref[OUTB : OUTB + 1, :])
    g_mid = g_out + norm_backward(g_a2, n2, rstd, gain)
    return out, g_mid, a2, g_mlp, acts, g_pres, g_a2, n2


def colsum(x):
    return jnp.sum(x, axis=0, keepdims=True)


def mlp_kernel(
    n_tiles,
    slabs,
    mid_ref,
    cs_ref,
    cl_ref,
    table_ref,
    wf_ref,
    wo_ref,
    os_ref,
    ol_ref,
    g_mid_ref,
    sums_ref,
    dwf_ref,
    dwo_ref,
    a2_ref,
    g_mlp_ref,
    act_ref,
    g_pre_ref,
):
    step = pl.program_id(0)
    short_tiles = n_tiles[0]
    tiles = n_tiles[0] + n_tiles[1]

    @pl.when(step == 0)
    def _():
        sums_ref[...] = jnp.zeros_like(sums_ref)

    @pl.when(step < tiles)
    def _():
        cot = jnp.where(step < short_tiles, cs_ref[...], cl_ref[...]).astype(F32)
        out, g_mid, a2, g_mlp, acts, g_pres, g_a2, n2 = mlp_tile(
            mid_ref[...], cot, table_ref, wf_ref, wo_ref
        )
        out = out.astype(BF16)

        @pl.when(step < short_tiles)
        def _():
            os_ref[...] = out

        @pl.when(step >= short_tiles)
        def _():
            ol_ref[...] = out

        g_mid_ref[...] = g_mid
        rows = rows_of(0, step)
        a2_ref[rows, :] = a2
        g_mlp_ref[rows, :] = g_mlp
        sums_ref[0:1, :] += colsum(g_a2 * n2)
        sums_ref[1:2, :] += colsum(g_a2)
        sums_ref[2:3, :] += colsum(g_mlp.astype(F32))
        for j in range(FF // D):
            act_ref[rows, j * D : (j + 1) * D] = acts[j]
            g_pre_ref[rows, j * D : (j + 1) * D] = g_pres[j]
            sums_ref[3 + j : 4 + j, :] += colsum(g_pres[j].astype(F32))

    for j in range(4):

        @pl.when(step == tiles + j)
        def _(j=j):
            res = dot_tn(act_ref[:, j * D : (j + 1) * D], g_mlp_ref[...])
            if slabs:
                dwo_ref[...] = res.astype(BF16).reshape(dwo_ref.shape)
            else:
                dwo_ref[...] = res

    for j in range(2 if slabs else 4):

        @pl.when(step == tiles + 4 + j)
        def _(j=j):
            if slabs:
                dev = D // 24
                left = dot_tn(a2_ref[...], g_pre_ref[:, 2 * j * D : (2 * j + 1) * D])
                right = dot_tn(a2_ref[...], g_pre_ref[:, (2 * j + 1) * D : (2 * j + 2) * D])
                both = jnp.concatenate(
                    [left.reshape(dev, 24, D), right.reshape(dev, 24, D)], axis=1
                )
                dwf_ref[...] = both.astype(BF16)
            else:
                dwf_ref[...] = dot_tn(a2_ref[...], g_pre_ref[:, j * D : (j + 1) * D])


def mlp_local(mid, cs, cl, table, w_fc, w_out, slabs):
    rows = mid.shape[0]
    ns, nl = cs.shape[0] // TILE, cl.shape[0] // TILE
    tiles = ns + nl
    steps = tiles + (6 if slabs else 8)
    whole = lambda shape: pl.BlockSpec(shape, lambda i: (0, 0), pipeline_mode=pl.Buffered(1))
    tile = lambda f: pl.BlockSpec((TILE, D), f)
    short_at = lambda i: (jnp.minimum(i, ns - 1), 0)
    long_at = lambda i: (jnp.clip(i - ns, 0, nl - 1), 0)
    all_at = lambda i: (jnp.minimum(i, tiles - 1), 0)
    if slabs:
        dev = D // 24
        dwo_shape = jax.ShapeDtypeStruct((dev, 96, D), BF16)
        dwo_spec = pl.BlockSpec((dev // 4, 96, D), lambda i: (jnp.clip(i - tiles, 0, 3), 0, 0))
        dwf_shape = jax.ShapeDtypeStruct((dev, 96, D), BF16)
        dwf_spec = pl.BlockSpec((dev, 48, D), lambda i: (0, jnp.clip(i - tiles - 4, 0, 1), 0))
    else:
        dwo_shape = jax.ShapeDtypeStruct((FF, D), F32)
        dwo_spec = pl.BlockSpec((D, D), lambda i: (jnp.clip(i - tiles, 0, 3), 0))
        dwf_shape = jax.ShapeDtypeStruct((D, FF), F32)
        dwf_spec = pl.BlockSpec((D, D), lambda i: (0, jnp.clip(i - tiles - 4, 0, 3)))
    return pl.pallas_call(
        functools.partial(mlp_kernel, (ns, nl), slabs),
        grid=(steps,),
        out_shape=(
            jax.ShapeDtypeStruct(cs.shape, BF16),
            jax.ShapeDtypeStruct(cl.shape, BF16),
            jax.ShapeDtypeStruct((rows, D), F32),
            jax.ShapeDtypeStruct((8, D), F32),
            dwf_shape,
            dwo_shape,
        ),
        in_specs=[
            tile(all_at),
            tile(short_at),
            tile(long_at),
            whole(table.shape),
            whole(w_fc.shape),
            whole(w_out.shape),
        ],
        out_specs=[
            tile(short_at),
            tile(long_at),
            tile(all_at),
            pl.BlockSpec((8, D), lambda i: (0, 0)),
            dwf_spec,
            dwo_spec,
        ],
        scratch_shapes=[
            pltpu.VMEM((rows, D), BF16),
            pltpu.VMEM((rows, D), BF16),
            pltpu.VMEM((rows, FF), BF16),
            pltpu.VMEM((rows, FF), BF16),
        ],
        compiler_params=pltpu.CompilerParams(vmem_limit_bytes=VMEM_LIMIT),
        name="mlp",
    )(mid, cs, cl, table, w_fc, w_out)


def inner_rows(g_att, att):
    prod = g_att.astype(F32) * att.astype(F32)
    high = prod.astype(BF16)
    rest = (prod - high.astype(F32)).astype(BF16)
    head = lax.broadcasted_iota(jnp.int32, (16, D), 0)
    lane = lax.broadcasted_iota(jnp.int32, (16, D), 1)
    pick = jnp.where((lane >= head * HEAD_DIM) & (lane < (head + 1) * HEAD_DIM), 1.0, 0.0).astype(BF16)
    return dot_nt(pick, high) + dot_nt(pick, rest)


def proj_back_tile(g_mid_ref, w_ref, att_ref, g_attn_ref, g_att_ref, inner_ref, sums_ref, t):
    rows = rows_of(0, t)
    g_attn = (BRANCH * g_mid_ref[rows, :]).astype(BF16)
    g_attn_ref[rows, :] = g_attn
    g_att = dot_nt(g_attn, w_ref[:, 3 * D : 4 * D]).astype(BF16)
    g_att_ref[rows, :] = g_att
    inner_ref[:, rows] = inner_rows(g_att, att_ref[rows, :])
    sums_ref[PROJB : PROJB + 1, :] += colsum(g_attn.astype(F32))


def attend_back_pair(
    split, qkv_ref, g_att_ref, lse_t_ref, inner_ref, g_qkv_ref, dk_ref, dv_ref, base, length, pair
):
    first = lax.broadcasted_iota(jnp.int32, (TILE, 128), 1) < HEAD_DIM
    k_t = jnp.transpose(qkv_ref[base : base + length, pair_cols(pair, 1)])
    for qb in range(length // TILE):
        start = qb * TILE
        qrows = slice(base + start, base + start + TILE)
        q_pair = qkv_ref[qrows, pair_cols(pair, 0)] * BF16(HEAD_DIM**-0.5)
        g_pair = g_att_ref[qrows, lanes_of(pair * 128)]
        q_pos = start + lax.broadcasted_iota(jnp.int32, (1, TILE), 1)
        low = jnp.where(q_pos >= split, split, 0)
        spans = []
        spans.append((0, start + TILE))
        halves = []
        for half in (0, 1):
            mine = first if half == 0 else ~first
            head = pl.ds(2 * pair + half, 1)
            halves.append(
                (
                    jnp.where(mine, q_pair, BF16(0)),
                    jnp.where(mine, g_pair, BF16(0)),
                    lse_t_ref[head, qrows],
                    inner_ref[head, qrows],
                )
            )
        dqs = [None, None]
        for lo, hi in spans:
            k_pos = lo + lax.broadcasted_iota(jnp.int32, (hi - lo, TILE), 0)
            visible = k_pos >= low
            if hi > start:
                visible = visible & (k_pos <= q_pos)
            keys = slice(base + lo, base + hi)
            k_pair = qkv_ref[keys, pair_cols(pair, 1)]
            v_pair = qkv_ref[keys, pair_cols(pair, 2)]
            dk = dv = None
            for half, (q_half, g_half, lse, inner) in enumerate(halves):
                s = jnp.where(visible, dot_nt(k_pair, q_half), NEG)
                p = jnp.exp(s - lse)
                ds = (p * (dot_nt(v_pair, g_half) - inner)).astype(BF16)
                part_v, part_k = dot(p.astype(BF16), g_half), dot(ds, q_half)
                dv = part_v if dv is None else dv + part_v
                dk = part_k if dk is None else dk + part_k
                part_q = dot(k_t[half * HEAD_DIM : (half + 1) * HEAD_DIM, lo:hi], ds)
                dqs[half] = part_q if dqs[half] is None else dqs[half] + part_q
            if qb:
                dk_ref[0:start, :] += dk[0:start]
                dv_ref[0:start, :] += dv[0:start]
            dk_ref[start:hi, :] = dk[start:hi]
            dv_ref[start:hi, :] = dv[start:hi]
        dq = jnp.transpose(jnp.concatenate(dqs, axis=0)) * (HEAD_DIM**-0.5)
        g_qkv_ref[qrows, pair_cols(pair, 0)] = dq.astype(BF16)
    all_rows = slice(base, base + length)
    g_qkv_ref[all_rows, pair_cols(pair, 1)] = dk_ref[0:length, :].astype(BF16)
    g_qkv_ref[all_rows, pair_cols(pair, 2)] = dv_ref[0:length, :].astype(BF16)


def ln1_back_tile(x_ref, g_mid_ref, table_ref, w_ref, g_qkv_ref, gx_ref, ln_sums_ref, base, t):
    rows = rows_of(base, t)
    g_qkv = g_qkv_ref[rows, :]
    g_a1 = dot_nt(g_qkv, w_ref[:, 0 : 3 * D])
    own = rows_of(0, t)
    n, rstd = normalize(x_ref[own, :].astype(F32))
    gx_ref[own, :] = g_mid_ref[rows, :] + norm_backward(
        g_a1, n, rstd, table_ref[LN1G : LN1G + 1, :]
    )
    ln_sums_ref[0:1, :] += colsum(g_a1 * n)
    ln_sums_ref[1:2, :] += colsum(g_a1)


def qv_sums(g_qkv_ref, sums_ref, g):
    for row, part in ((QB, 0), (VB, 2)):
        sums_ref[row : row + 1, vector_cols(g)] = colsum(g_qkv_ref[:, group_cols(g, part)].astype(F32))


def backward_kernel(
    ssplit,
    lsplit,
    xs,
    xl,
    table_ref,
    w_ref,
    a1_ref,
    qkv_ref,
    att_ref,
    lse_t_ref,
    g_mid_ref,
    gxs_ref,
    gxl_ref,
    dwp_ref,
    dwq_ref,
    sums_ref,
    g_attn_ref,
    g_att_ref,
    g_qkv_ref,
    inner_ref,
    dk_ref,
    dv_ref,
):
    sums_ref[...] = jnp.zeros_like(sums_ref)
    rows = xs.shape[0] + xl.shape[0]
    lax.fori_loop(
        0,
        rows // TILE,
        lambda t, c: (
            proj_back_tile(g_mid_ref, w_ref, att_ref, g_attn_ref, g_att_ref, inner_ref, sums_ref, t),
            c,
        )[1],
        0,
    )
    dwp_ref[...] = dot_tn(att_ref[...], g_attn_ref[...])

    def pair_step(pair, c):
        for split, x_ref, base in ((ssplit[0], xs, 0), (lsplit[0], xl, xs.shape[0])):
            attend_back_pair(
                split, qkv_ref, g_att_ref, lse_t_ref, inner_ref, g_qkv_ref, dk_ref, dv_ref, base, x_ref.shape[0], pair
            )
        return c

    lax.fori_loop(0, PAIRS, pair_step, 0)
    for g in range(GROUPS):
        qv_sums(g_qkv_ref, sums_ref, g)
    for j in range(3):
        dwq_ref[:, j * D : (j + 1) * D] = dot_tn(a1_ref[...], g_qkv_ref[:, j * D : (j + 1) * D])
    for x_ref, gx_ref, base in ((xs, gxs_ref, 0), (xl, gxl_ref, xs.shape[0])):
        lax.fori_loop(
            0,
            x_ref.shape[0] // TILE,
            lambda t, c: (
                ln1_back_tile(
                    x_ref, g_mid_ref, table_ref, w_ref, g_qkv_ref, gx_ref, sums_ref.at[LN1G : LN1B + 1], base, t
                ),
                c,
            )[1],
            0,
        )


def backward_local(ssplit, lsplit, xs, xl, table, w_attn, a1, qkv, att, lse_t, g_mid):
    rows = xs.shape[0] + xl.shape[0]
    return pl.pallas_call(
        backward_kernel,
        out_shape=(
            jax.ShapeDtypeStruct(xs.shape, F32),
            jax.ShapeDtypeStruct(xl.shape, F32),
            jax.ShapeDtypeStruct((D, D), F32),
            jax.ShapeDtypeStruct((D, 3 * D), F32),
            jax.ShapeDtypeStruct((8, D), F32),
        ),
        in_specs=[SM, SM] + [VM] * 9,
        out_specs=[VM] * 5,
        scratch_shapes=[
            pltpu.VMEM((rows, D), BF16),
            pltpu.VMEM((rows, D), BF16),
            pltpu.VMEM((rows, 3 * D), BF16),
            pltpu.VMEM((16, rows), F32),
            pltpu.VMEM((xl.shape[0], 128), F32),
            pltpu.VMEM((xl.shape[0], 128), F32),
        ],
        compiler_params=pltpu.CompilerParams(vmem_limit_bytes=VMEM_LIMIT),
        name="attention_backward",
    )(ssplit, lsplit, xs, xl, table, w_attn, a1, qkv, att, lse_t, g_mid)


MESH = pl.DeviceIdType.MESH
COLS, DEPTH = 4, 4


class Place:
    def __init__(self):
        q, f = lax.axis_index("dp"), lax.axis_index("fsdp")
        z = lax.div(f, 2)
        self.core = lax.rem(f, 2)
        self.col = [q, q + 1 - 2 * lax.rem(q, 2), lax.rem(q + 2, 4), 3 - q]
        self.depth = [lax.rem(z + k, DEPTH) for k in range(DEPTH)]
        self.index = q * 2 * DEPTH + f
        self.partner = (q, 2 * z + 1 - self.core)
        self.x = (self.col[1], f)
        self.y = (self.col[2], f)
        self.across = (self.col[3], f)
        self.over = [(q, 2 * d + 1 - self.core) for d in self.depth]
        self.along = [(q, 2 * d + self.core) for d in self.depth]

    def greet(self):
        barrier = pltpu.get_barrier_semaphore()
        others = [self.partner, self.x, self.y, self.across] + self.along[1:] + self.over[1:]
        for device in others:
            pl.semaphore_signal(barrier, inc=1, device_id=device, device_id_type=MESH)
        return lambda: pl.semaphore_wait(barrier, len(others))


def hooks(table):
    def run(i):
        for n, actions in table.items():

            @pl.when(i == n)
            def _():
                for action, *args in actions:
                    action(*args)

    return run


def remote(src, dst, send, recv, device):
    return pltpu.make_async_remote_copy(
        src_ref=src, dst_ref=dst, send_sem=send, recv_sem=recv, device_id=device, device_id_type=MESH
    )


def at(start, size, step):
    return pl.ds(pl.multiple_of(start, step), size)


Z, X, Y, VIA_X, VIA_Y, PAIR = 0, 3, 4, 5, 6, 7
N_GATHER = 11


class Gather:
    def __init__(self, place, spot, own, send, recv):
        self.place, self.own, self.send, self.recv = place, own, send, recv
        self.spot = spot

    def share(self, k):
        return self.spot(self.place.col[0], self.place.depth[k], 1, self.place.core)

    def column(self, r, z=0, n=DEPTH):
        return self.spot(self.place.col[r], z, n, self.place.core)

    def along(self, k, arriving=False):
        n = (k if arriving else DEPTH - k) - 1
        src, dst = (self.share(k),) * 2 if arriving else (self.own, self.share(0))
        return remote(src, dst, self.send.at[Z + k - 1], self.recv.at[Z + n], self.place.along[k])

    def near(self, kind, r):
        device = self.place.x if kind == X else self.place.y
        ref = self.column(r)
        return remote(ref, ref, self.send.at[kind], self.recv.at[kind], device)

    def across(self, kind, r):
        device, z = (self.place.x, DEPTH // 2) if kind == VIA_X else (self.place.y, 0)
        ref = self.column(r, z, DEPTH // 2)
        return remote(ref, ref, self.send.at[kind], self.recv.at[kind], device)

    def pair(self, r, arriving=False):
        core = 1 - self.place.core if arriving else self.place.core
        ref = self.spot(self.place.col[r], 0, DEPTH, core)
        return remote(ref, ref, self.send.at[PAIR + r], self.recv.at[PAIR + r], self.place.partner)

    def a(self):
        for k in (1, 3, 2):
            self.along(k).start()

    def b(self):
        for k in (1, 3, 2):
            self.along(k, True).wait_recv()
        self.near(X, 0).start()
        self.near(Y, 0).start()
        self.pair(0).start()

    def c(self):
        self.near(X, 1).wait_recv()
        self.across(VIA_Y, 1).start()
        self.pair(1).start()
        self.near(Y, 2).wait_recv()
        self.across(VIA_X, 2).start()
        self.pair(2).start()

    def d(self):
        self.across(VIA_Y, 3).wait_recv()
        self.across(VIA_X, 3).wait_recv()
        self.pair(3).start()

    def e(self):
        for r in range(COLS):
            self.pair(r, True).wait_recv()

    def end(self):
        for k in range(1, DEPTH):
            self.along(k).wait_send()
        self.near(X, 0).wait_send()
        self.near(Y, 0).wait_send()
        self.across(VIA_Y, 1).wait_send()
        self.across(VIA_X, 2).wait_send()
        for r in range(COLS):
            self.pair(r).wait_send()


def wide_spot(full, start, half):
    def spot(col, z, n, core):
        rows = at(col * (48 * DEPTH) + z * 48, 48 * n, 16)
        return full.at[rows, at(start + core * half, half, 128)]

    return spot


def tall_spot(full, start, size):
    def spot(col, z, n, core):
        return full.at[col, pl.ds(z, n), core, pl.ds(start, size)]

    return spot


def vector_parts(refs):
    parts = []
    for ref, row in zip(refs, (LN1G, LN1B, QB, PROJB, LN2G, LN2B, OUTB, FCB)):
        count = 2 if row == FCB else 1
        size = ref.shape[1] // count
        for n in range(count):
            parts.append((ref, n * size, size, row + n * (size * 32) // D))
    return parts


def place_vectors(place, vectors, out):
    lines = []
    for ref, lo, size, row in vector_parts(vectors):
        start = place.index * size
        at_row, at_lane = lax.div(start, D), lax.rem(start, D)
        lane = lax.broadcasted_iota(jnp.int32, (size, D), 1)
        pick = lax.broadcasted_iota(jnp.int32, (size, D), 0) + at_lane == lane
        values = dot(ref[:, lo : lo + size], jnp.where(pick, 1.0, 0.0).astype(BF16))
        rows = (size * 32) // D
        mine = lax.broadcasted_iota(jnp.int32, (rows, D), 0) == at_row
        lines.append(jnp.where(mine, values, 0.0))
    lines.append(jnp.zeros((4, D), F32))
    out[...] = jnp.concatenate(lines, axis=0).astype(out.dtype)


SUM_STEPS = 7
SUM_STAGES = ((0,), (1, 2, 3), (4, 5, 6))


class TableSum:
    def __init__(self, place, total, got, send, recv):
        self.place, self.total, self.got, self.send, self.recv = place, total, got, send, recv

    def copy(self, step, arriving=False):
        place = self.place
        if step == 0:
            device, n, stage = place.partner, 0, 0
        elif step <= 3:
            device, n, stage = place.along[step], (step if arriving else 4 - step), 1
        else:
            device, n, stage = (place.x, place.y, place.across)[step - 4], step, 2
        return remote(self.total.at[stage], self.got.at[n], self.send.at[step], self.recv.at[n], device)

    def begin(self, stage):
        for step in SUM_STAGES[stage]:
            self.copy(step).start()

    def add(self, stage):
        for step in SUM_STAGES[stage]:
            self.copy(step, True).wait_recv()
        total = self.total[stage]
        for step in SUM_STAGES[stage]:
            total = total + self.got[step]
        self.total[stage + 1] = total

    def next(self, stage):
        self.add(stage)
        self.begin(stage + 1)

    def end(self):
        for step in range(SUM_STEPS):
            self.copy(step).wait_send()


def forward_gather_kernel(
    ssplit,
    lsplit,
    xs_hbm,
    xl_hbm,
    wqkv,
    wproj,
    wfc,
    wout,
    v0,
    v1,
    v2,
    v3,
    v4,
    v5,
    v6,
    v7,
    table_ref,
    wa_hbm,
    wf_hbm,
    wo_hbm,
    slab_f1,
    a1_hbm,
    qkv_hbm,
    att_hbm,
    lse_t_ref,
    mid_hbm,
    xs,
    xl,
    wa,
    a1_ref,
    qkv_ref,
    att_ref,
    mid_ref,
    slab_f,
    swap_out,
    swap_in,
    total,
    got,
    io_sem,
    swap_send,
    swap_recv,
    sum_send,
    sum_recv,
    g_send,
    g_recv,
):
    place = Place()
    welcome = place.greet()
    loads = [pltpu.make_async_copy(xs_hbm, xs, io_sem.at[0]), pltpu.make_async_copy(xl_hbm, xl, io_sem.at[1])]
    for copy in loads:
        copy.start()
    part = D // 2
    first = place.core == 0
    swaps = [
        remote(swap_out.at[n], swap_in.at[n], swap_send.at[n], swap_recv.at[n], place.partner)
        for n in range(2)
    ]
    sums = TableSum(place, total, got, sum_send, sum_recv)

    def halves(share, step):
        starts = range(0, share.shape[1], 2 * step)
        lefts = jnp.concatenate([share[:, i : i + step] for i in starts], axis=1)
        rights = jnp.concatenate([share[:, i + step : i + 2 * step] for i in starts], axis=1)
        return jnp.where(first, lefts, rights), jnp.where(first, rights, lefts)

    cols = [wqkv[:, j * D + g * GROUP : j * D + (g + 1) * GROUP] for g in range(GROUPS) for j in range(3)]
    keep_a, swap_out[0] = halves(jnp.concatenate(cols + [wproj[...]], axis=1).astype(F32), part)
    welcome()
    swaps[0].start()
    place_vectors(place, (v0, v1, v2, v3, v4, v5, v6, v7), total.at[0])
    sums.begin(0)
    keep_f, swap_out[1] = halves(by_pieces(wfc[...].astype(F32)), D)
    swaps[1].start()
    sums.next(0)

    def joined(n, mine):
        swaps[n].wait_recv()
        other = swap_in[n]
        top, bottom = jnp.where(first, mine, other), jnp.where(first, other, mine)
        return jnp.concatenate([top, bottom], axis=0).astype(BF16)

    chip = place.col[0] * DEPTH + place.depth[0]
    rows = at(chip * 48, 48, 16)
    share = joined(0, keep_a)
    ps = []
    for n in range(4):
        cols = at(n * D + place.core * part, part, 128)
        wa[rows, cols] = share[:, n * part : (n + 1) * part]
        ps.append(Gather(place, wide_spot(wa, n * D, part), wa.at[rows, cols], g_send.at[n], g_recv.at[n]))
    ps.append(Gather(place, wide_spot(wf_hbm, 0, D), slab_f, g_send.at[4], g_recv.at[4]))
    ps.append(Gather(place, tall_spot(wo_hbm, 0, 48), wout.at[:, pl.ds(0, 48)], g_send.at[5], g_recv.at[5]))
    h0, h1, h2, pp, f0, o0 = ps
    for piece in ps[:4]:
        piece.a()
    share = joined(1, keep_f)
    slab_f[...] = share[:, 0:D]
    slab_f1[...] = share[:, D : 2 * D]
    for piece in ps[4:]:
        piece.a()
    own_copies = []
    for n, piece in enumerate((f0, o0)):
        copy = pltpu.make_async_copy(piece.own, piece.share(0), io_sem.at[2 + n])
        copy.start()
        own_copies.append(copy)
    sums.next(1)
    h0.b()
    sums.add(2)
    table_ref[...] = total[3].astype(F32)
    for copy in loads + own_copies:
        copy.wait()
    groups = group_refs(xs, xl)
    short_tiles, long_tiles = xs.shape[0] // TILE, xl.shape[0] // TILE
    loop(short_tiles, lambda t: norm_tile(xs, table_ref, a1_ref, 0, t))
    h0.c()
    h1.b()
    loop(2, lambda t: norm_tile(xl, table_ref, a1_ref, groups[1][1], t))
    h0.d()
    loop(long_tiles - 2, lambda t: norm_tile(xl, table_ref, a1_ref, groups[1][1], t + 2))
    h0.e()
    stores = [
        pltpu.make_async_copy(src, dst, io_sem.at[6 + n])
        for n, (src, dst) in enumerate(
            (
                (a1_ref, a1_hbm),
                (wa, wa_hbm),
                (qkv_ref, qkv_hbm),
                (att_ref, att_hbm),
                (mid_ref, mid_hbm),
            )
        )
    ]
    stores[0].start()
    lse_t_ref[...] = jnp.zeros_like(lse_t_ref)
    before_group = hooks({1: ((h1.e,),), 2: ((h2.e,),)})
    after_qkv = hooks({0: ((h1.c,), (h2.b,)), 1: ((o0.b,),)})
    after_short = hooks({0: ((pp.b,),), 1: ((f0.b,),), 3: ((pp.d,), (f0.c,)), 4: ((o0.c,),)})
    after_long = hooks(
        {
            0: ((h1.d,), (h2.c,)),
            1: ((pp.c,), (h2.d,)),
            4: ((f0.d,), (pp.e,)),
            5: ((o0.d,), (f0.e,)),
        }
    )

    def group_step(g):
        before_group(g)
        loop(a1_ref.shape[0] // TILE, lambda t: qkv_tile(table_ref, wa, a1_ref, qkv_ref, g, t))
        after_qkv(g)

        def pair_step(j):
            pair = 2 * g + j
            attend_pair(ssplit[0], qkv_ref, att_ref, lse_t_ref, 0, xs.shape[0], pair)
            after_short(pair)
            attend_pair(lsplit[0], qkv_ref, att_ref, lse_t_ref, xs.shape[0], xl.shape[0], pair)
            after_long(pair)

        loop(2, pair_step)

    loop(GROUPS, group_step)
    for copy in stores[1:4]:
        copy.start()
    for x_ref, base in groups:
        loop(
            x_ref.shape[0] // TILE,
            lambda t: mid_tile(x_ref, table_ref, wa, att_ref, mid_ref, base, t),
        )
    stores[4].start()
    o0.e()
    for swap in swaps:
        swap.wait_send()
    sums.end()
    for piece in ps:
        piece.end()
    for copy in stores:
        copy.wait()


ANY = pl.BlockSpec(memory_space=pl.ANY)


def forward_gather(ssplit, lsplit, xs, xl, wqkv, wproj, wfc, wout, vectors):
    rows = xs.shape[0] + xl.shape[0]
    wide = wqkv.shape[1] + wproj.shape[1]
    half_out = jax.ShapeDtypeStruct((COLS, DEPTH, 2) + SLAB, BF16)
    sem = pltpu.SemaphoreType.DMA
    return pl.pallas_call(
        forward_gather_kernel,
        out_shape=(
            jax.ShapeDtypeStruct((16, D), F32),
            jax.ShapeDtypeStruct((D, wide), BF16),
            jax.ShapeDtypeStruct((D, HALF), BF16),
            half_out,
            jax.ShapeDtypeStruct(SLAB, BF16),
            jax.ShapeDtypeStruct((rows, D), BF16),
            jax.ShapeDtypeStruct((rows, 3 * D), BF16),
            jax.ShapeDtypeStruct((rows, D), BF16),
            jax.ShapeDtypeStruct((16, rows), F32),
            jax.ShapeDtypeStruct((rows, D), F32),
        ),
        in_specs=[SM, SM, ANY, ANY] + [VM] * 12,
        out_specs=[VM, ANY, ANY, ANY, VM, ANY, ANY, ANY, VM, ANY],
        scratch_shapes=[
            pltpu.VMEM(xs.shape, BF16),
            pltpu.VMEM(xl.shape, BF16),
            pltpu.VMEM((D, wide), BF16),
            pltpu.VMEM((rows, D), BF16),
            pltpu.VMEM((rows, 3 * D), BF16),
            pltpu.VMEM((rows, D), BF16),
            pltpu.VMEM((rows, D), F32),
            pltpu.VMEM(SLAB, BF16),
            pltpu.VMEM((2, 24, wide // 2), F32),
            pltpu.VMEM((2, 24, wide // 2), F32),
            pltpu.VMEM((4, 16, D), BF16),
            pltpu.VMEM((SUM_STEPS, 16, D), BF16),
            sem((11,)),
            sem((2,)),
            sem((2,)),
            sem((SUM_STEPS,)),
            sem((SUM_STEPS,)),
            sem((6, N_GATHER)),
            sem((6, N_GATHER)),
        ],
        compiler_params=pltpu.CompilerParams(
            vmem_limit_bytes=VMEM_LIMIT, collective_id=0, has_side_effects=True
        ),
        name="attention_forward_gather",
    )(ssplit, lsplit, xs, xl, wqkv, wproj, wfc, wout[None], *[v.reshape(1, -1) for v in vectors])


R_PAIR, R_X, R_Y, R_XB, R_YB, R_Z = 0, 4, 6, 8, 9, 10
N_REDUCE = 13
ORDER = (3, 1, 2, 0)


class Reduce:
    def __init__(self, place, src, own, total, xa, ya, xb, yb, zr, send, recv, own_sem):
        self.place, self.src, self.own, self.total = place, src, own, total
        self.xa, self.ya, self.xb, self.yb, self.zr = xa, ya, xb, yb, zr
        self.send, self.recv, self.own_sem = send, recv, own_sem

    def slabs(self, r, core):
        return self.src.at[pl.ds(self.place.col[r] * DEPTH, DEPTH), core]

    def pair(self, r):
        place = self.place
        n = R_PAIR + r
        return remote(
            self.slabs(r, 1 - place.core), self.total.at[r], self.send.at[n], self.recv.at[n], place.partner
        )

    def load(self, r):
        slot = ORDER.index(r) % 2
        return pltpu.make_async_copy(self.slabs(r, self.place.core), self.own.at[slot], self.own_sem.at[r])

    def to_x(self, n):
        src = self.total.at[(1, 3)[n], pl.ds(0, 2)]
        return remote(src, self.xa.at[n], self.send.at[R_X + n], self.recv.at[R_X + n], self.place.x)

    def to_y(self, n):
        src = self.total.at[(2, 3)[n], pl.ds(2, 2)]
        return remote(src, self.ya.at[n], self.send.at[R_Y + n], self.recv.at[R_Y + n], self.place.y)

    def to_xb(self):
        src = self.total.at[1, pl.ds(2, 2)]
        return remote(src, self.xb, self.send.at[R_XB], self.recv.at[R_XB], self.place.x)

    def to_yb(self):
        src = self.total.at[2, pl.ds(0, 2)]
        return remote(src, self.yb, self.send.at[R_YB], self.recv.at[R_YB], self.place.y)

    def to_z(self, k, arriving=False):
        n = (k if arriving else DEPTH - k) - 1
        src = self.total.at[0, self.place.depth[k]]
        return remote(
            src, self.zr.at[n], self.send.at[R_Z + k - 1], self.recv.at[R_Z + n], self.place.along[k]
        )

    def begin(self, loads=True):
        for r in ORDER:
            self.pair(r).start()
        if loads:
            self.begin_loads()

    def begin_loads(self):
        if self.own is not None:
            for r in ORDER[:2]:
                self.load(r).start()

    def chip(self, r):
        if self.own is not None:
            self.load(r).wait()
            mine = self.own[ORDER.index(r) % 2]
        else:
            mine = self.src[pl.ds(self.place.col[r] * DEPTH, DEPTH), self.place.core]
        self.pair(r).wait_recv()
        self.total[r] = self.total[r] + mine
        if self.own is not None and ORDER.index(r) < 2:
            self.load(ORDER[ORDER.index(r) + 2]).start()
        if r == 1:
            self.to_x(1).start()
            self.to_x(0).start()
        if r == 2:
            self.to_y(1).start()
            self.to_y(0).start()

    def chip_all(self):
        for r in ORDER:
            self.chip(r)

    def cross(self):
        self.to_x(1).wait_recv()
        self.total[2, 0:2] = self.total[2, 0:2] + self.xa[1]
        self.to_yb().start()
        self.to_y(1).wait_recv()
        self.total[1, 2:4] = self.total[1, 2:4] + self.ya[1]
        self.to_xb().start()

    def column(self):
        self.to_x(0).wait_recv()
        self.to_yb().wait_recv()
        add = lambda a, b, c: (a.astype(F32) + b.astype(F32) + c.astype(F32)).astype(BF16)
        self.total[0, 0:2] = add(self.total[0, 0:2], self.xa[0], self.yb[...])
        self.to_y(0).wait_recv()
        self.to_xb().wait_recv()
        self.total[0, 2:4] = add(self.total[0, 2:4], self.ya[0], self.xb[...])
        for k in (2, 1, 3):
            self.to_z(k).start()

    def result(self):
        out = self.total[0, self.place.depth[0]].astype(F32)
        for k in range(1, DEPTH):
            self.to_z(k, True).wait_recv()
            out = out + self.zr[k - 1].astype(F32)
        return out

    def end(self):
        self.end_pairs()
        self.end_rest()

    def end_pairs(self):
        for r in range(COLS):
            self.pair(r).wait_send()

    def end_rest(self):
        for n in range(2):
            self.to_x(n).wait_send()
            self.to_y(n).wait_send()
        self.to_xb().wait_send()
        self.to_yb().wait_send()
        for k in range(1, DEPTH):
            self.to_z(k).wait_send()


class LastSum:
    def __init__(self, place, total, got, send, recv):
        self.place, self.total, self.got, self.send, self.recv = place, total, got, send, recv

    def copy(self, n, arriving=False):
        place = self.place
        if n < 3:
            device, m = place.along[n + 1], (n if arriving else 2 - n)
        elif n < 6:
            device, m = place.over[n - 2], (n if arriving else 8 - n)
        else:
            device, m = (place.partner, place.x, place.y, place.across)[n - 6], n
        stage = 0 if n < 7 else 1
        return remote(self.total.at[stage], self.got.at[m], self.send.at[n], self.recv.at[m], device)

    def run(self):
        for stage, steps in enumerate((range(7), range(7, 10))):
            for n in steps:
                self.copy(n).start()
            total = self.total[stage]
            for n in steps:
                self.copy(n, True).wait_recv()
                total = total + self.got[n]
            self.total[stage + 1] = total
        for n in range(10):
            self.copy(n).wait_send()


def take_vectors(place, table, outs):
    for ref, lo, size, row in vector_parts(outs):
        rows = (size * 32) // D
        start = place.index * size
        at_row, at_lane = lax.div(start, D), lax.rem(start, D)
        mine = lax.broadcasted_iota(jnp.int32, (rows, D), 0) == at_row
        line = jnp.sum(jnp.where(mine, table[row : row + rows, :], 0.0), axis=0, keepdims=True)
        lane = lax.broadcasted_iota(jnp.int32, (size, D), 1)
        pick = lax.broadcasted_iota(jnp.int32, (size, D), 0) + at_lane == lane
        ref[:, lo : lo + size] = lax.dot_general(
            line,
            jnp.where(pick, 1.0, 0.0),
            (((1,), (1,)), ((), ())),
            preferred_element_type=F32,
            precision=lax.Precision.HIGHEST,
        )


def small_slabs(whole):
    devices, half = 2 * COLS * DEPTH, D // 2
    left = whole[:, 0:half].reshape(devices, 24, half)
    right = whole[:, half:D].reshape(devices, 24, half)
    both = jnp.concatenate([left, right], axis=1).astype(BF16)
    return both.reshape(COLS * DEPTH, 2, 48, half)


HALF = FF // 2
SLAB = (48, D)


def by_pieces(w):
    size = w.shape[1] // 64
    cuts = [w[:, (2 * i + n) * size : (2 * i + n + 1) * size] for n in range(2) for i in range(32)]
    return jnp.concatenate(cuts, axis=1)


def from_pieces(first, second):
    size = first.shape[1] // 32
    cuts = [w[:, i * size : (i + 1) * size] for i in range(32) for w in (first, second)]
    return jnp.concatenate(cuts, axis=1)


def mlp_half_tile(n, t, refs):
    mid_ref, cot_ref, a2_ref, g_mlp_ref, act_ref, g_pre_ref, acc_ref, acc_g_ref, wf, wo, table_ref, sums_ref = refs
    rows = rows_of(0, t)
    gain = table_ref[LN2G : LN2G + 1, :]
    if n == 0:
        n2, _ = normalize(mid_ref[rows, :])
        a2 = (n2 * gain + table_ref[LN2B : LN2B + 1, :]).astype(BF16)
        g_mlp = (BRANCH * cot_ref[rows, :].astype(F32)).astype(BF16)
        a2_ref[rows, :] = a2
        g_mlp_ref[rows, :] = g_mlp
        sums_ref[2:3, :] += colsum(g_mlp.astype(F32))
    else:
        a2 = a2_ref[rows, :]
        g_mlp = g_mlp_ref[rows, :]
    out = None
    g_a2 = None
    for j in range(HALF // D):
        cols = slice(j * D, (j + 1) * D)
        row = 2 * n + j
        wf_j = wf[n, :, cols]
        wo_j = wo[n, 2 * j : 2 * j + 2].reshape(D, D)
        pre = dot(a2, wf_j) + table_ref[FCB + row : FCB + row + 1, :]
        g_act = dot_nt(g_mlp, wo_j)
        square = pre * pre
        th = jnp.tanh(pre * (GELU_A + (GELU_A * GELU_B) * square))
        half = 0.5 + 0.5 * th
        act = (pre * half).astype(BF16)
        slope = half + pre * (0.5 - 0.5 * th * th) * (GELU_A + (3 * GELU_A * GELU_B) * square)
        g_pre = (g_act * slope).astype(BF16)
        act_ref[rows, cols] = act
        g_pre_ref[rows, cols] = g_pre
        sums_ref[3 + row : 4 + row, :] += colsum(g_pre.astype(F32))
        part, part_g = dot(act, wo_j), dot_nt(g_pre, wf_j)
        out = part if out is None else out + part
        g_a2 = part_g if g_a2 is None else g_a2 + part_g
    if n == 0:
        acc_ref[rows, :] = out
        acc_g_ref[rows, :] = g_a2
        return
    out = acc_ref[rows, :] + out
    g_a2 = acc_g_ref[rows, :] + g_a2
    mid = mid_ref[rows, :]
    n2, rstd = normalize(mid)
    g_out = cot_ref[rows, :].astype(F32)
    cot_ref[rows, :] = (mid + BRANCH * (out + table_ref[OUTB : OUTB + 1, :])).astype(BF16)
    mid_ref[rows, :] = g_out + norm_backward(g_a2, n2, rstd, gain)
    sums_ref[0:1, :] += colsum(g_a2 * n2)
    sums_ref[1:2, :] += colsum(g_a2)


def out_slabs(act_ref, g_mlp_ref, dw_o):
    for j in range(HALF // D):
        res = dot_tn(act_ref[:, j * D : (j + 1) * D], g_mlp_ref[...])
        dw_o[8 * j : 8 * j + 8] = res.astype(BF16).reshape(8, 2, *SLAB)


def fc_slabs(a2_ref, g_pre_ref, dw_f):
    left = dot_tn(a2_ref[...], g_pre_ref[:, 0:D]).reshape(32, 24, D)
    right = dot_tn(a2_ref[...], g_pre_ref[:, D : 2 * D]).reshape(32, 24, D)
    dw_f[...] = jnp.concatenate([left, right], axis=1).astype(BF16).reshape(dw_f.shape)


def mlp_exchange_kernel(
    mid_hbm,
    cs_hbm,
    cl_hbm,
    table_ref,
    wf0_hbm,
    wo0_hbm,
    slab_f,
    wout,
    os_hbm,
    ol_hbm,
    g_mid_hbm,
    sums_ref,
    d_out0,
    d_fc0,
    so_hbm,
    sf_hbm,
    mid_ref,
    cot_ref,
    a2_ref,
    g_mlp_ref,
    act_ref,
    g_pre_ref,
    acc_ref,
    acc_g_ref,
    wf,
    wo,
    dw_o,
    dw_f,
    r_total,
    r_xa,
    r_ya,
    r_xb,
    r_yb,
    r_zr,
    io_sem,
    g_send,
    g_recv,
    r_send,
    r_recv,
):
    place = Place()
    welcome = place.greet()
    short, long = cs_hbm.shape[0], cl_hbm.shape[0]
    tiles = (short + long) // TILE
    parts = (pl.ds(0, short), pl.ds(short, long))
    pairs = (
        (mid_hbm, mid_ref),
        (cs_hbm, cot_ref.at[parts[0]]),
        (cl_hbm, cot_ref.at[parts[1]]),
        (wf0_hbm, wf.at[0]),
        (wo0_hbm, wo.at[0]),
    )
    loads = [pltpu.make_async_copy(src, dst, io_sem.at[n]) for n, (src, dst) in enumerate(pairs)]
    for copy in loads:
        copy.start()
    q, z, c = place.col[0], place.depth[0], place.core
    wf[1, at((q * DEPTH + z) * 48, 48, 16), at(c * D, D, 128)] = slab_f[...]
    wo[1, q, z, c] = wout[0, 48:96]
    f1 = Gather(place, wide_spot(wf.at[1], 0, D), slab_f, g_send.at[0], g_recv.at[0])
    o1 = Gather(place, tall_spot(wo.at[1], 0, 48), wout.at[:, pl.ds(48, 48)], g_send.at[1], g_recv.at[1])
    ro, rf = [
        Reduce(
            place, src, None, r_total.at[n], r_xa.at[n], r_ya.at[n], r_xb.at[n], r_yb.at[n],
            r_zr.at[n], r_send.at[n], r_recv.at[n], None,
        )
        for n, src in enumerate((dw_o, dw_f))
    ]
    sums_ref[...] = jnp.zeros_like(sums_ref)
    welcome()
    f1.a()
    o1.a()
    for copy in loads:
        copy.wait()
    refs = (
        mid_ref, cot_ref, a2_ref, g_mlp_ref, act_ref, g_pre_ref, acc_ref, acc_g_ref, wf, wo, table_ref, sums_ref,
    )
    after = hooks({2: ((f1.b,),), 3: ((o1.b,),), 4: ((f1.c,),)})

    def first_step(t):
        mlp_half_tile(0, t, refs)
        after(t)

    loop(tiles, first_step)
    out_slabs(act_ref, g_mlp_ref, dw_o)
    ro.begin()
    o1.c()
    fc_slabs(a2_ref, g_pre_ref, dw_f)
    rf.begin()
    ro.chip_all()
    f1.d()
    o1.d()
    f1.e()
    o1.e()

    def give_out():
        d_out0[...] = ro.result()

    after_second = hooks(
        {
            0: ((ro.cross,), (rf.chip_all,)),
            2: ((ro.column,),),
            3: ((rf.cross,),),
            5: ((rf.column,), (give_out,)),
        }
    )

    def second_step(t):
        mlp_half_tile(1, t, refs)
        after_second(t)

    loop(tiles, second_step)
    stores = [
        pltpu.make_async_copy(src, dst, io_sem.at[5 + n])
        for n, (src, dst) in enumerate(
            (
                (cot_ref.at[parts[0]], os_hbm),
                (cot_ref.at[parts[1]], ol_hbm),
                (mid_ref, g_mid_hbm),
                (dw_o, so_hbm),
                (dw_f, sf_hbm),
            )
        )
    ]
    for copy in stores[0:3]:
        copy.start()
    ro.end_pairs()
    out_slabs(act_ref, g_mlp_ref, dw_o)
    stores[3].start()
    rf.end_pairs()
    fc_slabs(a2_ref, g_pre_ref, dw_f)
    stores[4].start()
    res = rf.result()
    d_fc0[...] = jnp.concatenate([res[0:24], res[24:48]], axis=1)
    ro.end_rest()
    rf.end_rest()
    f1.end()
    o1.end()
    for copy in stores:
        copy.wait()


def reduce_buffers(n, shape):
    return [
        pltpu.VMEM((n, COLS, DEPTH) + shape, BF16),
        pltpu.VMEM((n, 2, 2) + shape, BF16),
        pltpu.VMEM((n, 2, 2) + shape, BF16),
        pltpu.VMEM((n, 2) + shape, BF16),
        pltpu.VMEM((n, 2) + shape, BF16),
        pltpu.VMEM((n, DEPTH - 1) + shape, BF16),
    ]


def mlp_exchange(mid, cs, cl, table, wf0, wo0, slab_f, wout):
    rows = mid.shape[0]
    chips = COLS * DEPTH
    sem = pltpu.SemaphoreType.DMA
    slabs = (chips, 2) + SLAB
    return pl.pallas_call(
        mlp_exchange_kernel,
        out_shape=(
            jax.ShapeDtypeStruct(cs.shape, BF16),
            jax.ShapeDtypeStruct(cl.shape, BF16),
            jax.ShapeDtypeStruct(mid.shape, F32),
            jax.ShapeDtypeStruct((8, D), F32),
            jax.ShapeDtypeStruct(SLAB, F32),
            jax.ShapeDtypeStruct((24, HALF), F32),
            jax.ShapeDtypeStruct(slabs, BF16),
            jax.ShapeDtypeStruct(slabs, BF16),
        ),
        in_specs=[ANY, ANY, ANY, VM, ANY, ANY, VM, VM],
        out_specs=[ANY, ANY, ANY, VM, VM, VM, ANY, ANY],
        scratch_shapes=[
            pltpu.VMEM((rows, D), F32),
            pltpu.VMEM((rows, D), BF16),
            pltpu.VMEM((rows, D), BF16),
            pltpu.VMEM((rows, D), BF16),
            pltpu.VMEM((rows, HALF), BF16),
            pltpu.VMEM((rows, HALF), BF16),
            pltpu.VMEM((rows, D), F32),
            pltpu.VMEM((rows, D), F32),
            pltpu.VMEM((2, D, HALF), BF16),
            pltpu.VMEM((2, COLS, DEPTH, 2) + SLAB, BF16),
            pltpu.VMEM(slabs, BF16),
            pltpu.VMEM(slabs, BF16),
            *reduce_buffers(2, SLAB),
            sem((10,)),
            sem((2, N_GATHER)),
            sem((2, N_GATHER)),
            sem((2, N_REDUCE)),
            sem((2, N_REDUCE)),
        ],
        compiler_params=pltpu.CompilerParams(
            vmem_limit_bytes=VMEM_LIMIT, collective_id=2, has_side_effects=True
        ),
        name="mlp_exchange",
    )(mid, cs, cl, table, wf0, wo0, slab_f, wout)


def backward_reduce_kernel(
    ssplit,
    lsplit,
    xs_hbm,
    xl_hbm,
    table_ref,
    wa_hbm,
    a1_hbm,
    qkv_hbm,
    att_hbm,
    lse_t_ref,
    g_mid_hbm,
    sums2_ref,
    go_hbm,
    gf_hbm,
    gxs_hbm,
    gxl_hbm,
    d0,
    d1,
    d2,
    d3,
    d4,
    d5,
    d6,
    d7,
    d_qkv,
    d_proj,
    d_fc1,
    d_out1,
    wa,
    a1_ref,
    qkv_ref,
    att_ref,
    g_mid_ref,
    g_att_ref,
    g_qkv_ref,
    inner_ref,
    dk_ref,
    dv_ref,
    big_own,
    big_total,
    big_xa,
    big_ya,
    big_xb,
    big_yb,
    big_zr,
    small_src,
    small_total,
    small_xa,
    small_ya,
    small_xb,
    small_yb,
    small_zr,
    total,
    got,
    io_sem,
    own_sem,
    r_send,
    r_recv,
    sum_send,
    sum_recv,
    ln_sums_ref,
    last_total,
    last_got,
    last_send,
    last_recv,
):
    place = Place()
    g_attn_ref = g_qkv_ref.at[:, pl.ds(0, D)]
    short, long = gxs_hbm.shape[0], gxl_hbm.shape[0]
    rows = short + long
    proj_cols = pl.ds(3 * D, D)
    qkv_cols = pl.ds(0, 3 * D)
    loads = [
        pltpu.make_async_copy(src, dst, io_sem.at[n])
        for n, (src, dst) in enumerate(
            (
                (wa_hbm.at[:, proj_cols], wa.at[:, proj_cols]),
                (g_mid_hbm, g_mid_ref),
                (att_hbm, att_ref),
                (qkv_hbm, qkv_ref),
                (a1_hbm, a1_ref),
                (wa_hbm.at[:, qkv_cols], wa.at[:, qkv_cols]),
            )
        )
    ]
    for copy in loads:
        copy.start()
    sums = TableSum(place, total, got, sum_send, sum_recv)
    sums_ref = total.at[0]
    sums_ref[...] = jnp.zeros_like(sums_ref)
    sums_ref[LN2G : LN2G + 7, :] = sums2_ref[0:7, :]
    big = [
        Reduce(
            place, src, big_own, big_total.at[n], big_xa.at[n], big_ya.at[n], big_xb.at[n],
            big_yb.at[n], big_zr.at[n], r_send.at[n], r_recv.at[n], own_sem.at[n],
        )
        for n, src in enumerate((go_hbm, gf_hbm))
    ]
    small = [
        Reduce(
            place, small_src.at[n], None, small_total.at[n], small_xa.at[n], small_ya.at[n], small_xb.at[n],
            small_yb.at[n], small_zr.at[n], r_send.at[2 + n], r_recv.at[2 + n], None,
        )
        for n in range(4)
    ]
    ro, rf = big
    rp, rh = small[3], small[0:3]
    place.greet()()
    ro.begin()
    rf.begin(False)
    last_total[...] = jnp.zeros_like(last_total)
    for copy in loads[0:3]:
        copy.wait()

    after = hooks(
        {
            0: ((ro.chip, 3),),
            1: ((ro.chip, 1),),
            2: ((ro.chip, 2),),
            3: ((ro.chip, 0), (rf.begin_loads,)),
            4: ((rf.chip, 3),),
            5: ((rf.chip, 1), (rf.chip, 2), (rf.chip, 0)),
        }
    )

    def proj_step(t):
        proj_back_tile(g_mid_ref, wa, att_ref, g_attn_ref, g_att_ref, inner_ref, sums_ref, t)
        after(t)

    loop(rows // TILE, proj_step)
    small_src[3] = small_slabs(dot_tn(att_ref[...], g_attn_ref[...]))
    rp.begin()
    x_loads = [
        pltpu.make_async_copy(xs_hbm, att_ref.at[pl.ds(0, short)], io_sem.at[6]),
        pltpu.make_async_copy(xl_hbm, att_ref.at[pl.ds(short, long)], io_sem.at[7]),
    ]
    for copy in x_loads:
        copy.start()
    for copy in loads[3:]:
        copy.wait()

    def give_out():
        d_out1[...] = ro.result()

    def give_fc():
        res = rf.result()
        d_fc1[...] = jnp.concatenate([res[0:24], res[24:48]], axis=1)

    def give_proj():
        res = rp.result()
        d_proj[:, 0 : D // 2] = res[0:24]
        d_proj[:, D // 2 : D] = res[24:48]

    def give_qkv(g):
        res = rh[g].result()
        line = jnp.concatenate([res[0:24], res[24:48]], axis=1)
        for j in range(3):
            d_qkv[:, j * D + g * 256 : j * D + g * 256 + 256] = line[:, j * 256 : j * 256 + 256]

    def heads_begin(g):
        rh[g].begin()

    after_short = hooks(
        {
            0: ((ro.cross,),),
            2: ((rh[0].chip_all,), (rf.column,), (rp.cross,)),
            3: ((rp.column,), (give_out,)),
            4: ((rh[1].chip_all,),),
            5: ((give_qkv, 0),),
        }
    )
    after_long = hooks(
        {
            0: ((rf.cross,), (rp.chip_all,)),
            1: ((heads_begin, 0), (ro.column,)),
            2: ((rh[0].cross,),),
            3: ((heads_begin, 1), (rh[0].column,), (give_fc,)),
            4: ((rh[1].cross,), (give_proj,)),
            5: ((heads_begin, 2), (sums.begin, 0), (rh[1].column,)),
        }
    )

    def pair_step(pair):
        attend_back_pair(
            ssplit[0], qkv_ref, g_att_ref, lse_t_ref, inner_ref, g_qkv_ref, dk_ref, dv_ref, 0, short, pair
        )
        after_short(pair)
        attend_back_pair(
            lsplit[0], qkv_ref, g_att_ref, lse_t_ref, inner_ref, g_qkv_ref, dk_ref, dv_ref, short, long, pair
        )

        @pl.when(lax.rem(pair, 2) == 1)
        def _():
            g = lax.div(pair, 2)
            cols = pl.ds(pl.multiple_of(g * D, 128), D)
            small_src[g] = small_slabs(dot_tn(a1_ref[...], g_qkv_ref[:, cols]))
            qv_sums(g_qkv_ref, sums_ref, g)

        after_long(pair)

    loop(PAIRS, pair_step)
    for copy in x_loads:
        copy.wait()
    after_norm = hooks(
        {
            0: ((rh[2].chip_all,), (sums.next, 0)),
            2: ((rh[2].cross,), (sums.next, 1)),
            3: ((give_qkv, 1),),
            4: ((rh[2].column,), (sums.add, 2)),
        }
    )

    def norm_step(t):
        ln1_back_tile(att_ref, g_mid_ref, table_ref, wa, g_qkv_ref, g_mid_ref, ln_sums_ref, 0, t)
        after_norm(t)

    ln_sums_ref[...] = jnp.zeros_like(ln_sums_ref)
    loop(short // TILE, norm_step)
    stores = [
        pltpu.make_async_copy(g_mid_ref.at[pl.ds(0, short)], gxs_hbm, io_sem.at[8]),
        pltpu.make_async_copy(g_mid_ref.at[pl.ds(short, long)], gxl_hbm, io_sem.at[9]),
    ]
    stores[0].start()
    loop(long // TILE, lambda t: norm_step(t + short // TILE))
    stores[1].start()
    lanes = D // 128
    lines = [ln_sums_ref[r : r + 1, 128 * j : 128 * j + 128] for r in range(2) for j in range(lanes)]
    last_total[0, 0 : 2 * lanes] = jnp.concatenate(lines, axis=0)
    last = LastSum(place, last_total, last_got, last_send, last_recv)
    last.run()
    give_qkv(2)
    final = total.at[3]
    for r in range(2):
        final[r : r + 1, :] = jnp.concatenate(
            [last_total[2, r * lanes + j : r * lanes + j + 1, :] for j in range(lanes)], axis=1
        )
    take_vectors(place, final, (d0, d1, d2, d3, d4, d5, d6, d7))
    sums.end()
    for reduce in big + small:
        reduce.end()
    for copy in stores:
        copy.wait()


def backward_reduce(ssplit, lsplit, xs, xl, table, w_attn, a1, qkv, att, lse_t, g_mid, sums2, dwo, dwf, sizes):
    short, long = xs.shape[0], xl.shape[0]
    rows = short + long
    chips = COLS * DEPTH
    devices = 2 * chips
    big, little = SLAB, (48, D // 2)
    sem = pltpu.SemaphoreType.DMA
    return pl.pallas_call(
        backward_reduce_kernel,
        out_shape=(
            jax.ShapeDtypeStruct(xs.shape, F32),
            jax.ShapeDtypeStruct(xl.shape, F32),
            *[jax.ShapeDtypeStruct((1, n), F32) for n in sizes],
            jax.ShapeDtypeStruct((D // devices, 3 * D), F32),
            jax.ShapeDtypeStruct((D // devices, D), F32),
            jax.ShapeDtypeStruct((D // devices, HALF), F32),
            jax.ShapeDtypeStruct(SLAB, F32),
        ),
        in_specs=[SM, SM, ANY, ANY, VM, ANY, ANY, ANY, ANY, VM, ANY, VM, ANY, ANY],
        out_specs=[ANY, ANY] + [VM] * 12,
        scratch_shapes=[
            pltpu.VMEM((D, 4 * D), BF16),
            pltpu.VMEM((rows, D), BF16),
            pltpu.VMEM((rows, 3 * D), BF16),
            pltpu.VMEM((rows, D), BF16),
            pltpu.VMEM((rows, D), F32),
            pltpu.VMEM((rows, D), BF16),
            pltpu.VMEM((rows, 3 * D), BF16),
            pltpu.VMEM((16, rows), F32),
            pltpu.VMEM((long, 128), F32),
            pltpu.VMEM((long, 128), F32),
            pltpu.VMEM((2, DEPTH) + big, BF16),
            *reduce_buffers(2, big),
            pltpu.VMEM((4, chips, 2) + little, BF16),
            *reduce_buffers(4, little),
            pltpu.VMEM((4, 16, D), F32),
            pltpu.VMEM((SUM_STEPS, 16, D), F32),
            sem((10,)),
            sem((2, COLS)),
            sem((6, N_REDUCE)),
            sem((6, N_REDUCE)),
            sem((SUM_STEPS,)),
            sem((SUM_STEPS,)),
            pltpu.VMEM((8, D), F32),
            pltpu.VMEM((3, 16, 128), F32),
            pltpu.VMEM((10, 16, 128), F32),
            sem((10,)),
            sem((10,)),
        ],
        compiler_params=pltpu.CompilerParams(
            vmem_limit_bytes=BACK_VMEM, collective_id=1, has_side_effects=True
        ),
        name="attention_backward_reduce",
    )(ssplit, lsplit, xs, xl, table, w_attn, a1, qkv, att, lse_t, g_mid, sums2, dwo, dwf)


BACK_VMEM = 60 * 2**20


PARTS = 4


def hand_over_kernel(os_hbm, ol_hbm, gs_hbm, gl_hbm, *refs):
    small_in, outs = refs[:14], refs[14:30]
    buffers, load_sem, store_sem = refs[30:34], refs[34], refs[35]
    loads, stores = [], []
    for n, (src, dst, mid) in enumerate(zip((os_hbm, ol_hbm, gs_hbm, gl_hbm), outs[:4], buffers)):
        size = src.shape[0] // PARTS
        for p in range(PARTS):
            rows = pl.ds(p * size, size)
            loads.append(pltpu.make_async_copy(src.at[rows], mid.at[rows], load_sem.at[n, p]))
            stores.append(pltpu.make_async_copy(mid.at[rows], dst.at[rows], store_sem.at[n, p]))
    for copy in loads:
        copy.start()
    for n in range(10):
        outs[4 + n][...] = small_in[n][...]
    fc0, fc1, out0, out1 = small_in[10:]
    outs[14][...] = from_pieces(fc0[...], fc1[...])
    outs[15][0:48, :] = out0[...]
    outs[15][48:96, :] = out1[...]
    for load, store in zip(loads, stores):
        load.wait()
        store.start()
    for copy in stores:
        copy.wait()


def hand_over(big, small):
    shape = lambda a: jax.ShapeDtypeStruct(a.shape, a.dtype)
    sem = pltpu.SemaphoreType.DMA
    return pl.pallas_call(
        hand_over_kernel,
        out_shape=(
            *map(shape, big),
            *map(shape, small[:10]),
            jax.ShapeDtypeStruct((24, FF), F32),
            jax.ShapeDtypeStruct((96, D), F32),
        ),
        in_specs=[ANY] * 4 + [VM] * 14,
        out_specs=[ANY] * 4 + [VM] * 12,
        scratch_shapes=[pltpu.VMEM(a.shape, a.dtype) for a in big] + [sem((4, PARTS))] * 2,
        compiler_params=pltpu.CompilerParams(vmem_limit_bytes=VMEM_LIMIT),
        name="hand_over",
    )(*big, *small)


AXES = ("dp", "fsdp")


def gather(x, axis=0):
    return lax.all_gather(x, AXES, axis=axis, tiled=True)


def scatter(x):
    return lax.psum_scatter(x, AXES, scatter_dimension=0, tiled=True)


def general(args, devices):
    (st, lt, ss, ls, ln1g, ln1b, wqkv, qvb, wproj, projb, ln2g, ln2b, wfc, fcb, wout, outb, sc, lc) = args
    xs, xl = st.reshape(-1, D), lt.reshape(-1, D)
    cs, cl = sc.reshape(-1, D), lc.reshape(-1, D)
    vectors = (ln1g, ln1b, qvb, projb, ln2g, ln2b, outb, fcb)
    sizes = [v.shape[0] for v in vectors]
    every = lax.all_gather(jnp.concatenate(vectors), AXES, axis=0)
    starts = [sum(sizes[:i]) for i in range(len(sizes))]
    full = [every[:, s : s + n].reshape(-1, D) for s, n in zip(starts, sizes)]
    table = jnp.concatenate(full + [jnp.zeros((4, D), BF16)]).astype(F32)
    by_group = lambda w: w.reshape(-1, 3, GROUPS, GROUP).swapaxes(1, 2).reshape(-1, 3 * D)
    w_attn = gather(jnp.concatenate([by_group(wqkv), wproj], axis=1))
    w_fc, w_out = gather(wfc), gather(wout)
    a1, qkv, att, lse_t, mid = forward_local(ss, ls, xs, xl, table, w_attn)
    out_s, out_l, g_mid, sums2, dwf, dwo = mlp_local(mid, cs, cl, table, w_fc, w_out, False)
    gxs, gxl, dwp, dwq, sums1 = backward_local(
        ss, ls, xs, xl, table, w_attn, a1, qkv, att, lse_t, g_mid
    )
    dwq = dwq.reshape(-1, GROUPS, 3, GROUP).swapaxes(1, 2).reshape(-1, 3 * D)
    return finish(args, devices, starts, sizes, out_s, out_l, gxs, gxl, sums1, sums2, dwq, dwp, dwf, dwo)


def finish(args, devices, starts, sizes, out_s, out_l, gxs, gxl, sums1, sums2, dwq, dwp, dwf, dwo):
    st, lt = args[0], args[1]
    rs = lambda x: x.reshape(devices, -1)
    small = jnp.concatenate(
        [
            rs(sums1[0]),
            rs(sums1[1]),
            rs(sums1[2:4]),
            rs(sums1[4]),
            rs(sums2[0]),
            rs(sums2[1]),
            rs(sums2[2]),
            rs(sums2[3:7]),
        ],
        axis=1,
    )
    small = scatter(small)[0]
    parts = [small[s : s + n] for s, n in zip(starts, sizes)]
    d_ln1g, d_ln1b, d_qvb, d_projb, d_ln2g, d_ln2b, d_outb, d_fcb = parts
    return (
        out_s.reshape(st.shape),
        out_l.reshape(lt.shape),
        gxs.reshape(st.shape),
        gxl.reshape(lt.shape),
        d_ln1g,
        d_ln1b,
        scatter(dwq),
        d_qvb,
        scatter(dwp),
        d_projb,
        d_ln2g,
        d_ln2b,
        scatter(dwf),
        d_fcb,
        scatter(dwo),
        d_outb,
    )


def on_torus(args):
    (st, lt, ss, ls, ln1g, ln1b, wqkv, qvb, wproj, projb, ln2g, ln2b, wfc, fcb, wout, outb, sc, lc) = args
    xs, xl = st.reshape(-1, D), lt.reshape(-1, D)
    cs, cl = sc.reshape(-1, D), lc.reshape(-1, D)
    vectors = (ln1g, ln1b, qvb, projb, ln2g, ln2b, outb, fcb)
    table, w_attn, wf0, wo0, slab_f1, a1, qkv, att, lse_t, mid = forward_gather(
        ss, ls, xs, xl, wqkv, wproj, wfc, wout, vectors
    )
    out_s, out_l, g_mid, sums2, d_out0, d_fc0, dwo, dwf = mlp_exchange(
        mid, cs, cl, table, wf0, wo0, slab_f1, wout[None]
    )
    gxs, gxl, *rest = backward_reduce(
        ss, ls, xs, xl, table, w_attn, a1, qkv, att, lse_t, g_mid, sums2, dwo, dwf, [v.shape[0] for v in vectors]
    )
    d_fc1, d_out1 = rest[10:]
    out_s, out_l, gxs, gxl, *rest = hand_over(
        (out_s, out_l, gxs, gxl), (*rest[:10], d_fc0, d_fc1, d_out0, d_out1)
    )
    d_ln1g, d_ln1b, d_qvb, d_projb, d_ln2g, d_ln2b, d_outb, d_fcb = [v.reshape(-1) for v in rest[:8]]
    d_qkv, d_proj, d_fc, d_out = rest[8:]
    return (
        out_s.reshape(st.shape),
        out_l.reshape(lt.shape),
        gxs.reshape(st.shape),
        gxl.reshape(lt.shape),
        d_ln1g,
        d_ln1b,
        d_qkv,
        d_qvb,
        d_proj,
        d_projb,
        d_ln2g,
        d_ln2b,
        d_fc,
        d_fcb,
        d_out,
        d_outb,
    )


def per_device(shape, *args):
    devices = shape["dp"] * shape["fsdp"]
    sizes = (args[0].shape[1], args[1].shape[1], args[6].shape, args[14].shape)
    if shape == {"dp": COLS, "fsdp": 2 * DEPTH} and sizes == (512, 1024, (24, 3 * D), (96, D)):
        return on_torus(args)
    return general(args, devices)


def solution(mesh):
    vec, mat, seq = P(AXES), P(AXES, None), P(AXES, None, None)
    in_specs = (seq, seq, vec, vec) + (vec, vec, mat, vec, mat, vec) * 1 + (vec, vec, mat, vec, mat, vec) + (seq, seq)
    out_specs = (seq,) * 4 + (vec, vec, mat, vec, mat, vec) * 2
    return jax.shard_map(
        functools.partial(per_device, dict(mesh.shape)),
        mesh=mesh,
        in_specs=in_specs,
        out_specs=out_specs,
        check_vma=False,
    )
```

```python
import functools

import jax
import jax.numpy as jnp
from jax import lax
from jax.experimental import pallas as pl
from jax.experimental.pallas import tpu as pltpu
from jax.sharding import PartitionSpec as P

F32 = jnp.float32
BF16 = jnp.bfloat16
D = 768
FF = 3072
HEAD_DIM = 64
PAIRS = D // 128
GROUP = 256
GROUPS = D // GROUP
TILE = 256
BRANCH = 0.14433756729740643
EPS = 1e-05
NEG = -1e30
VMEM_LIMIT = 60 * 2**20

LN1G, LN1B, QB, VB, PROJB, LN2G, LN2B, OUTB, FCB = 0, 1, 2, 3, 4, 5, 6, 7, 8


def dot(a, b):
    return jnp.dot(a, b, preferred_element_type=F32)


def dot_nt(a, b):
    return lax.dot_general(a, b, (((1,), (1,)), ((), ())), preferred_element_type=F32)


def dot_tn(a, b):
    return lax.dot_general(a, b, (((0,), (0,)), ((), ())), preferred_element_type=F32)


def normalize(x):
    center = x - jnp.mean(x, axis=-1, keepdims=True)
    rstd = lax.rsqrt(jnp.mean(center * center, axis=-1, keepdims=True) + EPS)
    return center * rstd, rstd


def norm_backward(g, n, rstd, gain):
    e = g * gain
    return rstd * (
        e
        - jnp.mean(e, axis=-1, keepdims=True)
        - n * jnp.mean(e * n, axis=-1, keepdims=True)
    )


def rows_of(base, tile):
    return pl.ds(pl.multiple_of(base + tile * TILE, TILE), TILE)


def lanes_of(start):
    return pl.ds(pl.multiple_of(start, 128), 128)


def loop(count, body):
    lax.fori_loop(0, count, lambda i, c: (body(i), c)[1], 0)


def group_refs(short, long):
    return ((short, 0), (long, short.shape[0]))


def norm_tile(x_ref, table_ref, a1_ref, base, t):
    n, _ = normalize(x_ref[rows_of(0, t), :].astype(F32))
    a1 = n * table_ref[LN1G : LN1G + 1, :] + table_ref[LN1B : LN1B + 1, :]
    a1_ref[rows_of(base, t), :] = a1.astype(BF16)


def group_cols(g, part):
    start = g * D + part * GROUP
    return pl.ds(start if isinstance(start, int) else pl.multiple_of(start, 128), GROUP)


def pair_cols(pair, part):
    return lanes_of(lax.div(pair, 2) * D + part * GROUP + lax.rem(pair, 2) * 128)


def vector_cols(g):
    return pl.ds(g * GROUP if isinstance(g, int) else pl.multiple_of(g * GROUP, 128), GROUP)


def qkv_tile(table_ref, w_ref, a1_ref, qkv_ref, g, t):
    rows = rows_of(0, t)
    a1 = a1_ref[rows, :]
    for part, bias in ((0, QB), (1, None), (2, VB)):
        out = dot(a1, w_ref[:, group_cols(g, part)])
        if bias is not None:
            out = out + table_ref[bias : bias + 1, vector_cols(g)]
        qkv_ref[rows, group_cols(g, part)] = out.astype(BF16)


def attend_pair(split, qkv_ref, att_ref, lse_t_ref, base, length, pair):
    first = lax.broadcasted_iota(jnp.int32, (TILE, 128), 1) < HEAD_DIM
    v_t = jnp.transpose(qkv_ref[base : base + length, pair_cols(pair, 2)])
    for qb in range(length // TILE):
        start = qb * TILE
        qrows = slice(base + start, base + start + TILE)
        q_pair = qkv_ref[qrows, pair_cols(pair, 0)] * BF16(HEAD_DIM**-0.5)
        q_pos = start + lax.broadcasted_iota(jnp.int32, (1, TILE), 1)
        low = jnp.where(q_pos >= split, split, 0)
        spans = []
        for lo, hi in ((0, start), (start, start + TILE)):
            if lo == hi:
                continue
            k_pos = lo + lax.broadcasted_iota(jnp.int32, (hi - lo, TILE), 0)
            visible = k_pos >= low
            if hi > start:
                visible = visible & (k_pos <= q_pos)
            spans.append((lo, hi, visible))
        outs = []
        for half in (0, 1):
            q_half = jnp.where(first if half == 0 else ~first, q_pair, BF16(0))
            scores = [
                jnp.where(visible, dot_nt(qkv_ref[base + lo : base + hi, pair_cols(pair, 1)], q_half), NEG)
                for lo, hi, visible in spans
            ]
            peak = functools.reduce(jnp.maximum, [jnp.max(s, axis=0, keepdims=True) for s in scores])
            out = total = None
            for s, (lo, hi, _) in zip(scores, spans):
                e = jnp.exp(s - peak)
                part = jnp.sum(e, axis=0, keepdims=True)
                total = part if total is None else total + part
                part = dot(v_t[half * HEAD_DIM : (half + 1) * HEAD_DIM, lo:hi], e.astype(BF16))
                out = part if out is None else out + part
            outs.append(out * (1.0 / total))
            lse_t_ref[pl.ds(2 * pair + half, 1), qrows] = peak + jnp.log(total)
        out = jnp.transpose(jnp.concatenate(outs, axis=0).astype(BF16))
        att_ref[qrows, lanes_of(pair * 128)] = out


def mid_tile(x_ref, table_ref, w_ref, att_ref, mid_ref, base, t):
    rows = rows_of(base, t)
    out = dot(att_ref[rows, :], w_ref[:, 3 * D : 4 * D]) + table_ref[PROJB : PROJB + 1, :]
    mid_ref[rows, :] = x_ref[rows_of(0, t), :].astype(F32) + BRANCH * out


def forward_kernel(
    ssplit, lsplit, xs, xl, table_ref, w_ref, a1_ref, qkv_ref, att_ref, lse_t_ref, mid_ref
):
    for x_ref, base in group_refs(xs, xl):
        loop(x_ref.shape[0] // TILE, lambda t: norm_tile(x_ref, table_ref, a1_ref, base, t))
    for g in range(GROUPS):
        loop(a1_ref.shape[0] // TILE, lambda t: qkv_tile(table_ref, w_ref, a1_ref, qkv_ref, g, t))
    lse_t_ref[...] = jnp.zeros_like(lse_t_ref)

    def pair_step(pair, c):
        attend_pair(ssplit[0], qkv_ref, att_ref, lse_t_ref, 0, xs.shape[0], pair)
        attend_pair(lsplit[0], qkv_ref, att_ref, lse_t_ref, xs.shape[0], xl.shape[0], pair)
        return c

    lax.fori_loop(0, PAIRS, pair_step, 0)
    for x_ref, base in group_refs(xs, xl):
        lax.fori_loop(
            0,
            x_ref.shape[0] // TILE,
            lambda t, c: (mid_tile(x_ref, table_ref, w_ref, att_ref, mid_ref, base, t), c)[1],
            0,
        )


VM = pl.BlockSpec(memory_space=pltpu.VMEM)
SM = pl.BlockSpec(memory_space=pltpu.SMEM)


def forward_local(ssplit, lsplit, xs, xl, table, w_attn):
    rows = xs.shape[0] + xl.shape[0]
    return pl.pallas_call(
        forward_kernel,
        out_shape=(
            jax.ShapeDtypeStruct((rows, D), BF16),
            jax.ShapeDtypeStruct((rows, 3 * D), BF16),
            jax.ShapeDtypeStruct((rows, D), BF16),
            jax.ShapeDtypeStruct((16, rows), F32),
            jax.ShapeDtypeStruct((rows, D), F32),
        ),
        in_specs=[SM, SM, VM, VM, VM, VM],
        out_specs=[VM] * 5,
        compiler_params=pltpu.CompilerParams(vmem_limit_bytes=VMEM_LIMIT),
        name="attention_forward",
    )(ssplit, lsplit, xs, xl, table, w_attn)


GELU_A = 0.7978845608028654
GELU_B = 0.044715


def mlp_tile(mid, g_out, table_ref, wf_ref, wo_ref):
    n2, rstd = normalize(mid)
    gain = table_ref[LN2G : LN2G + 1, :]
    a2 = (n2 * gain + table_ref[LN2B : LN2B + 1, :]).astype(BF16)
    g_mlp = (BRANCH * g_out).astype(BF16)
    out = None
    g_a2 = None
    acts, g_pres = [], []
    for j in range(FF // D):
        cols = slice(j * D, (j + 1) * D)
        pre = dot(a2, wf_ref[:, cols]) + table_ref[FCB + j : FCB + j + 1, :]
        g_act = dot_nt(g_mlp, wo_ref[cols, :])
        square = pre * pre
        t = jnp.tanh(pre * (GELU_A + (GELU_A * GELU_B) * square))
        half = 0.5 + 0.5 * t
        act = (pre * half).astype(BF16)
        slope = half + pre * (0.5 - 0.5 * t * t) * (GELU_A + (3 * GELU_A * GELU_B) * square)
        g_pre = (g_act * slope).astype(BF16)
        acts.append(act)
        g_pres.append(g_pre)
        part = dot(act, wo_ref[cols, :])
        out = part if out is None else out + part
        part = dot_nt(g_pre, wf_ref[:, cols])
        g_a2 = part if g_a2 is None else g_a2 + part
    out = mid + BRANCH * (out + table_ref[OUTB : OUTB + 1, :])
    g_mid = g_out + norm_backward(g_a2, n2, rstd, gain)
    return out, g_mid, a2, g_mlp, acts, g_pres, g_a2, n2


def colsum(x):
    return jnp.sum(x, axis=0, keepdims=True)


def mlp_kernel(
    n_tiles,
    slabs,
    mid_ref,
    cs_ref,
    cl_ref,
    table_ref,
    wf_ref,
    wo_ref,
    os_ref,
    ol_ref,
    g_mid_ref,
    sums_ref,
    dwf_ref,
    dwo_ref,
    a2_ref,
    g_mlp_ref,
    act_ref,
    g_pre_ref,
):
    step = pl.program_id(0)
    short_tiles = n_tiles[0]
    tiles = n_tiles[0] + n_tiles[1]

    @pl.when(step == 0)
    def _():
        sums_ref[...] = jnp.zeros_like(sums_ref)

    @pl.when(step < tiles)
    def _():
        cot = jnp.where(step < short_tiles, cs_ref[...], cl_ref[...]).astype(F32)
        out, g_mid, a2, g_mlp, acts, g_pres, g_a2, n2 = mlp_tile(
            mid_ref[...], cot, table_ref, wf_ref, wo_ref
        )
        out = out.astype(BF16)

        @pl.when(step < short_tiles)
        def _():
            os_ref[...] = out

        @pl.when(step >= short_tiles)
        def _():
            ol_ref[...] = out

        g_mid_ref[...] = g_mid
        rows = rows_of(0, step)
        a2_ref[rows, :] = a2
        g_mlp_ref[rows, :] = g_mlp
        sums_ref[0:1, :] += colsum(g_a2 * n2)
        sums_ref[1:2, :] += colsum(g_a2)
        sums_ref[2:3, :] += colsum(g_mlp.astype(F32))
        for j in range(FF // D):
            act_ref[rows, j * D : (j + 1) * D] = acts[j]
            g_pre_ref[rows, j * D : (j + 1) * D] = g_pres[j]
            sums_ref[3 + j : 4 + j, :] += colsum(g_pres[j].astype(F32))

    for j in range(4):

        @pl.when(step == tiles + j)
        def _(j=j):
            res = dot_tn(act_ref[:, j * D : (j + 1) * D], g_mlp_ref[...])
            if slabs:
                dwo_ref[...] = res.astype(BF16).reshape(dwo_ref.shape)
            else:
                dwo_ref[...] = res

    for j in range(2 if slabs else 4):

        @pl.when(step == tiles + 4 + j)
        def _(j=j):
            if slabs:
                dev = D // 24
                left = dot_tn(a2_ref[...], g_pre_ref[:, 2 * j * D : (2 * j + 1) * D])
                right = dot_tn(a2_ref[...], g_pre_ref[:, (2 * j + 1) * D : (2 * j + 2) * D])
                both = jnp.concatenate(
                    [left.reshape(dev, 24, D), right.reshape(dev, 24, D)], axis=1
                )
                dwf_ref[...] = both.astype(BF16)
            else:
                dwf_ref[...] = dot_tn(a2_ref[...], g_pre_ref[:, j * D : (j + 1) * D])


def mlp_local(mid, cs, cl, table, w_fc, w_out, slabs):
    rows = mid.shape[0]
    ns, nl = cs.shape[0] // TILE, cl.shape[0] // TILE
    tiles = ns + nl
    steps = tiles + (6 if slabs else 8)
    whole = lambda shape: pl.BlockSpec(shape, lambda i: (0, 0), pipeline_mode=pl.Buffered(1))
    tile = lambda f: pl.BlockSpec((TILE, D), f)
    short_at = lambda i: (jnp.minimum(i, ns - 1), 0)
    long_at = lambda i: (jnp.clip(i - ns, 0, nl - 1), 0)
    all_at = lambda i: (jnp.minimum(i, tiles - 1), 0)
    if slabs:
        dev = D // 24
        dwo_shape = jax.ShapeDtypeStruct((dev, 96, D), BF16)
        dwo_spec = pl.BlockSpec((dev // 4, 96, D), lambda i: (jnp.clip(i - tiles, 0, 3), 0, 0))
        dwf_shape = jax.ShapeDtypeStruct((dev, 96, D), BF16)
        dwf_spec = pl.BlockSpec((dev, 48, D), lambda i: (0, jnp.clip(i - tiles - 4, 0, 1), 0))
    else:
        dwo_shape = jax.ShapeDtypeStruct((FF, D), F32)
        dwo_spec = pl.BlockSpec((D, D), lambda i: (jnp.clip(i - tiles, 0, 3), 0))
        dwf_shape = jax.ShapeDtypeStruct((D, FF), F32)
        dwf_spec = pl.BlockSpec((D, D), lambda i: (0, jnp.clip(i - tiles - 4, 0, 3)))
    return pl.pallas_call(
        functools.partial(mlp_kernel, (ns, nl), slabs),
        grid=(steps,),
        out_shape=(
            jax.ShapeDtypeStruct(cs.shape, BF16),
            jax.ShapeDtypeStruct(cl.shape, BF16),
            jax.ShapeDtypeStruct((rows, D), F32),
            jax.ShapeDtypeStruct((8, D), F32),
            dwf_shape,
            dwo_shape,
        ),
        in_specs=[
            tile(all_at),
            tile(short_at),
            tile(long_at),
            whole(table.shape),
            whole(w_fc.shape),
            whole(w_out.shape),
        ],
        out_specs=[
            tile(short_at),
            tile(long_at),
            tile(all_at),
            pl.BlockSpec((8, D), lambda i: (0, 0)),
            dwf_spec,
            dwo_spec,
        ],
        scratch_shapes=[
            pltpu.VMEM((rows, D), BF16),
            pltpu.VMEM((rows, D), BF16),
            pltpu.VMEM((rows, FF), BF16),
            pltpu.VMEM((rows, FF), BF16),
        ],
        compiler_params=pltpu.CompilerParams(vmem_limit_bytes=VMEM_LIMIT),
        name="mlp",
    )(mid, cs, cl, table, w_fc, w_out)


def inner_rows(g_att, att):
    prod = g_att.astype(F32) * att.astype(F32)
    high = prod.astype(BF16)
    rest = (prod - high.astype(F32)).astype(BF16)
    head = lax.broadcasted_iota(jnp.int32, (16, D), 0)
    lane = lax.broadcasted_iota(jnp.int32, (16, D), 1)
    pick = jnp.where((lane >= head * HEAD_DIM) & (lane < (head + 1) * HEAD_DIM), 1.0, 0.0).astype(BF16)
    return dot_nt(pick, high) + dot_nt(pick, rest)


def proj_back_tile(g_mid_ref, w_ref, att_ref, g_attn_ref, g_att_ref, inner_ref, sums_ref, t):
    rows = rows_of(0, t)
    g_attn = (BRANCH * g_mid_ref[rows, :]).astype(BF16)
    g_attn_ref[rows, :] = g_attn
    g_att = dot_nt(g_attn, w_ref[:, 3 * D : 4 * D]).astype(BF16)
    g_att_ref[rows, :] = g_att
    inner_ref[:, rows] = inner_rows(g_att, att_ref[rows, :])
    sums_ref[PROJB : PROJB + 1, :] += colsum(g_attn.astype(F32))


def attend_back_pair(
    split, qkv_ref, g_att_ref, lse_t_ref, inner_ref, g_qkv_ref, dk_ref, dv_ref, base, length, pair
):
    first = lax.broadcasted_iota(jnp.int32, (TILE, 128), 1) < HEAD_DIM
    k_t = jnp.transpose(qkv_ref[base : base + length, pair_cols(pair, 1)])
    for qb in range(length // TILE):
        start = qb * TILE
        qrows = slice(base + start, base + start + TILE)
        q_pair = qkv_ref[qrows, pair_cols(pair, 0)] * BF16(HEAD_DIM**-0.5)
        g_pair = g_att_ref[qrows, lanes_of(pair * 128)]
        q_pos = start + lax.broadcasted_iota(jnp.int32, (1, TILE), 1)
        low = jnp.where(q_pos >= split, split, 0)
        spans = []
        spans.append((0, start + TILE))
        halves = []
        for half in (0, 1):
            mine = first if half == 0 else ~first
            head = pl.ds(2 * pair + half, 1)
            halves.append(
                (
                    jnp.where(mine, q_pair, BF16(0)),
                    jnp.where(mine, g_pair, BF16(0)),
                    lse_t_ref[head, qrows],
                    inner_ref[head, qrows],
                )
            )
        dqs = [None, None]
        for lo, hi in spans:
            k_pos = lo + lax.broadcasted_iota(jnp.int32, (hi - lo, TILE), 0)
            visible = k_pos >= low
            if hi > start:
                visible = visible & (k_pos <= q_pos)
            keys = slice(base + lo, base + hi)
            k_pair = qkv_ref[keys, pair_cols(pair, 1)]
            v_pair = qkv_ref[keys, pair_cols(pair, 2)]
            dk = dv = None
            for half, (q_half, g_half, lse, inner) in enumerate(halves):
                s = jnp.where(visible, dot_nt(k_pair, q_half), NEG)
                p = jnp.exp(s - lse)
                ds = (p * (dot_nt(v_pair, g_half) - inner)).astype(BF16)
                part_v, part_k = dot(p.astype(BF16), g_half), dot(ds, q_half)
                dv = part_v if dv is None else dv + part_v
                dk = part_k if dk is None else dk + part_k
                part_q = dot(k_t[half * HEAD_DIM : (half + 1) * HEAD_DIM, lo:hi], ds)
                dqs[half] = part_q if dqs[half] is None else dqs[half] + part_q
            if qb:
                dk_ref[0:start, :] += dk[0:start]
                dv_ref[0:start, :] += dv[0:start]
            dk_ref[start:hi, :] = dk[start:hi]
            dv_ref[start:hi, :] = dv[start:hi]
        dq = jnp.transpose(jnp.concatenate(dqs, axis=0)) * (HEAD_DIM**-0.5)
        g_qkv_ref[qrows, pair_cols(pair, 0)] = dq.astype(BF16)
    all_rows = slice(base, base + length)
    g_qkv_ref[all_rows, pair_cols(pair, 1)] = dk_ref[0:length, :].astype(BF16)
    g_qkv_ref[all_rows, pair_cols(pair, 2)] = dv_ref[0:length, :].astype(BF16)


def ln1_back_tile(x_ref, g_mid_ref, table_ref, w_ref, g_qkv_ref, gx_ref, ln_sums_ref, base, t):
    rows = rows_of(base, t)
    g_qkv = g_qkv_ref[rows, :]
    g_a1 = dot_nt(g_qkv, w_ref[:, 0 : 3 * D])
    own = rows_of(0, t)
    n, rstd = normalize(x_ref[own, :].astype(F32))
    gx_ref[own, :] = g_mid_ref[rows, :] + norm_backward(
        g_a1, n, rstd, table_ref[LN1G : LN1G + 1, :]
    )
    ln_sums_ref[0:1, :] += colsum(g_a1 * n)
    ln_sums_ref[1:2, :] += colsum(g_a1)


def qv_sums(g_qkv_ref, sums_ref, g):
    for row, part in ((QB, 0), (VB, 2)):
        sums_ref[row : row + 1, vector_cols(g)] = colsum(g_qkv_ref[:, group_cols(g, part)].astype(F32))


def backward_kernel(
    ssplit,
    lsplit,
    xs,
    xl,
    table_ref,
    w_ref,
    a1_ref,
    qkv_ref,
    att_ref,
    lse_t_ref,
    g_mid_ref,
    gxs_ref,
    gxl_ref,
    dwp_ref,
    dwq_ref,
    sums_ref,
    g_attn_ref,
    g_att_ref,
    g_qkv_ref,
    inner_ref,
    dk_ref,
    dv_ref,
):
    sums_ref[...] = jnp.zeros_like(sums_ref)
    rows = xs.shape[0] + xl.shape[0]
    lax.fori_loop(
        0,
        rows // TILE,
        lambda t, c: (
            proj_back_tile(g_mid_ref, w_ref, att_ref, g_attn_ref, g_att_ref, inner_ref, sums_ref, t),
            c,
        )[1],
        0,
    )
    dwp_ref[...] = dot_tn(att_ref[...], g_attn_ref[...])

    def pair_step(pair, c):
        for split, x_ref, base in ((ssplit[0], xs, 0), (lsplit[0], xl, xs.shape[0])):
            attend_back_pair(
                split, qkv_ref, g_att_ref, lse_t_ref, inner_ref, g_qkv_ref, dk_ref, dv_ref, base, x_ref.shape[0], pair
            )
        return c

    lax.fori_loop(0, PAIRS, pair_step, 0)
    for g in range(GROUPS):
        qv_sums(g_qkv_ref, sums_ref, g)
    for j in range(3):
        dwq_ref[:, j * D : (j + 1) * D] = dot_tn(a1_ref[...], g_qkv_ref[:, j * D : (j + 1) * D])
    for x_ref, gx_ref, base in ((xs, gxs_ref, 0), (xl, gxl_ref, xs.shape[0])):
        lax.fori_loop(
            0,
            x_ref.shape[0] // TILE,
            lambda t, c: (
                ln1_back_tile(
                    x_ref, g_mid_ref, table_ref, w_ref, g_qkv_ref, gx_ref, sums_ref.at[LN1G : LN1B + 1], base, t
                ),
                c,
            )[1],
            0,
        )


def backward_local(ssplit, lsplit, xs, xl, table, w_attn, a1, qkv, att, lse_t, g_mid):
    rows = xs.shape[0] + xl.shape[0]
    return pl.pallas_call(
        backward_kernel,
        out_shape=(
            jax.ShapeDtypeStruct(xs.shape, F32),
            jax.ShapeDtypeStruct(xl.shape, F32),
            jax.ShapeDtypeStruct((D, D), F32),
            jax.ShapeDtypeStruct((D, 3 * D), F32),
            jax.ShapeDtypeStruct((8, D), F32),
        ),
        in_specs=[SM, SM] + [VM] * 9,
        out_specs=[VM] * 5,
        scratch_shapes=[
            pltpu.VMEM((rows, D), BF16),
            pltpu.VMEM((rows, D), BF16),
            pltpu.VMEM((rows, 3 * D), BF16),
            pltpu.VMEM((16, rows), F32),
            pltpu.VMEM((xl.shape[0], 128), F32),
            pltpu.VMEM((xl.shape[0], 128), F32),
        ],
        compiler_params=pltpu.CompilerParams(vmem_limit_bytes=VMEM_LIMIT),
        name="attention_backward",
    )(ssplit, lsplit, xs, xl, table, w_attn, a1, qkv, att, lse_t, g_mid)


MESH = pl.DeviceIdType.MESH
COLS, DEPTH = 4, 4


class Place:
    def __init__(self):
        q, f = lax.axis_index("dp"), lax.axis_index("fsdp")
        z = lax.div(f, 2)
        self.core = lax.rem(f, 2)
        self.col = [q, q + 1 - 2 * lax.rem(q, 2), lax.rem(q + 2, 4), 3 - q]
        self.depth = [lax.rem(z + k, DEPTH) for k in range(DEPTH)]
        self.index = q * 2 * DEPTH + f
        self.partner = (q, 2 * z + 1 - self.core)
        self.x = (self.col[1], f)
        self.y = (self.col[2], f)
        self.across = (self.col[3], f)
        self.over = [(q, 2 * d + 1 - self.core) for d in self.depth]
        self.along = [(q, 2 * d + self.core) for d in self.depth]

    def greet(self):
        barrier = pltpu.get_barrier_semaphore()
        others = [self.partner, self.x, self.y, self.across] + self.along[1:] + self.over[1:]
        for device in others:
            pl.semaphore_signal(barrier, inc=1, device_id=device, device_id_type=MESH)
        return lambda: pl.semaphore_wait(barrier, len(others))


def hooks(table):
    def run(i):
        for n, actions in table.items():

            @pl.when(i == n)
            def _():
                for action, *args in actions:
                    action(*args)

    return run


def remote(src, dst, send, recv, device):
    return pltpu.make_async_remote_copy(
        src_ref=src, dst_ref=dst, send_sem=send, recv_sem=recv, device_id=device, device_id_type=MESH
    )


def at(start, size, step):
    return pl.ds(pl.multiple_of(start, step), size)


Z, X, Y, VIA_X, VIA_Y, PAIR = 0, 3, 4, 5, 6, 7
N_GATHER = 11


class Gather:
    def __init__(self, place, spot, own, send, recv):
        self.place, self.own, self.send, self.recv = place, own, send, recv
        self.spot = spot

    def share(self, k):
        return self.spot(self.place.col[0], self.place.depth[k], 1, self.place.core)

    def column(self, r, z=0, n=DEPTH):
        return self.spot(self.place.col[r], z, n, self.place.core)

    def along(self, k, arriving=False):
        n = (k if arriving else DEPTH - k) - 1
        src, dst = (self.share(k),) * 2 if arriving else (self.own, self.share(0))
        return remote(src, dst, self.send.at[Z + k - 1], self.recv.at[Z + n], self.place.along[k])

    def near(self, kind, r):
        device = self.place.x if kind == X else self.place.y
        ref = self.column(r)
        return remote(ref, ref, self.send.at[kind], self.recv.at[kind], device)

    def across(self, kind, r):
        device, z = (self.place.x, DEPTH // 2) if kind == VIA_X else (self.place.y, 0)
        ref = self.column(r, z, DEPTH // 2)
        return remote(ref, ref, self.send.at[kind], self.recv.at[kind], device)

    def pair(self, r, arriving=False):
        core = 1 - self.place.core if arriving else self.place.core
        ref = self.spot(self.place.col[r], 0, DEPTH, core)
        return remote(ref, ref, self.send.at[PAIR + r], self.recv.at[PAIR + r], self.place.partner)

    def a(self):
        for k in (1, 3, 2):
            self.along(k).start()

    def b(self):
        for k in (1, 3, 2):
            self.along(k, True).wait_recv()
        self.near(X, 0).start()
        self.near(Y, 0).start()
        self.pair(0).start()

    def c(self):
        self.near(X, 1).wait_recv()
        self.across(VIA_Y, 1).start()
        self.pair(1).start()
        self.near(Y, 2).wait_recv()
        self.across(VIA_X, 2).start()
        self.pair(2).start()

    def d(self):
        self.across(VIA_Y, 3).wait_recv()
        self.across(VIA_X, 3).wait_recv()
        self.pair(3).start()

    def e(self):
        for r in range(COLS):
            self.pair(r, True).wait_recv()

    def end(self):
        for k in range(1, DEPTH):
            self.along(k).wait_send()
        self.near(X, 0).wait_send()
        self.near(Y, 0).wait_send()
        self.across(VIA_Y, 1).wait_send()
        self.across(VIA_X, 2).wait_send()
        for r in range(COLS):
            self.pair(r).wait_send()


def wide_spot(full, start, half):
    def spot(col, z, n, core):
        rows = at(col * (48 * DEPTH) + z * 48, 48 * n, 16)
        return full.at[rows, at(start + core * half, half, 128)]

    return spot


def tall_spot(full, start, size):
    def spot(col, z, n, core):
        return full.at[col, pl.ds(z, n), core, pl.ds(start, size)]

    return spot


def picks(place, size):
    start = place.index * size
    at_row, at_lane = lax.div(start, D), lax.rem(start, D)
    lane = lax.broadcasted_iota(jnp.int32, (size, D), 1)
    pick = lax.broadcasted_iota(jnp.int32, (size, D), 0) + at_lane == lane
    return at_row, jnp.where(pick, 1.0, 0.0)


def place_vectors(place, vectors, out):
    v = [ref[...].astype(F32) for ref in vectors]
    _, pick = picks(place, 24)
    short = jnp.concatenate([v[0], v[1], v[3], v[4], v[5], v[6], jnp.zeros((2, 24), F32)], axis=0)
    short = dot(short.astype(BF16), pick.astype(BF16))
    at_row, pick = picks(place, 48)
    pairs = jnp.concatenate([v[2], v[7][:, 0:48], v[7][:, 48:96], jnp.zeros((5, 48), F32)], axis=0)
    pairs = dot(pairs.astype(BF16), pick.astype(BF16))
    mine = lax.broadcasted_iota(jnp.int32, (2, D), 0) == at_row
    two = [jnp.where(mine, pairs[n : n + 1], 0.0) for n in range(3)]
    lines = [short[0:2], two[0], short[2:6], two[1], two[2], jnp.zeros((4, D), F32)]
    out[...] = jnp.concatenate(lines, axis=0).astype(out.dtype)


SUM_STEPS = 7
SUM_STAGES = ((0,), (1, 2, 3), (4, 5, 6))


class TableSum:
    def __init__(self, place, total, got, send, recv):
        self.place, self.total, self.got, self.send, self.recv = place, total, got, send, recv

    def copy(self, step, arriving=False):
        place = self.place
        if step == 0:
            device, n, stage = place.partner, 0, 0
        elif step <= 3:
            device, n, stage = place.along[step], (step if arriving else 4 - step), 1
        else:
            device, n, stage = (place.x, place.y, place.across)[step - 4], step, 2
        return remote(self.total.at[stage], self.got.at[n], self.send.at[step], self.recv.at[n], device)

    def begin(self, stage):
        for step in SUM_STAGES[stage]:
            self.copy(step).start()

    def add(self, stage):
        for step in SUM_STAGES[stage]:
            self.copy(step, True).wait_recv()
        total = self.total[stage]
        for step in SUM_STAGES[stage]:
            total = total + self.got[step]
        self.total[stage + 1] = total

    def next(self, stage):
        self.add(stage)
        self.begin(stage + 1)

    def end(self):
        for step in range(SUM_STEPS):
            self.copy(step).wait_send()


def forward_gather_kernel(
    ssplit,
    lsplit,
    xs_hbm,
    xl_hbm,
    wqkv,
    wproj,
    wfc,
    wout,
    v0,
    v1,
    v2,
    v3,
    v4,
    v5,
    v6,
    v7,
    table_ref,
    wa_hbm,
    wf_hbm,
    wo_hbm,
    slab_f1,
    a1_hbm,
    qkv_hbm,
    att_hbm,
    lse_t_ref,
    mid_hbm,
    xs,
    xl,
    wa,
    a1_ref,
    qkv_ref,
    att_ref,
    mid_ref,
    slab_f,
    swap_out,
    swap_in,
    total,
    got,
    io_sem,
    swap_send,
    swap_recv,
    sum_send,
    sum_recv,
    g_send,
    g_recv,
):
    place = Place()
    welcome = place.greet()
    loads = [pltpu.make_async_copy(xs_hbm, xs, io_sem.at[0]), pltpu.make_async_copy(xl_hbm, xl, io_sem.at[1])]
    for copy in loads:
        copy.start()
    part = D // 2
    first = place.core == 0
    swaps = [
        remote(swap_out.at[n], swap_in.at[n], swap_send.at[n], swap_recv.at[n], place.partner)
        for n in range(2)
    ]
    sums = TableSum(place, total, got, sum_send, sum_recv)

    def halves(share, step):
        starts = range(0, share.shape[1], 2 * step)
        lefts = jnp.concatenate([share[:, i : i + step] for i in starts], axis=1)
        rights = jnp.concatenate([share[:, i + step : i + 2 * step] for i in starts], axis=1)
        return jnp.where(first, lefts, rights), jnp.where(first, rights, lefts)

    cols = [wqkv[:, j * D + g * GROUP : j * D + (g + 1) * GROUP] for g in range(GROUPS) for j in range(3)]
    keep_a, swap_out[0] = halves(jnp.concatenate(cols + [wproj[...]], axis=1).astype(F32), part)
    welcome()
    swaps[0].start()
    place_vectors(place, (v0, v1, v2, v3, v4, v5, v6, v7), total.at[0])
    sums.begin(0)
    keep_f, swap_out[1] = halves(by_pieces(wfc[...].astype(F32)), D)
    swaps[1].start()
    sums.next(0)

    def joined(n, mine):
        swaps[n].wait_recv()
        other = swap_in[n]
        top, bottom = jnp.where(first, mine, other), jnp.where(first, other, mine)
        return jnp.concatenate([top, bottom], axis=0).astype(BF16)

    chip = place.col[0] * DEPTH + place.depth[0]
    rows = at(chip * 48, 48, 16)
    share = joined(0, keep_a)
    ps = []
    for n in range(4):
        cols = at(n * D + place.core * part, part, 128)
        wa[rows, cols] = share[:, n * part : (n + 1) * part]
        ps.append(Gather(place, wide_spot(wa, n * D, part), wa.at[rows, cols], g_send.at[n], g_recv.at[n]))
    ps.append(Gather(place, wide_spot(wf_hbm, 0, D), slab_f, g_send.at[4], g_recv.at[4]))
    ps.append(Gather(place, tall_spot(wo_hbm, 0, 48), wout.at[:, pl.ds(0, 48)], g_send.at[5], g_recv.at[5]))
    h0, h1, h2, pp, f0, o0 = ps
    for piece in ps[:4]:
        piece.a()
    share = joined(1, keep_f)
    slab_f[...] = share[:, 0:D]
    slab_f1[...] = share[:, D : 2 * D]
    for piece in ps[4:]:
        piece.a()
    own_copies = []
    for n, piece in enumerate((f0, o0)):
        copy = pltpu.make_async_copy(piece.own, piece.share(0), io_sem.at[2 + n])
        copy.start()
        own_copies.append(copy)
    sums.next(1)
    h0.b()
    sums.add(2)
    table_ref[...] = total[3].astype(F32)
    for copy in loads + own_copies:
        copy.wait()
    groups = group_refs(xs, xl)
    short_tiles, long_tiles = xs.shape[0] // TILE, xl.shape[0] // TILE
    loop(short_tiles, lambda t: norm_tile(xs, table_ref, a1_ref, 0, t))
    h0.c()
    h1.b()
    loop(2, lambda t: norm_tile(xl, table_ref, a1_ref, groups[1][1], t))
    h0.d()
    loop(long_tiles - 2, lambda t: norm_tile(xl, table_ref, a1_ref, groups[1][1], t + 2))
    h0.e()
    short, rows = xs.shape[0], a1_ref.shape[0]
    store_a1 = pltpu.make_async_copy(a1_ref, a1_hbm, io_sem.at[4])
    store_wa = pltpu.make_async_copy(wa, wa_hbm, io_sem.at[5])
    store_mid = [
        pltpu.make_async_copy(mid_ref.at[part], mid_hbm.at[part], io_sem.at[6 + n])
        for n, part in enumerate((pl.ds(0, short), pl.ds(short, rows - short)))
    ]

    def store_qkv(g):
        cols = pl.ds(pl.multiple_of(g * D, 128), D)
        return pltpu.make_async_copy(qkv_ref.at[:, cols], qkv_hbm.at[:, cols], io_sem.at[8 + g])

    def store_att(g):
        cols = pl.ds(pl.multiple_of(g * GROUP, 128), GROUP)
        return pltpu.make_async_copy(att_ref.at[:, cols], att_hbm.at[:, cols], io_sem.at[11 + g])

    store_a1.start()
    lse_t_ref[...] = jnp.zeros_like(lse_t_ref)
    before_group = hooks({1: ((h1.e,),), 2: ((h2.e,),)})
    after_qkv = hooks({0: ((h1.c,), (h2.b,)), 1: ((o0.b,),)})
    after_short = hooks({0: ((pp.b,),), 1: ((f0.b,),), 3: ((pp.d,), (f0.c,)), 4: ((o0.c,),)})
    after_long = hooks(
        {
            0: ((h1.d,), (h2.c,)),
            1: ((pp.c,), (h2.d,)),
            4: ((f0.d,), (pp.e,), (store_wa.start,)),
            5: ((o0.d,), (f0.e,)),
        }
    )

    def group_step(g):
        before_group(g)
        loop(a1_ref.shape[0] // TILE, lambda t: qkv_tile(table_ref, wa, a1_ref, qkv_ref, g, t))
        store_qkv(g).start()
        after_qkv(g)

        def pair_step(j):
            pair = 2 * g + j
            attend_pair(ssplit[0], qkv_ref, att_ref, lse_t_ref, 0, xs.shape[0], pair)
            after_short(pair)
            attend_pair(lsplit[0], qkv_ref, att_ref, lse_t_ref, xs.shape[0], xl.shape[0], pair)
            after_long(pair)

        loop(2, pair_step)
        store_att(g).start()

    loop(GROUPS, group_step)
    for (x_ref, base), store in zip(groups, store_mid):
        loop(
            x_ref.shape[0] // TILE,
            lambda t: mid_tile(x_ref, table_ref, wa, att_ref, mid_ref, base, t),
        )
        store.start()
    o0.e()
    for swap in swaps:
        swap.wait_send()
    sums.end()
    for piece in ps:
        piece.end()
    for copy in [store_a1, store_wa] + store_mid:
        copy.wait()
    for g in range(GROUPS):
        store_qkv(g).wait()
        store_att(g).wait()


ANY = pl.BlockSpec(memory_space=pl.ANY)


def forward_gather(ssplit, lsplit, xs, xl, wqkv, wproj, wfc, wout, vectors):
    rows = xs.shape[0] + xl.shape[0]
    wide = wqkv.shape[1] + wproj.shape[1]
    half_out = jax.ShapeDtypeStruct((COLS, DEPTH, 2) + SLAB, BF16)
    sem = pltpu.SemaphoreType.DMA
    return pl.pallas_call(
        forward_gather_kernel,
        out_shape=(
            jax.ShapeDtypeStruct((16, D), F32),
            jax.ShapeDtypeStruct((D, wide), BF16),
            jax.ShapeDtypeStruct((D, HALF), BF16),
            half_out,
            jax.ShapeDtypeStruct(SLAB, BF16),
            jax.ShapeDtypeStruct((rows, D), BF16),
            jax.ShapeDtypeStruct((rows, 3 * D), BF16),
            jax.ShapeDtypeStruct((rows, D), BF16),
            jax.ShapeDtypeStruct((16, rows), F32),
            jax.ShapeDtypeStruct((rows, D), F32),
        ),
        in_specs=[SM, SM, ANY, ANY] + [VM] * 12,
        out_specs=[VM, ANY, ANY, ANY, VM, ANY, ANY, ANY, VM, ANY],
        scratch_shapes=[
            pltpu.VMEM(xs.shape, BF16),
            pltpu.VMEM(xl.shape, BF16),
            pltpu.VMEM((D, wide), BF16),
            pltpu.VMEM((rows, D), BF16),
            pltpu.VMEM((rows, 3 * D), BF16),
            pltpu.VMEM((rows, D), BF16),
            pltpu.VMEM((rows, D), F32),
            pltpu.VMEM(SLAB, BF16),
            pltpu.VMEM((2, 24, wide // 2), F32),
            pltpu.VMEM((2, 24, wide // 2), F32),
            pltpu.VMEM((4, 16, D), BF16),
            pltpu.VMEM((SUM_STEPS, 16, D), BF16),
            sem((14,)),
            sem((2,)),
            sem((2,)),
            sem((SUM_STEPS,)),
            sem((SUM_STEPS,)),
            sem((6, N_GATHER)),
            sem((6, N_GATHER)),
        ],
        compiler_params=pltpu.CompilerParams(
            vmem_limit_bytes=VMEM_LIMIT, collective_id=0, has_side_effects=True
        ),
        name="attention_forward_gather",
    )(ssplit, lsplit, xs, xl, wqkv, wproj, wfc, wout[None], *[v.reshape(1, -1) for v in vectors])


R_PAIR, R_X, R_Y, R_XB, R_YB, R_Z = 0, 4, 6, 8, 9, 10
N_REDUCE = 13
ORDER = (3, 1, 2, 0)


class Reduce:
    def __init__(self, place, src, own, total, xa, ya, xb, yb, zr, send, recv, own_sem):
        self.place, self.src, self.own, self.total = place, src, own, total
        self.xa, self.ya, self.xb, self.yb, self.zr = xa, ya, xb, yb, zr
        self.send, self.recv, self.own_sem = send, recv, own_sem

    def slabs(self, r, core):
        return self.src.at[pl.ds(self.place.col[r] * DEPTH, DEPTH), core]

    def pair(self, r):
        place = self.place
        n = R_PAIR + r
        return remote(
            self.slabs(r, 1 - place.core), self.total.at[r], self.send.at[n], self.recv.at[n], place.partner
        )

    def load(self, r):
        slot = ORDER.index(r) % 2
        return pltpu.make_async_copy(self.slabs(r, self.place.core), self.own.at[slot], self.own_sem.at[r])

    def to_x(self, n):
        src = self.total.at[(1, 3)[n], pl.ds(0, 2)]
        return remote(src, self.xa.at[n], self.send.at[R_X + n], self.recv.at[R_X + n], self.place.x)

    def to_y(self, n):
        src = self.total.at[(2, 3)[n], pl.ds(2, 2)]
        return remote(src, self.ya.at[n], self.send.at[R_Y + n], self.recv.at[R_Y + n], self.place.y)

    def to_xb(self):
        src = self.total.at[1, pl.ds(2, 2)]
        return remote(src, self.xb, self.send.at[R_XB], self.recv.at[R_XB], self.place.x)

    def to_yb(self):
        src = self.total.at[2, pl.ds(0, 2)]
        return remote(src, self.yb, self.send.at[R_YB], self.recv.at[R_YB], self.place.y)

    def to_z(self, k, arriving=False):
        n = (k if arriving else DEPTH - k) - 1
        src = self.total.at[0, self.place.depth[k]]
        return remote(
            src, self.zr.at[n], self.send.at[R_Z + k - 1], self.recv.at[R_Z + n], self.place.along[k]
        )

    def begin(self, loads=True):
        for r in ORDER:
            self.pair(r).start()
        if loads:
            self.begin_loads()

    def begin_loads(self):
        if self.own is not None:
            for r in ORDER[:2]:
                self.load(r).start()

    def chip(self, r):
        if self.own is not None:
            self.load(r).wait()
            mine = self.own[ORDER.index(r) % 2]
        else:
            mine = self.src[pl.ds(self.place.col[r] * DEPTH, DEPTH), self.place.core]
        self.pair(r).wait_recv()
        self.total[r] = self.total[r] + mine
        if self.own is not None and ORDER.index(r) < 2:
            self.load(ORDER[ORDER.index(r) + 2]).start()
        if r == 1:
            self.to_x(1).start()
            self.to_x(0).start()
        if r == 2:
            self.to_y(1).start()
            self.to_y(0).start()

    def chip_all(self):
        for r in ORDER:
            self.chip(r)

    def cross(self):
        self.to_x(1).wait_recv()
        self.total[2, 0:2] = self.total[2, 0:2] + self.xa[1]
        self.to_yb().start()
        self.to_y(1).wait_recv()
        self.total[1, 2:4] = self.total[1, 2:4] + self.ya[1]
        self.to_xb().start()

    def column(self):
        self.to_x(0).wait_recv()
        self.to_yb().wait_recv()
        add = lambda a, b, c: (a.astype(F32) + b.astype(F32) + c.astype(F32)).astype(BF16)
        self.total[0, 0:2] = add(self.total[0, 0:2], self.xa[0], self.yb[...])
        self.to_y(0).wait_recv()
        self.to_xb().wait_recv()
        self.total[0, 2:4] = add(self.total[0, 2:4], self.ya[0], self.xb[...])
        for k in (2, 1, 3):
            self.to_z(k).start()

    def result(self):
        out = self.total[0, self.place.depth[0]].astype(F32)
        for k in range(1, DEPTH):
            self.to_z(k, True).wait_recv()
            out = out + self.zr[k - 1].astype(F32)
        return out

    def end(self):
        self.end_pairs()
        self.end_rest()

    def end_pairs(self):
        for r in range(COLS):
            self.pair(r).wait_send()

    def end_rest(self):
        for n in range(2):
            self.to_x(n).wait_send()
            self.to_y(n).wait_send()
        self.to_xb().wait_send()
        self.to_yb().wait_send()
        for k in range(1, DEPTH):
            self.to_z(k).wait_send()


class ReduceAtOnce(Reduce):
    def __init__(self, place, src, total, other, zr, send, recv):
        super().__init__(place, src, None, total, None, None, None, None, zr, send, recv, None)
        self.other = other

    def to_column(self, r):
        device = (self.place.x, self.place.y, self.place.across)[r - 1]
        n = R_X + r - 1
        return remote(self.total.at[r], self.other.at[r - 1], self.send.at[n], self.recv.at[n], device)

    def chip(self, r):
        mine = self.src[pl.ds(self.place.col[r] * DEPTH, DEPTH), self.place.core]
        self.pair(r).wait_recv()
        self.total[r] = self.total[r] + mine
        if r:
            self.to_column(r).start()

    def column(self):
        out = self.total[0].astype(F32)
        for r in range(1, COLS):
            self.to_column(r).wait_recv()
            out = out + self.other[r - 1].astype(F32)
        self.total[0] = out.astype(BF16)
        for k in (2, 1, 3):
            self.to_z(k).start()

    def end_rest(self):
        for r in range(1, COLS):
            self.to_column(r).wait_send()
        for k in range(1, DEPTH):
            self.to_z(k).wait_send()


class LastSum:
    def __init__(self, place, total, got, send, recv):
        self.place, self.total, self.got, self.send, self.recv = place, total, got, send, recv

    def copy(self, n, arriving=False):
        place = self.place
        if n < 3:
            device, m = place.along[n + 1], (n if arriving else 2 - n)
        elif n < 6:
            device, m = place.over[n - 2], (n if arriving else 8 - n)
        else:
            device, m = (place.partner, place.x, place.y, place.across)[n - 6], n
        stage = 0 if n < 7 else 1
        return remote(self.total.at[stage], self.got.at[m], self.send.at[n], self.recv.at[m], device)

    def begin(self, stage):
        for n in (range(7), range(7, 10))[stage]:
            self.copy(n).start()

    def add(self, stage):
        total = self.total[stage]
        for n in (range(7), range(7, 10))[stage]:
            self.copy(n, True).wait_recv()
            total = total + self.got[n]
        self.total[stage + 1] = total

    def end(self):
        for n in range(10):
            self.copy(n).wait_send()


def take(lines, pick):
    return lax.dot_general(
        lines, pick, (((1,), (1,)), ((), ())), preferred_element_type=F32, precision=lax.Precision.HIGHEST
    )


def take_vectors(place, table, outs):
    _, pick = picks(place, 24)
    short = take(table[0:8, :], pick)
    for n, row in ((0, LN1G), (1, LN1B), (3, PROJB), (4, LN2G), (5, LN2B), (6, OUTB)):
        outs[n][...] = short[row : row + 1]
    at_row, pick = picks(place, 48)
    mine = lax.broadcasted_iota(jnp.int32, (2, D), 0) == at_row
    lines = [
        jnp.sum(jnp.where(mine, table[row : row + 2, :], 0.0), axis=0, keepdims=True) for row in (QB, FCB, FCB + 2)
    ]
    pairs = take(jnp.concatenate(lines + [jnp.zeros((5, D), F32)], axis=0), pick)
    outs[2][...] = pairs[0:1]
    outs[7][...] = jnp.concatenate([pairs[1:2], pairs[2:3]], axis=1)


def small_slabs(whole):
    devices, half = 2 * COLS * DEPTH, D // 2
    left = whole[:, 0:half].reshape(devices, 24, half)
    right = whole[:, half:D].reshape(devices, 24, half)
    both = jnp.concatenate([left, right], axis=1).astype(BF16)
    return both.reshape(COLS * DEPTH, 2, 48, half)


HALF = FF // 2
SLAB = (48, D)


def by_pieces(w):
    size = w.shape[1] // 64
    cuts = [w[:, (2 * i + n) * size : (2 * i + n + 1) * size] for n in range(2) for i in range(32)]
    return jnp.concatenate(cuts, axis=1)


def from_pieces(first, second):
    size = first.shape[1] // 32
    cuts = [w[:, i * size : (i + 1) * size] for i in range(32) for w in (first, second)]
    return jnp.concatenate(cuts, axis=1)


def mlp_half_tile(n, t, refs):
    mid_ref, cot_ref, a2_ref, g_mlp_ref, act_ref, g_pre_ref, acc_ref, acc_g_ref, wf, wo, table_ref, sums_ref = refs
    rows = rows_of(0, t)
    gain = table_ref[LN2G : LN2G + 1, :]
    if n == 0:
        n2, _ = normalize(mid_ref[rows, :])
        a2 = (n2 * gain + table_ref[LN2B : LN2B + 1, :]).astype(BF16)
        g_mlp = (BRANCH * cot_ref[rows, :].astype(F32)).astype(BF16)
        a2_ref[rows, :] = a2
        g_mlp_ref[rows, :] = g_mlp
        sums_ref[2:3, :] += colsum(g_mlp.astype(F32))
    else:
        a2 = a2_ref[rows, :]
        g_mlp = g_mlp_ref[rows, :]
    out = None
    g_a2 = None
    for j in range(HALF // D):
        cols = slice(j * D, (j + 1) * D)
        row = 2 * n + j
        wf_j = wf[n, :, cols]
        wo_j = wo[n, 2 * j : 2 * j + 2].reshape(D, D)
        pre = dot(a2, wf_j) + table_ref[FCB + row : FCB + row + 1, :]
        g_act = dot_nt(g_mlp, wo_j)
        square = pre * pre
        th = jnp.tanh(pre * (GELU_A + (GELU_A * GELU_B) * square))
        half = 0.5 + 0.5 * th
        act = (pre * half).astype(BF16)
        slope = half + pre * (0.5 - 0.5 * th * th) * (GELU_A + (3 * GELU_A * GELU_B) * square)
        g_pre = (g_act * slope).astype(BF16)
        act_ref[rows, cols] = act
        g_pre_ref[rows, cols] = g_pre
        sums_ref[3 + row : 4 + row, :] += colsum(g_pre.astype(F32))
        part, part_g = dot(act, wo_j), dot_nt(g_pre, wf_j)
        out = part if out is None else out + part
        g_a2 = part_g if g_a2 is None else g_a2 + part_g
    if n == 0:
        acc_ref[rows, :] = out
        acc_g_ref[rows, :] = g_a2
        return
    out = acc_ref[rows, :] + out
    g_a2 = acc_g_ref[rows, :] + g_a2
    mid = mid_ref[rows, :]
    n2, rstd = normalize(mid)
    g_out = cot_ref[rows, :].astype(F32)
    cot_ref[rows, :] = (mid + BRANCH * (out + table_ref[OUTB : OUTB + 1, :])).astype(BF16)
    mid_ref[rows, :] = g_out + norm_backward(g_a2, n2, rstd, gain)
    sums_ref[0:1, :] += colsum(g_a2 * n2)
    sums_ref[1:2, :] += colsum(g_a2)


def out_slabs(act_ref, g_mlp_ref, dw_o):
    for j in range(HALF // D):
        res = dot_tn(act_ref[:, j * D : (j + 1) * D], g_mlp_ref[...])
        dw_o[8 * j : 8 * j + 8] = res.astype(BF16).reshape(8, 2, *SLAB)


def fc_slabs(a2_ref, g_pre_ref, dw_f):
    left = dot_tn(a2_ref[...], g_pre_ref[:, 0:D]).reshape(32, 24, D)
    right = dot_tn(a2_ref[...], g_pre_ref[:, D : 2 * D]).reshape(32, 24, D)
    dw_f[...] = jnp.concatenate([left, right], axis=1).astype(BF16).reshape(dw_f.shape)


def mlp_exchange_kernel(
    mid_hbm,
    cs_hbm,
    cl_hbm,
    table_ref,
    wf0_hbm,
    wo0_hbm,
    slab_f,
    wout,
    os_hbm,
    ol_hbm,
    g_mid_hbm,
    sums_ref,
    d_out0,
    d_fc0,
    so_hbm,
    sf_hbm,
    mid_ref,
    cot_ref,
    a2_ref,
    g_mlp_ref,
    act_ref,
    g_pre_ref,
    acc_ref,
    acc_g_ref,
    wf,
    wo,
    dw_o,
    dw_f,
    r_total,
    r_xa,
    r_ya,
    r_xb,
    r_yb,
    r_zr,
    io_sem,
    g_send,
    g_recv,
    r_send,
    r_recv,
):
    place = Place()
    welcome = place.greet()
    short, long = cs_hbm.shape[0], cl_hbm.shape[0]
    tiles = (short + long) // TILE
    parts = (pl.ds(0, short), pl.ds(short, long))
    pairs = (
        (mid_hbm.at[parts[0]], mid_ref.at[parts[0]]),
        (cs_hbm, cot_ref.at[parts[0]]),
        (wf0_hbm, wf.at[0]),
        (wo0_hbm, wo.at[0]),
        (mid_hbm.at[parts[1]], mid_ref.at[parts[1]]),
        (cl_hbm, cot_ref.at[parts[1]]),
    )
    loads = [pltpu.make_async_copy(src, dst, io_sem.at[n]) for n, (src, dst) in enumerate(pairs)]
    for copy in loads:
        copy.start()
    q, z, c = place.col[0], place.depth[0], place.core
    wf[1, at((q * DEPTH + z) * 48, 48, 16), at(c * D, D, 128)] = slab_f[...]
    wo[1, q, z, c] = wout[0, 48:96]
    f1 = Gather(place, wide_spot(wf.at[1], 0, D), slab_f, g_send.at[0], g_recv.at[0])
    o1 = Gather(place, tall_spot(wo.at[1], 0, 48), wout.at[:, pl.ds(48, 48)], g_send.at[1], g_recv.at[1])
    ro, rf = [
        Reduce(
            place, src, None, r_total.at[n], r_xa.at[n], r_ya.at[n], r_xb.at[n], r_yb.at[n],
            r_zr.at[n], r_send.at[n], r_recv.at[n], None,
        )
        for n, src in enumerate((dw_o, dw_f))
    ]
    sums_ref[...] = jnp.zeros_like(sums_ref)
    welcome()
    f1.a()
    o1.a()
    for copy in loads[:4]:
        copy.wait()
    refs = (
        mid_ref, cot_ref, a2_ref, g_mlp_ref, act_ref, g_pre_ref, acc_ref, acc_g_ref, wf, wo, table_ref, sums_ref,
    )
    after = hooks({0: ((loads[4].wait,), (loads[5].wait,)), 2: ((f1.b,),), 3: ((o1.b,),), 4: ((f1.c,),)})

    def first_step(t):
        mlp_half_tile(0, t, refs)
        after(t)

    loop(tiles, first_step)
    out_slabs(act_ref, g_mlp_ref, dw_o)
    ro.begin()
    o1.c()
    fc_slabs(a2_ref, g_pre_ref, dw_f)
    rf.begin()
    ro.chip_all()
    f1.d()
    o1.d()
    f1.e()
    o1.e()

    def give_out():
        d_out0[...] = ro.result()

    after_second = hooks(
        {
            0: ((ro.cross,), (rf.chip_all,)),
            2: ((ro.column,),),
            3: ((rf.cross,),),
            5: ((rf.column,), (give_out,)),
        }
    )

    def second_step(t):
        mlp_half_tile(1, t, refs)
        after_second(t)

    loop(tiles, second_step)
    stores = [
        pltpu.make_async_copy(src, dst, io_sem.at[6 + n])
        for n, (src, dst) in enumerate(
            (
                (cot_ref.at[parts[0]], os_hbm),
                (cot_ref.at[parts[1]], ol_hbm),
                (mid_ref, g_mid_hbm),
                (dw_o, so_hbm),
                (dw_f, sf_hbm),
            )
        )
    ]
    for copy in stores[0:3]:
        copy.start()
    ro.end_pairs()
    out_slabs(act_ref, g_mlp_ref, dw_o)
    stores[3].start()
    rf.end_pairs()
    fc_slabs(a2_ref, g_pre_ref, dw_f)
    stores[4].start()
    res = rf.result()
    d_fc0[...] = jnp.concatenate([res[0:24], res[24:48]], axis=1)
    ro.end_rest()
    rf.end_rest()
    f1.end()
    o1.end()
    for copy in stores:
        copy.wait()


def reduce_buffers(n, shape):
    return [
        pltpu.VMEM((n, COLS, DEPTH) + shape, BF16),
        pltpu.VMEM((n, 2, 2) + shape, BF16),
        pltpu.VMEM((n, 2, 2) + shape, BF16),
        pltpu.VMEM((n, 2) + shape, BF16),
        pltpu.VMEM((n, 2) + shape, BF16),
        pltpu.VMEM((n, DEPTH - 1) + shape, BF16),
    ]


def mlp_exchange(mid, cs, cl, table, wf0, wo0, slab_f, wout):
    rows = mid.shape[0]
    chips = COLS * DEPTH
    sem = pltpu.SemaphoreType.DMA
    slabs = (chips, 2) + SLAB
    return pl.pallas_call(
        mlp_exchange_kernel,
        out_shape=(
            jax.ShapeDtypeStruct(cs.shape, BF16),
            jax.ShapeDtypeStruct(cl.shape, BF16),
            jax.ShapeDtypeStruct(mid.shape, F32),
            jax.ShapeDtypeStruct((8, D), F32),
            jax.ShapeDtypeStruct(SLAB, F32),
            jax.ShapeDtypeStruct((24, HALF), F32),
            jax.ShapeDtypeStruct(slabs, BF16),
            jax.ShapeDtypeStruct(slabs, BF16),
        ),
        in_specs=[ANY, ANY, ANY, VM, ANY, ANY, VM, VM],
        out_specs=[ANY, ANY, ANY, VM, VM, VM, ANY, ANY],
        scratch_shapes=[
            pltpu.VMEM((rows, D), F32),
            pltpu.VMEM((rows, D), BF16),
            pltpu.VMEM((rows, D), BF16),
            pltpu.VMEM((rows, D), BF16),
            pltpu.VMEM((rows, HALF), BF16),
            pltpu.VMEM((rows, HALF), BF16),
            pltpu.VMEM((rows, D), F32),
            pltpu.VMEM((rows, D), F32),
            pltpu.VMEM((2, D, HALF), BF16),
            pltpu.VMEM((2, COLS, DEPTH, 2) + SLAB, BF16),
            pltpu.VMEM(slabs, BF16),
            pltpu.VMEM(slabs, BF16),
            *reduce_buffers(2, SLAB),
            sem((11,)),
            sem((2, N_GATHER)),
            sem((2, N_GATHER)),
            sem((2, N_REDUCE)),
            sem((2, N_REDUCE)),
        ],
        compiler_params=pltpu.CompilerParams(
            vmem_limit_bytes=VMEM_LIMIT, collective_id=2, has_side_effects=True
        ),
        name="mlp_exchange",
    )(mid, cs, cl, table, wf0, wo0, slab_f, wout)


def backward_reduce_kernel(
    ssplit,
    lsplit,
    xs_hbm,
    xl_hbm,
    table_ref,
    wa_hbm,
    a1_hbm,
    qkv_hbm,
    att_hbm,
    lse_t_ref,
    g_mid_hbm,
    sums2_ref,
    go_hbm,
    gf_hbm,
    gxs_hbm,
    gxl_hbm,
    d0,
    d1,
    d2,
    d3,
    d4,
    d5,
    d6,
    d7,
    d_qkv,
    d_proj,
    d_fc1,
    d_out1,
    wa,
    a1_ref,
    qkv_ref,
    att_ref,
    g_mid_ref,
    g_att_ref,
    g_qkv_ref,
    inner_ref,
    dk_ref,
    dv_ref,
    big_own,
    big_total,
    big_xa,
    big_ya,
    big_xb,
    big_yb,
    big_zr,
    small_src,
    small_total,
    small_xa,
    small_ya,
    small_xb,
    small_yb,
    small_zr,
    total,
    got,
    io_sem,
    own_sem,
    r_send,
    r_recv,
    sum_send,
    sum_recv,
    ln_sums_ref,
    other,
    last_total,
    last_got,
    last_send,
    last_recv,
):
    place = Place()
    g_attn_ref = g_qkv_ref.at[:, pl.ds(0, D)]
    short, long = gxs_hbm.shape[0], gxl_hbm.shape[0]
    rows = short + long
    proj_cols = pl.ds(3 * D, D)
    qkv_cols = pl.ds(0, 3 * D)
    loads = [
        pltpu.make_async_copy(src, dst, io_sem.at[n])
        for n, (src, dst) in enumerate(
            (
                (wa_hbm.at[:, proj_cols], wa.at[:, proj_cols]),
                (g_mid_hbm, g_mid_ref),
                (att_hbm, att_ref),
                (qkv_hbm, qkv_ref),
                (a1_hbm, a1_ref),
                (wa_hbm.at[:, qkv_cols], wa.at[:, qkv_cols]),
            )
        )
    ]
    for copy in loads[:3]:
        copy.start()
    sums = TableSum(place, total, got, sum_send, sum_recv)
    sums_ref = total.at[0]
    sums_ref[...] = jnp.zeros_like(sums_ref)
    sums_ref[LN2G : LN2G + 7, :] = sums2_ref[0:7, :]
    big = [
        Reduce(
            place, src, big_own, big_total.at[n], big_xa.at[n], big_ya.at[n], big_xb.at[n],
            big_yb.at[n], big_zr.at[n], r_send.at[n], r_recv.at[n], own_sem.at[n],
        )
        for n, src in enumerate((go_hbm, gf_hbm))
    ]
    small = [
        Reduce(
            place, small_src.at[n], None, small_total.at[n], small_xa.at[n], small_ya.at[n], small_xb.at[n],
            small_yb.at[n], small_zr.at[n], r_send.at[2 + n], r_recv.at[2 + n], None,
        )
        for n in range(4)
    ]
    small[2] = ReduceAtOnce(
        place, small_src.at[2], small_total.at[2], other, small_zr.at[2], r_send.at[4], r_recv.at[4]
    )
    ro, rf = big
    rp, rh = small[3], small[0:3]
    place.greet()()
    ro.begin()
    rf.begin(False)
    for copy in loads[3:]:
        copy.start()
    last_total[...] = jnp.zeros_like(last_total)
    for copy in loads[0:3]:
        copy.wait()

    after = hooks(
        {
            0: ((ro.chip, 3),),
            1: ((ro.chip, 1),),
            2: ((ro.chip, 2),),
            3: ((ro.chip, 0), (rf.begin_loads,)),
            4: ((rf.chip, 3),),
            5: ((rf.chip, 1), (rf.chip, 2), (rf.chip, 0)),
        }
    )

    def proj_step(t):
        proj_back_tile(g_mid_ref, wa, att_ref, g_attn_ref, g_att_ref, inner_ref, sums_ref, t)
        after(t)

    loop(rows // TILE, proj_step)
    small_src[3] = small_slabs(dot_tn(att_ref[...], g_attn_ref[...]))
    rp.begin()
    x_loads = [
        pltpu.make_async_copy(xs_hbm, att_ref.at[pl.ds(0, short)], io_sem.at[6]),
        pltpu.make_async_copy(xl_hbm, att_ref.at[pl.ds(short, long)], io_sem.at[7]),
    ]
    for copy in x_loads:
        copy.start()
    for copy in loads[3:]:
        copy.wait()

    def give_out():
        d_out1[...] = ro.result()

    def give_fc():
        res = rf.result()
        d_fc1[...] = jnp.concatenate([res[0:24], res[24:48]], axis=1)

    def give_proj():
        res = rp.result()
        d_proj[:, 0 : D // 2] = res[0:24]
        d_proj[:, D // 2 : D] = res[24:48]

    def give_qkv(g):
        res = rh[g].result()
        line = jnp.concatenate([res[0:24], res[24:48]], axis=1)
        for j in range(3):
            d_qkv[:, j * D + g * 256 : j * D + g * 256 + 256] = line[:, j * 256 : j * 256 + 256]

    def heads_begin(g):
        rh[g].begin()

    after_short = hooks(
        {
            0: ((ro.cross,),),
            2: ((sums.next, 1), (rh[0].chip_all,), (rf.column,), (rp.cross,)),
            3: ((rp.column,), (give_out,)),
            1: ((sums.next, 0),),
            4: ((rh[1].chip_all,),),
            5: ((give_qkv, 0),),
        }
    )
    after_long = hooks(
        {
            0: ((sums.begin, 0), (rf.cross,), (rp.chip_all,)),
            1: ((heads_begin, 0), (ro.column,)),
            2: ((rh[0].cross,),),
            3: ((sums.add, 2), (heads_begin, 1), (rh[0].column,), (give_fc,)),
            4: ((rh[1].cross,), (give_proj,)),
            5: ((heads_begin, 2), (rh[1].column,)),
        }
    )

    def pair_step(pair):
        attend_back_pair(
            ssplit[0], qkv_ref, g_att_ref, lse_t_ref, inner_ref, g_qkv_ref, dk_ref, dv_ref, 0, short, pair
        )
        after_short(pair)
        attend_back_pair(
            lsplit[0], qkv_ref, g_att_ref, lse_t_ref, inner_ref, g_qkv_ref, dk_ref, dv_ref, short, long, pair
        )

        @pl.when(lax.rem(pair, 2) == 1)
        def _():
            g = lax.div(pair, 2)
            cols = pl.ds(pl.multiple_of(g * D, 128), D)
            small_src[g] = small_slabs(dot_tn(a1_ref[...], g_qkv_ref[:, cols]))

        after_long(pair)

    loop(PAIRS, pair_step)
    for copy in x_loads:
        copy.wait()
    after_norm = hooks({0: ((rh[2].chip_all,),), 3: ((give_qkv, 1),)})

    def norm_step(t):
        ln1_back_tile(att_ref, g_mid_ref, table_ref, wa, g_qkv_ref, g_mid_ref, ln_sums_ref, 0, t)
        after_norm(t)

    ln_sums_ref[...] = jnp.zeros_like(ln_sums_ref)
    for g in range(GROUPS):
        for r, part in enumerate((0, 2)):
            line = colsum(g_qkv_ref[:, group_cols(g, part)].astype(F32))
            ln_sums_ref[2 + r : 3 + r, vector_cols(g)] = line
    loop(short // TILE, norm_step)
    stores = [
        pltpu.make_async_copy(g_mid_ref.at[pl.ds(0, short)], gxs_hbm, io_sem.at[8]),
        pltpu.make_async_copy(g_mid_ref.at[pl.ds(short, long)], gxl_hbm, io_sem.at[9]),
    ]
    stores[0].start()
    loop(long // TILE, lambda t: norm_step(t + short // TILE))
    stores[1].start()
    lanes = D // 128
    lines = [ln_sums_ref[r : r + 1, 128 * j : 128 * j + 128] for r in range(4) for j in range(lanes)]
    last_total[0] = jnp.concatenate(lines, axis=0)
    last = LastSum(place, last_total, last_got, last_send, last_recv)
    last.begin(0)
    rh[2].column()
    final = total.at[3]
    last.add(0)
    last.begin(1)
    last.add(1)
    for r in range(4):
        final[r : r + 1, :] = jnp.concatenate(
            [last_total[2, r * lanes + j : r * lanes + j + 1, :] for j in range(lanes)], axis=1
        )
    take_vectors(place, final, (d0, d1, d2, d3, d4, d5, d6, d7))
    give_qkv(2)
    last.end()
    sums.end()
    for reduce in big + small:
        reduce.end()
    for copy in stores:
        copy.wait()


def backward_reduce(ssplit, lsplit, xs, xl, table, w_attn, a1, qkv, att, lse_t, g_mid, sums2, dwo, dwf, sizes):
    short, long = xs.shape[0], xl.shape[0]
    rows = short + long
    chips = COLS * DEPTH
    devices = 2 * chips
    big, little = SLAB, (48, D // 2)
    sem = pltpu.SemaphoreType.DMA
    return pl.pallas_call(
        backward_reduce_kernel,
        out_shape=(
            jax.ShapeDtypeStruct(xs.shape, F32),
            jax.ShapeDtypeStruct(xl.shape, F32),
            *[jax.ShapeDtypeStruct((1, n), F32) for n in sizes],
            jax.ShapeDtypeStruct((D // devices, 3 * D), F32),
            jax.ShapeDtypeStruct((D // devices, D), F32),
            jax.ShapeDtypeStruct((D // devices, HALF), F32),
            jax.ShapeDtypeStruct(SLAB, F32),
        ),
        in_specs=[SM, SM, ANY, ANY, VM, ANY, ANY, ANY, ANY, VM, ANY, VM, ANY, ANY],
        out_specs=[ANY, ANY] + [VM] * 12,
        scratch_shapes=[
            pltpu.VMEM((D, 4 * D), BF16),
            pltpu.VMEM((rows, D), BF16),
            pltpu.VMEM((rows, 3 * D), BF16),
            pltpu.VMEM((rows, D), BF16),
            pltpu.VMEM((rows, D), F32),
            pltpu.VMEM((rows, D), BF16),
            pltpu.VMEM((rows, 3 * D), BF16),
            pltpu.VMEM((16, rows), F32),
            pltpu.VMEM((long, 128), F32),
            pltpu.VMEM((long, 128), F32),
            pltpu.VMEM((2, DEPTH) + big, BF16),
            *reduce_buffers(2, big),
            pltpu.VMEM((4, chips, 2) + little, BF16),
            *reduce_buffers(4, little),
            pltpu.VMEM((4, 16, D), F32),
            pltpu.VMEM((SUM_STEPS, 16, D), F32),
            sem((10,)),
            sem((2, COLS)),
            sem((6, N_REDUCE)),
            sem((6, N_REDUCE)),
            sem((SUM_STEPS,)),
            sem((SUM_STEPS,)),
            pltpu.VMEM((8, D), F32),
            pltpu.VMEM((COLS - 1, DEPTH) + little, BF16),
            pltpu.VMEM((3, 24, 128), F32),
            pltpu.VMEM((10, 24, 128), F32),
            sem((10,)),
            sem((10,)),
        ],
        compiler_params=pltpu.CompilerParams(
            vmem_limit_bytes=BACK_VMEM, collective_id=1, has_side_effects=True
        ),
        name="attention_backward_reduce",
    )(ssplit, lsplit, xs, xl, table, w_attn, a1, qkv, att, lse_t, g_mid, sums2, dwo, dwf)


BACK_VMEM = 60 * 2**20


PARTS = 4


def hand_over_kernel(os_hbm, ol_hbm, gs_hbm, gl_hbm, *refs):
    small_in, outs = refs[:14], refs[14:30]
    buffers, smalls, joined = refs[30:34], refs[34:48], refs[48:50]
    load_sem, store_sem, small_load, small_store = refs[50:54]
    loads, stores = [], []
    for n, (src, dst, mid) in enumerate(zip((os_hbm, ol_hbm, gs_hbm, gl_hbm), outs[:4], buffers)):
        size = src.shape[0] // PARTS
        for p in range(PARTS):
            rows = pl.ds(p * size, size)
            loads.append(pltpu.make_async_copy(src.at[rows], mid.at[rows], load_sem.at[n, p]))
            stores.append(pltpu.make_async_copy(mid.at[rows], dst.at[rows], store_sem.at[n, p]))
    fetch = [pltpu.make_async_copy(small_in[n], smalls[n], small_load.at[n]) for n in range(14)]
    give = [
        pltpu.make_async_copy(src, dst, small_store.at[n])
        for n, (src, dst) in enumerate(zip(smalls[:10] + joined, outs[4:]))
    ]
    for copy in loads[:2] + fetch + loads[2:]:
        copy.start()
    for n in range(10):
        fetch[n].wait()
        give[n].start()
    for n in range(10, 14):
        fetch[n].wait()
    fc0, fc1, out0, out1 = smalls[10:]
    joined[0][...] = from_pieces(fc0[...], fc1[...])
    give[10].start()
    joined[1][0:48, :] = out0[...]
    joined[1][48:96, :] = out1[...]
    give[11].start()
    for load, store in zip(loads, stores):
        load.wait()
        store.start()
    for copy in stores + give:
        copy.wait()


def hand_over(big, small):
    shape = lambda a: jax.ShapeDtypeStruct(a.shape, a.dtype)
    buffer = lambda a: pltpu.VMEM(a.shape, a.dtype)
    sem = pltpu.SemaphoreType.DMA
    ends = (jax.ShapeDtypeStruct((24, FF), F32), jax.ShapeDtypeStruct((96, D), F32))
    return pl.pallas_call(
        hand_over_kernel,
        out_shape=(*map(shape, big), *map(shape, small[:10]), *ends),
        in_specs=[ANY] * 18,
        out_specs=[ANY] * 16,
        scratch_shapes=[
            *map(buffer, big),
            *map(buffer, small),
            *map(buffer, ends),
            sem((4, PARTS)),
            sem((4, PARTS)),
            sem((14,)),
            sem((12,)),
        ],
        compiler_params=pltpu.CompilerParams(vmem_limit_bytes=VMEM_LIMIT),
        name="hand_over",
    )(*big, *small)


AXES = ("dp", "fsdp")


def gather(x, axis=0):
    return lax.all_gather(x, AXES, axis=axis, tiled=True)


def scatter(x):
    return lax.psum_scatter(x, AXES, scatter_dimension=0, tiled=True)


def general(args, devices):
    (st, lt, ss, ls, ln1g, ln1b, wqkv, qvb, wproj, projb, ln2g, ln2b, wfc, fcb, wout, outb, sc, lc) = args
    xs, xl = st.reshape(-1, D), lt.reshape(-1, D)
    cs, cl = sc.reshape(-1, D), lc.reshape(-1, D)
    vectors = (ln1g, ln1b, qvb, projb, ln2g, ln2b, outb, fcb)
    sizes = [v.shape[0] for v in vectors]
    every = lax.all_gather(jnp.concatenate(vectors), AXES, axis=0)
    starts = [sum(sizes[:i]) for i in range(len(sizes))]
    full = [every[:, s : s + n].reshape(-1, D) for s, n in zip(starts, sizes)]
    table = jnp.concatenate(full + [jnp.zeros((4, D), BF16)]).astype(F32)
    by_group = lambda w: w.reshape(-1, 3, GROUPS, GROUP).swapaxes(1, 2).reshape(-1, 3 * D)
    w_attn = gather(jnp.concatenate([by_group(wqkv), wproj], axis=1))
    w_fc, w_out = gather(wfc), gather(wout)
    a1, qkv, att, lse_t, mid = forward_local(ss, ls, xs, xl, table, w_attn)
    out_s, out_l, g_mid, sums2, dwf, dwo = mlp_local(mid, cs, cl, table, w_fc, w_out, False)
    gxs, gxl, dwp, dwq, sums1 = backward_local(
        ss, ls, xs, xl, table, w_attn, a1, qkv, att, lse_t, g_mid
    )
    dwq = dwq.reshape(-1, GROUPS, 3, GROUP).swapaxes(1, 2).reshape(-1, 3 * D)
    return finish(args, devices, starts, sizes, out_s, out_l, gxs, gxl, sums1, sums2, dwq, dwp, dwf, dwo)


def finish(args, devices, starts, sizes, out_s, out_l, gxs, gxl, sums1, sums2, dwq, dwp, dwf, dwo):
    st, lt = args[0], args[1]
    rs = lambda x: x.reshape(devices, -1)
    small = jnp.concatenate(
        [
            rs(sums1[0]),
            rs(sums1[1]),
            rs(sums1[2:4]),
            rs(sums1[4]),
            rs(sums2[0]),
            rs(sums2[1]),
            rs(sums2[2]),
            rs(sums2[3:7]),
        ],
        axis=1,
    )
    small = scatter(small)[0]
    parts = [small[s : s + n] for s, n in zip(starts, sizes)]
    d_ln1g, d_ln1b, d_qvb, d_projb, d_ln2g, d_ln2b, d_outb, d_fcb = parts
    return (
        out_s.reshape(st.shape),
        out_l.reshape(lt.shape),
        gxs.reshape(st.shape),
        gxl.reshape(lt.shape),
        d_ln1g,
        d_ln1b,
        scatter(dwq),
        d_qvb,
        scatter(dwp),
        d_projb,
        d_ln2g,
        d_ln2b,
        scatter(dwf),
        d_fcb,
        scatter(dwo),
        d_outb,
    )


def on_torus(args):
    (st, lt, ss, ls, ln1g, ln1b, wqkv, qvb, wproj, projb, ln2g, ln2b, wfc, fcb, wout, outb, sc, lc) = args
    xs, xl = st.reshape(-1, D), lt.reshape(-1, D)
    cs, cl = sc.reshape(-1, D), lc.reshape(-1, D)
    vectors = (ln1g, ln1b, qvb, projb, ln2g, ln2b, outb, fcb)
    table, w_attn, wf0, wo0, slab_f1, a1, qkv, att, lse_t, mid = forward_gather(
        ss, ls, xs, xl, wqkv, wproj, wfc, wout, vectors
    )
    out_s, out_l, g_mid, sums2, d_out0, d_fc0, dwo, dwf = mlp_exchange(
        mid, cs, cl, table, wf0, wo0, slab_f1, wout[None]
    )
    gxs, gxl, *rest = backward_reduce(
        ss, ls, xs, xl, table, w_attn, a1, qkv, att, lse_t, g_mid, sums2, dwo, dwf, [v.shape[0] for v in vectors]
    )
    d_fc1, d_out1 = rest[10:]
    out_s, out_l, gxs, gxl, *rest = hand_over(
        (out_s, out_l, gxs, gxl), (*rest[:10], d_fc0, d_fc1, d_out0, d_out1)
    )
    d_ln1g, d_ln1b, d_qvb, d_projb, d_ln2g, d_ln2b, d_outb, d_fcb = [v.reshape(-1) for v in rest[:8]]
    d_qkv, d_proj, d_fc, d_out = rest[8:]
    return (
        out_s.reshape(st.shape),
        out_l.reshape(lt.shape),
        gxs.reshape(st.shape),
        gxl.reshape(lt.shape),
        d_ln1g,
        d_ln1b,
        d_qkv,
        d_qvb,
        d_proj,
        d_projb,
        d_ln2g,
        d_ln2b,
        d_fc,
        d_fcb,
        d_out,
        d_outb,
    )


def per_device(shape, *args):
    devices = shape["dp"] * shape["fsdp"]
    sizes = (args[0].shape[1], args[1].shape[1], args[6].shape, args[14].shape)
    if shape == {"dp": COLS, "fsdp": 2 * DEPTH} and sizes == (512, 1024, (24, 3 * D), (96, D)):
        return on_torus(args)
    return general(args, devices)


def solution(mesh):
    vec, mat, seq = P(AXES), P(AXES, None), P(AXES, None, None)
    in_specs = (seq, seq, vec, vec) + (vec, vec, mat, vec, mat, vec) * 1 + (vec, vec, mat, vec, mat, vec) + (seq, seq)
    out_specs = (seq,) * 4 + (vec, vec, mat, vec, mat, vec) * 2
    return jax.shard_map(
        functools.partial(per_device, dict(mesh.shape)),
        mesh=mesh,
        in_specs=in_specs,
        out_specs=out_specs,
        check_vma=False,
    )
```

```python
import functools

import jax
import jax.numpy as jnp
from jax import lax
from jax.experimental import pallas as pl
from jax.experimental.pallas import tpu as pltpu
from jax.sharding import PartitionSpec as P

F32 = jnp.float32
BF16 = jnp.bfloat16
D = 768
FF = 3072
HEAD_DIM = 64
PAIRS = D // 128
GROUP = 256
GROUPS = D // GROUP
TILE = 256
BRANCH = 0.14433756729740643
EPS = 1e-05
NEG = -1e30
VMEM_LIMIT = 60 * 2**20

LN1G, LN1B, QB, VB, PROJB, LN2G, LN2B, OUTB, FCB = 0, 1, 2, 3, 4, 5, 6, 7, 8


def dot(a, b):
    return jnp.dot(a, b, preferred_element_type=F32)


def dot_nt(a, b):
    return lax.dot_general(a, b, (((1,), (1,)), ((), ())), preferred_element_type=F32)


def dot_tn(a, b):
    return lax.dot_general(a, b, (((0,), (0,)), ((), ())), preferred_element_type=F32)


def normalize(x):
    center = x - jnp.mean(x, axis=-1, keepdims=True)
    rstd = lax.rsqrt(jnp.mean(center * center, axis=-1, keepdims=True) + EPS)
    return center * rstd, rstd


def norm_backward(g, n, rstd, gain):
    e = g * gain
    return rstd * (
        e
        - jnp.mean(e, axis=-1, keepdims=True)
        - n * jnp.mean(e * n, axis=-1, keepdims=True)
    )


def rows_of(base, tile):
    return pl.ds(pl.multiple_of(base + tile * TILE, TILE), TILE)


def lanes_of(start):
    return pl.ds(pl.multiple_of(start, 128), 128)


def loop(count, body):
    lax.fori_loop(0, count, lambda i, c: (body(i), c)[1], 0)


def group_refs(short, long):
    return ((short, 0), (long, short.shape[0]))


def norm_tile(x_ref, table_ref, a1_ref, base, t):
    n, _ = normalize(x_ref[rows_of(0, t), :].astype(F32))
    a1 = n * table_ref[LN1G : LN1G + 1, :] + table_ref[LN1B : LN1B + 1, :]
    a1_ref[rows_of(base, t), :] = a1.astype(BF16)


def group_cols(g, part):
    start = g * D + part * GROUP
    return pl.ds(start if isinstance(start, int) else pl.multiple_of(start, 128), GROUP)


def pair_cols(pair, part):
    return lanes_of(lax.div(pair, 2) * D + part * GROUP + lax.rem(pair, 2) * 128)


def vector_cols(g):
    return pl.ds(g * GROUP if isinstance(g, int) else pl.multiple_of(g * GROUP, 128), GROUP)


def qkv_tile(table_ref, w_ref, a1_ref, qkv_ref, g, t):
    rows = rows_of(0, t)
    a1 = a1_ref[rows, :]
    for part, bias in ((0, QB), (1, None), (2, VB)):
        out = dot(a1, w_ref[:, group_cols(g, part)])
        if bias is not None:
            out = out + table_ref[bias : bias + 1, vector_cols(g)]
        qkv_ref[rows, group_cols(g, part)] = out.astype(BF16)


def attend_pair(split, qkv_ref, att_ref, lse_t_ref, base, length, pair):
    first = lax.broadcasted_iota(jnp.int32, (TILE, 128), 1) < HEAD_DIM
    v_t = jnp.transpose(qkv_ref[base : base + length, pair_cols(pair, 2)])
    for qb in range(length // TILE):
        start = qb * TILE
        qrows = slice(base + start, base + start + TILE)
        q_pair = qkv_ref[qrows, pair_cols(pair, 0)] * BF16(HEAD_DIM**-0.5)
        q_pos = start + lax.broadcasted_iota(jnp.int32, (1, TILE), 1)
        low = jnp.where(q_pos >= split, split, 0)
        spans = []
        for lo, hi in ((0, start), (start, start + TILE)):
            if lo == hi:
                continue
            k_pos = lo + lax.broadcasted_iota(jnp.int32, (hi - lo, TILE), 0)
            visible = k_pos >= low
            if hi > start:
                visible = visible & (k_pos <= q_pos)
            spans.append((lo, hi, visible))
        outs = []
        for half in (0, 1):
            q_half = jnp.where(first if half == 0 else ~first, q_pair, BF16(0))
            scores = [
                jnp.where(visible, dot_nt(qkv_ref[base + lo : base + hi, pair_cols(pair, 1)], q_half), NEG)
                for lo, hi, visible in spans
            ]
            peak = functools.reduce(jnp.maximum, [jnp.max(s, axis=0, keepdims=True) for s in scores])
            out = total = None
            for s, (lo, hi, _) in zip(scores, spans):
                e = jnp.exp(s - peak)
                part = jnp.sum(e, axis=0, keepdims=True)
                total = part if total is None else total + part
                part = dot(v_t[half * HEAD_DIM : (half + 1) * HEAD_DIM, lo:hi], e.astype(BF16))
                out = part if out is None else out + part
            outs.append(out * (1.0 / total))
            lse_t_ref[pl.ds(2 * pair + half, 1), qrows] = peak + jnp.log(total)
        out = jnp.transpose(jnp.concatenate(outs, axis=0).astype(BF16))
        att_ref[qrows, lanes_of(pair * 128)] = out


def mid_tile(x_ref, table_ref, w_ref, att_ref, mid_ref, base, t):
    rows = rows_of(base, t)
    out = dot(att_ref[rows, :], w_ref[:, 3 * D : 4 * D]) + table_ref[PROJB : PROJB + 1, :]
    mid_ref[rows, :] = x_ref[rows_of(0, t), :].astype(F32) + BRANCH * out


def forward_kernel(
    ssplit, lsplit, xs, xl, table_ref, w_ref, a1_ref, qkv_ref, att_ref, lse_t_ref, mid_ref
):
    for x_ref, base in group_refs(xs, xl):
        loop(x_ref.shape[0] // TILE, lambda t: norm_tile(x_ref, table_ref, a1_ref, base, t))
    for g in range(GROUPS):
        loop(a1_ref.shape[0] // TILE, lambda t: qkv_tile(table_ref, w_ref, a1_ref, qkv_ref, g, t))
    lse_t_ref[...] = jnp.zeros_like(lse_t_ref)

    def pair_step(pair, c):
        attend_pair(ssplit[0], qkv_ref, att_ref, lse_t_ref, 0, xs.shape[0], pair)
        attend_pair(lsplit[0], qkv_ref, att_ref, lse_t_ref, xs.shape[0], xl.shape[0], pair)
        return c

    lax.fori_loop(0, PAIRS, pair_step, 0)
    for x_ref, base in group_refs(xs, xl):
        lax.fori_loop(
            0,
            x_ref.shape[0] // TILE,
            lambda t, c: (mid_tile(x_ref, table_ref, w_ref, att_ref, mid_ref, base, t), c)[1],
            0,
        )


VM = pl.BlockSpec(memory_space=pltpu.VMEM)
SM = pl.BlockSpec(memory_space=pltpu.SMEM)


def forward_local(ssplit, lsplit, xs, xl, table, w_attn):
    rows = xs.shape[0] + xl.shape[0]
    return pl.pallas_call(
        forward_kernel,
        out_shape=(
            jax.ShapeDtypeStruct((rows, D), BF16),
            jax.ShapeDtypeStruct((rows, 3 * D), BF16),
            jax.ShapeDtypeStruct((rows, D), BF16),
            jax.ShapeDtypeStruct((16, rows), F32),
            jax.ShapeDtypeStruct((rows, D), F32),
        ),
        in_specs=[SM, SM, VM, VM, VM, VM],
        out_specs=[VM] * 5,
        compiler_params=pltpu.CompilerParams(vmem_limit_bytes=VMEM_LIMIT),
        name="attention_forward",
    )(ssplit, lsplit, xs, xl, table, w_attn)


GELU_A = 0.7978845608028654
GELU_B = 0.044715


def mlp_tile(mid, g_out, table_ref, wf_ref, wo_ref):
    n2, rstd = normalize(mid)
    gain = table_ref[LN2G : LN2G + 1, :]
    a2 = (n2 * gain + table_ref[LN2B : LN2B + 1, :]).astype(BF16)
    g_mlp = (BRANCH * g_out).astype(BF16)
    out = None
    g_a2 = None
    acts, g_pres = [], []
    for j in range(FF // D):
        cols = slice(j * D, (j + 1) * D)
        pre = dot(a2, wf_ref[:, cols]) + table_ref[FCB + j : FCB + j + 1, :]
        g_act = dot_nt(g_mlp, wo_ref[cols, :])
        square = pre * pre
        t = jnp.tanh(pre * (GELU_A + (GELU_A * GELU_B) * square))
        half = 0.5 + 0.5 * t
        act = (pre * half).astype(BF16)
        slope = half + pre * (0.5 - 0.5 * t * t) * (GELU_A + (3 * GELU_A * GELU_B) * square)
        g_pre = (g_act * slope).astype(BF16)
        acts.append(act)
        g_pres.append(g_pre)
        part = dot(act, wo_ref[cols, :])
        out = part if out is None else out + part
        part = dot_nt(g_pre, wf_ref[:, cols])
        g_a2 = part if g_a2 is None else g_a2 + part
    out = mid + BRANCH * (out + table_ref[OUTB : OUTB + 1, :])
    g_mid = g_out + norm_backward(g_a2, n2, rstd, gain)
    return out, g_mid, a2, g_mlp, acts, g_pres, g_a2, n2


def colsum(x):
    return jnp.sum(x, axis=0, keepdims=True)


def mlp_kernel(
    n_tiles,
    slabs,
    mid_ref,
    cs_ref,
    cl_ref,
    table_ref,
    wf_ref,
    wo_ref,
    os_ref,
    ol_ref,
    g_mid_ref,
    sums_ref,
    dwf_ref,
    dwo_ref,
    a2_ref,
    g_mlp_ref,
    act_ref,
    g_pre_ref,
):
    step = pl.program_id(0)
    short_tiles = n_tiles[0]
    tiles = n_tiles[0] + n_tiles[1]

    @pl.when(step == 0)
    def _():
        sums_ref[...] = jnp.zeros_like(sums_ref)

    @pl.when(step < tiles)
    def _():
        cot = jnp.where(step < short_tiles, cs_ref[...], cl_ref[...]).astype(F32)
        out, g_mid, a2, g_mlp, acts, g_pres, g_a2, n2 = mlp_tile(
            mid_ref[...], cot, table_ref, wf_ref, wo_ref
        )
        out = out.astype(BF16)

        @pl.when(step < short_tiles)
        def _():
            os_ref[...] = out

        @pl.when(step >= short_tiles)
        def _():
            ol_ref[...] = out

        g_mid_ref[...] = g_mid
        rows = rows_of(0, step)
        a2_ref[rows, :] = a2
        g_mlp_ref[rows, :] = g_mlp
        sums_ref[0:1, :] += colsum(g_a2 * n2)
        sums_ref[1:2, :] += colsum(g_a2)
        sums_ref[2:3, :] += colsum(g_mlp.astype(F32))
        for j in range(FF // D):
            act_ref[rows, j * D : (j + 1) * D] = acts[j]
            g_pre_ref[rows, j * D : (j + 1) * D] = g_pres[j]
            sums_ref[3 + j : 4 + j, :] += colsum(g_pres[j].astype(F32))

    for j in range(4):

        @pl.when(step == tiles + j)
        def _(j=j):
            res = dot_tn(act_ref[:, j * D : (j + 1) * D], g_mlp_ref[...])
            if slabs:
                dwo_ref[...] = res.astype(BF16).reshape(dwo_ref.shape)
            else:
                dwo_ref[...] = res

    for j in range(2 if slabs else 4):

        @pl.when(step == tiles + 4 + j)
        def _(j=j):
            if slabs:
                dev = D // 24
                left = dot_tn(a2_ref[...], g_pre_ref[:, 2 * j * D : (2 * j + 1) * D])
                right = dot_tn(a2_ref[...], g_pre_ref[:, (2 * j + 1) * D : (2 * j + 2) * D])
                both = jnp.concatenate(
                    [left.reshape(dev, 24, D), right.reshape(dev, 24, D)], axis=1
                )
                dwf_ref[...] = both.astype(BF16)
            else:
                dwf_ref[...] = dot_tn(a2_ref[...], g_pre_ref[:, j * D : (j + 1) * D])


def mlp_local(mid, cs, cl, table, w_fc, w_out, slabs):
    rows = mid.shape[0]
    ns, nl = cs.shape[0] // TILE, cl.shape[0] // TILE
    tiles = ns + nl
    steps = tiles + (6 if slabs else 8)
    whole = lambda shape: pl.BlockSpec(shape, lambda i: (0, 0), pipeline_mode=pl.Buffered(1))
    tile = lambda f: pl.BlockSpec((TILE, D), f)
    short_at = lambda i: (jnp.minimum(i, ns - 1), 0)
    long_at = lambda i: (jnp.clip(i - ns, 0, nl - 1), 0)
    all_at = lambda i: (jnp.minimum(i, tiles - 1), 0)
    if slabs:
        dev = D // 24
        dwo_shape = jax.ShapeDtypeStruct((dev, 96, D), BF16)
        dwo_spec = pl.BlockSpec((dev // 4, 96, D), lambda i: (jnp.clip(i - tiles, 0, 3), 0, 0))
        dwf_shape = jax.ShapeDtypeStruct((dev, 96, D), BF16)
        dwf_spec = pl.BlockSpec((dev, 48, D), lambda i: (0, jnp.clip(i - tiles - 4, 0, 1), 0))
    else:
        dwo_shape = jax.ShapeDtypeStruct((FF, D), F32)
        dwo_spec = pl.BlockSpec((D, D), lambda i: (jnp.clip(i - tiles, 0, 3), 0))
        dwf_shape = jax.ShapeDtypeStruct((D, FF), F32)
        dwf_spec = pl.BlockSpec((D, D), lambda i: (0, jnp.clip(i - tiles - 4, 0, 3)))
    return pl.pallas_call(
        functools.partial(mlp_kernel, (ns, nl), slabs),
        grid=(steps,),
        out_shape=(
            jax.ShapeDtypeStruct(cs.shape, BF16),
            jax.ShapeDtypeStruct(cl.shape, BF16),
            jax.ShapeDtypeStruct((rows, D), F32),
            jax.ShapeDtypeStruct((8, D), F32),
            dwf_shape,
            dwo_shape,
        ),
        in_specs=[
            tile(all_at),
            tile(short_at),
            tile(long_at),
            whole(table.shape),
            whole(w_fc.shape),
            whole(w_out.shape),
        ],
        out_specs=[
            tile(short_at),
            tile(long_at),
            tile(all_at),
            pl.BlockSpec((8, D), lambda i: (0, 0)),
            dwf_spec,
            dwo_spec,
        ],
        scratch_shapes=[
            pltpu.VMEM((rows, D), BF16),
            pltpu.VMEM((rows, D), BF16),
            pltpu.VMEM((rows, FF), BF16),
            pltpu.VMEM((rows, FF), BF16),
        ],
        compiler_params=pltpu.CompilerParams(vmem_limit_bytes=VMEM_LIMIT),
        name="mlp",
    )(mid, cs, cl, table, w_fc, w_out)


def inner_rows(g_att, att):
    prod = g_att.astype(F32) * att.astype(F32)
    high = prod.astype(BF16)
    rest = (prod - high.astype(F32)).astype(BF16)
    head = lax.broadcasted_iota(jnp.int32, (16, D), 0)
    lane = lax.broadcasted_iota(jnp.int32, (16, D), 1)
    pick = jnp.where((lane >= head * HEAD_DIM) & (lane < (head + 1) * HEAD_DIM), 1.0, 0.0).astype(BF16)
    return dot_nt(pick, high) + dot_nt(pick, rest)


def proj_back_tile(g_mid_ref, w_ref, att_ref, g_attn_ref, g_att_ref, inner_ref, sums_ref, t):
    rows = rows_of(0, t)
    g_attn = (BRANCH * g_mid_ref[rows, :]).astype(BF16)
    g_attn_ref[rows, :] = g_attn
    g_att = dot_nt(g_attn, w_ref[:, 3 * D : 4 * D]).astype(BF16)
    g_att_ref[rows, :] = g_att
    inner_ref[:, rows] = inner_rows(g_att, att_ref[rows, :])
    sums_ref[PROJB : PROJB + 1, :] += colsum(g_attn.astype(F32))


def attend_back_pair(
    split, qkv_ref, g_att_ref, lse_t_ref, inner_ref, g_qkv_ref, dk_ref, dv_ref, base, length, pair
):
    first = lax.broadcasted_iota(jnp.int32, (TILE, 128), 1) < HEAD_DIM
    k_t = jnp.transpose(qkv_ref[base : base + length, pair_cols(pair, 1)])
    for qb in range(length // TILE):
        start = qb * TILE
        qrows = slice(base + start, base + start + TILE)
        q_pair = qkv_ref[qrows, pair_cols(pair, 0)] * BF16(HEAD_DIM**-0.5)
        g_pair = g_att_ref[qrows, lanes_of(pair * 128)]
        q_pos = start + lax.broadcasted_iota(jnp.int32, (1, TILE), 1)
        low = jnp.where(q_pos >= split, split, 0)
        spans = []
        spans.append((0, start + TILE))
        halves = []
        for half in (0, 1):
            mine = first if half == 0 else ~first
            head = pl.ds(2 * pair + half, 1)
            halves.append(
                (
                    jnp.where(mine, q_pair, BF16(0)),
                    jnp.where(mine, g_pair, BF16(0)),
                    lse_t_ref[head, qrows],
                    inner_ref[head, qrows],
                )
            )
        dqs = [None, None]
        for lo, hi in spans:
            k_pos = lo + lax.broadcasted_iota(jnp.int32, (hi - lo, TILE), 0)
            visible = k_pos >= low
            if hi > start:
                visible = visible & (k_pos <= q_pos)
            keys = slice(base + lo, base + hi)
            k_pair = qkv_ref[keys, pair_cols(pair, 1)]
            v_pair = qkv_ref[keys, pair_cols(pair, 2)]
            dk = dv = None
            for half, (q_half, g_half, lse, inner) in enumerate(halves):
                s = jnp.where(visible, dot_nt(k_pair, q_half), NEG)
                p = jnp.exp(s - lse)
                ds = (p * (dot_nt(v_pair, g_half) - inner)).astype(BF16)
                part_v, part_k = dot(p.astype(BF16), g_half), dot(ds, q_half)
                dv = part_v if dv is None else dv + part_v
                dk = part_k if dk is None else dk + part_k
                part_q = dot(k_t[half * HEAD_DIM : (half + 1) * HEAD_DIM, lo:hi], ds)
                dqs[half] = part_q if dqs[half] is None else dqs[half] + part_q
            if qb:
                dk_ref[0:start, :] += dk[0:start]
                dv_ref[0:start, :] += dv[0:start]
            dk_ref[start:hi, :] = dk[start:hi]
            dv_ref[start:hi, :] = dv[start:hi]
        dq = jnp.transpose(jnp.concatenate(dqs, axis=0)) * (HEAD_DIM**-0.5)
        g_qkv_ref[qrows, pair_cols(pair, 0)] = dq.astype(BF16)
    all_rows = slice(base, base + length)
    g_qkv_ref[all_rows, pair_cols(pair, 1)] = dk_ref[0:length, :].astype(BF16)
    g_qkv_ref[all_rows, pair_cols(pair, 2)] = dv_ref[0:length, :].astype(BF16)


def ln1_back_tile(x_ref, g_mid_ref, table_ref, w_ref, g_qkv_ref, gx_ref, ln_sums_ref, base, t):
    rows = rows_of(base, t)
    g_qkv = g_qkv_ref[rows, :]
    g_a1 = dot_nt(g_qkv, w_ref[:, 0 : 3 * D])
    own = rows_of(0, t)
    n, rstd = normalize(x_ref[own, :].astype(F32))
    gx_ref[own, :] = g_mid_ref[rows, :] + norm_backward(
        g_a1, n, rstd, table_ref[LN1G : LN1G + 1, :]
    )
    ln_sums_ref[0:1, :] += colsum(g_a1 * n)
    ln_sums_ref[1:2, :] += colsum(g_a1)


def qv_sums(g_qkv_ref, sums_ref, g):
    for row, part in ((QB, 0), (VB, 2)):
        sums_ref[row : row + 1, vector_cols(g)] = colsum(g_qkv_ref[:, group_cols(g, part)].astype(F32))


def backward_kernel(
    ssplit,
    lsplit,
    xs,
    xl,
    table_ref,
    w_ref,
    a1_ref,
    qkv_ref,
    att_ref,
    lse_t_ref,
    g_mid_ref,
    gxs_ref,
    gxl_ref,
    dwp_ref,
    dwq_ref,
    sums_ref,
    g_attn_ref,
    g_att_ref,
    g_qkv_ref,
    inner_ref,
    dk_ref,
    dv_ref,
):
    sums_ref[...] = jnp.zeros_like(sums_ref)
    rows = xs.shape[0] + xl.shape[0]
    lax.fori_loop(
        0,
        rows // TILE,
        lambda t, c: (
            proj_back_tile(g_mid_ref, w_ref, att_ref, g_attn_ref, g_att_ref, inner_ref, sums_ref, t),
            c,
        )[1],
        0,
    )
    dwp_ref[...] = dot_tn(att_ref[...], g_attn_ref[...])

    def pair_step(pair, c):
        for split, x_ref, base in ((ssplit[0], xs, 0), (lsplit[0], xl, xs.shape[0])):
            attend_back_pair(
                split, qkv_ref, g_att_ref, lse_t_ref, inner_ref, g_qkv_ref, dk_ref, dv_ref, base, x_ref.shape[0], pair
            )
        return c

    lax.fori_loop(0, PAIRS, pair_step, 0)
    for g in range(GROUPS):
        qv_sums(g_qkv_ref, sums_ref, g)
    for j in range(3):
        dwq_ref[:, j * D : (j + 1) * D] = dot_tn(a1_ref[...], g_qkv_ref[:, j * D : (j + 1) * D])
    for x_ref, gx_ref, base in ((xs, gxs_ref, 0), (xl, gxl_ref, xs.shape[0])):
        lax.fori_loop(
            0,
            x_ref.shape[0] // TILE,
            lambda t, c: (
                ln1_back_tile(
                    x_ref, g_mid_ref, table_ref, w_ref, g_qkv_ref, gx_ref, sums_ref.at[LN1G : LN1B + 1], base, t
                ),
                c,
            )[1],
            0,
        )


def backward_local(ssplit, lsplit, xs, xl, table, w_attn, a1, qkv, att, lse_t, g_mid):
    rows = xs.shape[0] + xl.shape[0]
    return pl.pallas_call(
        backward_kernel,
        out_shape=(
            jax.ShapeDtypeStruct(xs.shape, F32),
            jax.ShapeDtypeStruct(xl.shape, F32),
            jax.ShapeDtypeStruct((D, D), F32),
            jax.ShapeDtypeStruct((D, 3 * D), F32),
            jax.ShapeDtypeStruct((8, D), F32),
        ),
        in_specs=[SM, SM] + [VM] * 9,
        out_specs=[VM] * 5,
        scratch_shapes=[
            pltpu.VMEM((rows, D), BF16),
            pltpu.VMEM((rows, D), BF16),
            pltpu.VMEM((rows, 3 * D), BF16),
            pltpu.VMEM((16, rows), F32),
            pltpu.VMEM((xl.shape[0], 128), F32),
            pltpu.VMEM((xl.shape[0], 128), F32),
        ],
        compiler_params=pltpu.CompilerParams(vmem_limit_bytes=VMEM_LIMIT),
        name="attention_backward",
    )(ssplit, lsplit, xs, xl, table, w_attn, a1, qkv, att, lse_t, g_mid)


MESH = pl.DeviceIdType.MESH
COLS, DEPTH = 4, 4


class Place:
    def __init__(self):
        q, f = lax.axis_index("dp"), lax.axis_index("fsdp")
        z = lax.div(f, 2)
        self.core = lax.rem(f, 2)
        self.col = [q, q + 1 - 2 * lax.rem(q, 2), lax.rem(q + 2, 4), 3 - q]
        self.depth = [lax.rem(z + k, DEPTH) for k in range(DEPTH)]
        self.index = q * 2 * DEPTH + f
        self.partner = (q, 2 * z + 1 - self.core)
        self.x = (self.col[1], f)
        self.y = (self.col[2], f)
        self.across = (self.col[3], f)
        self.over = [(q, 2 * d + 1 - self.core) for d in self.depth]
        self.along = [(q, 2 * d + self.core) for d in self.depth]

    def greet(self):
        barrier = pltpu.get_barrier_semaphore()
        others = [self.partner, self.x, self.y, self.across] + self.along[1:] + self.over[1:]
        for device in others:
            pl.semaphore_signal(barrier, inc=1, device_id=device, device_id_type=MESH)
        return lambda: pl.semaphore_wait(barrier, len(others))


def hooks(table):
    def run(i):
        for n, actions in table.items():

            @pl.when(i == n)
            def _():
                for action, *args in actions:
                    action(*args)

    return run


def remote(src, dst, send, recv, device):
    return pltpu.make_async_remote_copy(
        src_ref=src, dst_ref=dst, send_sem=send, recv_sem=recv, device_id=device, device_id_type=MESH
    )


def at(start, size, step):
    return pl.ds(pl.multiple_of(start, step), size)


Z, X, Y, VIA_X, VIA_Y, PAIR = 0, 3, 4, 5, 6, 7
N_GATHER = 11


class Gather:
    def __init__(self, place, spot, own, send, recv):
        self.place, self.own, self.send, self.recv = place, own, send, recv
        self.spot = spot

    def share(self, k):
        return self.spot(self.place.col[0], self.place.depth[k], 1, self.place.core)

    def column(self, r, z=0, n=DEPTH):
        return self.spot(self.place.col[r], z, n, self.place.core)

    def along(self, k, arriving=False):
        n = (k if arriving else DEPTH - k) - 1
        src, dst = (self.share(k),) * 2 if arriving else (self.own, self.share(0))
        return remote(src, dst, self.send.at[Z + k - 1], self.recv.at[Z + n], self.place.along[k])

    def near(self, kind, r):
        device = self.place.x if kind == X else self.place.y
        ref = self.column(r)
        return remote(ref, ref, self.send.at[kind], self.recv.at[kind], device)

    def across(self, kind, r):
        device, z = (self.place.x, DEPTH // 2) if kind == VIA_X else (self.place.y, 0)
        ref = self.column(r, z, DEPTH // 2)
        return remote(ref, ref, self.send.at[kind], self.recv.at[kind], device)

    def pair(self, r, arriving=False):
        core = 1 - self.place.core if arriving else self.place.core
        ref = self.spot(self.place.col[r], 0, DEPTH, core)
        return remote(ref, ref, self.send.at[PAIR + r], self.recv.at[PAIR + r], self.place.partner)

    def a(self):
        for k in (1, 3, 2):
            self.along(k).start()

    def b(self):
        for k in (1, 3, 2):
            self.along(k, True).wait_recv()
        self.near(X, 0).start()
        self.near(Y, 0).start()
        self.pair(0).start()

    def c(self):
        self.near(X, 1).wait_recv()
        self.across(VIA_Y, 1).start()
        self.pair(1).start()
        self.near(Y, 2).wait_recv()
        self.across(VIA_X, 2).start()
        self.pair(2).start()

    def d(self):
        self.across(VIA_Y, 3).wait_recv()
        self.across(VIA_X, 3).wait_recv()
        self.pair(3).start()

    def e(self):
        for r in range(COLS):
            self.pair(r, True).wait_recv()

    def end(self):
        for k in range(1, DEPTH):
            self.along(k).wait_send()
        self.near(X, 0).wait_send()
        self.near(Y, 0).wait_send()
        self.across(VIA_Y, 1).wait_send()
        self.across(VIA_X, 2).wait_send()
        for r in range(COLS):
            self.pair(r).wait_send()


def wide_spot(full, start, half):
    def spot(col, z, n, core):
        rows = at(col * (48 * DEPTH) + z * 48, 48 * n, 16)
        return full.at[rows, at(start + core * half, half, 128)]

    return spot


def tall_spot(full, start, size):
    def spot(col, z, n, core):
        return full.at[col, pl.ds(z, n), core, pl.ds(start, size)]

    return spot


def picks(place, size):
    start = place.index * size
    at_row, at_lane = lax.div(start, D), lax.rem(start, D)
    lane = lax.broadcasted_iota(jnp.int32, (size, D), 1)
    pick = lax.broadcasted_iota(jnp.int32, (size, D), 0) + at_lane == lane
    return at_row, jnp.where(pick, 1.0, 0.0)


def place_vectors(place, vectors, out):
    v = [ref[...].astype(F32) for ref in vectors]
    _, pick = picks(place, 24)
    short = jnp.concatenate([v[0], v[1], v[3], v[4], v[5], v[6], jnp.zeros((2, 24), F32)], axis=0)
    short = dot(short.astype(BF16), pick.astype(BF16))
    at_row, pick = picks(place, 48)
    pairs = jnp.concatenate([v[2], v[7][:, 0:48], v[7][:, 48:96], jnp.zeros((5, 48), F32)], axis=0)
    pairs = dot(pairs.astype(BF16), pick.astype(BF16))
    mine = lax.broadcasted_iota(jnp.int32, (2, D), 0) == at_row
    two = [jnp.where(mine, pairs[n : n + 1], 0.0) for n in range(3)]
    lines = [short[0:2], two[0], short[2:6], two[1], two[2], jnp.zeros((4, D), F32)]
    out[...] = jnp.concatenate(lines, axis=0).astype(out.dtype)


SUM_STEPS = 7
SUM_STAGES = ((0,), (1, 2, 3), (4, 5, 6))


class TableSum:
    def __init__(self, place, total, got, send, recv):
        self.place, self.total, self.got, self.send, self.recv = place, total, got, send, recv

    def copy(self, step, arriving=False):
        place = self.place
        if step == 0:
            device, n, stage = place.partner, 0, 0
        elif step <= 3:
            device, n, stage = place.along[step], (step if arriving else 4 - step), 1
        else:
            device, n, stage = (place.x, place.y, place.across)[step - 4], step, 2
        return remote(self.total.at[stage], self.got.at[n], self.send.at[step], self.recv.at[n], device)

    def begin(self, stage):
        for step in SUM_STAGES[stage]:
            self.copy(step).start()

    def add(self, stage):
        for step in SUM_STAGES[stage]:
            self.copy(step, True).wait_recv()
        total = self.total[stage]
        for step in SUM_STAGES[stage]:
            total = total + self.got[step]
        self.total[stage + 1] = total

    def next(self, stage):
        self.add(stage)
        self.begin(stage + 1)

    def end(self):
        for step in range(SUM_STEPS):
            self.copy(step).wait_send()


def forward_gather_kernel(
    ssplit,
    lsplit,
    xs_hbm,
    xl_hbm,
    wqkv,
    wproj,
    wfc,
    wout,
    v0,
    v1,
    v2,
    v3,
    v4,
    v5,
    v6,
    v7,
    table_ref,
    wa_hbm,
    wf_hbm,
    wo_hbm,
    slab_f1,
    a1_hbm,
    qkv_hbm,
    att_hbm,
    lse_t_ref,
    mid_hbm,
    xs,
    xl,
    wa,
    a1_ref,
    qkv_ref,
    att_ref,
    mid_ref,
    slab_f,
    swap_out,
    swap_in,
    total,
    got,
    io_sem,
    swap_send,
    swap_recv,
    sum_send,
    sum_recv,
    g_send,
    g_recv,
):
    place = Place()
    welcome = place.greet()
    loads = [pltpu.make_async_copy(xs_hbm, xs, io_sem.at[0]), pltpu.make_async_copy(xl_hbm, xl, io_sem.at[1])]
    for copy in loads:
        copy.start()
    part = D // 2
    first = place.core == 0
    swaps = [
        remote(swap_out.at[n], swap_in.at[n], swap_send.at[n], swap_recv.at[n], place.partner)
        for n in range(2)
    ]
    sums = TableSum(place, total, got, sum_send, sum_recv)

    def halves(share, step):
        starts = range(0, share.shape[1], 2 * step)
        lefts = jnp.concatenate([share[:, i : i + step] for i in starts], axis=1)
        rights = jnp.concatenate([share[:, i + step : i + 2 * step] for i in starts], axis=1)
        return jnp.where(first, lefts, rights), jnp.where(first, rights, lefts)

    cols = [wqkv[:, j * D + g * GROUP : j * D + (g + 1) * GROUP] for g in range(GROUPS) for j in range(3)]
    keep_a, swap_out[0] = halves(jnp.concatenate(cols + [wproj[...]], axis=1).astype(F32), part)
    welcome()
    swaps[0].start()
    place_vectors(place, (v0, v1, v2, v3, v4, v5, v6, v7), total.at[0])
    sums.begin(0)
    sums.next(0)

    def joined(n, mine):
        swaps[n].wait_recv()
        other = swap_in[n]
        top, bottom = jnp.where(first, mine, other), jnp.where(first, other, mine)
        return jnp.concatenate([top, bottom], axis=0).astype(BF16)

    chip = place.col[0] * DEPTH + place.depth[0]
    rows = at(chip * 48, 48, 16)
    share = joined(0, keep_a)
    ps = []
    for n in range(4):
        cols = at(n * D + place.core * part, part, 128)
        wa[rows, cols] = share[:, n * part : (n + 1) * part]
        ps.append(Gather(place, wide_spot(wa, n * D, part), wa.at[rows, cols], g_send.at[n], g_recv.at[n]))
    ps.append(Gather(place, wide_spot(wf_hbm, 0, D), slab_f, g_send.at[4], g_recv.at[4]))
    ps.append(Gather(place, tall_spot(wo_hbm, 0, 48), wout.at[:, pl.ds(0, 48)], g_send.at[5], g_recv.at[5]))
    h0, h1, h2, pp, f0, o0 = ps
    for piece in ps[:4]:
        piece.a()
    keep_f, swap_out[1] = halves(by_pieces(wfc[...].astype(F32)), D)
    swaps[1].start()
    sums.next(1)
    h0.b()
    share = joined(1, keep_f)
    slab_f[...] = share[:, 0:D]
    slab_f1[...] = share[:, D : 2 * D]
    for piece in ps[4:]:
        piece.a()
    own_copies = []
    for n, piece in enumerate((f0, o0)):
        copy = pltpu.make_async_copy(piece.own, piece.share(0), io_sem.at[2 + n])
        copy.start()
        own_copies.append(copy)
    sums.add(2)
    table_ref[...] = total[3].astype(F32)
    for copy in loads + own_copies:
        copy.wait()
    groups = group_refs(xs, xl)
    short_tiles, long_tiles = xs.shape[0] // TILE, xl.shape[0] // TILE
    base = groups[1][1]
    loop(short_tiles, lambda t: norm_tile(xs, table_ref, a1_ref, 0, t))
    h0.c()
    h1.b()
    loop(2, lambda t: norm_tile(xl, table_ref, a1_ref, base, t))
    h0.d()
    h2.b()
    loop(long_tiles - 2, lambda t: norm_tile(xl, table_ref, a1_ref, base, t + 2))
    h0.e()
    short, rows = xs.shape[0], a1_ref.shape[0]
    store_a1 = pltpu.make_async_copy(a1_ref, a1_hbm, io_sem.at[4])
    store_wa = pltpu.make_async_copy(wa, wa_hbm, io_sem.at[5])
    store_mid = [
        pltpu.make_async_copy(mid_ref.at[part], mid_hbm.at[part], io_sem.at[6 + n])
        for n, part in enumerate((pl.ds(0, short), pl.ds(short, rows - short)))
    ]

    def store_qkv(g):
        cols = pl.ds(pl.multiple_of(g * D, 128), D)
        return pltpu.make_async_copy(qkv_ref.at[:, cols], qkv_hbm.at[:, cols], io_sem.at[8 + g])

    def store_att(g):
        cols = pl.ds(pl.multiple_of(g * GROUP, 128), GROUP)
        return pltpu.make_async_copy(att_ref.at[:, cols], att_hbm.at[:, cols], io_sem.at[11 + g])

    store_a1.start()
    lse_t_ref[...] = jnp.zeros_like(lse_t_ref)
    before_group = hooks({1: ((h1.e,),), 2: ((h2.e,),)})
    after_qkv = hooks({0: ((h1.c,), (pp.b,)), 1: ((o0.b,),)})
    after_short = hooks({1: ((f0.b,),), 3: ((pp.d,), (f0.c,)), 4: ((o0.c,),)})
    after_long = hooks(
        {
            0: ((h1.d,), (h2.c,)),
            1: ((pp.c,), (h2.d,)),
            4: ((f0.d,), (pp.e,), (store_wa.start,)),
            5: ((o0.d,), (f0.e,)),
        }
    )

    def group_step(g):
        before_group(g)
        loop(a1_ref.shape[0] // TILE, lambda t: qkv_tile(table_ref, wa, a1_ref, qkv_ref, g, t))
        store_qkv(g).start()
        after_qkv(g)

        def pair_step(j):
            pair = 2 * g + j
            attend_pair(ssplit[0], qkv_ref, att_ref, lse_t_ref, 0, xs.shape[0], pair)
            after_short(pair)
            attend_pair(lsplit[0], qkv_ref, att_ref, lse_t_ref, xs.shape[0], xl.shape[0], pair)
            after_long(pair)

        loop(2, pair_step)
        store_att(g).start()

    loop(GROUPS, group_step)
    for (x_ref, base), store in zip(groups, store_mid):
        loop(
            x_ref.shape[0] // TILE,
            lambda t: mid_tile(x_ref, table_ref, wa, att_ref, mid_ref, base, t),
        )
        store.start()
    o0.e()
    for swap in swaps:
        swap.wait_send()
    sums.end()
    for piece in ps:
        piece.end()
    for copy in [store_a1, store_wa] + store_mid:
        copy.wait()
    for g in range(GROUPS):
        store_qkv(g).wait()
        store_att(g).wait()


ANY = pl.BlockSpec(memory_space=pl.ANY)


def forward_gather(ssplit, lsplit, xs, xl, wqkv, wproj, wfc, wout, vectors):
    rows = xs.shape[0] + xl.shape[0]
    wide = wqkv.shape[1] + wproj.shape[1]
    half_out = jax.ShapeDtypeStruct((COLS, DEPTH, 2) + SLAB, BF16)
    sem = pltpu.SemaphoreType.DMA
    return pl.pallas_call(
        forward_gather_kernel,
        out_shape=(
            jax.ShapeDtypeStruct((16, D), F32),
            jax.ShapeDtypeStruct((D, wide), BF16),
            jax.ShapeDtypeStruct((D, HALF), BF16),
            half_out,
            jax.ShapeDtypeStruct(SLAB, BF16),
            jax.ShapeDtypeStruct((rows, D), BF16),
            jax.ShapeDtypeStruct((rows, 3 * D), BF16),
            jax.ShapeDtypeStruct((rows, D), BF16),
            jax.ShapeDtypeStruct((16, rows), F32),
            jax.ShapeDtypeStruct((rows, D), F32),
        ),
        in_specs=[SM, SM, ANY, ANY] + [VM] * 12,
        out_specs=[VM, ANY, ANY, ANY, VM, ANY, ANY, ANY, VM, ANY],
        scratch_shapes=[
            pltpu.VMEM(xs.shape, BF16),
            pltpu.VMEM(xl.shape, BF16),
            pltpu.VMEM((D, wide), BF16),
            pltpu.VMEM((rows, D), BF16),
            pltpu.VMEM((rows, 3 * D), BF16),
            pltpu.VMEM((rows, D), BF16),
            pltpu.VMEM((rows, D), F32),
            pltpu.VMEM(SLAB, BF16),
            pltpu.VMEM((2, 24, wide // 2), F32),
            pltpu.VMEM((2, 24, wide // 2), F32),
            pltpu.VMEM((4, 16, D), BF16),
            pltpu.VMEM((SUM_STEPS, 16, D), BF16),
            sem((14,)),
            sem((2,)),
            sem((2,)),
            sem((SUM_STEPS,)),
            sem((SUM_STEPS,)),
            sem((6, N_GATHER)),
            sem((6, N_GATHER)),
        ],
        compiler_params=pltpu.CompilerParams(
            vmem_limit_bytes=VMEM_LIMIT, collective_id=0, has_side_effects=True
        ),
        name="attention_forward_gather",
    )(ssplit, lsplit, xs, xl, wqkv, wproj, wfc, wout[None], *[v.reshape(1, -1) for v in vectors])


R_PAIR, R_X, R_Y, R_XB, R_YB, R_Z = 0, 4, 6, 8, 9, 10
N_REDUCE = 13
ORDER = (3, 1, 2, 0)


class Reduce:
    def __init__(self, place, src, own, total, xa, ya, xb, yb, zr, send, recv, own_sem):
        self.place, self.src, self.own, self.total = place, src, own, total
        self.xa, self.ya, self.xb, self.yb, self.zr = xa, ya, xb, yb, zr
        self.send, self.recv, self.own_sem = send, recv, own_sem

    def slabs(self, r, core):
        return self.src.at[pl.ds(self.place.col[r] * DEPTH, DEPTH), core]

    def pair(self, r):
        place = self.place
        n = R_PAIR + r
        return remote(
            self.slabs(r, 1 - place.core), self.total.at[r], self.send.at[n], self.recv.at[n], place.partner
        )

    def load(self, r):
        slot = ORDER.index(r) % 2
        return pltpu.make_async_copy(self.slabs(r, self.place.core), self.own.at[slot], self.own_sem.at[r])

    def to_x(self, n):
        src = self.total.at[(1, 3)[n], pl.ds(0, 2)]
        return remote(src, self.xa.at[n], self.send.at[R_X + n], self.recv.at[R_X + n], self.place.x)

    def to_y(self, n):
        src = self.total.at[(2, 3)[n], pl.ds(2, 2)]
        return remote(src, self.ya.at[n], self.send.at[R_Y + n], self.recv.at[R_Y + n], self.place.y)

    def to_xb(self):
        src = self.total.at[1, pl.ds(2, 2)]
        return remote(src, self.xb, self.send.at[R_XB], self.recv.at[R_XB], self.place.x)

    def to_yb(self):
        src = self.total.at[2, pl.ds(0, 2)]
        return remote(src, self.yb, self.send.at[R_YB], self.recv.at[R_YB], self.place.y)

    def to_z(self, k, arriving=False):
        n = (k if arriving else DEPTH - k) - 1
        src = self.total.at[0, self.place.depth[k]]
        return remote(
            src, self.zr.at[n], self.send.at[R_Z + k - 1], self.recv.at[R_Z + n], self.place.along[k]
        )

    def begin(self, loads=True):
        for r in ORDER:
            self.pair(r).start()
        if loads:
            self.begin_loads()

    def begin_loads(self):
        if self.own is not None:
            for r in ORDER[:2]:
                self.load(r).start()

    def chip(self, r):
        if self.own is not None:
            self.load(r).wait()
            mine = self.own[ORDER.index(r) % 2]
        else:
            mine = self.src[pl.ds(self.place.col[r] * DEPTH, DEPTH), self.place.core]
        self.pair(r).wait_recv()
        self.total[r] = self.total[r] + mine
        if self.own is not None and ORDER.index(r) < 2:
            self.load(ORDER[ORDER.index(r) + 2]).start()
        if r == 1:
            self.to_x(1).start()
            self.to_x(0).start()
        if r == 2:
            self.to_y(1).start()
            self.to_y(0).start()

    def chip_all(self):
        for r in ORDER:
            self.chip(r)

    def cross(self):
        self.to_x(1).wait_recv()
        self.total[2, 0:2] = self.total[2, 0:2] + self.xa[1]
        self.to_yb().start()
        self.to_y(1).wait_recv()
        self.total[1, 2:4] = self.total[1, 2:4] + self.ya[1]
        self.to_xb().start()

    def column(self):
        self.to_x(0).wait_recv()
        self.to_yb().wait_recv()
        add = lambda a, b, c: (a.astype(F32) + b.astype(F32) + c.astype(F32)).astype(BF16)
        self.total[0, 0:2] = add(self.total[0, 0:2], self.xa[0], self.yb[...])
        self.to_y(0).wait_recv()
        self.to_xb().wait_recv()
        self.total[0, 2:4] = add(self.total[0, 2:4], self.ya[0], self.xb[...])
        for k in (2, 1, 3):
            self.to_z(k).start()

    def result(self):
        out = self.total[0, self.place.depth[0]].astype(F32)
        for k in range(1, DEPTH):
            self.to_z(k, True).wait_recv()
            out = out + self.zr[k - 1].astype(F32)
        return out

    def end(self):
        self.end_pairs()
        self.end_rest()

    def end_pairs(self):
        for r in range(COLS):
            self.pair(r).wait_send()

    def end_rest(self):
        for n in range(2):
            self.to_x(n).wait_send()
            self.to_y(n).wait_send()
        self.to_xb().wait_send()
        self.to_yb().wait_send()
        for k in range(1, DEPTH):
            self.to_z(k).wait_send()


class ReduceAtOnce(Reduce):
    def __init__(self, place, src, total, other, zr, send, recv):
        super().__init__(place, src, None, total, None, None, None, None, zr, send, recv, None)
        self.other = other

    def to_column(self, r):
        device = (self.place.x, self.place.y, self.place.across)[r - 1]
        n = R_X + r - 1
        return remote(self.total.at[r], self.other.at[r - 1], self.send.at[n], self.recv.at[n], device)

    def chip(self, r):
        mine = self.src[pl.ds(self.place.col[r] * DEPTH, DEPTH), self.place.core]
        self.pair(r).wait_recv()
        self.total[r] = self.total[r] + mine
        if r:
            self.to_column(r).start()

    def column(self):
        out = self.total[0].astype(F32)
        for r in range(1, COLS):
            self.to_column(r).wait_recv()
            out = out + self.other[r - 1].astype(F32)
        self.total[0] = out.astype(BF16)
        for k in (2, 1, 3):
            self.to_z(k).start()

    def end_rest(self):
        for r in range(1, COLS):
            self.to_column(r).wait_send()
        for k in range(1, DEPTH):
            self.to_z(k).wait_send()


class LastSum:
    def __init__(self, place, total, got, send, recv):
        self.place, self.total, self.got, self.send, self.recv = place, total, got, send, recv

    def copy(self, n, arriving=False):
        place = self.place
        if n < 3:
            device, m = place.along[n + 1], (n if arriving else 2 - n)
        elif n < 6:
            device, m = place.over[n - 2], (n if arriving else 8 - n)
        else:
            device, m = (place.partner, place.x, place.y, place.across)[n - 6], n
        stage = 0 if n < 7 else 1
        return remote(self.total.at[stage], self.got.at[m], self.send.at[n], self.recv.at[m], device)

    def begin(self, stage):
        for n in (range(7), range(7, 10))[stage]:
            self.copy(n).start()

    def add(self, stage):
        total = self.total[stage]
        for n in (range(7), range(7, 10))[stage]:
            self.copy(n, True).wait_recv()
            total = total + self.got[n]
        self.total[stage + 1] = total

    def end(self):
        for n in range(10):
            self.copy(n).wait_send()


def take(lines, pick):
    return lax.dot_general(
        lines, pick, (((1,), (1,)), ((), ())), preferred_element_type=F32, precision=lax.Precision.HIGHEST
    )


def take_vectors(place, table, outs):
    _, pick = picks(place, 24)
    short = take(table[0:8, :], pick)
    for n, row in ((0, LN1G), (1, LN1B), (3, PROJB), (4, LN2G), (5, LN2B), (6, OUTB)):
        outs[n][...] = short[row : row + 1]
    at_row, pick = picks(place, 48)
    mine = lax.broadcasted_iota(jnp.int32, (2, D), 0) == at_row
    lines = [
        jnp.sum(jnp.where(mine, table[row : row + 2, :], 0.0), axis=0, keepdims=True) for row in (QB, FCB, FCB + 2)
    ]
    pairs = take(jnp.concatenate(lines + [jnp.zeros((5, D), F32)], axis=0), pick)
    outs[2][...] = pairs[0:1]
    outs[7][...] = jnp.concatenate([pairs[1:2], pairs[2:3]], axis=1)


def small_slabs(whole):
    devices, half = 2 * COLS * DEPTH, D // 2
    left = whole[:, 0:half].reshape(devices, 24, half)
    right = whole[:, half:D].reshape(devices, 24, half)
    both = jnp.concatenate([left, right], axis=1).astype(BF16)
    return both.reshape(COLS * DEPTH, 2, 48, half)


HALF = FF // 2
SLAB = (48, D)


def by_pieces(w):
    size = w.shape[1] // 64
    cuts = [w[:, (2 * i + n) * size : (2 * i + n + 1) * size] for n in range(2) for i in range(32)]
    return jnp.concatenate(cuts, axis=1)


def from_pieces(first, second):
    size = first.shape[1] // 32
    cuts = [w[:, i * size : (i + 1) * size] for i in range(32) for w in (first, second)]
    return jnp.concatenate(cuts, axis=1)


def mlp_half_tile(n, t, refs):
    mid_ref, cot_ref, a2_ref, g_mlp_ref, act_ref, g_pre_ref, acc_ref, acc_g_ref, wf, wo, table_ref, sums_ref = refs
    rows = rows_of(0, t)
    gain = table_ref[LN2G : LN2G + 1, :]
    if n == 0:
        n2, _ = normalize(mid_ref[rows, :])
        a2 = (n2 * gain + table_ref[LN2B : LN2B + 1, :]).astype(BF16)
        g_mlp = (BRANCH * cot_ref[rows, :].astype(F32)).astype(BF16)
        a2_ref[rows, :] = a2
        g_mlp_ref[rows, :] = g_mlp
        sums_ref[2:3, :] += colsum(g_mlp.astype(F32))
    else:
        a2 = a2_ref[rows, :]
        g_mlp = g_mlp_ref[rows, :]
    out = None
    g_a2 = None
    for j in range(HALF // D):
        cols = slice(j * D, (j + 1) * D)
        row = 2 * n + j
        wf_j = wf[n, :, cols]
        wo_j = wo[n, 2 * j : 2 * j + 2].reshape(D, D)
        pre = dot(a2, wf_j) + table_ref[FCB + row : FCB + row + 1, :]
        g_act = dot_nt(g_mlp, wo_j)
        square = pre * pre
        th = jnp.tanh(pre * (GELU_A + (GELU_A * GELU_B) * square))
        half = 0.5 + 0.5 * th
        act = (pre * half).astype(BF16)
        slope = half + pre * (0.5 - 0.5 * th * th) * (GELU_A + (3 * GELU_A * GELU_B) * square)
        g_pre = (g_act * slope).astype(BF16)
        act_ref[rows, cols] = act
        g_pre_ref[rows, cols] = g_pre
        sums_ref[3 + row : 4 + row, :] += colsum(g_pre.astype(F32))
        part, part_g = dot(act, wo_j), dot_nt(g_pre, wf_j)
        out = part if out is None else out + part
        g_a2 = part_g if g_a2 is None else g_a2 + part_g
    if n == 0:
        acc_ref[rows, :] = out
        acc_g_ref[rows, :] = g_a2
        return
    out = acc_ref[rows, :] + out
    g_a2 = acc_g_ref[rows, :] + g_a2
    mid = mid_ref[rows, :]
    n2, rstd = normalize(mid)
    g_out = cot_ref[rows, :].astype(F32)
    cot_ref[rows, :] = (mid + BRANCH * (out + table_ref[OUTB : OUTB + 1, :])).astype(BF16)
    mid_ref[rows, :] = g_out + norm_backward(g_a2, n2, rstd, gain)
    sums_ref[0:1, :] += colsum(g_a2 * n2)
    sums_ref[1:2, :] += colsum(g_a2)


def out_slabs(act_ref, g_mlp_ref, dw_o):
    for j in range(HALF // D):
        res = dot_tn(act_ref[:, j * D : (j + 1) * D], g_mlp_ref[...])
        dw_o[8 * j : 8 * j + 8] = res.astype(BF16).reshape(8, 2, *SLAB)


def fc_slabs(a2_ref, g_pre_ref, dw_f):
    left = dot_tn(a2_ref[...], g_pre_ref[:, 0:D]).reshape(32, 24, D)
    right = dot_tn(a2_ref[...], g_pre_ref[:, D : 2 * D]).reshape(32, 24, D)
    dw_f[...] = jnp.concatenate([left, right], axis=1).astype(BF16).reshape(dw_f.shape)


def mlp_exchange_kernel(
    mid_hbm,
    cs_hbm,
    cl_hbm,
    table_ref,
    wf0_hbm,
    wo0_hbm,
    slab_f,
    wout,
    os_hbm,
    ol_hbm,
    g_mid_hbm,
    sums_ref,
    d_out0,
    d_fc0,
    so_hbm,
    sf_hbm,
    mid_ref,
    cot_ref,
    a2_ref,
    g_mlp_ref,
    act_ref,
    g_pre_ref,
    acc_ref,
    acc_g_ref,
    wf,
    wo,
    dw_o,
    dw_f,
    r_total,
    r_xa,
    r_ya,
    r_xb,
    r_yb,
    r_zr,
    io_sem,
    g_send,
    g_recv,
    r_send,
    r_recv,
):
    place = Place()
    welcome = place.greet()
    short, long = cs_hbm.shape[0], cl_hbm.shape[0]
    tiles = (short + long) // TILE
    parts = (pl.ds(0, short), pl.ds(short, long))
    pairs = (
        (mid_hbm.at[parts[0]], mid_ref.at[parts[0]]),
        (cs_hbm, cot_ref.at[parts[0]]),
        (wf0_hbm, wf.at[0]),
        (wo0_hbm, wo.at[0]),
        (mid_hbm.at[parts[1]], mid_ref.at[parts[1]]),
        (cl_hbm, cot_ref.at[parts[1]]),
    )
    loads = [pltpu.make_async_copy(src, dst, io_sem.at[n]) for n, (src, dst) in enumerate(pairs)]
    for copy in loads:
        copy.start()
    q, z, c = place.col[0], place.depth[0], place.core
    wf[1, at((q * DEPTH + z) * 48, 48, 16), at(c * D, D, 128)] = slab_f[...]
    wo[1, q, z, c] = wout[0, 48:96]
    f1 = Gather(place, wide_spot(wf.at[1], 0, D), slab_f, g_send.at[0], g_recv.at[0])
    o1 = Gather(place, tall_spot(wo.at[1], 0, 48), wout.at[:, pl.ds(48, 48)], g_send.at[1], g_recv.at[1])
    ro, rf = [
        Reduce(
            place, src, None, r_total.at[n], r_xa.at[n], r_ya.at[n], r_xb.at[n], r_yb.at[n],
            r_zr.at[n], r_send.at[n], r_recv.at[n], None,
        )
        for n, src in enumerate((dw_o, dw_f))
    ]
    sums_ref[...] = jnp.zeros_like(sums_ref)
    welcome()
    f1.a()
    o1.a()
    for copy in loads[:4]:
        copy.wait()
    refs = (
        mid_ref, cot_ref, a2_ref, g_mlp_ref, act_ref, g_pre_ref, acc_ref, acc_g_ref, wf, wo, table_ref, sums_ref,
    )
    after = hooks({0: ((loads[4].wait,), (loads[5].wait,)), 1: ((f1.b,),), 3: ((o1.b,),), 4: ((f1.c,),)})

    def first_step(t):
        mlp_half_tile(0, t, refs)
        after(t)

    loop(tiles, first_step)
    out_slabs(act_ref, g_mlp_ref, dw_o)
    ro.begin()
    o1.c()
    fc_slabs(a2_ref, g_pre_ref, dw_f)
    rf.begin()
    f1.d()
    ro.chip_all()
    o1.d()
    f1.e()
    o1.e()

    def give_out():
        d_out0[...] = ro.result()

    after_second = hooks(
        {
            0: ((ro.cross,), (rf.chip_all,)),
            2: ((ro.column,),),
            3: ((rf.cross,),),
            5: ((rf.column,), (give_out,)),
        }
    )

    def second_step(t):
        mlp_half_tile(1, t, refs)
        after_second(t)

    loop(tiles, second_step)
    stores = [
        pltpu.make_async_copy(src, dst, io_sem.at[6 + n])
        for n, (src, dst) in enumerate(
            (
                (cot_ref.at[parts[0]], os_hbm),
                (cot_ref.at[parts[1]], ol_hbm),
                (mid_ref, g_mid_hbm),
                (dw_o, so_hbm),
                (dw_f, sf_hbm),
            )
        )
    ]
    for copy in stores[0:3]:
        copy.start()
    ro.end_pairs()
    out_slabs(act_ref, g_mlp_ref, dw_o)
    stores[3].start()
    rf.end_pairs()
    fc_slabs(a2_ref, g_pre_ref, dw_f)
    stores[4].start()
    res = rf.result()
    d_fc0[...] = jnp.concatenate([res[0:24], res[24:48]], axis=1)
    ro.end_rest()
    rf.end_rest()
    f1.end()
    o1.end()
    for copy in stores:
        copy.wait()


def reduce_buffers(n, shape):
    return [
        pltpu.VMEM((n, COLS, DEPTH) + shape, BF16),
        pltpu.VMEM((n, 2, 2) + shape, BF16),
        pltpu.VMEM((n, 2, 2) + shape, BF16),
        pltpu.VMEM((n, 2) + shape, BF16),
        pltpu.VMEM((n, 2) + shape, BF16),
        pltpu.VMEM((n, DEPTH - 1) + shape, BF16),
    ]


def mlp_exchange(mid, cs, cl, table, wf0, wo0, slab_f, wout):
    rows = mid.shape[0]
    chips = COLS * DEPTH
    sem = pltpu.SemaphoreType.DMA
    slabs = (chips, 2) + SLAB
    return pl.pallas_call(
        mlp_exchange_kernel,
        out_shape=(
            jax.ShapeDtypeStruct(cs.shape, BF16),
            jax.ShapeDtypeStruct(cl.shape, BF16),
            jax.ShapeDtypeStruct(mid.shape, F32),
            jax.ShapeDtypeStruct((8, D), F32),
            jax.ShapeDtypeStruct(SLAB, F32),
            jax.ShapeDtypeStruct((24, HALF), F32),
            jax.ShapeDtypeStruct(slabs, BF16),
            jax.ShapeDtypeStruct(slabs, BF16),
        ),
        in_specs=[ANY, ANY, ANY, VM, ANY, ANY, VM, VM],
        out_specs=[ANY, ANY, ANY, VM, VM, VM, ANY, ANY],
        scratch_shapes=[
            pltpu.VMEM((rows, D), F32),
            pltpu.VMEM((rows, D), BF16),
            pltpu.VMEM((rows, D), BF16),
            pltpu.VMEM((rows, D), BF16),
            pltpu.VMEM((rows, HALF), BF16),
            pltpu.VMEM((rows, HALF), BF16),
            pltpu.VMEM((rows, D), F32),
            pltpu.VMEM((rows, D), F32),
            pltpu.VMEM((2, D, HALF), BF16),
            pltpu.VMEM((2, COLS, DEPTH, 2) + SLAB, BF16),
            pltpu.VMEM(slabs, BF16),
            pltpu.VMEM(slabs, BF16),
            *reduce_buffers(2, SLAB),
            sem((11,)),
            sem((2, N_GATHER)),
            sem((2, N_GATHER)),
            sem((2, N_REDUCE)),
            sem((2, N_REDUCE)),
        ],
        compiler_params=pltpu.CompilerParams(
            vmem_limit_bytes=VMEM_LIMIT, collective_id=2, has_side_effects=True
        ),
        name="mlp_exchange",
    )(mid, cs, cl, table, wf0, wo0, slab_f, wout)


def backward_reduce_kernel(
    ssplit,
    lsplit,
    xs_hbm,
    xl_hbm,
    table_ref,
    wa_hbm,
    a1_hbm,
    qkv_hbm,
    att_hbm,
    lse_t_ref,
    g_mid_hbm,
    sums2_ref,
    go_hbm,
    gf_hbm,
    gxs_hbm,
    gxl_hbm,
    d0,
    d1,
    d2,
    d3,
    d4,
    d5,
    d6,
    d7,
    d_qkv,
    d_proj,
    d_fc1,
    d_out1,
    wa,
    a1_ref,
    qkv_ref,
    att_ref,
    g_mid_ref,
    g_att_ref,
    g_qkv_ref,
    inner_ref,
    dk_ref,
    dv_ref,
    big_own,
    big_total,
    big_xa,
    big_ya,
    big_xb,
    big_yb,
    big_zr,
    small_src,
    small_total,
    small_xa,
    small_ya,
    small_xb,
    small_yb,
    small_zr,
    total,
    got,
    io_sem,
    own_sem,
    r_send,
    r_recv,
    sum_send,
    sum_recv,
    ln_sums_ref,
    other,
    last_total,
    last_got,
    last_send,
    last_recv,
):
    place = Place()
    g_attn_ref = g_qkv_ref.at[:, pl.ds(0, D)]
    short, long = gxs_hbm.shape[0], gxl_hbm.shape[0]
    rows = short + long
    proj_cols = pl.ds(3 * D, D)
    qkv_cols = pl.ds(0, 3 * D)
    loads = [
        pltpu.make_async_copy(src, dst, io_sem.at[n])
        for n, (src, dst) in enumerate(
            (
                (wa_hbm.at[:, proj_cols], wa.at[:, proj_cols]),
                (g_mid_hbm, g_mid_ref),
                (att_hbm, att_ref),
                (qkv_hbm, qkv_ref),
                (a1_hbm, a1_ref),
                (wa_hbm.at[:, qkv_cols], wa.at[:, qkv_cols]),
            )
        )
    ]
    for copy in loads[:3]:
        copy.start()
    sums = TableSum(place, total, got, sum_send, sum_recv)
    sums_ref = total.at[0]
    sums_ref[...] = jnp.zeros_like(sums_ref)
    sums_ref[LN2G : LN2G + 7, :] = sums2_ref[0:7, :]
    big = [
        Reduce(
            place, src, big_own, big_total.at[n], big_xa.at[n], big_ya.at[n], big_xb.at[n],
            big_yb.at[n], big_zr.at[n], r_send.at[n], r_recv.at[n], own_sem.at[n],
        )
        for n, src in enumerate((go_hbm, gf_hbm))
    ]
    small = [
        Reduce(
            place, small_src.at[n], None, small_total.at[n], small_xa.at[n], small_ya.at[n], small_xb.at[n],
            small_yb.at[n], small_zr.at[n], r_send.at[2 + n], r_recv.at[2 + n], None,
        )
        for n in range(4)
    ]
    small[2] = ReduceAtOnce(
        place, small_src.at[2], small_total.at[2], other, small_zr.at[2], r_send.at[4], r_recv.at[4]
    )
    ro, rf = big
    rp, rh = small[3], small[0:3]
    place.greet()()
    ro.begin()
    rf.begin(False)
    for copy in loads[3:]:
        copy.start()
    last_total[...] = jnp.zeros_like(last_total)
    for copy in loads[0:3]:
        copy.wait()

    after = hooks(
        {
            0: ((ro.chip, 3),),
            1: ((ro.chip, 1),),
            2: ((ro.chip, 2),),
            3: ((ro.chip, 0), (rf.begin_loads,)),
            4: ((rf.chip, 3),),
            5: ((rf.chip, 1), (rf.chip, 2), (rf.chip, 0)),
        }
    )

    def proj_step(t):
        proj_back_tile(g_mid_ref, wa, att_ref, g_attn_ref, g_att_ref, inner_ref, sums_ref, t)
        after(t)

    loop(rows // TILE, proj_step)
    small_src[3] = small_slabs(dot_tn(att_ref[...], g_attn_ref[...]))
    rp.begin()
    x_loads = [
        pltpu.make_async_copy(xs_hbm, att_ref.at[pl.ds(0, short)], io_sem.at[6]),
        pltpu.make_async_copy(xl_hbm, att_ref.at[pl.ds(short, long)], io_sem.at[7]),
    ]
    for copy in x_loads:
        copy.start()
    for copy in loads[3:]:
        copy.wait()

    def give_out():
        d_out1[...] = ro.result()

    def give_fc():
        res = rf.result()
        d_fc1[...] = jnp.concatenate([res[0:24], res[24:48]], axis=1)

    def give_proj():
        res = rp.result()
        d_proj[:, 0 : D // 2] = res[0:24]
        d_proj[:, D // 2 : D] = res[24:48]

    def give_qkv(g):
        res = rh[g].result()
        line = jnp.concatenate([res[0:24], res[24:48]], axis=1)
        for j in range(3):
            d_qkv[:, j * D + g * 256 : j * D + g * 256 + 256] = line[:, j * 256 : j * 256 + 256]

    def heads_begin(g):
        rh[g].begin()

    after_short = hooks(
        {
            0: ((ro.cross,),),
            2: ((sums.next, 1), (rh[0].chip_all,), (rf.column,), (rp.cross,)),
            3: ((rp.column,), (give_out,)),
            1: ((sums.next, 0),),
            4: ((rh[1].chip_all,),),
            5: ((give_qkv, 0),),
        }
    )
    after_long = hooks(
        {
            0: ((sums.begin, 0), (rf.cross,), (rp.chip_all,)),
            1: ((heads_begin, 0), (ro.column,)),
            2: ((rh[0].cross,),),
            3: ((sums.add, 2), (heads_begin, 1), (rh[0].column,), (give_fc,)),
            4: ((rh[1].cross,), (give_proj,)),
            5: ((heads_begin, 2), (rh[1].column,)),
        }
    )

    def pair_step(pair):
        attend_back_pair(
            ssplit[0], qkv_ref, g_att_ref, lse_t_ref, inner_ref, g_qkv_ref, dk_ref, dv_ref, 0, short, pair
        )
        after_short(pair)
        attend_back_pair(
            lsplit[0], qkv_ref, g_att_ref, lse_t_ref, inner_ref, g_qkv_ref, dk_ref, dv_ref, short, long, pair
        )

        @pl.when(lax.rem(pair, 2) == 1)
        def _():
            g = lax.div(pair, 2)
            cols = pl.ds(pl.multiple_of(g * D, 128), D)
            small_src[g] = small_slabs(dot_tn(a1_ref[...], g_qkv_ref[:, cols]))

        after_long(pair)

    loop(PAIRS, pair_step)
    for copy in x_loads:
        copy.wait()
    after_norm = hooks({0: ((rh[2].chip_all,),), 3: ((give_qkv, 1),)})

    def norm_step(t):
        ln1_back_tile(att_ref, g_mid_ref, table_ref, wa, g_qkv_ref, g_mid_ref, ln_sums_ref, 0, t)
        after_norm(t)

    ln_sums_ref[...] = jnp.zeros_like(ln_sums_ref)
    for g in range(GROUPS):
        for r, part in enumerate((0, 2)):
            line = colsum(g_qkv_ref[:, group_cols(g, part)].astype(F32))
            ln_sums_ref[2 + r : 3 + r, vector_cols(g)] = line
    loop(short // TILE, norm_step)
    stores = [
        pltpu.make_async_copy(g_mid_ref.at[pl.ds(0, short)], gxs_hbm, io_sem.at[8]),
        pltpu.make_async_copy(g_mid_ref.at[pl.ds(short, long)], gxl_hbm, io_sem.at[9]),
    ]
    stores[0].start()
    loop(long // TILE, lambda t: norm_step(t + short // TILE))
    stores[1].start()
    lanes = D // 128
    lines = [ln_sums_ref[r : r + 1, 128 * j : 128 * j + 128] for r in range(4) for j in range(lanes)]
    last_total[0] = jnp.concatenate(lines, axis=0)
    last = LastSum(place, last_total, last_got, last_send, last_recv)
    last.begin(0)
    rh[2].column()
    final = total.at[3]
    last.add(0)
    last.begin(1)
    last.add(1)
    for r in range(4):
        final[r : r + 1, :] = jnp.concatenate(
            [last_total[2, r * lanes + j : r * lanes + j + 1, :] for j in range(lanes)], axis=1
        )
    take_vectors(place, final, (d0, d1, d2, d3, d4, d5, d6, d7))
    give_qkv(2)
    last.end()
    sums.end()
    for reduce in big + small:
        reduce.end()
    for copy in stores:
        copy.wait()


def backward_reduce(ssplit, lsplit, xs, xl, table, w_attn, a1, qkv, att, lse_t, g_mid, sums2, dwo, dwf, sizes):
    short, long = xs.shape[0], xl.shape[0]
    rows = short + long
    chips = COLS * DEPTH
    devices = 2 * chips
    big, little = SLAB, (48, D // 2)
    sem = pltpu.SemaphoreType.DMA
    return pl.pallas_call(
        backward_reduce_kernel,
        out_shape=(
            jax.ShapeDtypeStruct(xs.shape, F32),
            jax.ShapeDtypeStruct(xl.shape, F32),
            *[jax.ShapeDtypeStruct((1, n), F32) for n in sizes],
            jax.ShapeDtypeStruct((D // devices, 3 * D), F32),
            jax.ShapeDtypeStruct((D // devices, D), F32),
            jax.ShapeDtypeStruct((D // devices, HALF), F32),
            jax.ShapeDtypeStruct(SLAB, F32),
        ),
        in_specs=[SM, SM, ANY, ANY, VM, ANY, ANY, ANY, ANY, VM, ANY, VM, ANY, ANY],
        out_specs=[ANY, ANY] + [VM] * 12,
        scratch_shapes=[
            pltpu.VMEM((D, 4 * D), BF16),
            pltpu.VMEM((rows, D), BF16),
            pltpu.VMEM((rows, 3 * D), BF16),
            pltpu.VMEM((rows, D), BF16),
            pltpu.VMEM((rows, D), F32),
            pltpu.VMEM((rows, D), BF16),
            pltpu.VMEM((rows, 3 * D), BF16),
            pltpu.VMEM((16, rows), F32),
            pltpu.VMEM((long, 128), F32),
            pltpu.VMEM((long, 128), F32),
            pltpu.VMEM((2, DEPTH) + big, BF16),
            *reduce_buffers(2, big),
            pltpu.VMEM((4, chips, 2) + little, BF16),
            *reduce_buffers(4, little),
            pltpu.VMEM((4, 16, D), F32),
            pltpu.VMEM((SUM_STEPS, 16, D), F32),
            sem((10,)),
            sem((2, COLS)),
            sem((6, N_REDUCE)),
            sem((6, N_REDUCE)),
            sem((SUM_STEPS,)),
            sem((SUM_STEPS,)),
            pltpu.VMEM((8, D), F32),
            pltpu.VMEM((COLS - 1, DEPTH) + little, BF16),
            pltpu.VMEM((3, 24, 128), F32),
            pltpu.VMEM((10, 24, 128), F32),
            sem((10,)),
            sem((10,)),
        ],
        compiler_params=pltpu.CompilerParams(
            vmem_limit_bytes=BACK_VMEM, collective_id=1, has_side_effects=True
        ),
        name="attention_backward_reduce",
    )(ssplit, lsplit, xs, xl, table, w_attn, a1, qkv, att, lse_t, g_mid, sums2, dwo, dwf)


BACK_VMEM = 60 * 2**20


PARTS = 4


def hand_over_kernel(os_hbm, ol_hbm, gs_hbm, gl_hbm, *refs):
    small_in, outs = refs[:14], refs[14:30]
    buffers, smalls, joined = refs[30:34], refs[34:48], refs[48:50]
    load_sem, store_sem, small_load, small_store = refs[50:54]
    loads, stores = [], []
    for n, (src, dst, mid) in enumerate(zip((os_hbm, ol_hbm, gs_hbm, gl_hbm), outs[:4], buffers)):
        size = src.shape[0] // PARTS
        for p in range(PARTS):
            rows = pl.ds(p * size, size)
            loads.append(pltpu.make_async_copy(src.at[rows], mid.at[rows], load_sem.at[n, p]))
            stores.append(pltpu.make_async_copy(mid.at[rows], dst.at[rows], store_sem.at[n, p]))
    fetch = [pltpu.make_async_copy(small_in[n], smalls[n], small_load.at[n]) for n in range(14)]
    give = [
        pltpu.make_async_copy(src, dst, small_store.at[n])
        for n, (src, dst) in enumerate(zip(smalls[:10] + joined, outs[4:]))
    ]
    for copy in loads[:2] + fetch + loads[2:]:
        copy.start()
    for n in range(10):
        fetch[n].wait()
        give[n].start()
    for n in range(10, 14):
        fetch[n].wait()
    fc0, fc1, out0, out1 = smalls[10:]
    joined[0][...] = from_pieces(fc0[...], fc1[...])
    give[10].start()
    joined[1][0:48, :] = out0[...]
    joined[1][48:96, :] = out1[...]
    give[11].start()
    for load, store in zip(loads, stores):
        load.wait()
        store.start()
    for copy in stores + give:
        copy.wait()


def hand_over(big, small):
    shape = lambda a: jax.ShapeDtypeStruct(a.shape, a.dtype)
    buffer = lambda a: pltpu.VMEM(a.shape, a.dtype)
    sem = pltpu.SemaphoreType.DMA
    ends = (jax.ShapeDtypeStruct((24, FF), F32), jax.ShapeDtypeStruct((96, D), F32))
    return pl.pallas_call(
        hand_over_kernel,
        out_shape=(*map(shape, big), *map(shape, small[:10]), *ends),
        in_specs=[ANY] * 18,
        out_specs=[ANY] * 16,
        scratch_shapes=[
            *map(buffer, big),
            *map(buffer, small),
            *map(buffer, ends),
            sem((4, PARTS)),
            sem((4, PARTS)),
            sem((14,)),
            sem((12,)),
        ],
        compiler_params=pltpu.CompilerParams(vmem_limit_bytes=VMEM_LIMIT),
        name="hand_over",
    )(*big, *small)


AXES = ("dp", "fsdp")


def gather(x, axis=0):
    return lax.all_gather(x, AXES, axis=axis, tiled=True)


def scatter(x):
    return lax.psum_scatter(x, AXES, scatter_dimension=0, tiled=True)


def general(args, devices):
    (st, lt, ss, ls, ln1g, ln1b, wqkv, qvb, wproj, projb, ln2g, ln2b, wfc, fcb, wout, outb, sc, lc) = args
    xs, xl = st.reshape(-1, D), lt.reshape(-1, D)
    cs, cl = sc.reshape(-1, D), lc.reshape(-1, D)
    vectors = (ln1g, ln1b, qvb, projb, ln2g, ln2b, outb, fcb)
    sizes = [v.shape[0] for v in vectors]
    every = lax.all_gather(jnp.concatenate(vectors), AXES, axis=0)
    starts = [sum(sizes[:i]) for i in range(len(sizes))]
    full = [every[:, s : s + n].reshape(-1, D) for s, n in zip(starts, sizes)]
    table = jnp.concatenate(full + [jnp.zeros((4, D), BF16)]).astype(F32)
    by_group = lambda w: w.reshape(-1, 3, GROUPS, GROUP).swapaxes(1, 2).reshape(-1, 3 * D)
    w_attn = gather(jnp.concatenate([by_group(wqkv), wproj], axis=1))
    w_fc, w_out = gather(wfc), gather(wout)
    a1, qkv, att, lse_t, mid = forward_local(ss, ls, xs, xl, table, w_attn)
    out_s, out_l, g_mid, sums2, dwf, dwo = mlp_local(mid, cs, cl, table, w_fc, w_out, False)
    gxs, gxl, dwp, dwq, sums1 = backward_local(
        ss, ls, xs, xl, table, w_attn, a1, qkv, att, lse_t, g_mid
    )
    dwq = dwq.reshape(-1, GROUPS, 3, GROUP).swapaxes(1, 2).reshape(-1, 3 * D)
    return finish(args, devices, starts, sizes, out_s, out_l, gxs, gxl, sums1, sums2, dwq, dwp, dwf, dwo)


def finish(args, devices, starts, sizes, out_s, out_l, gxs, gxl, sums1, sums2, dwq, dwp, dwf, dwo):
    st, lt = args[0], args[1]
    rs = lambda x: x.reshape(devices, -1)
    small = jnp.concatenate(
        [
            rs(sums1[0]),
            rs(sums1[1]),
            rs(sums1[2:4]),
            rs(sums1[4]),
            rs(sums2[0]),
            rs(sums2[1]),
            rs(sums2[2]),
            rs(sums2[3:7]),
        ],
        axis=1,
    )
    small = scatter(small)[0]
    parts = [small[s : s + n] for s, n in zip(starts, sizes)]
    d_ln1g, d_ln1b, d_qvb, d_projb, d_ln2g, d_ln2b, d_outb, d_fcb = parts
    return (
        out_s.reshape(st.shape),
        out_l.reshape(lt.shape),
        gxs.reshape(st.shape),
        gxl.reshape(lt.shape),
        d_ln1g,
        d_ln1b,
        scatter(dwq),
        d_qvb,
        scatter(dwp),
        d_projb,
        d_ln2g,
        d_ln2b,
        scatter(dwf),
        d_fcb,
        scatter(dwo),
        d_outb,
    )


def on_torus(args):
    (st, lt, ss, ls, ln1g, ln1b, wqkv, qvb, wproj, projb, ln2g, ln2b, wfc, fcb, wout, outb, sc, lc) = args
    xs, xl = st.reshape(-1, D), lt.reshape(-1, D)
    cs, cl = sc.reshape(-1, D), lc.reshape(-1, D)
    vectors = (ln1g, ln1b, qvb, projb, ln2g, ln2b, outb, fcb)
    table, w_attn, wf0, wo0, slab_f1, a1, qkv, att, lse_t, mid = forward_gather(
        ss, ls, xs, xl, wqkv, wproj, wfc, wout, vectors
    )
    out_s, out_l, g_mid, sums2, d_out0, d_fc0, dwo, dwf = mlp_exchange(
        mid, cs, cl, table, wf0, wo0, slab_f1, wout[None]
    )
    gxs, gxl, *rest = backward_reduce(
        ss, ls, xs, xl, table, w_attn, a1, qkv, att, lse_t, g_mid, sums2, dwo, dwf, [v.shape[0] for v in vectors]
    )
    d_fc1, d_out1 = rest[10:]
    out_s, out_l, gxs, gxl, *rest = hand_over(
        (out_s, out_l, gxs, gxl), (*rest[:10], d_fc0, d_fc1, d_out0, d_out1)
    )
    d_ln1g, d_ln1b, d_qvb, d_projb, d_ln2g, d_ln2b, d_outb, d_fcb = [v.reshape(-1) for v in rest[:8]]
    d_qkv, d_proj, d_fc, d_out = rest[8:]
    return (
        out_s.reshape(st.shape),
        out_l.reshape(lt.shape),
        gxs.reshape(st.shape),
        gxl.reshape(lt.shape),
        d_ln1g,
        d_ln1b,
        d_qkv,
        d_qvb,
        d_proj,
        d_projb,
        d_ln2g,
        d_ln2b,
        d_fc,
        d_fcb,
        d_out,
        d_outb,
    )


def per_device(shape, *args):
    devices = shape["dp"] * shape["fsdp"]
    sizes = (args[0].shape[1], args[1].shape[1], args[6].shape, args[14].shape)
    if shape == {"dp": COLS, "fsdp": 2 * DEPTH} and sizes == (512, 1024, (24, 3 * D), (96, D)):
        return on_torus(args)
    return general(args, devices)


def solution(mesh):
    vec, mat, seq = P(AXES), P(AXES, None), P(AXES, None, None)
    in_specs = (seq, seq, vec, vec) + (vec, vec, mat, vec, mat, vec) * 1 + (vec, vec, mat, vec, mat, vec) + (seq, seq)
    out_specs = (seq,) * 4 + (vec, vec, mat, vec, mat, vec) * 2
    return jax.shard_map(
        functools.partial(per_device, dict(mesh.shape)),
        mesh=mesh,
        in_specs=in_specs,
        out_specs=out_specs,
        check_vma=False,
    )
```
